32 devices in a mesh: blk: 4 (over z), head: 4 (over x, core), fsdp: 2 (over y).
Axes of the slice: x: 2, y: 2, z: 4, core: 2. Of those that a mesh axis runs over, the one named last changes fastest.
Arguments:
- tokens: bfloat16 [2, 4096, 1536], P('fsdp', ('blk', 'head')), may hold values from -6 to 6
- documents: int32 [2, 4096], P('fsdp'), may hold values from 0 to 3, as said below
- routes: int32 [2, 4096, 4], P('fsdp', ('blk', 'head')), may hold values from 0 to 7, all different within a row; in each aligned block of 256 rows (0 to 255, 256 to 511, ..., all dimensions but the last counted through in order) at most 192 rows name the same one
- cotangent: bfloat16 [2, 4096, 1536], P('fsdp', ('blk', 'head')), may hold values from -6 to 6
- first_gain: bfloat16 [1536], P('fsdp'), may hold values from 0.5 to 1.5
- query_weight: bfloat16 [1536, 1536], P('fsdp'), may hold values from -0.15625 to 0.15625
- keyvalue_weight: bfloat16 [1536, 512], P('fsdp'), may hold values from -0.15625 to 0.15625
- output_weight: bfloat16 [1536, 1536], P('fsdp'), may hold values from -3 to 3
- second_gain: bfloat16 [1536], P('fsdp'), may hold values from 0.5 to 1.5
- router_weight: bfloat16 [1536, 8], P('fsdp'), may hold values from -0.078125 to 0.078125
- expert_in: bfloat16 [8, 1536, 1536], P('blk', 'fsdp'), may hold values from -0.15625 to 0.15625
- expert_out: bfloat16 [8, 768, 1536], P('blk', None, 'fsdp'), may hold values from -0.625 to 0.625
Outputs:
- block_out: bfloat16 [2, 4096, 1536], P('fsdp', ('blk', 'head'))
- tokens_grad: bfloat16 [2, 4096, 1536], P('fsdp', ('blk', 'head'))
- first_gain_grad: float32 [1536], P('fsdp')
- query_grad: float32 [1536, 1536], P('fsdp')
- keyval_grad: float32 [1536, 512], P('fsdp')
- output_grad: float32 [1536, 1536], P('fsdp')
- second_gain_grad: float32 [1536], P('fsdp')
- router_grad: float32 [1536, 8], P('fsdp')
- expert_in_grad: float32 [8, 1536, 1536], P('blk', 'fsdp')
- expert_out_grad: float32 [8, 768, 1536], P('blk', None, 'fsdp')
The draws below stay inside these ranges and needn't reach their ends.
Inputs may be any that keep to these rules, and one draw needn't show every extreme that they name: `documents`: document numbers never fall along a sequence. `routes`: A token names 4 different experts; within the 256 rows of one device of a sequence no expert is named more than 192 times.
All inputs are finite; a program needn't handle non-finite values.
Results may differ from the reference program's by a relative error of at most 0.025.
Values may be sent and summed in bfloat16 or wider, within the bound.
A program may use at most 256 MiB of HBM per device.

```python
import math
import jax
import jax.numpy as jnp
import numpy as np
from jax import lax

MODEL_DIM = 1536
QUERY_HEADS = 12
KEYVALUE_HEADS = 2
HEAD_SIZE = 128
FFE = 768
TOP = 4
SEQ_TOK = 256
EXPERTS = 8
BATCH = 2
LENGTH = 4096
CAP = 192


def draw_documents(key, part):
    key = jax.random.fold_in(key, 7)
    key_start, key_rest, key_split = jax.random.split(key, 3)
    opening = jax.random.randint(key_start, (BATCH, 1), 1, SEQ_TOK // 2 + 1)
    tail_rows = jax.random.randint(key_rest, (BATCH, 1), 1, SEQ_TOK)
    first_end = LENGTH - tail_rows
    second_end = first_end + jax.random.randint(key_split, (BATCH, 1), 0, SEQ_TOK + 1) % tail_rows
    places = jnp.arange(LENGTH, dtype=jnp.int32)[None, :]
    return (places >= opening).astype(jnp.int32) + (places >= first_end).astype(jnp.int32) + (places >= second_end).astype(jnp.int32)


def levels(own_key, dims, cuts, smallest, top_value):
    loudness = 1.0
    for position, parts in cuts:
        steps = jax.random.uniform(jax.random.fold_in(jax.random.fold_in(own_key, 6), position), (parts,), jnp.float32, smallest / len(cuts), top_value / len(cuts))
        loudness = loudness * jnp.repeat(jnp.exp(steps), dims[position] // parts).reshape((-1,) + (1,) * (len(dims) - 1 - position))
    return loudness


def routed_block(stream_key, own, number, rows, number_of, top, most, lean):
    sequence = jax.random.permutation(stream_key, number_of)
    crowded, ordinary = portions_of(number_of, rows * top, most, lean, True), portions_of(number_of, rows * top, most, lean, False)
    places = jnp.arange(number_of)

    def named(lengths, offset_by):
        used = int((lengths > 0).sum())
        fixed = max(1, used // 4)
        shifted = fixed + (places - fixed + offset_by * (used - fixed)) % max(1, number_of - fixed)
        return jnp.zeros((number_of,), jnp.int32).at[sequence[jnp.where(places < fixed, places, shifted)]].set(jnp.asarray(lengths, jnp.int32))

    lengths = jnp.where(number % 4 == 0, named(crowded, number // 4), named(ordinary, number - number // 4 - 1))
    mixed = jax.random.permutation(jax.random.fold_in(own, 3), number_of)
    giver, receiver = mixed[0:number_of // 2 * 2:2], mixed[1:number_of // 2 * 2:2]
    room = jnp.minimum(lengths[giver] - 1, most - lengths[receiver]) // 2
    room = jnp.where((giver == sequence[0]) | (receiver == sequence[0]) | (lengths[receiver] == 0), 0, jnp.maximum(room, 0))
    shifted = jax.random.randint(jax.random.fold_in(own, 4), (number_of // 2,), 0, 1 << 20) % (room + 1)
    lengths = lengths.at[giver].add(-shifted).at[receiver].add(shifted)
    members = jnp.searchsorted(jnp.cumsum(lengths), jnp.arange(rows * top), side="right").astype(jnp.int32)
    listing = members.reshape(top, rows).T
    listing = listing[jax.random.permutation(jax.random.fold_in(own, 1), rows)]
    offset_by = jax.random.randint(jax.random.fold_in(own, 2), (rows, 1), 0, top)
    return jnp.take_along_axis(listing, (jnp.arange(top)[None, :] + offset_by) % top, axis=1)


def portions_of(count, total, most, skew, full):
    portions = [(1 << 20) // math.isqrt(rank ** skew) + 1 for rank in range(1, count + 1)]
    largest = most if full else min(most, max(-(-total // count), total * portions[0] // sum(portions)))
    least = 1 if total - largest >= count - 1 else 0
    holding, spare = [largest] + [least] * (count - 1), total - largest - least * (count - 1)
    while spare > 0:
        candidates = [i for i in range(1, count) if holding[i] < largest] or [i for i in range(1, count) if holding[i] < most]
        pool, budget = sum([portions[i] for i in candidates]), spare
        for i in candidates:
            extra = min(most - holding[i], max(1, budget * portions[i] // pool), spare)
            holding[i] = holding[i] + extra
            spare = spare - extra
    return np.array(holding)


def bell_draw(rng, dims, deviation, reach, cuts=(), kind=jnp.bfloat16):
    drawn = jax.random.normal(rng, dims, jnp.float32) * deviation
    if len(cuts) > 0:
        drawn = levels(rng, dims, cuts, -0.22, 0.18) * drawn
    return jnp.clip(drawn, min=-reach, max=reach).astype(kind)


def setup_inputs(seed: int = 0) -> dict:
    streams_of = jax.random.split(jax.random.key(seed), 13)
    tokens = bell_draw(streams_of[0], (BATCH, LENGTH, MODEL_DIM), 1.0, 6.0, ((0, 2), (1, 16)))
    documents = draw_documents(jax.random.fold_in(streams_of[12], 71), 0)
    routes_keys = jax.random.split(jax.random.fold_in(streams_of[2], 1), BATCH * LENGTH // SEQ_TOK)
    routes_turns = jax.random.permutation(jax.random.fold_in(streams_of[2], 3), BATCH * LENGTH // SEQ_TOK)
    routes = jax.vmap(lambda own, number: routed_block(jax.random.fold_in(streams_of[2], 2), own, number, SEQ_TOK, EXPERTS, TOP, CAP, 1))(routes_keys, routes_turns).reshape((BATCH, LENGTH, TOP))
    cotangent = bell_draw(streams_of[3], (BATCH, LENGTH, MODEL_DIM), 1.0, 6.0, ((0, 2), (1, 16)))
    first_gain = jnp.clip(1.0 + 0.1 * jax.random.normal(streams_of[4], (MODEL_DIM,), jnp.float32), 0.5, 1.5).astype(jnp.bfloat16)
    query_weight = bell_draw(streams_of[5], (MODEL_DIM, QUERY_HEADS * HEAD_SIZE), MODEL_DIM ** -0.5, 0.15625, ((0, 2),))
    keyvalue_weight = bell_draw(streams_of[6], (MODEL_DIM, 2 * KEYVALUE_HEADS * HEAD_SIZE), MODEL_DIM ** -0.5, 0.15625, ((0, 2),))
    output_weight = bell_draw(streams_of[7], (QUERY_HEADS * HEAD_SIZE, MODEL_DIM), (max(1, QUERY_HEADS * HEAD_SIZE // 384)) ** -0.5, 3.0, ((0, 2),))
    second_gain = jnp.clip(1.0 + 0.1 * jax.random.normal(streams_of[8], (MODEL_DIM,), jnp.float32), 0.5, 1.5).astype(jnp.bfloat16)
    router_weight = bell_draw(streams_of[9], (MODEL_DIM, EXPERTS), (4 * MODEL_DIM) ** -0.5, 0.078125, ((0, 2),))
    expert_in = bell_draw(streams_of[10], (EXPERTS, MODEL_DIM, 2 * FFE), MODEL_DIM ** -0.5, 0.15625, ((0, 4), (1, 2)))
    expert_out = bell_draw(streams_of[11], (EXPERTS, FFE, MODEL_DIM), (FFE // 8) ** -0.5, 0.625, ((0, 4), (2, 2)))
    return {"tokens": tokens, "documents": documents, "routes": routes, "cotangent": cotangent, "first_gain": first_gain, "query_weight": query_weight, "keyvalue_weight": keyvalue_weight, "output_weight": output_weight, "second_gain": second_gain, "router_weight": router_weight, "expert_in": expert_in, "expert_out": expert_out}


NORM_EPSILON = 1e-06
ROPE_BASE = 1000000.0
MASKED_SCORE = -1e+30
EXACT = lax.Precision.HIGHEST

@jax.custom_vjp
def lowered_tensor(v):
    return lax.optimization_barrier(v.astype(jnp.bfloat16)).astype(jnp.float32)

@jax.custom_vjp
def low_back(v):
    return v

def low_keep(v):
    return (lowered_tensor(v), None)

def low_pass(kept, grad):
    return (grad,)

def back_keep(v):
    return (v, None)

def back_low(kept, grad):
    return (lowered_tensor(grad),)
lowered_tensor.defvjp(low_keep, low_pass)
low_back.defvjp(back_keep, back_low)

def rms_scale(value_tensor, gain):
    return value_tensor * lax.rsqrt(lax.optimization_barrier(jnp.mean(value_tensor * value_tensor, axis=-1, keepdims=True)) + NORM_EPSILON) * gain

def apply_rotary(value_tensor, token_positions):
    half_dim = value_tensor.shape[-1] // 2
    inverse = jnp.power(ROPE_BASE, -jnp.arange(half_dim).astype(jnp.float32) * 2.0 / value_tensor.shape[-1])
    angle = token_positions[:, None] * inverse[None, :]
    cosine = jnp.cos(angle)[:, None, :]
    sine = jnp.sin(angle)[:, None, :]
    first_half = value_tensor[..., :half_dim]
    second_half = value_tensor[..., half_dim:]
    return jnp.concatenate([first_half * cosine - second_half * sine, second_half * cosine + first_half * sine], axis=-1)

def attend_row(queries, key_tensor, value_tensor, doc_row):
    sequence_length = queries.shape[0]
    queries_per_keyvalue = QUERY_HEADS // KEYVALUE_HEADS
    keys_all = jnp.repeat(key_tensor, queries_per_keyvalue, axis=1)
    values_all = jnp.repeat(value_tensor, queries_per_keyvalue, axis=1)
    block_rows = math.gcd(512, sequence_length)
    key_pos = jnp.arange(sequence_length, dtype=jnp.int32)

    def one_block(index):
        row_start = index * block_rows
        query_block = lax.dynamic_slice_in_dim(queries, row_start, block_rows, 0)
        query_ids = lax.dynamic_slice_in_dim(doc_row, row_start, block_rows, 0)
        query_pos = row_start + jnp.arange(block_rows, dtype=jnp.int32)
        scores = low_back(jnp.einsum('qhd,khd->hqk', query_block, keys_all, precision=EXACT) * HEAD_SIZE ** (-0.5))
        allowed = (key_pos[None, :] <= query_pos[:, None]) & (doc_row[None, :] == query_ids[:, None])
        scores = jnp.where(allowed[None], scores, MASKED_SCORE)
        log_total = jax.nn.logsumexp(scores, axis=-1, keepdims=True)
        probs = lowered_tensor(jnp.exp(scores - log_total))
        return jnp.einsum('hqk,khd->qhd', probs, values_all, precision=EXACT)
    mixed = lax.map(jax.checkpoint(one_block), jnp.arange(sequence_length // block_rows, dtype=jnp.int32))
    return mixed.reshape(sequence_length, QUERY_HEADS, HEAD_SIZE)

def expert_sum(hidden, route_weights, expert_in, expert_out):

    def one_expert(total, item):
        weight_in, weight_out, share = item
        copied = low_back(hidden)
        gate_up = low_back(jnp.dot(copied, weight_in, precision=EXACT, preferred_element_type=jnp.float32))
        active = lowered_tensor(jax.nn.gelu(gate_up[:, :FFE], approximate=True) * gate_up[:, FFE:])
        result = low_back(lowered_tensor(jnp.dot(active, weight_out, precision=EXACT, preferred_element_type=jnp.float32)))
        return (total + share[:, None] * result, None)
    total, _ = lax.scan(jax.checkpoint(one_expert), jnp.zeros(hidden.shape, jnp.float32), (expert_in, expert_out, route_weights.T))
    return total

def forward(x_float, first_gain, query_weight, keyvalue_weight, output_weight, second_gain, router_weight, expert_in, expert_out, documents, routes):
    batch_row_list, sequence_length, model_width = x_float.shape
    token_positions = jnp.arange(sequence_length, dtype=jnp.int32).astype(jnp.float32)
    normed_one = lowered_tensor(rms_scale(x_float, first_gain))
    query_pre = low_back(jnp.einsum('bld,de->ble', normed_one, query_weight, precision=EXACT))
    prerotation_keyvalue = low_back(jnp.einsum('bld,de->ble', normed_one, keyvalue_weight, precision=EXACT))

    def rotary_rows(value_tensor):
        return jax.vmap(lambda single: apply_rotary(single, token_positions))(value_tensor)
    queries = lowered_tensor(rotary_rows(query_pre.reshape(batch_row_list, sequence_length, QUERY_HEADS, HEAD_SIZE)))
    key_tensor = lowered_tensor(rotary_rows(prerotation_keyvalue[..., :KEYVALUE_HEADS * HEAD_SIZE].reshape(batch_row_list, sequence_length, KEYVALUE_HEADS, HEAD_SIZE)))
    value_tensor = lowered_tensor(prerotation_keyvalue[..., KEYVALUE_HEADS * HEAD_SIZE:].reshape(batch_row_list, sequence_length, KEYVALUE_HEADS, HEAD_SIZE))

    def attend_one(packed):
        return attend_row(packed[0], packed[1], packed[2], packed[3])
    mixed = lax.map(attend_one, (queries, key_tensor, value_tensor, documents))
    mixed = low_back(lowered_tensor(mixed.reshape(batch_row_list, sequence_length, QUERY_HEADS * HEAD_SIZE)))
    residual_one = x_float + low_back(jnp.einsum('blc,cd->bld', mixed, output_weight, precision=EXACT))
    normed_two = lowered_tensor(rms_scale(residual_one, second_gain))
    logits = low_back(jnp.einsum('bld,de->ble', normed_two, router_weight, precision=EXACT))
    onehot = (routes[..., None] == jnp.arange(EXPERTS, dtype=jnp.int32)).astype(jnp.float32)
    chosen = jnp.einsum('blke,ble->blk', onehot, logits, precision=EXACT)
    gates = jax.nn.softmax(chosen, axis=-1)
    shares = jnp.einsum('blke,blk->ble', onehot, gates, precision=EXACT)
    mixture = expert_sum(normed_two.reshape(-1, model_width), shares.reshape(-1, EXPERTS), expert_in, expert_out)
    return residual_one + mixture.reshape(batch_row_list, sequence_length, model_width)

def reference(tokens, documents, routes, cotangent, first_gain, query_weight, keyvalue_weight, output_weight, second_gain, router_weight, expert_in, expert_out):
    floats = tuple((array_in.astype(jnp.float32) for array_in in (tokens, first_gain, query_weight, keyvalue_weight, output_weight, second_gain, router_weight, expert_in, expert_out)))

    def forward_fn(*params):
        return forward(*params, documents, routes)
    block_out, pull = jax.vjp(forward_fn, *floats)
    grads = pull(cotangent.astype(jnp.float32))
    return (block_out.astype(jnp.bfloat16), grads[0].astype(jnp.bfloat16), grads[1], grads[2], grads[3], grads[4], grads[5], grads[6], grads[7], grads[8])
```

```python
import functools

import jax
import jax.numpy as jnp
from jax import lax
from jax.experimental import pallas as pl
from jax.experimental.pallas import tpu as pltpu
from jax.sharding import PartitionSpec as P

QUERY_HEADS = 12
KEYVALUE_HEADS = 2
HEAD = 128
NORM_EPSILON = 1e-06
ROPE_BASE = 1000000.0
MASKED = -1e30
DOCUMENTS = 4
LOG2E = 1.4426950408889634
SCORE_LOG2 = HEAD ** (-0.5) * LOG2E
SCORE_SCALE = HEAD ** (-0.5)
TILE = 256
BF16 = jnp.bfloat16
F32 = jnp.float32
VMEM_BYTES = 63 * 1024 * 1024

NN = (((1,), (0,)), ((), ()))
NT = (((1,), (1,)), ((), ()))
TN = (((0,), (0,)), ((), ()))


def mm(a, b, dims=NN):
    return lax.dot_general(a, b, dims, preferred_element_type=F32)


def gelu_parts(gate):
    c = 0.7978845608028654
    cube = 0.044715 * gate * gate * gate
    t = jnp.tanh(c * (gate + cube))
    value = 0.5 * gate * (1.0 + t)
    slope = 0.5 * (1.0 + t) + 0.5 * gate * (1.0 - t * t) * c * (1.0 + 3.0 * 0.044715 * gate * gate)
    return value, slope


def score_tile(key_rows, q_tile, start_row, first_key, q_first):
    scores = mm(key_rows, q_tile, NT) * SCORE_LOG2
    key_pos = first_key + lax.broadcasted_iota(jnp.int32, scores.shape, 0)
    allowed = key_pos >= start_row
    if q_first is not None:
        q_pos = q_first + lax.broadcasted_iota(jnp.int32, scores.shape, 1)
        allowed = allowed & (key_pos <= q_pos)
    return jnp.where(allowed, scores, MASKED)


def attend_tile(hh, cols, key_rows, value_cols, q_ref, start_ref, m_ref, l_ref, acc_ref, first_key, q_first):
    q_tile = q_ref[hh, cols, :]
    scores = score_tile(key_rows, q_tile, start_ref[:, cols], first_key, q_first)
    old = m_ref[hh, :, cols]
    new = jnp.maximum(old, jnp.max(scores, axis=0, keepdims=True))
    factor = jnp.exp2(old - new)
    prob = jnp.exp2(scores - new)
    m_ref[hh, :, cols] = new
    l_ref[hh, :, cols] = l_ref[hh, :, cols] * factor + jnp.sum(prob, axis=0, keepdims=True)
    acc_ref[hh, :, cols] = acc_ref[hh, :, cols] * factor + mm(value_cols, prob.astype(BF16))


def unattend_tile(hh, cols, key_rows, value_rows, key_cols, q_ref, do_ref, start_ref, lse_ref, delta_ref,
                  dq_ref, dk_ref, dv_ref, first_key, q_first):
    n = key_rows.shape[0]
    q_tile = q_ref[hh, cols, :]
    do_tile = do_ref[hh, cols, :]
    scores = score_tile(key_rows, q_tile, start_ref[:, cols], first_key, q_first)
    prob = jnp.exp2(scores - lse_ref[hh, :, cols])
    dv_ref[:n, :] += mm(prob.astype(BF16), do_tile)
    prob_grad = mm(value_rows, do_tile, NT)
    score_grad = (prob * (prob_grad - delta_ref[hh, :, cols])).astype(BF16)
    dk_ref[:n, :] += mm(score_grad, q_tile)
    dq_ref[hh, :, cols] += mm(key_cols, score_grad)


def remote(src, dst, send_sem, recv_sem, **to):
    return pltpu.make_async_remote_copy(
        src_ref=src, dst_ref=dst, send_sem=send_sem, recv_sem=recv_sem, device_id=to,
        device_id_type=pl.DeviceIdType.MESH)


class Lanes:
    def __init__(self, send, recv):
        self.send, self.recv, self.used, self.sent, self.pending = send, recv, 0, 0, []

    def slots(self, count=1):
        first = self.used
        self.used += count
        assert self.used <= self.recv.shape[0]
        return first

    def sends(self, count):
        first = self.sent
        self.sent += count
        assert self.sent <= self.send.shape[0]
        return first

    def put(self, slot, src, dst, when=None, **to):
        assert self.sent < self.send.shape[0]
        copy = remote(src, dst, self.send.at[self.sent], self.recv.at[slot], **to)
        self.sent += 1
        if when is None:
            copy.start()
        else:
            pl.when(when)(copy.start)
        self.pending.append((copy, when))
        return self.pending[-1]

    def settle(self, entry):
        copy, when = entry
        self.pending = [other for other in self.pending if other is not entry]
        if when is None:
            copy.wait_send()
        else:
            pl.when(when)(copy.wait_send)

    def arrived(self, slot, dst, when=None, **origin):
        copy = remote(dst, dst, self.send.at[0], self.recv.at[slot], **origin)
        if when is None:
            copy.wait_recv()
        else:
            pl.when(when)(copy.wait_recv)

    def drain(self):
        for copy, when in self.pending:
            if when is None:
                copy.wait_send()
            else:
                pl.when(when)(copy.wait_send)
        self.pending = []


class Place:
    def __init__(self, blocks):
        self.z, self.h, self.y = lax.axis_index("blk"), lax.axis_index("head"), lax.axis_index("fsdp")
        self.blocks = blocks
        self.x, self.c = self.h // 2, self.h % 2
        self.sib = 2 * self.x + 1 - self.c
        self.xn = 2 * (1 - self.x) + self.c
        self.xs = 2 * (1 - self.x) + 1 - self.c
        self.oy = 1 - self.y

    def others(self):
        return [(self.z + d) % self.blocks for d in range(1, self.blocks)]

    def enter(self):
        barrier = pltpu.get_barrier_semaphore()

        def greet(**to):
            pl.semaphore_signal(barrier, inc=1, device_id=to, device_id_type=pl.DeviceIdType.MESH)

        for head in (self.sib, self.xn, self.xs):
            greet(head=head)
        greet(fsdp=self.oy)
        for z in self.others():
            greet(blk=z)
        pl.semaphore_wait(barrier, 4 + self.blocks - 1)


def gather_heads(at, lanes, own, land):
    s = lanes.slots(3)
    rows = own.shape[0]

    def slot(head):
        return land.at[pl.ds(pl.multiple_of(head * rows, rows), rows), :]

    lanes.put(s, own, slot(at.h), head=at.xn)
    lanes.put(s + 1, own, slot(at.h), head=at.sib)

    passed = []

    def forward():
        lanes.arrived(s, slot(at.xn), head=at.xn)
        passed.append(lanes.put(s + 2, slot(at.xn), slot(at.xn), head=at.sib))

    def near():
        lanes.arrived(s + 1, slot(at.sib), head=at.sib)

    def far():
        lanes.arrived(s + 2, slot(at.xs), head=at.sib)

    return forward, near, far, passed


def aligned(index, size):
    return pl.ds(pl.multiple_of(index, 16), size)


def semaphores(blocks):
    count = 128 + 16 * blocks
    return [pltpu.SemaphoreType.DMA((count,)), pltpu.SemaphoreType.DMA((count,))]


class Shared:
    def __init__(self, at, lanes, chunks, give, hold):
        self.at, self.lanes, self.chunks, self.give, self.hold = at, lanes, chunks, give, hold
        self.pieces = len(give(0)) if give else 0
        self.ys = lanes.slots(chunks * self.pieces)
        self.xn, self.sib, self.far = lanes.slots(chunks), lanes.slots(chunks), lanes.slots(chunks)
        self.sent = []

    def begin(self, k):
        for i, (src, dst) in enumerate(self.give(k)):
            self.lanes.put(self.ys + k * self.pieces + i, src, dst(self.at.y), fsdp=self.at.oy)

    def landed(self, k):
        for i, (src, dst) in enumerate(self.give(k)):
            self.lanes.arrived(self.ys + k * self.pieces + i, dst(self.at.oy), fsdp=self.at.oy)

    def spread(self, k):
        self.landed(k)
        self.scatter(k)

    def scatter(self, k):
        at = self.at
        place = self.hold(k, at.h, at.oy)
        self.sent.append(self.lanes.put(self.xn + k, place, place, head=at.xn))
        self.sent.append(self.lanes.put(self.sib + k, place, place, head=at.sib))

    def forward(self, k):
        at = self.at
        place = self.hold(k, at.xn, at.oy)
        self.lanes.arrived(self.xn + k, place, head=at.xn)
        self.sent.append(self.lanes.put(self.far + k, place, place, head=at.sib))

    def settle(self):
        for entry in self.sent:
            self.lanes.settle(entry)

    def finish(self, k):
        at = self.at
        self.lanes.arrived(self.sib + k, self.hold(k, at.sib, at.oy), head=at.sib)
        self.lanes.arrived(self.far + k, self.hold(k, at.xs, at.oy), head=at.sib)


def weight_chunk(w_ref, k, head, y):
    quarter = w_ref.shape[2] // 4
    piece = quarter // 2
    return w_ref.at[k // 2, y, aligned(head * quarter + k % 2 * piece, piece), :]


class Column:
    def __init__(self, at, lanes, land):
        self.at, self.lanes, self.land = at, lanes, land
        self.slot = lanes.slots(at.blocks)

    def begin(self, own):
        at = self.at
        place = self.land.at[at.z]
        self.lanes.put(self.slot + at.z, own, place, when=at.z < at.blocks - 1, blk=at.z + 1)
        self.lanes.put(self.slot + at.z, own, place, when=at.z > 0, blk=at.z - 1)

    def hand_on(self, d):
        at = self.at
        for b, origin, next_z in ((at.z - d, at.z - 1, at.z + 1), (at.z + d, at.z + 1, at.z - 1)):
            there = (b >= 0) & (b < at.blocks)
            safe = jnp.clip(b, 0, at.blocks - 1)
            self.lanes.arrived(self.slot + safe, self.land.at[safe], when=there, blk=origin)
            self.lanes.put(self.slot + safe, self.land.at[safe], self.land.at[safe],
                           when=there & (next_z >= 0) & (next_z < at.blocks), blk=next_z)


def front_kernel(x_ref, small_ref, wq_hbm, wkv_hbm, wo_hbm, win_hbm, wout_hbm, cot_hbm, cos_ref, sin_ref, start_ref,
                 q_ref, o_ref, ot_ref, lse_ref, n1_ref, small_out, wqkv_out, kv_out, wo_out, w_out, cot_out,
                 xg_ref, small_land, wqkv_ref, kv_ref, m_ref, l_ref, acc_ref, vt_ref, wo_ref, w_ref, cot_ref,
                 load_sem, send_sem, recv_sem):
    heads, rows, _ = q_ref.shape
    own_rows, width = x_ref.shape
    blocks = kv_ref.shape[0]
    half = wq_hbm.shape[0]
    qcols = heads * HEAD
    experts = 2 * blocks
    at = Place(blocks)
    me = at.z
    lanes = Lanes(send_sem, recv_sem)
    at.enter()
    local = []

    def copy_here(src, dst):
        copy = pltpu.make_async_copy(src, dst, load_sem.at[len(local)])
        copy.start()
        local.append(copy)
        return copy

    forward, near, far, _ = gather_heads(at, lanes, x_ref, xg_ref)
    g = at.x
    q_from = pl.ds(pl.multiple_of(at.h * qcols, HEAD), qcols)
    k_from = pl.ds(pl.multiple_of(g * HEAD, HEAD), HEAD)
    v_from = pl.ds(pl.multiple_of((KEYVALUE_HEADS + g) * HEAD, HEAD), HEAD)
    columns = ((wq_hbm.at[:, q_from], slice(0, qcols)), (wkv_hbm.at[:, k_from], slice(qcols, qcols + HEAD)),
               (wkv_hbm.at[:, v_from], slice(qcols + HEAD, qcols + 2 * HEAD)))

    def weight_rows(y, cols):
        return wqkv_ref.at[aligned(y * half, half), cols]

    ws = lanes.slots(3)
    for i, (src, cols) in enumerate(columns):
        lanes.put(ws + i, src, weight_rows(at.y, cols), fsdp=at.oy)
    smalls = lanes.slots()
    lanes.put(smalls, small_ref, small_land, fsdp=at.oy)
    own_weights = [copy_here(src, weight_rows(at.y, cols)) for src, cols in columns]
    cots = Column(at, lanes, cot_ref)
    own_half = pl.ds(pl.multiple_of(at.y * half, half), half)
    cot_load = copy_here(cot_hbm, cot_ref.at[me])
    wo_load = copy_here(wo_hbm, wo_ref.at[own_half, :])
    w_loads = [copy_here(win_hbm, w_ref.at[:, at.y, :, :width]), copy_here(wout_hbm, w_ref.at[:, at.y, :, width:])]
    cot_load.wait()
    cots.begin(cot_ref.at[me])

    quarter = half // 4

    def wo_place(k, head, y):
        return wo_ref.at[aligned(y * half + head * quarter, quarter), :]

    shared_wo = Shared(at, lanes, 1,
                       lambda k: [(wo_place(0, at.h, at.y), lambda y: wo_place(0, at.h, y))],
                       wo_place)
    chunks, spread_here = 4, 2

    def w_place(k, head, y):
        return weight_chunk(w_ref, k, head, y)

    def w_give(k):
        return [(w_place(k, at.h, at.y), lambda y: w_place(k, at.h, y))]

    shared_w = Shared(at, lanes, chunks, w_give, w_place)

    small_out[:, :half] = jnp.zeros((small_ref.shape[0], half), BF16)
    lanes.arrived(smalls, small_land, fsdp=at.oy)
    for y in range(2):
        @pl.when(at.y == y)
        def _(y=y):
            small_out[:, y * half:(y + 1) * half] = small_ref[...]
            small_out[:, (1 - y) * half:(2 - y) * half] = small_land[...]

    def norm(head, block):
        x = block.astype(F32)
        inv = lax.rsqrt(jnp.mean(x * x, axis=-1, keepdims=True) + NORM_EPSILON)
        n1_ref[aligned(head * own_rows, own_rows), :] = (x * inv * small_out[experts:experts + 1, :].astype(F32)).astype(BF16)

    def gathered(head):
        return xg_ref[aligned(head * own_rows, own_rows), :]

    norm(at.h, x_ref[...])
    near()
    norm(at.sib, gathered(at.sib))
    forward()
    norm(at.xn, gathered(at.xn))
    far()
    norm(at.xs, gathered(at.xs))
    for copy in own_weights:
        copy.wait()
    for i, (_, cols) in enumerate(columns):
        lanes.arrived(ws + i, weight_rows(at.oy, cols), fsdp=at.oy)
    wo_load.wait()
    shared_wo.begin(0)
    for load in w_loads:
        load.wait()
    for k in range(chunks):
        shared_w.begin(k)
    cots.hand_on(1)

    def project(i, _):
        band = aligned(i * TILE, TILE)
        pre = mm(n1_ref[band, :], wqkv_ref[...])
        cosine, sine = cos_ref[band, :], sin_ref[band, :]

        def turned(u):
            return (u * cosine + pltpu.roll(u, HEAD // 2, 1) * sine).astype(BF16)

        for hh in range(heads):
            q_ref[hh, band, :] = turned(pre[:, hh * HEAD:(hh + 1) * HEAD])
        kv_ref[me, band, :HEAD] = turned(pre[:, qcols:qcols + HEAD])
        kv_ref[me, band, HEAD:] = pre[:, qcols + HEAD:].astype(BF16)
        return 0

    lax.fori_loop(0, rows // TILE, project, 0)

    kvs, kvc = lanes.slots(blocks), lanes.slots(blocks)
    half_rows = rows // 2

    def kv_half(b, core):
        return kv_ref.at[b, aligned(core * half_rows, half_rows), :]

    lanes.put(kvs + me, kv_half(me, at.c), kv_half(me, at.c), when=me < blocks - 1, blk=me + 1)
    late = [copy_here(wqkv_ref, wqkv_out), copy_here(wo_ref.at[own_half, :], wo_out.at[own_half, :]),
            copy_here(w_ref.at[:, at.y], w_out.at[:, at.y])]

    m_ref[...] = jnp.full_like(m_ref, MASKED)
    l_ref[...] = jnp.zeros_like(l_ref)
    acc_ref[...] = jnp.zeros_like(acc_ref)

    def transpose_values(b):
        vt_ref[...] = kv_ref[b, :, HEAD:].astype(F32).T.astype(BF16)

    transpose_values(me)
    for i in range(rows // TILE):
        n = (i + 1) * TILE

        def diagonal(hh, _, i=i, n=n):
            attend_tile(hh, slice(i * TILE, n), kv_ref[me, :n, :HEAD], vt_ref[:, :n], q_ref, start_ref,
                        m_ref, l_ref, acc_ref, me * rows, me * rows + i * TILE)
            return 0

        lax.fori_loop(0, heads, diagonal, 0)

    def block(b):
        transpose_values(b)

        def tile(t, _):
            hh, i = t // (rows // TILE), t % (rows // TILE)
            cols = pl.ds(pl.multiple_of(i * TILE, TILE), TILE)
            attend_tile(hh, cols, kv_ref[b, :, :HEAD], vt_ref[...], q_ref, start_ref,
                        m_ref, l_ref, acc_ref, b * rows, None)
            return 0

        lax.fori_loop(0, heads * (rows // TILE), tile, 0)

    ticks = [[functools.partial(shared_wo.spread, 0), functools.partial(shared_w.spread, 0)],
             [functools.partial(shared_w.spread, 1), functools.partial(shared_wo.forward, 0),
              functools.partial(cots.hand_on, 2)],
             [functools.partial(shared_w.forward, 0)] + [functools.partial(cots.hand_on, d) for d in range(3, blocks)],
             [functools.partial(shared_w.forward, 1)]]

    def tick():
        if ticks:
            for f in ticks.pop(0):
                f()

    for d in range(1, blocks):
        b = jnp.maximum(me - d, 0)
        there = me >= d
        lanes.arrived(kvs + b, kv_half(b, at.c), when=there, blk=me - 1)
        lanes.put(kvs + b, kv_half(b, at.c), kv_half(b, at.c), when=there & (me < blocks - 1), blk=me + 1)
        lanes.put(kvc + b, kv_half(b, at.c), kv_half(b, at.c), when=there, head=at.sib)
        lanes.arrived(kvc + b, kv_half(b, 1 - at.c), when=there, head=at.sib)
        pl.when(there)(functools.partial(block, b))
        tick()

    for hh in range(heads):
        total = l_ref[hh]
        done = acc_ref[hh] / total
        ot_ref[hh * HEAD:(hh + 1) * HEAD, :] = done.astype(BF16)
        o_ref[:, hh * HEAD:(hh + 1) * HEAD] = done.T.astype(BF16)
        lse_ref[hh] = m_ref[hh] + jnp.log2(total)
    kv_copies = [pltpu.make_async_copy(kv_ref.at[b], kv_out.at[b], load_sem.at[15]) for b in range(blocks)]
    for b, copy in enumerate(kv_copies):
        @pl.when(b <= me)
        def _(copy=copy):
            copy.start()
            copy.wait()
    while ticks:
        tick()
    shared_wo.finish(0)
    other_half = pl.ds(pl.multiple_of(at.oy * half, half), half)
    late.append(copy_here(wo_ref.at[other_half, :], wo_out.at[other_half, :]))
    late.append(copy_here(cot_ref, cot_out))
    for k in range(spread_here):
        shared_w.finish(k)
    for k in range(spread_here, chunks):
        shared_w.landed(k)
    late.append(copy_here(w_ref.at[:, at.oy], w_out.at[:, at.oy]))
    for copy in late:
        copy.wait()
    lanes.drain()


def front(blocks, x, small, wq, wkv, wo, win, wout, cot, cosine, sine, start):
    own_rows, width = x.shape
    rows = cosine.shape[0]
    half = wq.shape[0]
    heads = QUERY_HEADS * own_rows // rows
    qcols = heads * HEAD
    ffe = wout.shape[1]
    vm = pl.BlockSpec(memory_space=pltpu.VMEM)
    hbm = pl.BlockSpec(memory_space=pl.ANY)
    sds = jax.ShapeDtypeStruct
    return pl.pallas_call(
        front_kernel,
        out_shape=(
            sds((heads, rows, HEAD), BF16),
            sds((rows, qcols), BF16),
            sds((qcols, rows), BF16),
            sds((heads, 1, rows), F32),
            sds((rows, width), BF16),
            sds((small.shape[0], width), BF16),
            sds((width, qcols + 2 * HEAD), BF16),
            sds((blocks, rows, 2 * HEAD), BF16),
            sds((width, width), BF16),
            sds((2, 2, half, width + half), BF16),
            sds((blocks, own_rows, width), BF16),
        ),
        in_specs=[vm, vm] + [hbm] * 6 + [vm] * 3,
        out_specs=[vm] * 6 + [hbm] * 5,
        scratch_shapes=[
            pltpu.VMEM((rows, width), BF16),
            pltpu.VMEM(small.shape, BF16),
            pltpu.VMEM((width, qcols + 2 * HEAD), BF16),
            pltpu.VMEM((blocks, rows, 2 * HEAD), BF16),
            pltpu.VMEM((heads, 1, rows), F32),
            pltpu.VMEM((heads, 1, rows), F32),
            pltpu.VMEM((heads, HEAD, rows), F32),
            pltpu.VMEM((HEAD, rows), BF16),
            pltpu.VMEM((width, width), BF16),
            pltpu.VMEM((2, 2, half, width + half), BF16),
            pltpu.VMEM((blocks, own_rows, width), BF16),
            pltpu.SemaphoreType.DMA((16,)),
        ] + semaphores(blocks),
        compiler_params=pltpu.CompilerParams(
            vmem_limit_bytes=VMEM_BYTES, collective_id=0, has_side_effects=True),
    )(x, small, wq, wkv, wo, win, wout, cot, cosine, sine, start)


class ColumnSum:
    CHUNKS = 4

    def __init__(self, at, lanes, part, land):
        self.at, self.lanes, self.part, self.land = at, lanes, part, land
        self.rows = part.shape[1] // self.CHUNKS
        self.recv = lanes.slots((at.blocks + 1) * self.CHUNKS)
        self.sent = lanes.sends(at.blocks * self.CHUNKS)

    def copy(self, b, ch):
        at = self.at
        travel = jnp.where(b < at.z, -1, 1)
        there = at.z + travel
        slot = jnp.where((there == b) & (b > at.z), at.blocks, b)
        rows = pl.ds(ch * self.rows, self.rows)
        return remote(self.part.at[b, rows, :], self.land.at[slot, rows, :],
                      self.lanes.send.at[self.sent + b * self.CHUNKS + ch],
                      self.lanes.recv.at[self.recv + slot * self.CHUNKS + ch], blk=there)

    def landed(self, slot, ch, origin):
        rows = pl.ds(ch * self.rows, self.rows)
        place = self.land.at[slot, rows, :]
        remote(place, place, self.lanes.send.at[0], self.lanes.recv.at[self.recv + slot * self.CHUNKS + ch],
               blk=origin).wait_recv()

    def first_send(self, b):
        at = self.at

        @pl.when(((b < at.z) & (at.z == at.blocks - 1)) | ((b > at.z) & (at.z == 0)))
        def _():
            for ch in range(self.CHUNKS):
                self.copy(b, ch).start()

    def relay(self, phase, d, add):
        at = self.at
        s = jnp.where(at.z * 2 >= at.blocks, -1, 1) * (1 - 2 * phase)
        b, origin = at.z + s * d, at.z - s
        safe = jnp.clip(b, 0, at.blocks - 1)

        @pl.when((b >= 0) & (b < at.blocks) & (origin >= 0) & (origin < at.blocks))
        def _():
            for ch in range(self.CHUNKS):
                self.landed(safe, ch, origin)
                add(safe, pl.ds(ch * self.rows, self.rows))
                self.copy(safe, ch).start()

    def arrive(self, side, use):
        at = self.at
        slot, origin = (at.z, at.z + 1) if side == 0 else (at.blocks, at.z - 1)

        @pl.when((origin >= 0) & (origin < at.blocks))
        def _():
            for ch in range(self.CHUNKS):
                self.landed(slot, ch, origin)
            use(slot)

    def finish(self):
        at = self.at
        for b in range(at.blocks):
            @pl.when(b != at.z)
            def _(b=b):
                for ch in range(self.CHUNKS):
                    self.copy(b, ch).wait_send()


LANES = 128
HALF_LANES = LANES // 2


def split_lanes(value):
    high = value.astype(BF16).astype(F32)
    return (high + pltpu.roll(value - high, HALF_LANES, 1)).astype(BF16)


def expert_kernel(o_ref, x_ref, small_ref, chosen_ref, wo_hbm, w_hbm, cot_hbm,
                  res_out, grad_out, attn_out, small_out, sums_out, y_out, core_land, *rest):
    big = cot_hbm.shape[0] > 4
    if big:
        xb_ref, dx_ref, land_ref, *rest = rest
        (xb_stage, dx_stage, land_stage, g_ref, *rest) = rest
    else:
        xb_ref, dx_ref, land_ref, *rest = rest
    (mix_ref, w_ref, cot_ref, acc_ref, gate_ref, dgu_ref, ga_ref, xt_ref, gat_ref, gg_ref, y_ref, stage_ref,
     gates_ref, router_ref, load_sem, y_sem, send_sem, recv_sem) = rest
    own_rows, width = x_ref.shape
    blocks = cot_hbm.shape[0]
    qcols = o_ref.shape[1]
    half = width // 2
    experts, _, ffe, _ = w_ref.shape
    at = Place(blocks)
    me = at.z
    lanes = Lanes(send_sem, recv_sem)
    at.enter()
    every = blocks * own_rows
    if big:
        wo_rows = [(slice(y * half, (y + 1) * half), g_ref.at[0, y, :, :width]) for y in range(2)]
    else:
        wo_rows = [(slice(0, every), dgu_ref.at[0]), (slice(every, width), dgu_ref.at[1, :width - every])]
    wo_load = [pltpu.make_async_copy(wo_hbm.at[rows, :], place, load_sem.at[y])
               for y, (rows, place) in enumerate(wo_rows)]
    for load in wo_load:
        load.start()
    quarter = half // 4
    here = aligned(at.h * quarter, quarter)
    w_loads = [pltpu.make_async_copy(w_hbm.at[place], w_ref.at[place], load_sem.at[4 + i])
               for i, place in enumerate(((0,), (1, at.y), (1, at.oy, here)))]
    for load in w_loads:
        load.start()
    late = Shared(at, lanes, 4, None, functools.partial(weight_chunk, w_ref))
    if not big:
        cot_loads = [pltpu.make_async_copy(cot_hbm.at[b], cot_ref.at[b * own_rows:(b + 1) * own_rows, :],
                                           load_sem.at[7 + b]) for b in range(blocks)]
        for load in cot_loads:
            load.start()

    total_experts = experts * blocks
    srows = small_ref.shape[0]
    is_router = lax.broadcasted_iota(jnp.int32, (srows, width), 0) < total_experts
    router_ref[...] = jnp.zeros_like(router_ref)
    router_ref[:srows, :] = jnp.where(is_router, small_ref[...].astype(F32), 0.0).astype(BF16)
    gain_two = small_ref[total_experts + 1:total_experts + 2, :].astype(F32)

    mixes = lanes.slots(4)

    def mix_cols(head):
        return mix_ref.at[:, pl.ds(pl.multiple_of(head * qcols, HEAD), qcols)]

    for head in (at.xn, at.xs, at.sib):
        lanes.put(mixes + at.h, o_ref.at[aligned(head * own_rows, own_rows), :], mix_cols(at.h), head=head)
    mix_ref[:, pl.ds(pl.multiple_of(at.h * qcols, HEAD), qcols)] = o_ref[aligned(at.h * own_rows, own_rows), :]
    for head in (at.sib, at.xn, at.xs):
        lanes.arrived(mixes + head, mix_cols(head), head=head)
    for load in w_loads:
        load.wait()
    for k in (2, 3):
        late.scatter(k)
    for load in wo_load:
        load.wait()
    step = 512
    for i in range(width // step):
        cols = slice(i * step, (i + 1) * step)
        res_out[:, cols] = x_ref[:, cols].astype(F32) + sum(
            mm(mix_ref[:, rows], place[:, cols]) for rows, place in wo_rows)

    def inverse_two():
        res = res_out[...]
        return lax.rsqrt(jnp.mean(res * res, axis=-1, keepdims=True) + NORM_EPSILON)

    n2 = (res_out[...] * inverse_two() * gain_two).astype(BF16)
    chosen = chosen_ref[...] > 0.0
    logits = jnp.where(chosen, mm(n2, router_ref[...], NT), MASKED)
    e_top = jnp.where(chosen, jnp.exp(logits - jnp.max(logits, axis=-1, keepdims=True)), 0.0)
    gates = e_top / jnp.sum(e_top, axis=-1, keepdims=True)
    gates_ref[...] = gates
    own_x = xb_stage if big else xb_ref.at[me]
    own_x[:, :width] = n2
    own_x[:, width:] = split_lanes(gates)

    def move(src, dst):
        copy = pltpu.make_async_copy(src, dst, load_sem.at[3])
        copy.start()
        copy.wait()

    if big:
        move(xb_stage, xb_ref.at[me])
    xs_slot, xs_sent = lanes.slots(blocks), lanes.sends(blocks + 2)

    def xs_copy(b, to, send):
        return remote(xb_ref.at[b], xb_ref.at[b], send_sem.at[xs_sent + send], recv_sem.at[xs_slot + b], blk=to)

    pl.when(me > 0)(lambda: xs_copy(me, me - 1, blocks).start())
    pl.when(me < blocks - 1)(lambda: xs_copy(me, me + 1, blocks + 1).start())

    if big:
        def clear(i, _):
            for e in range(experts):
                for y in range(2):
                    g_ref[e, y, aligned(i * 64, 64), :] = jnp.zeros((64, g_ref.shape[3]), BF16)
            return 0

        lax.fori_loop(0, half // 64, clear, 0)
    else:
        for load in cot_loads:
            load.wait()
    for k in (2, 3):
        late.forward(k)
    for k in (2, 3):
        late.finish(k)
    back = ColumnSum(at, lanes, dx_ref, land_ref)
    lane = lax.broadcasted_iota(jnp.int32, (own_rows, LANES), 1)
    tile = 256

    def y_copy(b):
        return pltpu.make_async_copy(y_ref, y_out.at[b], y_sem)

    def block(b, first):
        if big:
            move(xb_ref.at[b], xb_stage)
            move(cot_hbm.at[b], cot_ref)
        x_in = xb_stage if big else xb_ref.at[b]
        band_all = slice(None) if big else aligned(b * own_rows, own_rows)
        lanes_all = pl.ds(pl.multiple_of(b * own_rows, own_rows), own_rows)
        acc_ref[...] = jnp.zeros_like(acc_ref)
        gg_ref[...] = jnp.zeros_like(gg_ref)

        def hidden(e, _):
            index = me * experts + e
            pack = x_in[:, width:].astype(F32)
            mine = (lane == index) | (lane == index + HALF_LANES)
            gate_ref[...] = jnp.sum(jnp.where(mine, pack, 0.0), axis=1, keepdims=True)

            def inner(t, total):
                low = pl.ds(pl.multiple_of(t * tile, tile), tile)
                high = pl.ds(pl.multiple_of(ffe + t * tile, tile), tile)
                out_cols = slice(width, width + half)
                gate_pre = mm(x_in[:, :half], w_ref[e, 0, :, low]) + mm(x_in[:, half:width], w_ref[e, 1, :, low])
                up = mm(x_in[:, :half], w_ref[e, 0, :, high]) + mm(x_in[:, half:width], w_ref[e, 1, :, high])
                back_h = (mm(cot_ref[band_all, :half], w_ref[e, 0, low, out_cols], NT)
                          + mm(cot_ref[band_all, half:], w_ref[e, 1, low, out_cols], NT))
                value, slope = gelu_parts(gate_pre)
                act = (value * up).astype(BF16).astype(F32)
                gate = gate_ref[...]
                ga_ref[e, :, low] = (gate * act).astype(BF16)
                if not big:
                    gat_ref[e, low, lanes_all] = (gate * act).T.astype(BF16)
                d_act = gate * back_h
                dgu_ref[e, band_all, low] = (d_act * up * slope).astype(BF16)
                dgu_ref[e, band_all, high] = (d_act * value).astype(BF16)
                return total + jnp.sum(act * back_h, axis=1, keepdims=True)

            total = lax.fori_loop(0, ffe // tile, inner, jnp.zeros((own_rows, 1), F32))
            gg_ref[...] += jnp.where(lane == index, total, 0.0)
            for y in range(2):
                acc_ref[:, y * half:(y + 1) * half] += mm(dgu_ref[e, band_all, :], w_ref[e, y, :, :width], NT)
            return 0

        lax.fori_loop(0, experts, hidden, 0)
        part = dx_stage if big else dx_ref.at[b]
        part[:, :width] = acc_ref[...].astype(BF16)
        part[:, width:] = split_lanes(gg_ref[...])
        if big:
            move(dx_stage, dx_ref.at[b])
        back.first_send(b)

        if big:
            xt_ref[...] = x_in[:, :width].astype(F32).T.astype(BF16)

            def weights(e, _):
                gat_ref[0] = ga_ref[e].astype(F32).T.astype(BF16)

                def rows(i, _):
                    band = aligned(i * tile, tile)
                    for y in range(2):
                        x_cols = xt_ref[aligned(y * half + i * tile, tile), :]
                        for n in range(width // step):
                            cols = slice(n * step, (n + 1) * step)
                            total = g_ref[e, y, band, cols].astype(F32) + mm(x_cols, dgu_ref[e, :, cols])
                            g_ref[e, y, band, cols] = total.astype(BF16)
                        out_cols = slice(width, width + half)
                        total = (g_ref[e, y, band, out_cols].astype(F32)
                                 + mm(gat_ref[0, band, :], cot_ref[:, y * half:(y + 1) * half]))
                        g_ref[e, y, band, out_cols] = total.astype(BF16)
                    return 0

                return lax.fori_loop(0, half // tile, rows, 0)

            lax.fori_loop(0, experts, weights, 0)
        else:
            xt_ref[:, lanes_all] = x_in[:, :width].astype(F32).T.astype(BF16)

        pl.when(jnp.logical_not(first))(lambda: y_copy(b).wait())
        for y in range(2):
            total = mm(ga_ref[0], w_ref[0, y, :, width:])
            for e in range(1, experts):
                total = total + mm(ga_ref[e], w_ref[e, y, :, width:])
            y_ref[:, y * half:(y + 1) * half] = total.astype(BF16)
        y_copy(b).start()

    def distance(d, _):
        for b, origin, to in ((me - d, me - 1, me + 1), (me + d, me + 1, me - 1)):
            @pl.when((d > 0) & (b >= 0) & (b < blocks))
            def _(b=b, origin=origin, to=to):
                xs_copy(b, origin, 0).wait_recv()
                pl.when((to >= 0) & (to < blocks))(lambda: xs_copy(b, to, b).start())

        def side(s, _):
            b = jnp.where(s == 0, me - d, me + d)

            @pl.when((b >= 0) & (b < blocks) & ((d > 0) | (s == 0)))
            def _():
                block(jnp.clip(b, 0, blocks - 1), d == 0)

            return 0

        return lax.fori_loop(0, 2, side, 0)

    lax.fori_loop(0, blocks, distance, 0)
    y_copy(me).wait()

    late.settle()
    total_ref = g_ref if big else w_ref

    def weights_of(e):
        def rows(i, _):
            cols = pl.ds(pl.multiple_of(i * tile, tile), tile)
            for y in range(2):
                total = mm(xt_ref[y * half:(y + 1) * half, :], dgu_ref[e, :, cols])
                total_ref[e, y, :, cols] = total.astype(BF16)
            return 0

        def outs(i, _):
            for y in range(2):
                cols = pl.ds(pl.multiple_of(y * half + i * tile, tile), tile)
                place = pl.ds(pl.multiple_of(width + i * tile, tile), tile)
                total_ref[e, y, :, place] = mm(gat_ref[e], cot_ref[:, cols]).astype(BF16)
            return 0

        lax.fori_loop(0, 2 * ffe // tile, rows, 0)
        lax.fori_loop(0, half // tile, outs, 0)

    chunks = 4
    piece = half // chunks
    cores = lanes.slots(chunks)
    if not big:
        weights_of(1 - at.c)
    for k in range(chunks):
        band = pl.ds(k * piece, piece)
        lanes.put(cores + k, total_ref.at[1 - at.c, :, band, :], core_land.at[:, band, :], head=at.sib)

    def add(b, rows):
        if big:
            move(dx_ref.at[b, rows, :], dx_stage.at[rows, :])
            move(land_ref.at[b, rows, :], land_stage.at[rows, :])
            dx_stage[rows, :] = (dx_stage[rows, :].astype(F32) + land_stage[rows, :].astype(F32)).astype(BF16)
            move(dx_stage.at[rows, :], dx_ref.at[b, rows, :])
        else:
            dx_ref[b, rows, :] = (dx_ref[b, rows, :].astype(F32) + land_ref[b, rows, :].astype(F32)).astype(BF16)

    def core_sum(k):
        band = pl.ds(k * piece, piece)
        lanes.arrived(cores + k, core_land.at[:, band, :], head=at.sib)
        move(core_land.at[:, band, :], stage_ref)
        for y in range(2):
            total = total_ref[at.c, y, band, :].astype(F32) + stage_ref[y].astype(F32)
            total_ref[at.c, y, band, :] = total.astype(BF16)

    for phase in range(2):
        for d in range(1, blocks):
            back.relay(phase, d, add)
    if not big:
        weights_of(at.c)
    for k in range(chunks):
        core_sum(k)
    keep = pltpu.make_async_copy(total_ref.at[at.c], sums_out, load_sem.at[0])
    keep.start()

    if big:
        move(dx_ref.at[me], dx_stage)
    own_part = dx_stage if big else dx_ref.at[me]
    acc_ref[...] = own_part[:, :width].astype(F32)
    gg_ref[...] = own_part[:, width:].astype(F32)

    def take(slot):
        if big:
            move(land_ref.at[slot], land_stage)
        came = land_stage if big else land_ref.at[slot]
        acc_ref[...] += came[:, :width].astype(F32)
        gg_ref[...] += came[:, width:].astype(F32)

    for side in range(2):
        back.arrive(side, take)
    both = gg_ref[...]
    gate_grads = jnp.where(lane < HALF_LANES, both + pltpu.roll(both, HALF_LANES, 1), 0.0)
    gates = gates_ref[...]
    d_logits = (gates * (gate_grads - jnp.sum(gates * gate_grads, axis=-1, keepdims=True))).astype(BF16)
    inv = inverse_two()
    hat = res_out[...] * inv
    n2 = (hat * gain_two).astype(BF16)
    small_out[...] = mm(d_logits.astype(F32).T.astype(BF16), n2)[:small_out.shape[0], :]
    d_n2 = acc_ref[...] + mm(d_logits, router_ref[...])
    small_out[total_experts + 1:total_experts + 2, :] = jnp.sum(d_n2 * hat, axis=0, keepdims=True)
    pulled = d_n2 * gain_two
    if big:
        move(cot_hbm.at[me], cot_ref)
    own_cot = cot_ref[...] if big else cot_ref[aligned(me * own_rows, own_rows), :]
    grad = own_cot.astype(F32) + inv * (pulled - hat * jnp.mean(pulled * hat, axis=-1, keepdims=True))
    grad_out[...] = grad
    attn_out[...] = grad.astype(BF16)
    keep.wait()
    for b in range(blocks):
        up, down = (b < me) & (me < blocks - 1), (b > me) & (me > 0)
        pl.when(up)(lambda b=b: xs_copy(b, me + 1, b).wait_send())
        pl.when(down)(lambda b=b: xs_copy(b, me - 1, b).wait_send())
    pl.when(me > 0)(lambda: xs_copy(me, me - 1, blocks).wait_send())
    pl.when(me < blocks - 1)(lambda: xs_copy(me, me + 1, blocks + 1).wait_send())
    back.finish()
    lanes.drain()


def expert_layer(o, x, small, chosen, wo, w, cot):
    own_rows, width = x.shape
    blocks = cot.shape[0]
    experts, _, half, wide = w.shape
    ffe = half
    pack = width + LANES
    big = blocks > 4
    kept = own_rows if big else blocks * own_rows
    vm = pl.BlockSpec(memory_space=pltpu.VMEM)
    hbm = pl.BlockSpec(memory_space=pl.ANY)
    sds = jax.ShapeDtypeStruct
    column = [((blocks, own_rows, pack), BF16), ((blocks, own_rows, pack), BF16), ((blocks + 1, own_rows, pack), BF16)]
    if big:
        extra_out, extra_spec = tuple(sds(*c) for c in column), [hbm] * 3
        extra_scratch = [pltpu.VMEM((own_rows, pack), BF16)] * 3 + [pltpu.VMEM(w.shape, BF16)]
    else:
        extra_out, extra_spec = (), []
        extra_scratch = [pltpu.VMEM(*c) for c in column]
    outs = pl.pallas_call(
        expert_kernel,
        out_shape=(
            sds((own_rows, width), F32),
            sds((own_rows, width), F32),
            sds((own_rows, width), BF16),
            sds((-(-(experts * blocks + 2) // 8) * 8, width), F32),
            sds((2, half, wide), BF16),
            sds((blocks, own_rows, width), BF16),
            sds((2, half, wide), BF16),
        ) + extra_out,
        in_specs=[vm] * 4 + [hbm] * 3,
        out_specs=[vm] * 4 + [hbm] * 3 + extra_spec,
        scratch_shapes=extra_scratch + [
            pltpu.VMEM((own_rows, width), BF16),
            pltpu.VMEM(w.shape, BF16),
            pltpu.VMEM((kept, width), BF16),
            pltpu.VMEM((own_rows, width), F32),
            pltpu.VMEM((own_rows, 1), F32),
            pltpu.VMEM((experts, kept, 2 * ffe), BF16),
            pltpu.VMEM((experts, own_rows, ffe), BF16),
            pltpu.VMEM((width, kept), BF16),
            pltpu.VMEM((experts, ffe, kept), BF16),
            pltpu.VMEM((own_rows, LANES), F32),
            pltpu.VMEM((own_rows, width), BF16),
            pltpu.VMEM((2, half // 4, wide), BF16),
            pltpu.VMEM((own_rows, LANES), F32),
            pltpu.VMEM((LANES, width), BF16),
            pltpu.SemaphoreType.DMA((7 + blocks,)),
            pltpu.SemaphoreType.DMA,
        ] + semaphores(blocks),
        compiler_params=pltpu.CompilerParams(
            vmem_limit_bytes=VMEM_BYTES, collective_id=1, has_side_effects=True),
    )(o, x, small, chosen, wo, w, cot)
    return outs[:6]


class ExpertSums:
    CHUNKS = 8

    def __init__(self, at, lanes, grads, own, land_y, land_x, out, load_sem, keep_sem):
        self.at, self.lanes = at, lanes
        self.grads, self.own, self.out = grads, own, out
        self.land_y, self.land_x = land_y, land_x
        self.load_sem, self.keep_sem = load_sem, keep_sem
        self.rows = grads.shape[1] // self.CHUNKS
        n = self.CHUNKS
        self.ys, self.xr, self.cg = [lanes.slots(n) for _ in range(3)]
        self.sent = []
        self.kept = []

    def chunk(self, k):
        return pl.ds(k * self.rows, self.rows)

    def load(self):
        self.loads = [pltpu.make_async_copy(self.grads.at[y], self.own.at[y], self.load_sem.at[i])
                      for i, y in enumerate((self.at.oy, self.at.y))]
        for copy in self.loads:
            copy.start()

    def to_y(self):
        self.loads[0].wait()
        for k in range(self.CHUNKS):
            rows = self.chunk(k)
            self.sent.append(self.lanes.put(
                self.ys + k, self.own.at[self.at.oy, rows, :], self.land_y.at[rows, :], fsdp=self.at.oy))

    def y_sent(self):
        for copy in self.sent:
            self.lanes.settle(copy)

    def to_x(self, k):
        at, rows = self.at, self.chunk(k)
        if k == 0:
            self.loads[1].wait()
        self.lanes.arrived(self.ys + k, self.land_y.at[rows, :], fsdp=at.oy)
        total = self.own[at.y, rows, :].astype(F32) + self.land_y[rows, :].astype(F32)
        self.own[at.y, rows, :] = total.astype(BF16)
        self.lanes.put(self.xr + k, self.own.at[at.y, rows, :], self.land_x.at[rows, :], head=at.xn)

    def share(self, k):
        at, rows = self.at, self.chunk(k)
        self.lanes.arrived(self.xr + k, self.land_x.at[rows, :], head=at.xn)
        total = self.own[at.y, rows, :].astype(F32) + self.land_x[rows, :].astype(F32)
        self.land_x[rows, :] = total.astype(BF16)
        done, place = self.land_x.at[rows, :], self.out.at[at.c, rows, :]
        self.lanes.put(self.cg + k, done, place, head=at.sib)
        keep = pltpu.make_async_copy(done, place, self.keep_sem.at[k])
        keep.start()
        self.kept.append(keep)

    def finish(self):
        at = self.at
        for k in range(self.CHUNKS):
            self.lanes.arrived(self.cg + k, self.out.at[1 - at.c, self.chunk(k), :], head=at.sib)
            self.kept[k].wait()


class OutputSums:
    PARTS = 4

    def __init__(self, at, lanes, grad, land_y, land_z, out):
        self.at, self.lanes, self.grad = at, lanes, grad
        self.land_y, self.land_z, self.out = land_y, land_z, out
        self.rows = grad.shape[0] // self.PARTS
        self.ys = lanes.slots()
        self.zr, self.zg = lanes.slots(at.blocks), lanes.slots(self.PARTS)
        self.xg, self.cg = lanes.slots(self.PARTS), lanes.slots(self.PARTS)
        self.owner, self.giver = at.y == at.x, at.y != at.x
        self.summer = at.z < self.PARTS
        self.part = at.z % self.PARTS
        self.mine = aligned(self.part * self.rows, self.rows)

    def to_z(self):
        at = self.at
        for p in range(self.PARTS):
            self.lanes.put(self.zr + at.z, self.grad.at[pl.ds(p * self.rows, self.rows), :], self.land_z.at[at.z],
                           when=at.z != p, blk=p)

    def to_y(self, fetch):
        at = self.at
        for z in at.others():
            self.lanes.arrived(self.zr + z, self.land_z.at[z], when=self.summer, blk=z)

        @pl.when(self.summer)
        def _():
            total = self.grad[self.mine, :].astype(F32)
            for z in at.others():
                total = total + fetch(self.land_z.at[z])[...].astype(F32)
            self.grad[self.mine, :] = total.astype(BF16)

        self.lanes.put(self.ys, self.grad.at[self.mine, :], self.land_y, when=self.summer & self.giver, fsdp=at.oy)

    def place(self, core, p):
        return self.out.at[aligned(core * self.PARTS * self.rows + p * self.rows, self.rows), :]

    def share(self):
        at, p = self.at, self.part
        ready = self.summer & self.owner
        self.lanes.arrived(self.ys, self.land_y, when=ready, fsdp=at.oy)
        at_rows = aligned(at.c * self.PARTS * self.rows + p * self.rows, self.rows)

        @pl.when(ready)
        def _():
            total = self.grad[self.mine, :].astype(F32) + self.land_y[...].astype(F32)
            self.out[at_rows, :] = total.astype(BF16)

        place = self.place(at.c, p)
        for z in at.others():
            self.lanes.put(self.zg + p, place, place, when=ready, blk=z)
        self.lanes.put(self.xg + p, place, place, when=ready, head=at.xn)
        self.lanes.put(self.cg + p, place, place, when=ready, head=at.sib)

    def pass_on(self):
        at = self.at
        for p in range(self.PARTS):
            place = self.place(at.c, p)
            later = self.owner & (at.z != p)
            self.lanes.arrived(self.zg + p, place, when=later, blk=p)
            self.lanes.put(self.xg + p, place, place, when=later, head=at.xn)
            self.lanes.put(self.cg + p, place, place, when=later, head=at.sib)

    def take_over(self):
        at = self.at
        for p in range(self.PARTS):
            place = self.place(at.c, p)
            self.lanes.arrived(self.xg + p, place, when=self.giver, head=at.xn)
            self.lanes.put(self.cg + p, place, place, when=self.giver, head=at.sib)

    def finish(self):
        at = self.at
        for p in range(self.PARTS):
            self.lanes.arrived(self.cg + p, self.place(1 - at.c, p), head=at.sib)


def back_kernel(attn_ref, q_ref, ot_ref, start_ref, lse_ref, x_ref, cos_ref, sin_ref, gain_ref, small_ref,
                kv_in, wo_hbm, grads_hbm, y_in, res_hbm, res_grad_hbm, n1_hbm, w_hbm,
                block_out, tokens_out, small_out, kv_out, experts_out, output_out, query_out, y_land, *rest):
    blocks = kv_in.shape[0]
    big = blocks > 4
    dkv_stage = dwo_stage = None
    if big:
        yp_ref, dkv_land, dkv_sib, dwo_z, kv_ref, dkv_stage, dwo_stage, y_stage, kv_stage, *rest = rest
    else:
        yp_ref, dkv_land, dkv_sib, dwo_z, kv_ref, *rest = rest
    (dq_ref, dk_ref, dv_ref, kt_ref, delta_ref, do_ref, ag_ref, wo_ref, dwo_ref, dwo_y, dwo_land,
     own_ref, ey_ref, ex_ref, acc_ref, y_other, w_ref, dpre_ref, dn_sib, dn_x, dw_ref, dw_y, dw_z,
     sm_ref, sm_a, sm_b, sm_y, sm_z, land_ref, dkv_ref, load_sem, keep_sem, send_sem, recv_sem) = rest
    heads, rows, _ = q_ref.shape
    own_rows, width = attn_ref.shape
    half = width // 2
    half_rows = rows // 2
    qcols = heads * HEAD
    gain_row = 2 * blocks
    at = Place(blocks)
    me = at.z
    lanes = Lanes(send_sem, recv_sem)
    at.enter()
    experts = ExpertSums(at, lanes, grads_hbm, own_ref, ey_ref, ex_ref, experts_out, load_sem, keep_sem)
    output = OutputSums(at, lanes, dwo_ref, dwo_y, dwo_z, dwo_land)
    sums = ColumnSum(at, lanes, yp_ref, y_land)
    experts.load()
    forward, near, far, passed = gather_heads(at, lanes, attn_ref, ag_ref)

    def load(src, dst, sem):
        copy = pltpu.make_async_copy(src, dst, load_sem.at[sem])
        copy.start()
        return copy

    def move(src, dst):
        load(src, dst, 5).wait()

    wo_load = load(wo_hbm.at[aligned(at.h * qcols, qcols), :], wo_ref, 2)
    y_load = load(y_in, yp_ref, 3)
    if not big:
        kv_load = load(kv_in, kv_ref, 4)
    experts.to_y()
    y_load.wait()
    for b in range(blocks):
        sums.first_send(b)

    def add(b, band):
        move(y_land.at[b, band, :], y_other.at[band, :])
        if big:
            move(yp_ref.at[b, band, :], y_stage.at[band, :])
            y_stage[band, :] = (y_stage[band, :].astype(F32) + y_other[band, :].astype(F32)).astype(BF16)
            move(y_stage.at[band, :], yp_ref.at[b, band, :])
        else:
            yp_ref[b, band, :] = (yp_ref[b, band, :].astype(F32) + y_other[band, :].astype(F32)).astype(BF16)

    def fetch(stage):
        def get(ref):
            if big:
                move(ref, stage)
                return stage
            return ref
        return get

    wo_load.wait()

    def mix_back(head):
        band = aligned(head * own_rows, own_rows)
        grad = mm(ag_ref[band, :], wo_ref[...], NT).astype(BF16)
        for hh in range(heads):
            do_ref[hh, band, :] = grad[:, hh * HEAD:(hh + 1) * HEAD]

    ag_ref[aligned(at.h * own_rows, own_rows), :] = attn_ref[...]
    mix_back(at.h)
    near()
    mix_back(at.sib)
    forward()
    mix_back(at.xn)
    far()
    mix_back(at.xs)
    step = 512

    def weight_back(i, _):
        cols = pl.ds(pl.multiple_of(i * step, step), step)
        dwo_ref[:, cols] = mm(ot_ref[...], ag_ref[:, cols]).astype(BF16)
        return 0

    lax.fori_loop(0, width // step, weight_back, 0)
    output.to_z()
    lanes.settle(passed[0])
    n1_load = load(n1_hbm, ag_ref, 2)
    w_load = load(w_hbm, w_ref, 3)
    dq_ref[...] = jnp.zeros_like(dq_ref)
    for hh in range(heads):
        prod = do_ref[hh].astype(F32).T * ot_ref[hh * HEAD:(hh + 1) * HEAD, :].astype(F32)
        delta_ref[hh] = jnp.sum(prod, axis=0, keepdims=True)
    if not big:
        kv_load.wait()

    for k in (0, 1):
        experts.to_x(k)
    beside = [[(experts.to_x, 2), (experts.share, 0)],
              [(experts.to_x, 3), (experts.share, 1), (experts.to_x, 4)],
              [(experts.to_x, 5), (experts.share, 2), (experts.share, 3)]]

    def advance():
        for f, k in (beside.pop(0) if beside else ()):
            f(k)

    def opening(b):
        if big:
            move(kv_in.at[b], kv_stage)
        kv = kv_stage if big else kv_ref.at[b]
        kt_ref[...] = kv[:, :HEAD].astype(F32).T.astype(BF16)
        dk_ref[...] = jnp.zeros_like(dk_ref)
        dv_ref[...] = jnp.zeros_like(dv_ref)
        return kv

    def closing(b, kv):
        kv[:, :HEAD] = (dk_ref[...] * SCORE_SCALE).astype(BF16)
        kv[:, HEAD:] = dv_ref[...].astype(BF16)
        if big:
            move(kv_stage, kv_ref.at[b])

    def block(b):
        kv = opening(b)

        def tile(t, _):
            hh, i = t // (rows // TILE), t % (rows // TILE)
            cols = pl.ds(pl.multiple_of(i * TILE, TILE), TILE)
            unattend_tile(hh, cols, kv[:, :HEAD], kv[:, HEAD:], kt_ref[...], q_ref, do_ref,
                          start_ref, lse_ref, delta_ref, dq_ref, dk_ref, dv_ref, b * rows, None)
            return 0

        lax.fori_loop(0, heads * (rows // TILE), tile, 0)
        closing(b, kv)

    def half_of(core):
        return aligned(core * half_rows, half_rows)

    mine, other = half_of(at.c), half_of(1 - at.c)
    pair, column = lanes.slots(blocks), lanes.slots(blocks)

    def to_sibling(b, when):
        lanes.put(pair + b, kv_ref.at[b, other, :], dkv_sib.at[b], when=when, head=at.sib)

    def to_column(b):
        lanes.arrived(pair + b, dkv_sib.at[b], when=b < me, head=at.sib)

        @pl.when(b < me)
        def _():
            came = fetch(dkv_stage)(dkv_sib.at[b])
            if big:
                move(kv_ref.at[b, mine, :], kv_stage.at[mine, :])
            kv = kv_stage if big else kv_ref.at[b]
            kv[mine, :] = (kv[mine, :].astype(F32) + came[...].astype(F32)).astype(BF16)
            if big:
                move(kv_stage.at[mine, :], kv_ref.at[b, mine, :])

        lanes.put(column + me, kv_ref.at[b, mine, :], dkv_land.at[me], when=b < me, blk=b)

    for b in range(blocks - 1):
        pl.when(b < me)(functools.partial(block, b))
        to_sibling(b, b < me)
        sums.relay(0, b + 1, add)
        advance()
        if b > 0:
            to_column(b - 1)
    while beside:
        advance()
    to_column(blocks - 2)

    kv_own = opening(me)
    for i in range(rows // TILE):
        n = (i + 1) * TILE

        def diagonal(hh, _, i=i, n=n):
            unattend_tile(hh, slice(i * TILE, n), kv_own[:n, :HEAD], kv_own[:n, HEAD:], kt_ref[:, :n], q_ref, do_ref,
                          start_ref, lse_ref, delta_ref, dq_ref, dk_ref, dv_ref,
                          me * rows, me * rows + i * TILE)
            return 0

        lax.fori_loop(0, heads, diagonal, 0)
    closing(me, kv_own)
    to_sibling(me, None)
    for d in range(1, blocks):
        sums.relay(1, d, add)

    def unrotate(u, band):
        return u * cos_ref[band, :] - pltpu.roll(u, HEAD // 2, 1) * sin_ref[band, :]

    for hh in range(heads):
        dpre_ref[:, hh * HEAD:(hh + 1) * HEAD] = unrotate((dq_ref[hh] * SCORE_SCALE).T, slice(None)).astype(BF16)
    n1_load.wait()
    w_load.wait()
    n1_ref = ag_ref
    parts = 4
    part = half // parts
    band_rows = 256
    query_cols, keyval_cols = slice(0, qcols), slice(qcols, qcols + 2 * HEAD)

    def weight_half(y, cols_out):
        def body(i, _):
            cols = pl.ds(pl.multiple_of(y * half + i * band_rows, band_rows), band_rows)
            dw_ref[aligned(y * half + i * band_rows, band_rows), cols_out] = (
                mm(n1_ref[:, cols], dpre_ref[:, cols_out], TN).astype(BF16))
            return 0

        lax.fori_loop(0, half // band_rows, body, 0)

    def weight_part(y, p):
        return aligned(y * half + p * part, part)

    ys = (lanes.slots(parts), lanes.slots(parts))

    def weight_to_y(i, cols_out):
        weight_half(at.oy, cols_out)
        for p in range(parts):
            lanes.put(ys[i] + p, dw_ref.at[weight_part(at.oy, p), cols_out],
                      dw_y.at[pl.ds(p * part, part), cols_out], fsdp=at.oy)

    weight_to_y(0, query_cols)
    experts.to_x(6)

    dpre_ref[other, qcols:] = jnp.zeros((half_rows, 2 * HEAD), BF16)
    dkv_ref[:, :HEAD] = dk_ref[mine, :] * SCORE_SCALE
    dkv_ref[:, HEAD:] = dv_ref[mine, :]
    lanes.arrived(pair + me, dkv_sib.at[me], head=at.sib)
    dkv_ref[...] += fetch(dkv_stage)(dkv_sib.at[me])[...].astype(F32)
    for z in range(1, blocks):
        @pl.when(me < z)
        def _(z=z):
            lanes.arrived(column + z, dkv_land.at[z], blk=z)
            dkv_ref[...] += fetch(dkv_stage)(dkv_land.at[z])[...].astype(F32)

    dpre_ref[mine, qcols:qcols + HEAD] = unrotate(dkv_ref[:, :HEAD], mine).astype(BF16)
    dpre_ref[mine, qcols + HEAD:] = dkv_ref[:, HEAD:].astype(BF16)
    weight_to_y(1, keyval_cols)

    def input_part(head):
        return mm(dpre_ref[aligned(head * own_rows, own_rows), :], w_ref[...], NT)

    experts.y_sent()

    def dn_ref(i):
        return own_ref.at[at.oy, i * own_rows:(i + 1) * own_rows, :width]

    relay, direct, across = lanes.slots(), lanes.slots(), lanes.slots()
    dn_ref(0)[...] = input_part(at.xs).astype(BF16)
    lanes.put(relay, dn_ref(0), dn_sib.at[0], head=at.sib)
    dn_ref(2)[...] = input_part(at.sib).astype(BF16)
    lanes.put(direct, dn_ref(2), dn_sib.at[1], head=at.sib)
    lanes.arrived(relay, dn_sib.at[0], head=at.sib)
    dn_ref(1)[...] = (input_part(at.xn) + dn_sib[0].astype(F32)).astype(BF16)
    lanes.put(across, dn_ref(1), dn_x, head=at.xn)
    experts.to_x(7)
    experts.share(4)
    weight_half(at.y, slice(None))
    output.to_y(fetch(dwo_stage))

    zr = lanes.slots(blocks)
    for p in range(parts):
        rows_p = weight_part(at.y, p)
        for i, cols_out in enumerate((query_cols, keyval_cols)):
            lanes.arrived(ys[i] + p, dw_y.at[pl.ds(p * part, part), cols_out], fsdp=at.oy)
        total = dw_ref[rows_p, :].astype(F32) + dw_y[pl.ds(p * part, part), :].astype(F32)
        dw_ref[rows_p, :] = total.astype(BF16)
        lanes.put(zr + at.z, dw_ref.at[rows_p, :], dw_z.at[at.z], when=at.z != p, blk=p)
    experts.share(5)
    output.share()

    move(res_hbm, acc_ref)
    if big:
        move(yp_ref.at[me], y_stage)
    acc_ref[...] += (y_stage if big else yp_ref.at[me])[...].astype(F32)

    def take(slot):
        move(y_land.at[slot], y_other)
        acc_ref[...] += y_other[...].astype(F32)

    for side in range(2):
        sums.arrive(side, take)
    block_out[...] = acc_ref[...].astype(BF16)

    res_load = load(res_grad_hbm, acc_ref, 5)
    own = input_part(at.h)
    lanes.arrived(direct, dn_sib.at[1], head=at.sib)
    own = own + dn_sib[1].astype(F32)
    lanes.arrived(across, dn_x, head=at.xn)
    own = own + dn_x[...].astype(F32)
    x = x_ref[...].astype(F32)
    inv = lax.rsqrt(jnp.mean(x * x, axis=-1, keepdims=True) + NORM_EPSILON)
    hat = x * inv
    pulled = own * gain_ref[gain_row:gain_row + 1, :].astype(F32)
    slope = inv * (pulled - hat * jnp.mean(pulled * hat, axis=-1, keepdims=True))
    res_load.wait()
    tokens_out[...] = (acc_ref[...] + slope).astype(BF16)
    sm_ref[...] = small_ref[...]
    sm_ref[gain_row:gain_row + 1, :] = jnp.sum(own * hat, axis=0, keepdims=True)
    sa, sb, sy, sz = lanes.slots(), lanes.slots(), lanes.slots(), lanes.slots(blocks)
    lanes.put(sa, sm_ref, sm_a, head=at.sib)
    experts.share(6)

    p = at.z % parts
    summer = at.z < parts
    zg, xg, cg, cf = lanes.slots(parts), lanes.slots(parts), lanes.slots(parts), lanes.slots(parts)

    def place(head, q):
        return land_ref.at[head, pl.ds(q * part, part), :]

    for z in at.others():
        lanes.arrived(zr + z, dw_z.at[z], when=summer, blk=z)
    mine_w = weight_part(at.y, p)

    @pl.when(summer)
    def _():
        total = dw_ref[mine_w, :].astype(F32)
        for z in at.others():
            total = total + dw_z[z].astype(F32)
        dw_ref[mine_w, :] = total.astype(BF16)
        land_ref[at.h, aligned(p * part, part), :] = total.astype(BF16)

    for z in at.others():
        lanes.put(zg + p, dw_ref.at[mine_w, :], place(at.h, p), when=summer, blk=z)
    lanes.put(xg + p, dw_ref.at[mine_w, :], place(at.h, p), when=summer, head=at.xn)
    lanes.put(cg + p, dw_ref.at[mine_w, :], place(at.h, p), when=summer, head=at.sib)
    lanes.arrived(sa, sm_a, head=at.sib)
    sm_a[...] = sm_a[...] + sm_ref[...]
    lanes.put(sb, sm_a, sm_b, head=at.xn)
    output.pass_on()
    experts.share(7)

    lanes.arrived(sb, sm_b, head=at.xn)
    sm_b[...] = sm_a[...] + sm_b[...]
    mine_cols = pl.ds(pl.multiple_of(at.y * half, half), half)
    other_cols = pl.ds(pl.multiple_of(at.oy * half, half), half)
    lanes.put(sy, sm_b.at[:, other_cols], sm_y, fsdp=at.oy)
    for q in range(parts):
        later = at.z != q
        lanes.arrived(zg + q, place(at.h, q), when=later, blk=q)
        lanes.put(xg + q, place(at.h, q), place(at.h, q), when=later, head=at.xn)
        lanes.put(cg + q, place(at.h, q), place(at.h, q), when=later, head=at.sib)
    lanes.arrived(sy, sm_y, fsdp=at.oy)
    sm_z[at.z] = sm_b[:, mine_cols] + sm_y[...]
    for z in at.others():
        lanes.put(sz + at.z, sm_z.at[at.z], sm_z.at[at.z], blk=z)
    output.take_over()
    for q in range(parts):
        lanes.arrived(xg + q, place(at.xn, q), head=at.xn)
        lanes.put(cf + q, place(at.xn, q), place(at.xn, q), head=at.sib)
    for z in at.others():
        lanes.arrived(sz + z, sm_z.at[z], blk=z)
    total = sm_z[0]
    for z in range(1, blocks):
        total = total + sm_z[z]
    small_out[...] = total
    output.finish()
    keeps = [load(dwo_land, output_out, 0)]
    for q in range(parts):
        lanes.arrived(cg + q, place(at.sib, q), head=at.sib)
        lanes.arrived(cf + q, place(at.xs, q), head=at.sib)
    for head in range(4):
        keeps.append(load(land_ref.at[head, :, :qcols], query_out.at[:, head * qcols:(head + 1) * qcols], 1 + head))
    for g in range(KEYVALUE_HEADS):
        both = land_ref[2 * g, :, qcols:].astype(F32) + land_ref[2 * g + 1, :, qcols:].astype(F32)
        kv_out[:, g * HEAD:(g + 1) * HEAD] = both[:, :HEAD]
        kv_out[:, (KEYVALUE_HEADS + g) * HEAD:(KEYVALUE_HEADS + g + 1) * HEAD] = both[:, HEAD:]
    experts.finish()
    for keep in keeps:
        keep.wait()
    sums.finish()
    lanes.drain()


def backward(attn_grad, q, ot, start, lse, x, cosine, sine, gain, small, kv, wo, grads, y_parts, res, res_grad, n1, w):
    heads, rows, _ = q.shape
    blocks = kv.shape[0]
    own_rows, width = attn_grad.shape
    qcols = heads * HEAD
    _, half, wide = grads.shape
    cols = w.shape[1]
    srows = small.shape[0]
    n = ExpertSums.CHUNKS
    vm = pl.BlockSpec(memory_space=pltpu.VMEM)
    hbm = pl.BlockSpec(memory_space=pl.ANY)
    part = qcols // OutputSums.PARTS
    sds = jax.ShapeDtypeStruct
    column = [((blocks, own_rows, width), BF16), ((blocks, rows // 2, 2 * HEAD), BF16),
              ((blocks, rows // 2, 2 * HEAD), BF16), ((blocks, part, width), BF16), (kv.shape, BF16)]
    if blocks > 4:
        extra_out, extra_spec = tuple(sds(*c) for c in column), [hbm] * 5
        extra_scratch = [pltpu.VMEM((rows // 2, 2 * HEAD), BF16), pltpu.VMEM((part, width), BF16),
                         pltpu.VMEM((own_rows, width), BF16), pltpu.VMEM((rows, 2 * HEAD), BF16)]
    else:
        extra_out, extra_spec = (), []
        extra_scratch = [pltpu.VMEM(*c) for c in column]
    return pl.pallas_call(
        back_kernel,
        out_shape=(
            sds((own_rows, width), BF16),
            sds((own_rows, width), BF16),
            sds((srows, half), F32),
            sds((half, 2 * KEYVALUE_HEADS * HEAD), F32),
            sds((2, half, wide), BF16),
            sds((2 * qcols, width), BF16),
            sds((half, rows // own_rows * qcols), BF16),
            sds((blocks + 1, own_rows, width), BF16),
        ) + extra_out,
        in_specs=[vm] * 10 + [hbm] * 8,
        out_specs=[vm] * 4 + [hbm] * 4 + extra_spec,
        scratch_shapes=extra_scratch + [
            pltpu.VMEM((heads, HEAD, rows), F32),
            pltpu.VMEM((rows, HEAD), F32),
            pltpu.VMEM((rows, HEAD), F32),
            pltpu.VMEM((HEAD, rows), BF16),
            pltpu.VMEM((heads, 1, rows), F32),
            pltpu.VMEM((heads, rows, HEAD), BF16),
            pltpu.VMEM((rows, width), BF16),
            pltpu.VMEM((qcols, width), BF16),
            pltpu.VMEM((qcols, width), BF16),
            pltpu.VMEM((part, width), BF16),
            pltpu.VMEM((2 * qcols, width), BF16),
            pltpu.VMEM((2, half, wide), BF16),
            pltpu.VMEM((half, wide), BF16),
            pltpu.VMEM((half, wide), BF16),
            pltpu.VMEM((own_rows, width), F32),
            pltpu.VMEM((own_rows, width), BF16),
            pltpu.VMEM((width, cols), BF16),
            pltpu.VMEM((rows, cols), BF16),
            pltpu.VMEM((2, own_rows, width), BF16),
            pltpu.VMEM((own_rows, width), BF16),
            pltpu.VMEM((width, cols), BF16),
            pltpu.VMEM((half, cols), BF16),
            pltpu.VMEM((blocks, half // 4, cols), BF16),
            pltpu.VMEM((srows, width), F32),
            pltpu.VMEM((srows, width), F32),
            pltpu.VMEM((srows, width), F32),
            pltpu.VMEM((srows, half), F32),
            pltpu.VMEM((blocks, srows, half), F32),
            pltpu.VMEM((rows // own_rows, half, cols), BF16),
            pltpu.VMEM((rows // 2, 2 * HEAD), F32),
            pltpu.SemaphoreType.DMA((6,)),
            pltpu.SemaphoreType.DMA((n,)),
        ] + semaphores(blocks),
        compiler_params=pltpu.CompilerParams(
            vmem_limit_bytes=VMEM_BYTES, collective_id=2, has_side_effects=True),
    )(attn_grad, q, ot, start, lse, x, cosine, sine, gain, small, kv, wo, grads, y_parts, res, res_grad, n1, w)[:7]


def on_device(tokens, documents, routes, cotangent, first_gain, query_weight, keyvalue_weight, output_weight,
              second_gain, router_weight, expert_in, expert_out):
    z = lax.axis_index("blk")
    blocks = lax.axis_size("blk")
    rows, width = tokens.shape[1:]
    group = lax.axis_size("head") * rows
    experts = router_weight.shape[1]
    half = query_weight.shape[0]

    small_rows = -(-(2 + experts) // 16) * 16
    small = jnp.concatenate([router_weight.T, first_gain[None], second_gain[None],
                             jnp.zeros((small_rows - 2 - experts, half), BF16)], axis=0)
    pos = (z * group + jnp.arange(group, dtype=jnp.int32)).astype(F32)
    inverse = jnp.power(ROPE_BASE, -jnp.arange(HEAD // 2).astype(F32) * 2.0 / HEAD)
    angle = pos[:, None] * inverse[None, :]
    cos, sin = jnp.cos(angle), jnp.sin(angle)
    cosine = jnp.concatenate([cos, cos], axis=-1)
    sine = jnp.concatenate([-sin, sin], axis=-1)
    doc = documents[0]
    doc_q = lax.dynamic_slice_in_dim(doc, z * group, group, 0)
    start = sum(jnp.where(doc_q > d, jnp.sum((doc == d).astype(jnp.int32)), 0) for d in range(DOCUMENTS - 1))[None, :]
    chosen = jnp.any(routes[0][:, :, None] == jnp.arange(LANES, dtype=jnp.int32), axis=1).astype(F32)

    q, mixed, mixed_t, lse, n1, small, wqkv, kv_all, wo, w_experts, cots = front(
        blocks, tokens[0], small, query_weight, keyvalue_weight, output_weight, expert_in, expert_out,
        cotangent[0], cosine, sine, start)
    res1, res_grad, attn_grad, d_small, grads, y_parts = expert_layer(
        mixed, tokens[0], small, chosen, wo, w_experts, cots)
    block_out, tokens_grad, d_small, d_keyval, d_experts, d_wo, d_query = backward(
        attn_grad, q, mixed_t, start, lse, tokens[0], cosine, sine, small, d_small,
        kv_all, wo, grads, y_parts, res1, res_grad, n1, wqkv)
    return (block_out[None], tokens_grad[None], d_small[experts], d_query.astype(F32), d_keyval, d_wo.astype(F32),
            d_small[experts + 1], d_small[:experts].T, d_experts[:, :, :width].astype(F32),
            d_experts[:, :, width:].astype(F32))


def solution(mesh):
    token_spec = P("fsdp", ("blk", "head"), None)
    row_spec = P("fsdp", None)
    in_spec = P("blk", "fsdp", None)
    out_spec = P("blk", None, "fsdp")
    return jax.shard_map(
        on_device,
        mesh=mesh,
        in_specs=(token_spec, row_spec, token_spec, token_spec, P("fsdp"), row_spec, row_spec, row_spec, P("fsdp"),
                  row_spec, in_spec, out_spec),
        out_specs=(token_spec, token_spec, P("fsdp"), row_spec, row_spec, row_spec, P("fsdp"), row_spec, in_spec,
                   out_spec),
        check_vma=False,
    )
```

```python
import functools

import jax
import jax.numpy as jnp
from jax import lax
from jax.experimental import pallas as pl
from jax.experimental.pallas import tpu as pltpu
from jax.sharding import PartitionSpec as P

QUERY_HEADS = 12
KEYVALUE_HEADS = 2
HEAD = 128
NORM_EPSILON = 1e-06
ROPE_BASE = 1000000.0
MASKED = -1e30
DOCUMENTS = 4
LOG2E = 1.4426950408889634
SCORE_LOG2 = HEAD ** (-0.5) * LOG2E
SCORE_SCALE = HEAD ** (-0.5)
TILE = 256
BF16 = jnp.bfloat16
F32 = jnp.float32
VMEM_BYTES = 63 * 1024 * 1024

NN = (((1,), (0,)), ((), ()))
NT = (((1,), (1,)), ((), ()))
TN = (((0,), (0,)), ((), ()))


def mm(a, b, dims=NN):
    return lax.dot_general(a, b, dims, preferred_element_type=F32)


def gelu_parts(gate):
    c = 0.7978845608028654
    cube = 0.044715 * gate * gate * gate
    t = jnp.tanh(c * (gate + cube))
    value = 0.5 * gate * (1.0 + t)
    slope = 0.5 * (1.0 + t) + 0.5 * gate * (1.0 - t * t) * c * (1.0 + 3.0 * 0.044715 * gate * gate)
    return value, slope


def score_tile(key_rows, q_tile, start_row, first_key, q_first):
    scores = mm(key_rows, q_tile, NT) * SCORE_LOG2
    key_pos = first_key + lax.broadcasted_iota(jnp.int32, scores.shape, 0)
    allowed = key_pos >= start_row
    if q_first is not None:
        q_pos = q_first + lax.broadcasted_iota(jnp.int32, scores.shape, 1)
        allowed = allowed & (key_pos <= q_pos)
    return jnp.where(allowed, scores, MASKED)


def attend_tile(hh, cols, key_rows, value_cols, q_ref, start_ref, m_ref, l_ref, acc_ref, first_key, q_first):
    q_tile = q_ref[hh, cols, :]
    scores = score_tile(key_rows, q_tile, start_ref[:, cols], first_key, q_first)
    old = m_ref[hh, :, cols]
    new = jnp.maximum(old, jnp.max(scores, axis=0, keepdims=True))
    factor = jnp.exp2(old - new)
    prob = jnp.exp2(scores - new)
    m_ref[hh, :, cols] = new
    l_ref[hh, :, cols] = l_ref[hh, :, cols] * factor + jnp.sum(prob, axis=0, keepdims=True)
    acc_ref[hh, :, cols] = acc_ref[hh, :, cols] * factor + mm(value_cols, prob.astype(BF16))


def unattend_tile(hh, cols, key_rows, value_rows, key_cols, q_ref, do_ref, start_ref, lse_ref, delta_ref,
                  dq_ref, dk_ref, dv_ref, first_key, q_first):
    n = key_rows.shape[0]
    q_tile = q_ref[hh, cols, :]
    do_tile = do_ref[hh, cols, :]
    scores = score_tile(key_rows, q_tile, start_ref[:, cols], first_key, q_first)
    prob = jnp.exp2(scores - lse_ref[hh, :, cols])
    dv_ref[:n, :] += mm(prob.astype(BF16), do_tile)
    prob_grad = mm(value_rows, do_tile, NT)
    score_grad = (prob * (prob_grad - delta_ref[hh, :, cols])).astype(BF16)
    dk_ref[:n, :] += mm(score_grad, q_tile)
    dq_ref[hh, :, cols] += mm(key_cols, score_grad)


def remote(src, dst, send_sem, recv_sem, **to):
    return pltpu.make_async_remote_copy(
        src_ref=src, dst_ref=dst, send_sem=send_sem, recv_sem=recv_sem, device_id=to,
        device_id_type=pl.DeviceIdType.MESH)


class Lanes:
    def __init__(self, send, recv):
        self.send, self.recv, self.used, self.sent, self.pending = send, recv, 0, 0, []

    def slots(self, count=1):
        first = self.used
        self.used += count
        assert self.used <= self.recv.shape[0]
        return first

    def sends(self, count):
        first = self.sent
        self.sent += count
        assert self.sent <= self.send.shape[0]
        return first

    def put(self, slot, src, dst, when=None, **to):
        assert self.sent < self.send.shape[0]
        copy = remote(src, dst, self.send.at[self.sent], self.recv.at[slot], **to)
        self.sent += 1
        if when is None:
            copy.start()
        else:
            pl.when(when)(copy.start)
        self.pending.append((copy, when))
        return self.pending[-1]

    def settle(self, entry):
        copy, when = entry
        self.pending = [other for other in self.pending if other is not entry]
        if when is None:
            copy.wait_send()
        else:
            pl.when(when)(copy.wait_send)

    def arrived(self, slot, dst, when=None, **origin):
        copy = remote(dst, dst, self.send.at[0], self.recv.at[slot], **origin)
        if when is None:
            copy.wait_recv()
        else:
            pl.when(when)(copy.wait_recv)

    def drain(self):
        for copy, when in self.pending:
            if when is None:
                copy.wait_send()
            else:
                pl.when(when)(copy.wait_send)
        self.pending = []


class Place:
    def __init__(self, blocks):
        self.z, self.h, self.y = lax.axis_index("blk"), lax.axis_index("head"), lax.axis_index("fsdp")
        self.blocks = blocks
        self.x, self.c = self.h // 2, self.h % 2
        self.sib = 2 * self.x + 1 - self.c
        self.xn = 2 * (1 - self.x) + self.c
        self.xs = 2 * (1 - self.x) + 1 - self.c
        self.oy = 1 - self.y

    def others(self):
        return [(self.z + d) % self.blocks for d in range(1, self.blocks)]

    def enter(self):
        barrier = pltpu.get_barrier_semaphore()

        def greet(**to):
            pl.semaphore_signal(barrier, inc=1, device_id=to, device_id_type=pl.DeviceIdType.MESH)

        for head in (self.sib, self.xn, self.xs):
            greet(head=head)
        greet(fsdp=self.oy)
        for z in self.others():
            greet(blk=z)
        pl.semaphore_wait(barrier, 4 + self.blocks - 1)


def gather_heads(at, lanes, own, land):
    s = lanes.slots(3)
    rows = own.shape[0]

    def slot(head):
        return land.at[pl.ds(pl.multiple_of(head * rows, rows), rows), :]

    lanes.put(s, own, slot(at.h), head=at.xn)
    lanes.put(s + 1, own, slot(at.h), head=at.sib)

    passed = []

    def forward():
        lanes.arrived(s, slot(at.xn), head=at.xn)
        passed.append(lanes.put(s + 2, slot(at.xn), slot(at.xn), head=at.sib))

    def near():
        lanes.arrived(s + 1, slot(at.sib), head=at.sib)

    def far():
        lanes.arrived(s + 2, slot(at.xs), head=at.sib)

    return forward, near, far, passed


def aligned(index, size):
    return pl.ds(pl.multiple_of(index, 16), size)


def semaphores(blocks):
    count = 128 + 16 * blocks
    return [pltpu.SemaphoreType.DMA((count,)), pltpu.SemaphoreType.DMA((count,))]


class Shared:
    def __init__(self, at, lanes, chunks, give, hold):
        self.at, self.lanes, self.chunks, self.give, self.hold = at, lanes, chunks, give, hold
        self.pieces = len(give(0)) if give else 0
        self.ys = lanes.slots(chunks * self.pieces)
        self.xn, self.sib, self.far = lanes.slots(chunks), lanes.slots(chunks), lanes.slots(chunks)
        self.sent = []

    def begin(self, k):
        for i, (src, dst) in enumerate(self.give(k)):
            self.lanes.put(self.ys + k * self.pieces + i, src, dst(self.at.y), fsdp=self.at.oy)

    def landed(self, k):
        for i, (src, dst) in enumerate(self.give(k)):
            self.lanes.arrived(self.ys + k * self.pieces + i, dst(self.at.oy), fsdp=self.at.oy)

    def spread(self, k):
        self.landed(k)
        self.scatter(k)

    def scatter(self, k):
        at = self.at
        place = self.hold(k, at.h, at.oy)
        self.sent.append(self.lanes.put(self.xn + k, place, place, head=at.xn))
        self.sent.append(self.lanes.put(self.sib + k, place, place, head=at.sib))

    def forward(self, k):
        at = self.at
        place = self.hold(k, at.xn, at.oy)
        self.lanes.arrived(self.xn + k, place, head=at.xn)
        self.sent.append(self.lanes.put(self.far + k, place, place, head=at.sib))

    def settle(self):
        for entry in self.sent:
            self.lanes.settle(entry)

    def finish(self, k):
        at = self.at
        self.lanes.arrived(self.sib + k, self.hold(k, at.sib, at.oy), head=at.sib)
        self.lanes.arrived(self.far + k, self.hold(k, at.xs, at.oy), head=at.sib)


def weight_chunk(w_ref, k, head, y):
    quarter = w_ref.shape[2] // 4
    piece = quarter // 2
    return w_ref.at[k // 2, y, aligned(head * quarter + k % 2 * piece, piece), :]


class Column:
    def __init__(self, at, lanes, land):
        self.at, self.lanes, self.land = at, lanes, land
        self.slot = lanes.slots(at.blocks)

    def begin(self, own):
        at = self.at
        place = self.land.at[at.z]
        self.lanes.put(self.slot + at.z, own, place, when=at.z < at.blocks - 1, blk=at.z + 1)
        self.lanes.put(self.slot + at.z, own, place, when=at.z > 0, blk=at.z - 1)

    def hand_on(self, d):
        at = self.at
        for b, origin, next_z in ((at.z - d, at.z - 1, at.z + 1), (at.z + d, at.z + 1, at.z - 1)):
            there = (b >= 0) & (b < at.blocks)
            safe = jnp.clip(b, 0, at.blocks - 1)
            self.lanes.arrived(self.slot + safe, self.land.at[safe], when=there, blk=origin)
            self.lanes.put(self.slot + safe, self.land.at[safe], self.land.at[safe],
                           when=there & (next_z >= 0) & (next_z < at.blocks), blk=next_z)


def front_kernel(x_ref, small_ref, wq_hbm, wkv_hbm, wo_hbm, win_hbm, wout_hbm, cot_hbm, cos_ref, sin_ref, start_ref,
                 q_ref, o_ref, ot_ref, lse_ref, n1_ref, small_out, wqkv_out, kv_out, wo_out, w_out, cot_out,
                 xg_ref, small_land, wqkv_ref, kv_ref, m_ref, l_ref, acc_ref, vt_ref, wo_ref, w_ref, cot_ref,
                 load_sem, send_sem, recv_sem):
    heads, rows, _ = q_ref.shape
    own_rows, width = x_ref.shape
    blocks = kv_ref.shape[0]
    half = wq_hbm.shape[0]
    qcols = heads * HEAD
    experts = 2 * blocks
    at = Place(blocks)
    me = at.z
    lanes = Lanes(send_sem, recv_sem)
    at.enter()
    local = []

    def copy_here(src, dst):
        copy = pltpu.make_async_copy(src, dst, load_sem.at[len(local)])
        copy.start()
        local.append(copy)
        return copy

    forward, near, far, _ = gather_heads(at, lanes, x_ref, xg_ref)
    g = at.x
    q_from = pl.ds(pl.multiple_of(at.h * qcols, HEAD), qcols)
    k_from = pl.ds(pl.multiple_of(g * HEAD, HEAD), HEAD)
    v_from = pl.ds(pl.multiple_of((KEYVALUE_HEADS + g) * HEAD, HEAD), HEAD)
    columns = ((wq_hbm.at[:, q_from], slice(0, qcols)), (wkv_hbm.at[:, k_from], slice(qcols, qcols + HEAD)),
               (wkv_hbm.at[:, v_from], slice(qcols + HEAD, qcols + 2 * HEAD)))

    def weight_rows(y, cols):
        return wqkv_ref.at[aligned(y * half, half), cols]

    ws = lanes.slots(3)
    for i, (src, cols) in enumerate(columns):
        lanes.put(ws + i, src, weight_rows(at.y, cols), fsdp=at.oy)
    smalls = lanes.slots()
    lanes.put(smalls, small_ref, small_land, fsdp=at.oy)
    own_weights = [copy_here(src, weight_rows(at.y, cols)) for src, cols in columns]
    cots = Column(at, lanes, cot_ref)
    own_half = pl.ds(pl.multiple_of(at.y * half, half), half)
    cot_load = copy_here(cot_hbm, cot_ref.at[me])
    wo_load = copy_here(wo_hbm, wo_ref.at[own_half, :])
    w_loads = [copy_here(win_hbm, w_ref.at[:, at.y, :, :width]), copy_here(wout_hbm, w_ref.at[:, at.y, :, width:])]
    cot_load.wait()
    cots.begin(cot_ref.at[me])

    quarter = half // 4

    def wo_place(k, head, y):
        return wo_ref.at[aligned(y * half + head * quarter, quarter), :]

    shared_wo = Shared(at, lanes, 1,
                       lambda k: [(wo_place(0, at.h, at.y), lambda y: wo_place(0, at.h, y))],
                       wo_place)
    chunks, spread_here = 4, 2

    def w_place(k, head, y):
        return weight_chunk(w_ref, k, head, y)

    def w_give(k):
        return [(w_place(k, at.h, at.y), lambda y: w_place(k, at.h, y))]

    shared_w = Shared(at, lanes, chunks, w_give, w_place)

    small_out[:, :half] = jnp.zeros((small_ref.shape[0], half), BF16)
    lanes.arrived(smalls, small_land, fsdp=at.oy)
    for y in range(2):
        @pl.when(at.y == y)
        def _(y=y):
            small_out[:, y * half:(y + 1) * half] = small_ref[...]
            small_out[:, (1 - y) * half:(2 - y) * half] = small_land[...]

    def norm(head, block):
        x = block.astype(F32)
        inv = lax.rsqrt(jnp.mean(x * x, axis=-1, keepdims=True) + NORM_EPSILON)
        n1_ref[aligned(head * own_rows, own_rows), :] = (x * inv * small_out[experts:experts + 1, :].astype(F32)).astype(BF16)

    def gathered(head):
        return xg_ref[aligned(head * own_rows, own_rows), :]

    norm(at.h, x_ref[...])
    near()
    norm(at.sib, gathered(at.sib))
    forward()
    norm(at.xn, gathered(at.xn))
    far()
    norm(at.xs, gathered(at.xs))
    for copy in own_weights:
        copy.wait()
    for i, (_, cols) in enumerate(columns):
        lanes.arrived(ws + i, weight_rows(at.oy, cols), fsdp=at.oy)
    wo_load.wait()
    shared_wo.begin(0)
    for load in w_loads:
        load.wait()
    for k in range(chunks):
        shared_w.begin(k)
    cots.hand_on(1)

    def project(i, _):
        band = aligned(i * TILE, TILE)
        pre = mm(n1_ref[band, :], wqkv_ref[...])
        cosine, sine = cos_ref[band, :], sin_ref[band, :]

        def turned(u):
            return (u * cosine + pltpu.roll(u, HEAD // 2, 1) * sine).astype(BF16)

        for hh in range(heads):
            q_ref[hh, band, :] = turned(pre[:, hh * HEAD:(hh + 1) * HEAD])
        kv_ref[me, 0, band, :] = turned(pre[:, qcols:qcols + HEAD])
        kv_ref[me, 1, band, :] = pre[:, qcols + HEAD:].astype(BF16)
        return 0

    lax.fori_loop(0, rows // TILE, project, 0)

    kvs, kvc = lanes.slots(blocks), lanes.slots(blocks)

    def kv_half(b, core):
        return kv_ref.at[b, core]

    lanes.put(kvs + me, kv_half(me, at.c), kv_half(me, at.c), when=me < blocks - 1, blk=me + 1)
    late = [copy_here(wqkv_ref, wqkv_out), copy_here(wo_ref.at[own_half, :], wo_out.at[own_half, :]),
            copy_here(w_ref.at[:, at.y], w_out.at[:, at.y])]

    m_ref[...] = jnp.full_like(m_ref, MASKED)
    l_ref[...] = jnp.zeros_like(l_ref)
    acc_ref[...] = jnp.zeros_like(acc_ref)

    def transpose_values(b):
        vt_ref[...] = kv_ref[b, 1].astype(F32).T.astype(BF16)

    transpose_values(me)
    for i in range(rows // TILE):
        n = (i + 1) * TILE

        def diagonal(hh, _, i=i, n=n):
            attend_tile(hh, slice(i * TILE, n), kv_ref[me, 0, :n, :], vt_ref[:, :n], q_ref, start_ref,
                        m_ref, l_ref, acc_ref, me * rows, me * rows + i * TILE)
            return 0

        lax.fori_loop(0, heads, diagonal, 0)

    def block(b):
        transpose_values(b)

        def tile(t, _):
            hh, i = t // (rows // TILE), t % (rows // TILE)
            cols = pl.ds(pl.multiple_of(i * TILE, TILE), TILE)
            attend_tile(hh, cols, kv_ref[b, 0], vt_ref[...], q_ref, start_ref,
                        m_ref, l_ref, acc_ref, b * rows, None)
            return 0

        lax.fori_loop(0, heads * (rows // TILE), tile, 0)

    ticks = [[functools.partial(shared_wo.spread, 0), functools.partial(shared_w.spread, 0)],
             [functools.partial(shared_w.spread, 1), functools.partial(shared_wo.forward, 0),
              functools.partial(cots.hand_on, 2)],
             [functools.partial(shared_w.forward, 0)] + [functools.partial(cots.hand_on, d) for d in range(3, blocks)],
             [functools.partial(shared_w.forward, 1)]]

    def tick():
        if ticks:
            for f in ticks.pop(0):
                f()

    for d in range(1, blocks):
        b = jnp.maximum(me - d, 0)
        there = me >= d
        lanes.arrived(kvs + b, kv_half(b, at.c), when=there, blk=me - 1)
        lanes.put(kvs + b, kv_half(b, at.c), kv_half(b, at.c), when=there & (me < blocks - 1), blk=me + 1)
        lanes.put(kvc + b, kv_half(b, at.c), kv_half(b, at.c), when=there, head=at.sib)
        lanes.arrived(kvc + b, kv_half(b, 1 - at.c), when=there, head=at.sib)
        pl.when(there)(functools.partial(block, b))
        tick()

    for hh in range(heads):
        total = l_ref[hh]
        done = acc_ref[hh] / total
        ot_ref[hh * HEAD:(hh + 1) * HEAD, :] = done.astype(BF16)
        o_ref[:, hh * HEAD:(hh + 1) * HEAD] = done.T.astype(BF16)
        lse_ref[hh] = m_ref[hh] + jnp.log2(total)
    kv_copies = [pltpu.make_async_copy(kv_ref.at[b], kv_out.at[b], load_sem.at[15]) for b in range(blocks)]
    for b, copy in enumerate(kv_copies):
        @pl.when(b <= me)
        def _(copy=copy):
            copy.start()
            copy.wait()
    while ticks:
        tick()
    shared_wo.finish(0)
    other_half = pl.ds(pl.multiple_of(at.oy * half, half), half)
    late.append(copy_here(wo_ref.at[other_half, :], wo_out.at[other_half, :]))
    late.append(copy_here(cot_ref, cot_out))
    for k in range(spread_here):
        shared_w.finish(k)
    for k in range(spread_here, chunks):
        shared_w.landed(k)
    late.append(copy_here(w_ref.at[:, at.oy], w_out.at[:, at.oy]))
    for copy in late:
        copy.wait()
    lanes.drain()


def front(blocks, x, small, wq, wkv, wo, win, wout, cot, cosine, sine, start):
    own_rows, width = x.shape
    rows = cosine.shape[0]
    half = wq.shape[0]
    heads = QUERY_HEADS * own_rows // rows
    qcols = heads * HEAD
    ffe = wout.shape[1]
    vm = pl.BlockSpec(memory_space=pltpu.VMEM)
    hbm = pl.BlockSpec(memory_space=pl.ANY)
    sds = jax.ShapeDtypeStruct
    return pl.pallas_call(
        front_kernel,
        out_shape=(
            sds((heads, rows, HEAD), BF16),
            sds((rows, qcols), BF16),
            sds((qcols, rows), BF16),
            sds((heads, 1, rows), F32),
            sds((rows, width), BF16),
            sds((small.shape[0], width), BF16),
            sds((width, qcols + 2 * HEAD), BF16),
            sds((blocks, 2, rows, HEAD), BF16),
            sds((width, width), BF16),
            sds((2, 2, half, width + half), BF16),
            sds((blocks, own_rows, width), BF16),
        ),
        in_specs=[vm, vm] + [hbm] * 6 + [vm] * 3,
        out_specs=[vm] * 6 + [hbm] * 5,
        scratch_shapes=[
            pltpu.VMEM((rows, width), BF16),
            pltpu.VMEM(small.shape, BF16),
            pltpu.VMEM((width, qcols + 2 * HEAD), BF16),
            pltpu.VMEM((blocks, 2, rows, HEAD), BF16),
            pltpu.VMEM((heads, 1, rows), F32),
            pltpu.VMEM((heads, 1, rows), F32),
            pltpu.VMEM((heads, HEAD, rows), F32),
            pltpu.VMEM((HEAD, rows), BF16),
            pltpu.VMEM((width, width), BF16),
            pltpu.VMEM((2, 2, half, width + half), BF16),
            pltpu.VMEM((blocks, own_rows, width), BF16),
            pltpu.SemaphoreType.DMA((16,)),
        ] + semaphores(blocks),
        compiler_params=pltpu.CompilerParams(
            vmem_limit_bytes=VMEM_BYTES, collective_id=0, has_side_effects=True),
    )(x, small, wq, wkv, wo, win, wout, cot, cosine, sine, start)


class ColumnSum:
    CHUNKS = 4

    def __init__(self, at, lanes, part, land):
        self.at, self.lanes, self.part, self.land = at, lanes, part, land
        self.rows = part.shape[1] // self.CHUNKS
        self.recv = lanes.slots((at.blocks + 1) * self.CHUNKS)
        self.sent = lanes.sends(at.blocks * self.CHUNKS)

    def copy(self, b, ch):
        at = self.at
        travel = jnp.where(b < at.z, -1, 1)
        there = at.z + travel
        slot = jnp.where((there == b) & (b > at.z), at.blocks, b)
        rows = pl.ds(ch * self.rows, self.rows)
        return remote(self.part.at[b, rows, :], self.land.at[slot, rows, :],
                      self.lanes.send.at[self.sent + b * self.CHUNKS + ch],
                      self.lanes.recv.at[self.recv + slot * self.CHUNKS + ch], blk=there)

    def landed(self, slot, ch, origin):
        rows = pl.ds(ch * self.rows, self.rows)
        place = self.land.at[slot, rows, :]
        remote(place, place, self.lanes.send.at[0], self.lanes.recv.at[self.recv + slot * self.CHUNKS + ch],
               blk=origin).wait_recv()

    def first_send(self, b):
        at = self.at

        @pl.when(((b < at.z) & (at.z == at.blocks - 1)) | ((b > at.z) & (at.z == 0)))
        def _():
            for ch in range(self.CHUNKS):
                self.copy(b, ch).start()

    def relay(self, phase, d, add):
        at = self.at
        s = jnp.where(at.z * 2 >= at.blocks, -1, 1) * (1 - 2 * phase)
        b, origin = at.z + s * d, at.z - s
        safe = jnp.clip(b, 0, at.blocks - 1)

        @pl.when((b >= 0) & (b < at.blocks) & (origin >= 0) & (origin < at.blocks))
        def _():
            for ch in range(self.CHUNKS):
                self.landed(safe, ch, origin)
                add(safe, pl.ds(ch * self.rows, self.rows))
                self.copy(safe, ch).start()

    def arrive(self, side, use):
        at = self.at
        slot, origin = (at.z, at.z + 1) if side == 0 else (at.blocks, at.z - 1)

        @pl.when((origin >= 0) & (origin < at.blocks))
        def _():
            for ch in range(self.CHUNKS):
                self.landed(slot, ch, origin)
            use(slot)

    def finish(self):
        at = self.at
        for b in range(at.blocks):
            @pl.when(b != at.z)
            def _(b=b):
                for ch in range(self.CHUNKS):
                    self.copy(b, ch).wait_send()


LANES = 128
HALF_LANES = LANES // 2


def split_lanes(value):
    high = value.astype(BF16).astype(F32)
    return (high + pltpu.roll(value - high, HALF_LANES, 1)).astype(BF16)


def expert_kernel(o_ref, x_ref, small_ref, chosen_ref, wo_hbm, w_hbm, cot_hbm,
                  res_out, grad_out, attn_out, small_out, sums_out, y_out, core_land, *rest):
    big = cot_hbm.shape[0] > 4
    if big:
        xb_ref, dx_ref, land_ref, *rest = rest
        (xb_stage, dx_stage, land_stage, g_ref, *rest) = rest
    else:
        xb_ref, dx_ref, land_ref, *rest = rest
    (mix_ref, w_ref, cot_ref, acc_ref, gate_ref, dgu_ref, ga_ref, xt_ref, gat_ref, gg_ref, y_ref, stage_ref,
     gates_ref, router_ref, load_sem, y_sem, send_sem, recv_sem) = rest
    own_rows, width = x_ref.shape
    blocks = cot_hbm.shape[0]
    qcols = o_ref.shape[1]
    half = width // 2
    experts, _, ffe, _ = w_ref.shape
    at = Place(blocks)
    me = at.z
    lanes = Lanes(send_sem, recv_sem)
    at.enter()
    every = blocks * own_rows
    if big:
        wo_rows = [(slice(y * half, (y + 1) * half), g_ref.at[0, y, :, :width]) for y in range(2)]
    else:
        wo_rows = [(slice(0, every), dgu_ref.at[0]), (slice(every, width), dgu_ref.at[1, :width - every])]
    wo_load = [pltpu.make_async_copy(wo_hbm.at[rows, :], place, load_sem.at[y])
               for y, (rows, place) in enumerate(wo_rows)]
    for load in wo_load:
        load.start()
    quarter = half // 4
    here = aligned(at.h * quarter, quarter)
    w_loads = [pltpu.make_async_copy(w_hbm.at[place], w_ref.at[place], load_sem.at[4 + i])
               for i, place in enumerate(((0,), (1, at.y), (1, at.oy, here)))]
    for load in w_loads:
        load.start()
    late = Shared(at, lanes, 4, None, functools.partial(weight_chunk, w_ref))
    if not big:
        cot_loads = [pltpu.make_async_copy(cot_hbm.at[b], cot_ref.at[b * own_rows:(b + 1) * own_rows, :],
                                           load_sem.at[7 + b]) for b in range(blocks)]
        for load in cot_loads:
            load.start()

    total_experts = experts * blocks
    srows = small_ref.shape[0]
    is_router = lax.broadcasted_iota(jnp.int32, (srows, width), 0) < total_experts
    router_ref[...] = jnp.zeros_like(router_ref)
    router_ref[:srows, :] = jnp.where(is_router, small_ref[...].astype(F32), 0.0).astype(BF16)
    gain_two = small_ref[total_experts + 1:total_experts + 2, :].astype(F32)

    mixes = lanes.slots(4)

    def mix_cols(head):
        return mix_ref.at[:, pl.ds(pl.multiple_of(head * qcols, HEAD), qcols)]

    for head in (at.xn, at.xs, at.sib):
        lanes.put(mixes + at.h, o_ref.at[aligned(head * own_rows, own_rows), :], mix_cols(at.h), head=head)
    mix_ref[:, pl.ds(pl.multiple_of(at.h * qcols, HEAD), qcols)] = o_ref[aligned(at.h * own_rows, own_rows), :]
    for head in (at.sib, at.xn, at.xs):
        lanes.arrived(mixes + head, mix_cols(head), head=head)
    for load in w_loads:
        load.wait()
    for k in (2, 3):
        late.scatter(k)
    for load in wo_load:
        load.wait()
    step = 512
    for i in range(width // step):
        cols = slice(i * step, (i + 1) * step)
        res_out[:, cols] = x_ref[:, cols].astype(F32) + sum(
            mm(mix_ref[:, rows], place[:, cols]) for rows, place in wo_rows)

    def inverse_two():
        res = res_out[...]
        return lax.rsqrt(jnp.mean(res * res, axis=-1, keepdims=True) + NORM_EPSILON)

    n2 = (res_out[...] * inverse_two() * gain_two).astype(BF16)
    chosen = chosen_ref[...] > 0.0
    logits = jnp.where(chosen, mm(n2, router_ref[...], NT), MASKED)
    e_top = jnp.where(chosen, jnp.exp(logits - jnp.max(logits, axis=-1, keepdims=True)), 0.0)
    gates = e_top / jnp.sum(e_top, axis=-1, keepdims=True)
    gates_ref[...] = gates
    own_x = xb_stage if big else xb_ref.at[me]
    own_x[:, :width] = n2
    own_x[:, width:] = split_lanes(gates)

    def move(src, dst):
        copy = pltpu.make_async_copy(src, dst, load_sem.at[3])
        copy.start()
        copy.wait()

    if big:
        move(xb_stage, xb_ref.at[me])
    xs_slot, xs_sent = lanes.slots(blocks), lanes.sends(blocks + 2)

    def xs_copy(b, to, send):
        return remote(xb_ref.at[b], xb_ref.at[b], send_sem.at[xs_sent + send], recv_sem.at[xs_slot + b], blk=to)

    pl.when(me > 0)(lambda: xs_copy(me, me - 1, blocks).start())
    pl.when(me < blocks - 1)(lambda: xs_copy(me, me + 1, blocks + 1).start())

    if big:
        def clear(i, _):
            for e in range(experts):
                for y in range(2):
                    g_ref[e, y, aligned(i * 64, 64), :] = jnp.zeros((64, g_ref.shape[3]), BF16)
            return 0

        lax.fori_loop(0, half // 64, clear, 0)
    else:
        for load in cot_loads:
            load.wait()
    for k in (2, 3):
        late.forward(k)
    for k in (2, 3):
        late.finish(k)
    back = ColumnSum(at, lanes, dx_ref, land_ref)
    lane = lax.broadcasted_iota(jnp.int32, (own_rows, LANES), 1)
    tile = 256

    def y_copy(b):
        return pltpu.make_async_copy(y_ref, y_out.at[b], y_sem)

    def block(b, first):
        if big:
            move(xb_ref.at[b], xb_stage)
            move(cot_hbm.at[b], cot_ref)
        x_in = xb_stage if big else xb_ref.at[b]
        band_all = slice(None) if big else aligned(b * own_rows, own_rows)
        lanes_all = pl.ds(pl.multiple_of(b * own_rows, own_rows), own_rows)
        acc_ref[...] = jnp.zeros_like(acc_ref)
        gg_ref[...] = jnp.zeros_like(gg_ref)

        def hidden(e, _):
            index = me * experts + e
            pack = x_in[:, width:].astype(F32)
            mine = (lane == index) | (lane == index + HALF_LANES)
            gate_ref[...] = jnp.sum(jnp.where(mine, pack, 0.0), axis=1, keepdims=True)

            def inner(t, total):
                low = pl.ds(pl.multiple_of(t * tile, tile), tile)
                high = pl.ds(pl.multiple_of(ffe + t * tile, tile), tile)
                out_cols = slice(width, width + half)
                gate_pre = mm(x_in[:, :half], w_ref[e, 0, :, low]) + mm(x_in[:, half:width], w_ref[e, 1, :, low])
                up = mm(x_in[:, :half], w_ref[e, 0, :, high]) + mm(x_in[:, half:width], w_ref[e, 1, :, high])
                back_h = (mm(cot_ref[band_all, :half], w_ref[e, 0, low, out_cols], NT)
                          + mm(cot_ref[band_all, half:], w_ref[e, 1, low, out_cols], NT))
                value, slope = gelu_parts(gate_pre)
                act = (value * up).astype(BF16).astype(F32)
                gate = gate_ref[...]
                ga_ref[e, :, low] = (gate * act).astype(BF16)
                if not big:
                    gat_ref[e, low, lanes_all] = (gate * act).T.astype(BF16)
                d_act = gate * back_h
                dgu_ref[e, band_all, low] = (d_act * up * slope).astype(BF16)
                dgu_ref[e, band_all, high] = (d_act * value).astype(BF16)
                return total + jnp.sum(act * back_h, axis=1, keepdims=True)

            total = lax.fori_loop(0, ffe // tile, inner, jnp.zeros((own_rows, 1), F32))
            gg_ref[...] += jnp.where(lane == index, total, 0.0)
            for y in range(2):
                acc_ref[:, y * half:(y + 1) * half] += mm(dgu_ref[e, band_all, :], w_ref[e, y, :, :width], NT)
            return 0

        lax.fori_loop(0, experts, hidden, 0)
        part = dx_stage if big else dx_ref.at[b]
        part[:, :width] = acc_ref[...].astype(BF16)
        part[:, width:] = split_lanes(gg_ref[...])
        if big:
            move(dx_stage, dx_ref.at[b])
        back.first_send(b)

        if big:
            xt_ref[...] = x_in[:, :width].astype(F32).T.astype(BF16)

            def weights(e, _):
                gat_ref[0] = ga_ref[e].astype(F32).T.astype(BF16)

                def rows(i, _):
                    band = aligned(i * tile, tile)
                    for y in range(2):
                        x_cols = xt_ref[aligned(y * half + i * tile, tile), :]
                        for n in range(width // step):
                            cols = slice(n * step, (n + 1) * step)
                            total = g_ref[e, y, band, cols].astype(F32) + mm(x_cols, dgu_ref[e, :, cols])
                            g_ref[e, y, band, cols] = total.astype(BF16)
                        out_cols = slice(width, width + half)
                        total = (g_ref[e, y, band, out_cols].astype(F32)
                                 + mm(gat_ref[0, band, :], cot_ref[:, y * half:(y + 1) * half]))
                        g_ref[e, y, band, out_cols] = total.astype(BF16)
                    return 0

                return lax.fori_loop(0, half // tile, rows, 0)

            lax.fori_loop(0, experts, weights, 0)
        else:
            xt_ref[:, lanes_all] = x_in[:, :width].astype(F32).T.astype(BF16)

        pl.when(jnp.logical_not(first))(lambda: y_copy(b).wait())
        for y in range(2):
            total = mm(ga_ref[0], w_ref[0, y, :, width:])
            for e in range(1, experts):
                total = total + mm(ga_ref[e], w_ref[e, y, :, width:])
            y_ref[:, y * half:(y + 1) * half] = total.astype(BF16)
        y_copy(b).start()

    def distance(d, _):
        for b, origin, to in ((me - d, me - 1, me + 1), (me + d, me + 1, me - 1)):
            @pl.when((d > 0) & (b >= 0) & (b < blocks))
            def _(b=b, origin=origin, to=to):
                xs_copy(b, origin, 0).wait_recv()
                pl.when((to >= 0) & (to < blocks))(lambda: xs_copy(b, to, b).start())

        def side(s, _):
            b = jnp.where(s == 0, me - d, me + d)

            @pl.when((b >= 0) & (b < blocks) & ((d > 0) | (s == 0)))
            def _():
                block(jnp.clip(b, 0, blocks - 1), d == 0)

            return 0

        return lax.fori_loop(0, 2, side, 0)

    lax.fori_loop(0, blocks, distance, 0)
    y_copy(me).wait()

    def add(b, rows):
        if big:
            move(dx_ref.at[b, rows, :], dx_stage.at[rows, :])
            move(land_ref.at[b, rows, :], land_stage.at[rows, :])
            dx_stage[rows, :] = (dx_stage[rows, :].astype(F32) + land_stage[rows, :].astype(F32)).astype(BF16)
            move(dx_stage.at[rows, :], dx_ref.at[b, rows, :])
        else:
            dx_ref[b, rows, :] = (dx_ref[b, rows, :].astype(F32) + land_ref[b, rows, :].astype(F32)).astype(BF16)

    late.settle()
    total_ref = g_ref if big else w_ref

    def weights_of(e):
        def rows(i, _):
            cols = pl.ds(pl.multiple_of(i * tile, tile), tile)
            for y in range(2):
                total = mm(xt_ref[y * half:(y + 1) * half, :], dgu_ref[e, :, cols])
                total_ref[e, y, :, cols] = total.astype(BF16)
            return 0

        def outs(i, _):
            for y in range(2):
                cols = pl.ds(pl.multiple_of(y * half + i * tile, tile), tile)
                place = pl.ds(pl.multiple_of(width + i * tile, tile), tile)
                total_ref[e, y, :, place] = mm(gat_ref[e], cot_ref[:, cols]).astype(BF16)
            return 0

        lax.fori_loop(0, 2 * ffe // tile, rows, 0)
        lax.fori_loop(0, half // tile, outs, 0)

    chunks = 4
    piece = half // chunks
    cores = lanes.slots(chunks)
    back.relay(0, 1, add)
    if not big:
        weights_of(1 - at.c)
    for k in range(chunks):
        band = pl.ds(k * piece, piece)
        lanes.put(cores + k, total_ref.at[1 - at.c, :, band, :], core_land.at[:, band, :], head=at.sib)

    def core_sum(k):
        band = pl.ds(k * piece, piece)
        lanes.arrived(cores + k, core_land.at[:, band, :], head=at.sib)
        move(core_land.at[:, band, :], stage_ref)
        for y in range(2):
            total = total_ref[at.c, y, band, :].astype(F32) + stage_ref[y].astype(F32)
            total_ref[at.c, y, band, :] = total.astype(BF16)

    for d in range(2, blocks):
        back.relay(0, d, add)
    if not big:
        weights_of(at.c)
    for d in range(1, blocks):
        back.relay(1, d, add)
    for k in range(chunks):
        core_sum(k)
    keep = pltpu.make_async_copy(total_ref.at[at.c], sums_out, load_sem.at[0])
    keep.start()

    if big:
        move(dx_ref.at[me], dx_stage)
    own_part = dx_stage if big else dx_ref.at[me]
    acc_ref[...] = own_part[:, :width].astype(F32)
    gg_ref[...] = own_part[:, width:].astype(F32)

    def take(slot):
        if big:
            move(land_ref.at[slot], land_stage)
        came = land_stage if big else land_ref.at[slot]
        acc_ref[...] += came[:, :width].astype(F32)
        gg_ref[...] += came[:, width:].astype(F32)

    for side in range(2):
        back.arrive(side, take)
    both = gg_ref[...]
    gate_grads = jnp.where(lane < HALF_LANES, both + pltpu.roll(both, HALF_LANES, 1), 0.0)
    gates = gates_ref[...]
    d_logits = (gates * (gate_grads - jnp.sum(gates * gate_grads, axis=-1, keepdims=True))).astype(BF16)
    inv = inverse_two()
    hat = res_out[...] * inv
    n2 = (hat * gain_two).astype(BF16)
    small_out[...] = mm(d_logits.astype(F32).T.astype(BF16), n2)[:small_out.shape[0], :]
    d_n2 = acc_ref[...] + mm(d_logits, router_ref[...])
    small_out[total_experts + 1:total_experts + 2, :] = jnp.sum(d_n2 * hat, axis=0, keepdims=True)
    pulled = d_n2 * gain_two
    if big:
        move(cot_hbm.at[me], cot_ref)
    own_cot = cot_ref[...] if big else cot_ref[aligned(me * own_rows, own_rows), :]
    grad = own_cot.astype(F32) + inv * (pulled - hat * jnp.mean(pulled * hat, axis=-1, keepdims=True))
    grad_out[...] = grad
    attn_out[...] = grad.astype(BF16)
    keep.wait()
    for b in range(blocks):
        up, down = (b < me) & (me < blocks - 1), (b > me) & (me > 0)
        pl.when(up)(lambda b=b: xs_copy(b, me + 1, b).wait_send())
        pl.when(down)(lambda b=b: xs_copy(b, me - 1, b).wait_send())
    pl.when(me > 0)(lambda: xs_copy(me, me - 1, blocks).wait_send())
    pl.when(me < blocks - 1)(lambda: xs_copy(me, me + 1, blocks + 1).wait_send())
    back.finish()
    lanes.drain()


def expert_layer(o, x, small, chosen, wo, w, cot):
    own_rows, width = x.shape
    blocks = cot.shape[0]
    experts, _, half, wide = w.shape
    ffe = half
    pack = width + LANES
    big = blocks > 4
    kept = own_rows if big else blocks * own_rows
    vm = pl.BlockSpec(memory_space=pltpu.VMEM)
    hbm = pl.BlockSpec(memory_space=pl.ANY)
    sds = jax.ShapeDtypeStruct
    column = [((blocks, own_rows, pack), BF16), ((blocks, own_rows, pack), BF16), ((blocks + 1, own_rows, pack), BF16)]
    if big:
        extra_out, extra_spec = tuple(sds(*c) for c in column), [hbm] * 3
        extra_scratch = [pltpu.VMEM((own_rows, pack), BF16)] * 3 + [pltpu.VMEM(w.shape, BF16)]
    else:
        extra_out, extra_spec = (), []
        extra_scratch = [pltpu.VMEM(*c) for c in column]
    outs = pl.pallas_call(
        expert_kernel,
        out_shape=(
            sds((own_rows, width), F32),
            sds((own_rows, width), F32),
            sds((own_rows, width), BF16),
            sds((-(-(experts * blocks + 2) // 8) * 8, width), F32),
            sds((2, half, wide), BF16),
            sds((blocks, own_rows, width), BF16),
            sds((2, half, wide), BF16),
        ) + extra_out,
        in_specs=[vm] * 4 + [hbm] * 3,
        out_specs=[vm] * 4 + [hbm] * 3 + extra_spec,
        scratch_shapes=extra_scratch + [
            pltpu.VMEM((own_rows, width), BF16),
            pltpu.VMEM(w.shape, BF16),
            pltpu.VMEM((kept, width), BF16),
            pltpu.VMEM((own_rows, width), F32),
            pltpu.VMEM((own_rows, 1), F32),
            pltpu.VMEM((experts, kept, 2 * ffe), BF16),
            pltpu.VMEM((experts, own_rows, ffe), BF16),
            pltpu.VMEM((width, kept), BF16),
            pltpu.VMEM((experts, ffe, kept), BF16),
            pltpu.VMEM((own_rows, LANES), F32),
            pltpu.VMEM((own_rows, width), BF16),
            pltpu.VMEM((2, half // 4, wide), BF16),
            pltpu.VMEM((own_rows, LANES), F32),
            pltpu.VMEM((LANES, width), BF16),
            pltpu.SemaphoreType.DMA((7 + blocks,)),
            pltpu.SemaphoreType.DMA,
        ] + semaphores(blocks),
        compiler_params=pltpu.CompilerParams(
            vmem_limit_bytes=VMEM_BYTES, collective_id=1, has_side_effects=True),
    )(o, x, small, chosen, wo, w, cot)
    return outs[:6]


class ExpertSums:
    CHUNKS = 8

    def __init__(self, at, lanes, grads, own, land_y, land_x, out, load_sem, keep_sem):
        self.at, self.lanes = at, lanes
        self.grads, self.own, self.out = grads, own, out
        self.land_y, self.land_x = land_y, land_x
        self.load_sem, self.keep_sem = load_sem, keep_sem
        self.rows = grads.shape[1] // self.CHUNKS
        n = self.CHUNKS
        self.ys, self.xr, self.cg = [lanes.slots(n) for _ in range(3)]
        self.sent = []
        self.kept = []

    def chunk(self, k):
        return pl.ds(k * self.rows, self.rows)

    def load(self):
        self.loads = [pltpu.make_async_copy(self.grads.at[y], self.own.at[y], self.load_sem.at[i])
                      for i, y in enumerate((self.at.oy, self.at.y))]
        for copy in self.loads:
            copy.start()

    def to_y(self):
        self.loads[0].wait()
        for k in range(self.CHUNKS):
            rows = self.chunk(k)
            self.sent.append(self.lanes.put(
                self.ys + k, self.own.at[self.at.oy, rows, :], self.land_y.at[rows, :], fsdp=self.at.oy))

    def y_sent(self):
        for copy in self.sent:
            self.lanes.settle(copy)

    def to_x(self, k):
        at, rows = self.at, self.chunk(k)
        if k == 0:
            self.loads[1].wait()
        self.lanes.arrived(self.ys + k, self.land_y.at[rows, :], fsdp=at.oy)
        total = self.own[at.y, rows, :].astype(F32) + self.land_y[rows, :].astype(F32)
        self.own[at.y, rows, :] = total.astype(BF16)
        self.lanes.put(self.xr + k, self.own.at[at.y, rows, :], self.land_x.at[rows, :], head=at.xn)

    def share(self, k):
        at, rows = self.at, self.chunk(k)
        self.lanes.arrived(self.xr + k, self.land_x.at[rows, :], head=at.xn)
        total = self.own[at.y, rows, :].astype(F32) + self.land_x[rows, :].astype(F32)
        self.land_x[rows, :] = total.astype(BF16)
        done, place = self.land_x.at[rows, :], self.out.at[at.c, rows, :]
        self.lanes.put(self.cg + k, done, place, head=at.sib)
        keep = pltpu.make_async_copy(done, place, self.keep_sem.at[k])
        keep.start()
        self.kept.append(keep)

    def finish(self):
        at = self.at
        for k in range(self.CHUNKS):
            self.lanes.arrived(self.cg + k, self.out.at[1 - at.c, self.chunk(k), :], head=at.sib)
            self.kept[k].wait()


class OutputSums:
    PARTS = 4

    def __init__(self, at, lanes, grad, land_y, land_z, out):
        self.at, self.lanes, self.grad = at, lanes, grad
        self.land_y, self.land_z, self.out = land_y, land_z, out
        self.rows = grad.shape[0] // self.PARTS
        self.ys = lanes.slots()
        self.zr, self.zg = lanes.slots(at.blocks), lanes.slots(self.PARTS)
        self.xg, self.cg = lanes.slots(self.PARTS), lanes.slots(self.PARTS)
        self.owner, self.giver = at.y == at.x, at.y != at.x
        self.summer = at.z < self.PARTS
        self.part = at.z % self.PARTS
        self.mine = aligned(self.part * self.rows, self.rows)

    def to_z(self):
        at = self.at
        for p in range(self.PARTS):
            self.lanes.put(self.zr + at.z, self.grad.at[pl.ds(p * self.rows, self.rows), :], self.land_z.at[at.z],
                           when=at.z != p, blk=p)

    def to_y(self, fetch):
        at = self.at
        for z in at.others():
            self.lanes.arrived(self.zr + z, self.land_z.at[z], when=self.summer, blk=z)

        @pl.when(self.summer)
        def _():
            total = self.grad[self.mine, :].astype(F32)
            for z in at.others():
                total = total + fetch(self.land_z.at[z])[...].astype(F32)
            self.grad[self.mine, :] = total.astype(BF16)

        self.lanes.put(self.ys, self.grad.at[self.mine, :], self.land_y, when=self.summer & self.giver, fsdp=at.oy)

    def place(self, core, p):
        return self.out.at[aligned(core * self.PARTS * self.rows + p * self.rows, self.rows), :]

    def share(self):
        at, p = self.at, self.part
        ready = self.summer & self.owner
        self.lanes.arrived(self.ys, self.land_y, when=ready, fsdp=at.oy)
        at_rows = aligned(at.c * self.PARTS * self.rows + p * self.rows, self.rows)

        @pl.when(ready)
        def _():
            total = self.grad[self.mine, :].astype(F32) + self.land_y[...].astype(F32)
            self.out[at_rows, :] = total.astype(BF16)

        place = self.place(at.c, p)
        for z in at.others():
            self.lanes.put(self.zg + p, place, place, when=ready, blk=z)
        self.lanes.put(self.xg + p, place, place, when=ready, head=at.xn)
        self.lanes.put(self.cg + p, place, place, when=ready, head=at.sib)

    def pass_on(self):
        at = self.at
        for p in range(self.PARTS):
            place = self.place(at.c, p)
            later = self.owner & (at.z != p)
            self.lanes.arrived(self.zg + p, place, when=later, blk=p)
            self.lanes.put(self.xg + p, place, place, when=later, head=at.xn)
            self.lanes.put(self.cg + p, place, place, when=later, head=at.sib)

    def take_over(self):
        at = self.at
        for p in range(self.PARTS):
            place = self.place(at.c, p)
            self.lanes.arrived(self.xg + p, place, when=self.giver, head=at.xn)
            self.lanes.put(self.cg + p, place, place, when=self.giver, head=at.sib)

    def finish(self):
        at = self.at
        for p in range(self.PARTS):
            self.lanes.arrived(self.cg + p, self.place(1 - at.c, p), head=at.sib)


def back_kernel(attn_ref, q_ref, ot_ref, start_ref, lse_ref, x_ref, cos_ref, sin_ref, gain_ref, small_ref,
                kv_in, wo_hbm, grads_hbm, y_in, res_hbm, res_grad_hbm, n1_hbm, w_hbm,
                block_out, tokens_out, small_out, kv_out, experts_out, output_out, query_out, y_land, *rest):
    blocks = kv_in.shape[0]
    big = blocks > 4
    dkv_stage = dwo_stage = None
    if big:
        yp_ref, dkv_land, dkv_sib, dwo_z, kv_ref, dkv_stage, dwo_stage, y_stage, kv_stage, *rest = rest
    else:
        yp_ref, dkv_land, dkv_sib, dwo_z, kv_ref, *rest = rest
    (dq_ref, dk_ref, dv_ref, kt_ref, delta_ref, do_ref, ag_ref, wo_ref, dwo_ref, dwo_y, dwo_land,
     own_ref, ey_ref, ex_ref, acc_ref, y_other, w_ref, dpre_ref, dn_sib, dn_x, dw_ref, dw_y, dw_z,
     sm_ref, sm_a, sm_b, sm_y, sm_z, land_ref, dkv_ref, n1t_ref, load_sem, keep_sem, send_sem, recv_sem) = rest
    heads, rows, _ = q_ref.shape
    own_rows, width = attn_ref.shape
    half = width // 2
    qcols = heads * HEAD
    gain_row = 2 * blocks
    at = Place(blocks)
    me = at.z
    lanes = Lanes(send_sem, recv_sem)
    at.enter()
    experts = ExpertSums(at, lanes, grads_hbm, own_ref, ey_ref, ex_ref, experts_out, load_sem, keep_sem)
    output = OutputSums(at, lanes, dwo_ref, dwo_y, dwo_z, dwo_land)
    sums = ColumnSum(at, lanes, yp_ref, y_land)
    experts.load()
    forward, near, far, _ = gather_heads(at, lanes, attn_ref, ag_ref)

    def load(src, dst, sem):
        copy = pltpu.make_async_copy(src, dst, load_sem.at[sem])
        copy.start()
        return copy

    def move(src, dst):
        load(src, dst, 5).wait()

    wo_load = load(wo_hbm.at[aligned(at.h * qcols, qcols), :], wo_ref, 2)
    y_load = load(y_in, yp_ref, 3)
    if not big:
        kv_load = load(kv_in, kv_ref, 4)
    experts.to_y()
    y_load.wait()
    for b in range(blocks):
        sums.first_send(b)

    def add(b, band):
        move(y_land.at[b, band, :], y_other.at[band, :])
        if big:
            move(yp_ref.at[b, band, :], y_stage.at[band, :])
            y_stage[band, :] = (y_stage[band, :].astype(F32) + y_other[band, :].astype(F32)).astype(BF16)
            move(y_stage.at[band, :], yp_ref.at[b, band, :])
        else:
            yp_ref[b, band, :] = (yp_ref[b, band, :].astype(F32) + y_other[band, :].astype(F32)).astype(BF16)

    def fetch(stage):
        def get(ref):
            if big:
                move(ref, stage)
                return stage
            return ref
        return get

    wo_load.wait()

    def mix_back(head):
        band = aligned(head * own_rows, own_rows)
        grad = mm(ag_ref[band, :], wo_ref[...], NT).astype(BF16)
        for hh in range(heads):
            do_ref[hh, band, :] = grad[:, hh * HEAD:(hh + 1) * HEAD]

    def turn(i):
        band = slice(i * own_rows, (i + 1) * own_rows)
        move(n1_hbm.at[band, :], y_other)
        n1t_ref[:, band] = y_other[...].astype(F32).T.astype(BF16)

    ag_ref[aligned(at.h * own_rows, own_rows), :] = attn_ref[...]
    mix_back(at.h)
    turn(0)
    near()
    mix_back(at.sib)
    for i in range(1, rows // own_rows):
        turn(i)
    experts.to_x(0)
    forward()
    mix_back(at.xn)
    far()
    mix_back(at.xs)
    step = 512

    def weight_back(i, _):
        cols = pl.ds(pl.multiple_of(i * step, step), step)
        dwo_ref[:, cols] = mm(ot_ref[...], ag_ref[:, cols]).astype(BF16)
        return 0

    lax.fori_loop(0, width // step, weight_back, 0)
    output.to_z()
    kv_from = pl.ds(pl.multiple_of(qcols + at.c * HEAD, HEAD), HEAD)
    w_loads = [load(w_hbm.at[:, :qcols], w_ref.at[:, :qcols], 2), load(w_hbm.at[:, kv_from], w_ref.at[:, qcols:], 3)]
    dq_ref[...] = jnp.zeros_like(dq_ref)
    for hh in range(heads):
        prod = do_ref[hh].astype(F32).T * ot_ref[hh * HEAD:(hh + 1) * HEAD, :].astype(F32)
        delta_ref[hh] = jnp.sum(prod, axis=0, keepdims=True)
    if not big:
        kv_load.wait()

    experts.to_x(1)
    beside = [[(experts.to_x, 2), (experts.share, 0)],
              [(experts.to_x, 3), (experts.share, 1)],
              [(experts.to_x, 4), (experts.share, 2)]]

    def advance():
        for f, k in (beside.pop(0) if beside else ()):
            f(k)

    def opening(b):
        if big:
            move(kv_in.at[b], kv_stage)
        kv = kv_stage if big else kv_ref.at[b]
        kt_ref[...] = kv[0].astype(F32).T.astype(BF16)
        dk_ref[...] = jnp.zeros_like(dk_ref)
        dv_ref[...] = jnp.zeros_like(dv_ref)
        return kv

    def closing(b, kv):
        kv[0] = (dk_ref[...] * SCORE_SCALE).astype(BF16)
        kv[1] = dv_ref[...].astype(BF16)
        if big:
            move(kv_stage, kv_ref.at[b])

    def block(b):
        kv = opening(b)

        def tile(t, _):
            hh, i = t // (rows // TILE), t % (rows // TILE)
            cols = pl.ds(pl.multiple_of(i * TILE, TILE), TILE)
            unattend_tile(hh, cols, kv[0], kv[1], kt_ref[...], q_ref, do_ref,
                          start_ref, lse_ref, delta_ref, dq_ref, dk_ref, dv_ref, b * rows, None)
            return 0

        lax.fori_loop(0, heads * (rows // TILE), tile, 0)
        closing(b, kv)

    pair, column = lanes.slots(blocks), lanes.slots(blocks)

    def to_sibling(b, when):
        lanes.put(pair + b, kv_ref.at[b, 1 - at.c], dkv_sib.at[b], when=when, head=at.sib)

    def to_column(b):
        lanes.arrived(pair + b, dkv_sib.at[b], when=b < me, head=at.sib)

        @pl.when(b < me)
        def _():
            came = fetch(dkv_stage)(dkv_sib.at[b])
            if big:
                move(kv_ref.at[b, at.c], kv_stage.at[at.c])
            kv = kv_stage if big else kv_ref.at[b]
            kv[at.c] = (kv[at.c].astype(F32) + came[...].astype(F32)).astype(BF16)
            if big:
                move(kv_stage.at[at.c], kv_ref.at[b, at.c])

        lanes.put(column + me, kv_ref.at[b, at.c], dkv_land.at[me], when=b < me, blk=b)

    for b in range(blocks - 1):
        pl.when(b < me)(functools.partial(block, b))
        to_sibling(b, b < me)
        sums.relay(0, b + 1, add)
        advance()
        if b > 0:
            to_column(b - 1)
    while beside:
        advance()
    to_column(blocks - 2)

    kv_own = opening(me)
    for i in range(rows // TILE):
        n = (i + 1) * TILE

        def diagonal(hh, _, i=i, n=n):
            unattend_tile(hh, slice(i * TILE, n), kv_own[0, :n, :], kv_own[1, :n, :], kt_ref[:, :n], q_ref, do_ref,
                          start_ref, lse_ref, delta_ref, dq_ref, dk_ref, dv_ref,
                          me * rows, me * rows + i * TILE)
            return 0

        lax.fori_loop(0, heads, diagonal, 0)
    closing(me, kv_own)
    to_sibling(me, None)
    experts.to_x(5)
    for d in range(1, blocks):
        sums.relay(1, d, add)

    def unrotate(u):
        return u * cos_ref[...] - pltpu.roll(u, HEAD // 2, 1) * sin_ref[...]

    for hh in range(heads):
        dpre_ref[:, hh * HEAD:(hh + 1) * HEAD] = unrotate((dq_ref[hh] * SCORE_SCALE).T).astype(BF16)
    for w_load in w_loads:
        w_load.wait()
    parts = 4
    part = half // parts
    band_rows = 256
    query_cols, keyval_cols = slice(0, qcols), slice(qcols, qcols + HEAD)

    def weight_half(y, cols_out):
        def body(i, _):
            band = aligned(y * half + i * band_rows, band_rows)
            dw_ref[band, cols_out] = mm(n1t_ref[band, :], dpre_ref[:, cols_out]).astype(BF16)
            return 0

        lax.fori_loop(0, half // band_rows, body, 0)

    def weight_part(y, p):
        return aligned(y * half + p * part, part)

    ys = (lanes.slots(parts), lanes.slots(parts))

    def weight_to_y(i, cols_out):
        weight_half(at.oy, cols_out)
        for p in range(parts):
            lanes.put(ys[i] + p, dw_ref.at[weight_part(at.oy, p), cols_out],
                      dw_y.at[pl.ds(p * part, part), cols_out], fsdp=at.oy)

    weight_to_y(0, query_cols)
    experts.to_x(6)

    @pl.when(at.c == 0)
    def _():
        dkv_ref[...] = dk_ref[...] * SCORE_SCALE

    @pl.when(at.c == 1)
    def _():
        dkv_ref[...] = dv_ref[...]

    lanes.arrived(pair + me, dkv_sib.at[me], head=at.sib)
    dkv_ref[...] += fetch(dkv_stage)(dkv_sib.at[me])[...].astype(F32)
    for z in range(1, blocks):
        @pl.when(me < z)
        def _(z=z):
            lanes.arrived(column + z, dkv_land.at[z], blk=z)
            dkv_ref[...] += fetch(dkv_stage)(dkv_land.at[z])[...].astype(F32)

    dpre_ref[:, qcols:] = jnp.where(at.c == 0, unrotate(dkv_ref[...]), dkv_ref[...]).astype(BF16)
    weight_to_y(1, keyval_cols)

    def input_part(head):
        return mm(dpre_ref[aligned(head * own_rows, own_rows), :], w_ref[...], NT)

    experts.y_sent()

    def dn_ref(i):
        return own_ref.at[at.oy, i * own_rows:(i + 1) * own_rows, :width]

    relay, direct, across = lanes.slots(), lanes.slots(), lanes.slots()
    dn_ref(0)[...] = input_part(at.xs).astype(BF16)
    lanes.put(relay, dn_ref(0), dn_sib.at[0], head=at.sib)
    dn_ref(2)[...] = input_part(at.sib).astype(BF16)
    lanes.put(direct, dn_ref(2), dn_sib.at[1], head=at.sib)
    lanes.arrived(relay, dn_sib.at[0], head=at.sib)
    dn_ref(1)[...] = (input_part(at.xn) + dn_sib[0].astype(F32)).astype(BF16)
    lanes.put(across, dn_ref(1), dn_x, head=at.xn)
    experts.to_x(7)
    experts.share(3)
    experts.share(4)
    weight_half(at.y, slice(None))
    output.to_y(fetch(dwo_stage))

    zr = lanes.slots(blocks)
    for p in range(parts):
        rows_p = weight_part(at.y, p)
        for i, cols_out in enumerate((query_cols, keyval_cols)):
            lanes.arrived(ys[i] + p, dw_y.at[pl.ds(p * part, part), cols_out], fsdp=at.oy)
        total = dw_ref[rows_p, :].astype(F32) + dw_y[pl.ds(p * part, part), :].astype(F32)
        dw_ref[rows_p, :] = total.astype(BF16)
        lanes.put(zr + at.z, dw_ref.at[rows_p, :], dw_z.at[at.z], when=at.z != p, blk=p)
    experts.share(5)
    output.share()

    move(res_hbm, acc_ref)
    if big:
        move(yp_ref.at[me], y_stage)
    acc_ref[...] += (y_stage if big else yp_ref.at[me])[...].astype(F32)

    def take(slot):
        move(y_land.at[slot], y_other)
        acc_ref[...] += y_other[...].astype(F32)

    for side in range(2):
        sums.arrive(side, take)
    block_out[...] = acc_ref[...].astype(BF16)

    res_load = load(res_grad_hbm, acc_ref, 5)
    own = input_part(at.h)
    lanes.arrived(direct, dn_sib.at[1], head=at.sib)
    own = own + dn_sib[1].astype(F32)
    lanes.arrived(across, dn_x, head=at.xn)
    own = own + dn_x[...].astype(F32)
    x = x_ref[...].astype(F32)
    inv = lax.rsqrt(jnp.mean(x * x, axis=-1, keepdims=True) + NORM_EPSILON)
    hat = x * inv
    pulled = own * gain_ref[gain_row:gain_row + 1, :].astype(F32)
    slope = inv * (pulled - hat * jnp.mean(pulled * hat, axis=-1, keepdims=True))
    res_load.wait()
    tokens_out[...] = (acc_ref[...] + slope).astype(BF16)
    sm_ref[...] = small_ref[...]
    sm_ref[gain_row:gain_row + 1, :] = jnp.sum(own * hat, axis=0, keepdims=True)
    sa, sb, sy, sz = lanes.slots(), lanes.slots(), lanes.slots(), lanes.slots(blocks)
    lanes.put(sa, sm_ref, sm_a, head=at.sib)
    experts.share(6)

    p = at.z % parts
    summer = at.z < parts
    zg, xg, cg, cf = lanes.slots(parts), lanes.slots(parts), lanes.slots(parts), lanes.slots(parts)

    def place(head, q):
        return land_ref.at[head, pl.ds(q * part, part), :]

    for z in at.others():
        lanes.arrived(zr + z, dw_z.at[z], when=summer, blk=z)
    mine_w = weight_part(at.y, p)

    @pl.when(summer)
    def _():
        total = dw_ref[mine_w, :].astype(F32)
        for z in at.others():
            total = total + dw_z[z].astype(F32)
        dw_ref[mine_w, :] = total.astype(BF16)
        land_ref[at.h, aligned(p * part, part), :] = total.astype(BF16)

    for z in at.others():
        lanes.put(zg + p, dw_ref.at[mine_w, :], place(at.h, p), when=summer, blk=z)
    lanes.put(xg + p, dw_ref.at[mine_w, :], place(at.h, p), when=summer, head=at.xn)
    lanes.put(cg + p, dw_ref.at[mine_w, :], place(at.h, p), when=summer, head=at.sib)
    lanes.arrived(sa, sm_a, head=at.sib)
    sm_a[...] = sm_a[...] + sm_ref[...]
    lanes.put(sb, sm_a, sm_b, head=at.xn)
    output.pass_on()
    experts.share(7)

    lanes.arrived(sb, sm_b, head=at.xn)
    sm_b[...] = sm_a[...] + sm_b[...]
    mine_cols = pl.ds(pl.multiple_of(at.y * half, half), half)
    other_cols = pl.ds(pl.multiple_of(at.oy * half, half), half)
    lanes.put(sy, sm_b.at[:, other_cols], sm_y, fsdp=at.oy)
    for q in range(parts):
        later = at.z != q
        lanes.arrived(zg + q, place(at.h, q), when=later, blk=q)
        lanes.put(xg + q, place(at.h, q), place(at.h, q), when=later, head=at.xn)
        lanes.put(cg + q, place(at.h, q), place(at.h, q), when=later, head=at.sib)
    lanes.arrived(sy, sm_y, fsdp=at.oy)
    sm_z[at.z] = sm_b[:, mine_cols] + sm_y[...]
    for z in at.others():
        lanes.put(sz + at.z, sm_z.at[at.z], sm_z.at[at.z], blk=z)
    output.take_over()
    for q in range(parts):
        lanes.arrived(xg + q, place(at.xn, q), head=at.xn)
        lanes.put(cf + q, place(at.xn, q), place(at.xn, q), head=at.sib)
    for z in at.others():
        lanes.arrived(sz + z, sm_z.at[z], blk=z)
    total = sm_z[0]
    for z in range(1, blocks):
        total = total + sm_z[z]
    small_out[...] = total
    output.finish()
    keeps = [load(dwo_land, output_out, 0)]
    for q in range(parts):
        lanes.arrived(cg + q, place(at.sib, q), head=at.sib)
        lanes.arrived(cf + q, place(at.xs, q), head=at.sib)
    for head in range(4):
        keeps.append(load(land_ref.at[head, :, :qcols], query_out.at[:, head * qcols:(head + 1) * qcols], 1 + head))
        column_of = (head % 2 * KEYVALUE_HEADS + head // 2) * HEAD
        keeps.append(load(land_ref.at[head, :, qcols:], kv_out.at[:, column_of:column_of + HEAD], 6 + head))
    experts.finish()
    for keep in keeps:
        keep.wait()
    sums.finish()
    lanes.drain()


def backward(attn_grad, q, ot, start, lse, x, cosine, sine, gain, small, kv, wo, grads, y_parts, res, res_grad, n1, w):
    heads, rows, _ = q.shape
    blocks = kv.shape[0]
    own_rows, width = attn_grad.shape
    qcols = heads * HEAD
    _, half, wide = grads.shape
    cols = qcols + HEAD
    srows = small.shape[0]
    n = ExpertSums.CHUNKS
    vm = pl.BlockSpec(memory_space=pltpu.VMEM)
    hbm = pl.BlockSpec(memory_space=pl.ANY)
    part = qcols // OutputSums.PARTS
    sds = jax.ShapeDtypeStruct
    column = [((blocks, own_rows, width), BF16), ((blocks, rows, HEAD), BF16),
              ((blocks, rows, HEAD), BF16), ((blocks, part, width), BF16), (kv.shape, BF16)]
    if blocks > 4:
        extra_out, extra_spec = tuple(sds(*c) for c in column), [hbm] * 5
        extra_scratch = [pltpu.VMEM((rows, HEAD), BF16), pltpu.VMEM((part, width), BF16),
                         pltpu.VMEM((own_rows, width), BF16), pltpu.VMEM((2, rows, HEAD), BF16)]
    else:
        extra_out, extra_spec = (), []
        extra_scratch = [pltpu.VMEM(*c) for c in column]
    return pl.pallas_call(
        back_kernel,
        out_shape=(
            sds((own_rows, width), BF16),
            sds((own_rows, width), BF16),
            sds((srows, half), F32),
            sds((half, 2 * KEYVALUE_HEADS * HEAD), BF16),
            sds((2, half, wide), BF16),
            sds((2 * qcols, width), BF16),
            sds((half, rows // own_rows * qcols), BF16),
            sds((blocks + 1, own_rows, width), BF16),
        ) + extra_out,
        in_specs=[vm] * 10 + [hbm] * 8,
        out_specs=[vm] * 3 + [hbm] * 5 + extra_spec,
        scratch_shapes=extra_scratch + [
            pltpu.VMEM((heads, HEAD, rows), F32),
            pltpu.VMEM((rows, HEAD), F32),
            pltpu.VMEM((rows, HEAD), F32),
            pltpu.VMEM((HEAD, rows), BF16),
            pltpu.VMEM((heads, 1, rows), F32),
            pltpu.VMEM((heads, rows, HEAD), BF16),
            pltpu.VMEM((rows, width), BF16),
            pltpu.VMEM((qcols, width), BF16),
            pltpu.VMEM((qcols, width), BF16),
            pltpu.VMEM((part, width), BF16),
            pltpu.VMEM((2 * qcols, width), BF16),
            pltpu.VMEM((2, half, wide), BF16),
            pltpu.VMEM((half, wide), BF16),
            pltpu.VMEM((half, wide), BF16),
            pltpu.VMEM((own_rows, width), F32),
            pltpu.VMEM((own_rows, width), BF16),
            pltpu.VMEM((width, cols), BF16),
            pltpu.VMEM((rows, cols), BF16),
            pltpu.VMEM((2, own_rows, width), BF16),
            pltpu.VMEM((own_rows, width), BF16),
            pltpu.VMEM((width, cols), BF16),
            pltpu.VMEM((half, cols), BF16),
            pltpu.VMEM((blocks, half // 4, cols), BF16),
            pltpu.VMEM((srows, width), F32),
            pltpu.VMEM((srows, width), F32),
            pltpu.VMEM((srows, width), F32),
            pltpu.VMEM((srows, half), F32),
            pltpu.VMEM((blocks, srows, half), F32),
            pltpu.VMEM((rows // own_rows, half, cols), BF16),
            pltpu.VMEM((rows, HEAD), F32),
            pltpu.VMEM((width, rows), BF16),
            pltpu.SemaphoreType.DMA((10,)),
            pltpu.SemaphoreType.DMA((n,)),
        ] + semaphores(blocks),
        compiler_params=pltpu.CompilerParams(
            vmem_limit_bytes=VMEM_BYTES, collective_id=2, has_side_effects=True),
    )(attn_grad, q, ot, start, lse, x, cosine, sine, gain, small, kv, wo, grads, y_parts, res, res_grad, n1, w)[:7]


def on_device(tokens, documents, routes, cotangent, first_gain, query_weight, keyvalue_weight, output_weight,
              second_gain, router_weight, expert_in, expert_out):
    z = lax.axis_index("blk")
    blocks = lax.axis_size("blk")
    rows, width = tokens.shape[1:]
    group = lax.axis_size("head") * rows
    experts = router_weight.shape[1]
    half = query_weight.shape[0]

    small_rows = -(-(2 + experts) // 16) * 16
    small = jnp.concatenate([router_weight.T, first_gain[None], second_gain[None],
                             jnp.zeros((small_rows - 2 - experts, half), BF16)], axis=0)
    pos = (z * group + jnp.arange(group, dtype=jnp.int32)).astype(F32)
    inverse = jnp.power(ROPE_BASE, -jnp.arange(HEAD // 2).astype(F32) * 2.0 / HEAD)
    angle = pos[:, None] * inverse[None, :]
    cos, sin = jnp.cos(angle), jnp.sin(angle)
    cosine = jnp.concatenate([cos, cos], axis=-1)
    sine = jnp.concatenate([-sin, sin], axis=-1)
    doc = documents[0]
    doc_q = lax.dynamic_slice_in_dim(doc, z * group, group, 0)
    start = sum(jnp.where(doc_q > d, jnp.sum((doc == d).astype(jnp.int32)), 0) for d in range(DOCUMENTS - 1))[None, :]
    chosen = jnp.any(routes[0][:, :, None] == jnp.arange(LANES, dtype=jnp.int32), axis=1).astype(F32)

    q, mixed, mixed_t, lse, n1, small, wqkv, kv_all, wo, w_experts, cots = front(
        blocks, tokens[0], small, query_weight, keyvalue_weight, output_weight, expert_in, expert_out,
        cotangent[0], cosine, sine, start)
    res1, res_grad, attn_grad, d_small, grads, y_parts = expert_layer(
        mixed, tokens[0], small, chosen, wo, w_experts, cots)
    block_out, tokens_grad, d_small, d_keyval, d_experts, d_wo, d_query = backward(
        attn_grad, q, mixed_t, start, lse, tokens[0], cosine, sine, small, d_small,
        kv_all, wo, grads, y_parts, res1, res_grad, n1, wqkv)
    return (block_out[None], tokens_grad[None], d_small[experts], d_query.astype(F32), d_keyval.astype(F32), d_wo.astype(F32),
            d_small[experts + 1], d_small[:experts].T, d_experts[:, :, :width].astype(F32),
            d_experts[:, :, width:].astype(F32))


def solution(mesh):
    token_spec = P("fsdp", ("blk", "head"), None)
    row_spec = P("fsdp", None)
    in_spec = P("blk", "fsdp", None)
    out_spec = P("blk", None, "fsdp")
    return jax.shard_map(
        on_device,
        mesh=mesh,
        in_specs=(token_spec, row_spec, token_spec, token_spec, P("fsdp"), row_spec, row_spec, row_spec, P("fsdp"),
                  row_spec, in_spec, out_spec),
        out_specs=(token_spec, token_spec, P("fsdp"), row_spec, row_spec, row_spec, P("fsdp"), row_spec, in_spec,
                   out_spec),
        check_vma=False,
    )
```

```python
import functools

import jax
import jax.numpy as jnp
from jax import lax
from jax.experimental import pallas as pl
from jax.experimental.pallas import tpu as pltpu
from jax.sharding import PartitionSpec as P

QUERY_HEADS = 12
KEYVALUE_HEADS = 2
HEAD = 128
NORM_EPSILON = 1e-06
ROPE_BASE = 1000000.0
MASKED = -1e30
DOCUMENTS = 4
LOG2E = 1.4426950408889634
SCORE_LOG2 = HEAD ** (-0.5) * LOG2E
SCORE_SCALE = HEAD ** (-0.5)
LN2 = 1.0 / LOG2E
TILE = 256
BF16 = jnp.bfloat16
F32 = jnp.float32
VMEM_BYTES = 63 * 1024 * 1024

NN = (((1,), (0,)), ((), ()))
NT = (((1,), (1,)), ((), ()))
TN = (((0,), (0,)), ((), ()))


def mm(a, b, dims=NN):
    return lax.dot_general(a, b, dims, preferred_element_type=F32)


def gelu_parts(gate):
    c = 0.7978845608028654
    cube = 0.044715 * gate * gate * gate
    t = jnp.tanh(c * (gate + cube))
    value = 0.5 * gate * (1.0 + t)
    slope = 0.5 * (1.0 + t) + 0.5 * gate * (1.0 - t * t) * c * (1.0 + 3.0 * 0.044715 * gate * gate)
    return value, slope


def score_tile(key_rows, q_tile, start_row, first_key, q_first):
    scores = mm(key_rows, q_tile, NT)
    key_row = lax.broadcasted_iota(jnp.int32, scores.shape, 0)
    allowed = key_row >= start_row - first_key
    if q_first is not None:
        allowed = allowed & (key_row - lax.broadcasted_iota(jnp.int32, scores.shape, 1) <= q_first - first_key)
    return jnp.where(allowed, scores, MASKED)


def attend_tile(hh, cols, key_rows, value_cols, q_ref, start_ref, m_ref, l_ref, acc_ref, first_key, q_first):
    q_tile = q_ref[hh, cols, :]
    scores = score_tile(key_rows, q_tile, start_ref[:, cols], first_key, q_first)
    old = m_ref[hh, :, cols]
    new = jnp.maximum(old, jnp.max(scores, axis=0, keepdims=True))
    factor = jnp.exp2(old - new)
    prob = jnp.exp2(scores - new)
    m_ref[hh, :, cols] = new
    l_ref[hh, :, cols] = l_ref[hh, :, cols] * factor + jnp.sum(prob, axis=0, keepdims=True)
    acc_ref[hh, :, cols] = acc_ref[hh, :, cols] * factor + mm(value_cols, prob.astype(BF16))


def unattend_tile(hh, cols, key_rows, value_rows, key_cols, q_ref, do_ref, start_ref, lse_ref, delta_ref,
                  dq_ref, dk_ref, dv_ref, first_key, q_first):
    n = key_rows.shape[0]
    q_tile = q_ref[hh, cols, :]
    do_tile = do_ref[hh, cols, :]
    scores = score_tile(key_rows, q_tile, start_ref[:, cols], first_key, q_first)
    prob = jnp.exp2(scores - lse_ref[hh, :, cols])
    dv_ref[:n, :] += mm(prob.astype(BF16), do_tile)
    prob_grad = mm(value_rows, do_tile, NT)
    score_grad = (prob * (prob_grad - delta_ref[hh, :, cols])).astype(BF16)
    dk_ref[:n, :] += mm(score_grad, q_tile)
    dq_ref[hh, :, cols] += mm(key_cols, score_grad)


def remote(src, dst, send_sem, recv_sem, **to):
    return pltpu.make_async_remote_copy(
        src_ref=src, dst_ref=dst, send_sem=send_sem, recv_sem=recv_sem, device_id=to,
        device_id_type=pl.DeviceIdType.MESH)


class Lanes:
    def __init__(self, send, recv):
        self.send, self.recv, self.used, self.sent, self.pending = send, recv, 0, 0, []

    def slots(self, count=1):
        first = self.used
        self.used += count
        assert self.used <= self.recv.shape[0]
        return first

    def sends(self, count):
        first = self.sent
        self.sent += count
        assert self.sent <= self.send.shape[0]
        return first

    def put(self, slot, src, dst, when=None, **to):
        assert self.sent < self.send.shape[0]
        copy = remote(src, dst, self.send.at[self.sent], self.recv.at[slot], **to)
        self.sent += 1
        if when is None:
            copy.start()
        else:
            pl.when(when)(copy.start)
        self.pending.append((copy, when))
        return self.pending[-1]

    def settle(self, entry):
        copy, when = entry
        self.pending = [other for other in self.pending if other is not entry]
        if when is None:
            copy.wait_send()
        else:
            pl.when(when)(copy.wait_send)

    def arrived(self, slot, dst, when=None, **origin):
        copy = remote(dst, dst, self.send.at[0], self.recv.at[slot], **origin)
        if when is None:
            copy.wait_recv()
        else:
            pl.when(when)(copy.wait_recv)

    def drain(self):
        for copy, when in self.pending:
            if when is None:
                copy.wait_send()
            else:
                pl.when(when)(copy.wait_send)
        self.pending = []


class Place:
    def __init__(self, blocks):
        self.z, self.h, self.y = lax.axis_index("blk"), lax.axis_index("head"), lax.axis_index("fsdp")
        self.blocks = blocks
        self.x, self.c = self.h // 2, self.h % 2
        self.sib = 2 * self.x + 1 - self.c
        self.xn = 2 * (1 - self.x) + self.c
        self.xs = 2 * (1 - self.x) + 1 - self.c
        self.oy = 1 - self.y

    def others(self):
        return [(self.z + d) % self.blocks for d in range(1, self.blocks)]

    def enter(self):
        barrier = pltpu.get_barrier_semaphore()

        def greet(**to):
            pl.semaphore_signal(barrier, inc=1, device_id=to, device_id_type=pl.DeviceIdType.MESH)

        for head in (self.sib, self.xn, self.xs):
            greet(head=head)
        greet(fsdp=self.oy)
        for z in self.others():
            greet(blk=z)
        pl.semaphore_wait(barrier, 4 + self.blocks - 1)


def gather_heads(at, lanes, own, land):
    s = lanes.slots(3)
    rows = own.shape[0]

    def slot(head):
        return land.at[pl.ds(pl.multiple_of(head * rows, rows), rows), :]

    lanes.put(s, own, slot(at.h), head=at.xn)
    lanes.put(s + 1, own, slot(at.h), head=at.sib)

    passed = []

    def forward():
        lanes.arrived(s, slot(at.xn), head=at.xn)
        passed.append(lanes.put(s + 2, slot(at.xn), slot(at.xn), head=at.sib))

    def near():
        lanes.arrived(s + 1, slot(at.sib), head=at.sib)

    def far():
        lanes.arrived(s + 2, slot(at.xs), head=at.sib)

    return forward, near, far, passed


def aligned(index, size):
    return pl.ds(pl.multiple_of(index, 16), size)


def semaphores(blocks):
    count = 128 + 16 * blocks
    return [pltpu.SemaphoreType.DMA((count,)), pltpu.SemaphoreType.DMA((count,))]


class Shared:
    def __init__(self, at, lanes, chunks, give, hold):
        self.at, self.lanes, self.chunks, self.give, self.hold = at, lanes, chunks, give, hold
        self.pieces = len(give(0)) if give else 0
        self.ys = lanes.slots(chunks * self.pieces)
        self.xn, self.sib, self.far = lanes.slots(chunks), lanes.slots(chunks), lanes.slots(chunks)
        self.sent = []

    def begin(self, k):
        for i, (src, dst) in enumerate(self.give(k)):
            self.lanes.put(self.ys + k * self.pieces + i, src, dst(self.at.y), fsdp=self.at.oy)

    def landed(self, k):
        for i, (src, dst) in enumerate(self.give(k)):
            self.lanes.arrived(self.ys + k * self.pieces + i, dst(self.at.oy), fsdp=self.at.oy)

    def spread(self, k):
        self.landed(k)
        self.scatter(k)

    def scatter(self, k):
        at = self.at
        place = self.hold(k, at.h, at.oy)
        self.sent.append(self.lanes.put(self.xn + k, place, place, head=at.xn))
        self.sent.append(self.lanes.put(self.sib + k, place, place, head=at.sib))

    def forward(self, k):
        at = self.at
        place = self.hold(k, at.xn, at.oy)
        self.lanes.arrived(self.xn + k, place, head=at.xn)
        self.sent.append(self.lanes.put(self.far + k, place, place, head=at.sib))

    def settle(self):
        for entry in self.sent:
            self.lanes.settle(entry)

    def finish(self, k):
        at = self.at
        self.lanes.arrived(self.sib + k, self.hold(k, at.sib, at.oy), head=at.sib)
        self.lanes.arrived(self.far + k, self.hold(k, at.xs, at.oy), head=at.sib)


def weight_chunk(w_ref, k, head, y):
    quarter = w_ref.shape[2] // 4
    piece = quarter // 2
    return w_ref.at[k // 2, y, aligned(head * quarter + k % 2 * piece, piece), :]


class Column:
    def __init__(self, at, lanes, land):
        self.at, self.lanes, self.land = at, lanes, land
        self.slot = lanes.slots(at.blocks)

    def begin(self, own):
        at = self.at
        place = self.land.at[at.z]
        self.lanes.put(self.slot + at.z, own, place, when=at.z < at.blocks - 1, blk=at.z + 1)
        self.lanes.put(self.slot + at.z, own, place, when=at.z > 0, blk=at.z - 1)

    def hand_on(self, d):
        at = self.at
        for b, origin, next_z in ((at.z - d, at.z - 1, at.z + 1), (at.z + d, at.z + 1, at.z - 1)):
            there = (b >= 0) & (b < at.blocks)
            safe = jnp.clip(b, 0, at.blocks - 1)
            self.lanes.arrived(self.slot + safe, self.land.at[safe], when=there, blk=origin)
            self.lanes.put(self.slot + safe, self.land.at[safe], self.land.at[safe],
                           when=there & (next_z >= 0) & (next_z < at.blocks), blk=next_z)


def front_kernel(x_ref, small_ref, wq_hbm, wkv_hbm, wo_hbm, win_hbm, wout_hbm, cot_hbm, cos_ref, sin_ref, start_ref,
                 q_ref, o_ref, ot_ref, lse_ref, n1_ref, small_out, wqkv_out, kv_out, wo_out, w_out, cot_out,
                 xg_ref, small_land, wqkv_ref, kv_ref, m_ref, l_ref, acc_ref, vt_ref, wo_ref, w_ref, cot_ref,
                 load_sem, send_sem, recv_sem):
    heads, rows, _ = q_ref.shape
    own_rows, width = x_ref.shape
    blocks = kv_ref.shape[0]
    half = wq_hbm.shape[0]
    qcols = heads * HEAD
    experts = 2 * blocks
    at = Place(blocks)
    me = at.z
    lanes = Lanes(send_sem, recv_sem)
    at.enter()
    local = []

    def copy_here(src, dst):
        copy = pltpu.make_async_copy(src, dst, load_sem.at[len(local)])
        copy.start()
        local.append(copy)
        return copy

    forward, near, far, _ = gather_heads(at, lanes, x_ref, xg_ref)
    g = at.x
    q_from = pl.ds(pl.multiple_of(at.h * qcols, HEAD), qcols)
    kv_from = pl.ds(pl.multiple_of((at.c * KEYVALUE_HEADS + g) * HEAD, HEAD), HEAD)

    def kv_cols(core):
        return pl.ds(pl.multiple_of(qcols + core * HEAD, HEAD), HEAD)

    columns = ((wq_hbm.at[:, q_from], slice(0, qcols)), (wkv_hbm.at[:, kv_from], kv_cols(at.c)))

    def weight_rows(y, cols):
        return wqkv_ref.at[aligned(y * half, half), cols]

    ws, wc = lanes.slots(2), lanes.slots()
    for i, (src, cols) in reversed(list(enumerate(columns))):
        lanes.put(ws + i, src, weight_rows(at.y, cols), fsdp=at.oy)
    smalls = lanes.slots()
    lanes.put(smalls, small_ref, small_land, fsdp=at.oy)
    kv_other = pl.ds(pl.multiple_of(((1 - at.c) * KEYVALUE_HEADS + g) * HEAD, HEAD), HEAD)
    own_weights = [copy_here(src, weight_rows(at.y, cols))
                   for src, cols in columns + ((wkv_hbm.at[:, kv_other], kv_cols(1 - at.c)),)]
    cots = Column(at, lanes, cot_ref)
    own_half = pl.ds(pl.multiple_of(at.y * half, half), half)
    cot_load = copy_here(cot_hbm, cot_ref.at[me])
    wo_load = copy_here(wo_hbm, wo_ref.at[own_half, :])
    w_loads = [copy_here(win_hbm, w_ref.at[:, at.y, :, :width]), copy_here(wout_hbm, w_ref.at[:, at.y, :, width:])]
    cot_load.wait()
    cots.begin(cot_ref.at[me])

    quarter = half // 4

    def wo_place(k, head, y):
        return wo_ref.at[aligned(y * half + head * quarter, quarter), :]

    shared_wo = Shared(at, lanes, 1,
                       lambda k: [(wo_place(0, at.h, at.y), lambda y: wo_place(0, at.h, y))],
                       wo_place)
    chunks, spread_here = 4, 2

    def w_place(k, head, y):
        return weight_chunk(w_ref, k, head, y)

    def w_give(k):
        return [(w_place(k, at.h, at.y), lambda y: w_place(k, at.h, y))]

    shared_w = Shared(at, lanes, chunks, w_give, w_place)

    small_out[:, :half] = jnp.zeros((small_ref.shape[0], half), BF16)
    lanes.arrived(smalls, small_land, fsdp=at.oy)
    for y in range(2):
        @pl.when(at.y == y)
        def _(y=y):
            small_out[:, y * half:(y + 1) * half] = small_ref[...]
            small_out[:, (1 - y) * half:(2 - y) * half] = small_land[...]

    def norm(head, block):
        x = block.astype(F32)
        inv = lax.rsqrt(jnp.mean(x * x, axis=-1, keepdims=True) + NORM_EPSILON)
        n1_ref[aligned(head * own_rows, own_rows), :] = (x * inv * small_out[experts:experts + 1, :].astype(F32)).astype(BF16)

    def gathered(head):
        return xg_ref[aligned(head * own_rows, own_rows), :]

    norm(at.h, x_ref[...])
    near()
    norm(at.sib, gathered(at.sib))
    forward()
    norm(at.xn, gathered(at.xn))
    far()
    norm(at.xs, gathered(at.xs))
    for copy in own_weights:
        copy.wait()
    for i, (_, cols) in reversed(list(enumerate(columns))):
        lanes.arrived(ws + i, weight_rows(at.oy, cols), fsdp=at.oy)
        if i == 1:
            lanes.put(wc, weight_rows(at.oy, cols), weight_rows(at.oy, cols), head=at.sib)
    lanes.arrived(wc, weight_rows(at.oy, kv_cols(1 - at.c)), head=at.sib)
    wo_load.wait()
    shared_wo.begin(0)
    for load in w_loads:
        load.wait()
    for k in range(chunks):
        shared_w.begin(k)
    cots.hand_on(1)

    def project(i, _):
        band = aligned(i * TILE, TILE)
        pre = mm(n1_ref[band, :], wqkv_ref[...])
        cosine, sine = cos_ref[band, :], sin_ref[band, :]

        def turned(u):
            return (u * cosine + pltpu.roll(u, HEAD // 2, 1) * sine).astype(BF16)

        for hh in range(heads):
            q_ref[hh, band, :] = turned(pre[:, hh * HEAD:(hh + 1) * HEAD] * SCORE_LOG2)
        kv_ref[me, 0, band, :] = turned(pre[:, qcols:qcols + HEAD])
        kv_ref[me, 1, band, :] = pre[:, qcols + HEAD:].astype(BF16)
        return 0

    lax.fori_loop(0, rows // TILE, project, 0)

    kvs, kvc = lanes.slots(blocks), lanes.slots(blocks)

    def kv_half(b, core):
        return kv_ref.at[b, core]

    lanes.put(kvs + me, kv_half(me, at.c), kv_half(me, at.c), when=me < blocks - 1, blk=me + 1)
    late = [copy_here(wqkv_ref, wqkv_out), copy_here(wo_ref.at[own_half, :], wo_out.at[own_half, :]),
            copy_here(w_ref.at[:, at.y], w_out.at[:, at.y])]

    m_ref[...] = jnp.full_like(m_ref, MASKED)
    l_ref[...] = jnp.zeros_like(l_ref)
    acc_ref[...] = jnp.zeros_like(acc_ref)

    def transpose_values(b):
        vt_ref[...] = kv_ref[b, 1].astype(F32).T.astype(BF16)

    transpose_values(me)
    for i in range(rows // TILE):
        n = (i + 1) * TILE

        def diagonal(hh, _, i=i, n=n):
            attend_tile(hh, slice(i * TILE, n), kv_ref[me, 0, :n, :], vt_ref[:, :n], q_ref, start_ref,
                        m_ref, l_ref, acc_ref, me * rows, me * rows + i * TILE)
            return 0

        lax.fori_loop(0, heads, diagonal, 0)

    def block(b):
        transpose_values(b)

        def tile(t, _):
            hh, i = t // (rows // TILE), t % (rows // TILE)
            cols = pl.ds(pl.multiple_of(i * TILE, TILE), TILE)
            attend_tile(hh, cols, kv_ref[b, 0], vt_ref[...], q_ref, start_ref,
                        m_ref, l_ref, acc_ref, b * rows, None)
            return 0

        lax.fori_loop(0, heads * (rows // TILE), tile, 0)

    ticks = [[functools.partial(shared_wo.spread, 0), functools.partial(shared_w.spread, 0)],
             [functools.partial(shared_w.spread, 1), functools.partial(shared_wo.forward, 0),
              functools.partial(cots.hand_on, 2)],
             [functools.partial(shared_w.forward, 0)] + [functools.partial(cots.hand_on, d) for d in range(3, blocks)],
             [functools.partial(shared_w.forward, 1)]]

    def tick():
        if ticks:
            for f in ticks.pop(0):
                f()

    for d in range(1, blocks):
        b = jnp.maximum(me - d, 0)
        there = me >= d
        lanes.arrived(kvs + b, kv_half(b, at.c), when=there, blk=me - 1)
        lanes.put(kvs + b, kv_half(b, at.c), kv_half(b, at.c), when=there & (me < blocks - 1), blk=me + 1)
        lanes.put(kvc + b, kv_half(b, at.c), kv_half(b, at.c), when=there, head=at.sib)
        lanes.arrived(kvc + b, kv_half(b, 1 - at.c), when=there, head=at.sib)
        pl.when(there)(functools.partial(block, b))
        tick()

    for hh in range(heads):
        total = l_ref[hh]
        done = acc_ref[hh] / total
        ot_ref[hh * HEAD:(hh + 1) * HEAD, :] = done.astype(BF16)
        o_ref[:, hh * HEAD:(hh + 1) * HEAD] = done.T.astype(BF16)
        lse_ref[hh] = m_ref[hh] + jnp.log2(total)
    kv_copies = [pltpu.make_async_copy(kv_ref.at[b], kv_out.at[b], load_sem.at[15]) for b in range(blocks)]
    for b, copy in enumerate(kv_copies):
        @pl.when(b <= me)
        def _(copy=copy):
            copy.start()
            copy.wait()
    while ticks:
        tick()
    shared_wo.finish(0)
    other_half = pl.ds(pl.multiple_of(at.oy * half, half), half)
    late.append(copy_here(wo_ref.at[other_half, :], wo_out.at[other_half, :]))
    late.append(copy_here(cot_ref, cot_out))
    for k in range(spread_here):
        shared_w.finish(k)
    for k in range(spread_here, chunks):
        shared_w.landed(k)
    late.append(copy_here(w_ref.at[:, at.oy], w_out.at[:, at.oy]))
    for copy in late:
        copy.wait()
    lanes.drain()


def front(blocks, x, small, wq, wkv, wo, win, wout, cot, cosine, sine, start):
    own_rows, width = x.shape
    rows = cosine.shape[0]
    half = wq.shape[0]
    heads = QUERY_HEADS * own_rows // rows
    qcols = heads * HEAD
    ffe = wout.shape[1]
    vm = pl.BlockSpec(memory_space=pltpu.VMEM)
    hbm = pl.BlockSpec(memory_space=pl.ANY)
    sds = jax.ShapeDtypeStruct
    return pl.pallas_call(
        front_kernel,
        out_shape=(
            sds((heads, rows, HEAD), BF16),
            sds((rows, qcols), BF16),
            sds((qcols, rows), BF16),
            sds((heads, 1, rows), F32),
            sds((rows, width), BF16),
            sds((small.shape[0], width), BF16),
            sds((width, qcols + 2 * HEAD), BF16),
            sds((blocks, 2, rows, HEAD), BF16),
            sds((width, width), BF16),
            sds((2, 2, half, width + half), BF16),
            sds((blocks, own_rows, width), BF16),
        ),
        in_specs=[vm, vm] + [hbm] * 6 + [vm] * 3,
        out_specs=[vm] * 6 + [hbm] * 5,
        scratch_shapes=[
            pltpu.VMEM((rows, width), BF16),
            pltpu.VMEM(small.shape, BF16),
            pltpu.VMEM((width, qcols + 2 * HEAD), BF16),
            pltpu.VMEM((blocks, 2, rows, HEAD), BF16),
            pltpu.VMEM((heads, 1, rows), F32),
            pltpu.VMEM((heads, 1, rows), F32),
            pltpu.VMEM((heads, HEAD, rows), F32),
            pltpu.VMEM((HEAD, rows), BF16),
            pltpu.VMEM((width, width), BF16),
            pltpu.VMEM((2, 2, half, width + half), BF16),
            pltpu.VMEM((blocks, own_rows, width), BF16),
            pltpu.SemaphoreType.DMA((16,)),
        ] + semaphores(blocks),
        compiler_params=pltpu.CompilerParams(
            vmem_limit_bytes=VMEM_BYTES, collective_id=0, has_side_effects=True),
    )(x, small, wq, wkv, wo, win, wout, cot, cosine, sine, start)


class ColumnSum:
    CHUNKS = 4

    def __init__(self, at, lanes, part, land):
        self.at, self.lanes, self.part, self.land = at, lanes, part, land
        self.rows = part.shape[1] // self.CHUNKS
        self.recv = lanes.slots((at.blocks + 1) * self.CHUNKS)
        self.sent = lanes.sends(at.blocks * self.CHUNKS)

    def copy(self, b, ch):
        at = self.at
        travel = jnp.where(b < at.z, -1, 1)
        there = at.z + travel
        slot = jnp.where((there == b) & (b > at.z), at.blocks, b)
        rows = pl.ds(ch * self.rows, self.rows)
        return remote(self.part.at[b, rows, :], self.land.at[slot, rows, :],
                      self.lanes.send.at[self.sent + b * self.CHUNKS + ch],
                      self.lanes.recv.at[self.recv + slot * self.CHUNKS + ch], blk=there)

    def landed(self, slot, ch, origin):
        rows = pl.ds(ch * self.rows, self.rows)
        place = self.land.at[slot, rows, :]
        remote(place, place, self.lanes.send.at[0], self.lanes.recv.at[self.recv + slot * self.CHUNKS + ch],
               blk=origin).wait_recv()

    def first_send(self, b):
        at = self.at

        @pl.when(((b < at.z) & (at.z == at.blocks - 1)) | ((b > at.z) & (at.z == 0)))
        def _():
            for ch in range(self.CHUNKS):
                self.copy(b, ch).start()

    def relay(self, phase, d, add):
        at = self.at
        s = jnp.where(at.z * 2 >= at.blocks, -1, 1) * (1 - 2 * phase)
        b, origin = at.z + s * d, at.z - s
        safe = jnp.clip(b, 0, at.blocks - 1)

        @pl.when((b >= 0) & (b < at.blocks) & (origin >= 0) & (origin < at.blocks))
        def _():
            for ch in range(self.CHUNKS):
                self.landed(safe, ch, origin)
                add(safe, pl.ds(ch * self.rows, self.rows))
                self.copy(safe, ch).start()

    def arrive(self, side, use):
        at = self.at
        slot, origin = (at.z, at.z + 1) if side == 0 else (at.blocks, at.z - 1)

        @pl.when((origin >= 0) & (origin < at.blocks))
        def _():
            for ch in range(self.CHUNKS):
                self.landed(slot, ch, origin)
            use(slot)

    def finish(self):
        at = self.at
        for b in range(at.blocks):
            @pl.when(b != at.z)
            def _(b=b):
                for ch in range(self.CHUNKS):
                    self.copy(b, ch).wait_send()


LANES = 128
HALF_LANES = LANES // 2


def split_lanes(value):
    high = value.astype(BF16).astype(F32)
    return (high + pltpu.roll(value - high, HALF_LANES, 1)).astype(BF16)


def expert_kernel(o_ref, x_ref, small_ref, chosen_ref, wo_hbm, w_hbm, cot_hbm,
                  res_out, grad_out, attn_out, small_out, sums_out, y_out, core_land, *rest):
    big = cot_hbm.shape[0] > 4
    if big:
        xb_ref, dx_ref, land_ref, *rest = rest
        (xb_stage, dx_stage, land_stage, g_ref, *rest) = rest
    else:
        xb_ref, dx_ref, land_ref, *rest = rest
    (mix_ref, w_ref, cot_ref, acc_ref, gate_ref, dgu_ref, ga_ref, xt_ref, gat_ref, gg_ref, y_ref, stage_ref,
     gates_ref, router_ref, load_sem, y_sem, send_sem, recv_sem) = rest
    own_rows, width = x_ref.shape
    blocks = cot_hbm.shape[0]
    qcols = o_ref.shape[1]
    half = width // 2
    experts, _, ffe, _ = w_ref.shape
    at = Place(blocks)
    me = at.z
    lanes = Lanes(send_sem, recv_sem)
    at.enter()
    every = blocks * own_rows
    if big:
        wo_rows = [(slice(y * half, (y + 1) * half), g_ref.at[0, y, :, :width]) for y in range(2)]
    else:
        wo_rows = [(slice(0, every), dgu_ref.at[0]), (slice(every, width), dgu_ref.at[1, :width - every])]
    wo_load = [pltpu.make_async_copy(wo_hbm.at[rows, :], place, load_sem.at[y])
               for y, (rows, place) in enumerate(wo_rows)]
    for load in wo_load:
        load.start()
    quarter = half // 4
    here = aligned(at.h * quarter, quarter)
    w_loads = [pltpu.make_async_copy(w_hbm.at[place], w_ref.at[place], load_sem.at[4 + i])
               for i, place in enumerate(((0,), (1, at.y), (1, at.oy, here)))]
    for load in w_loads:
        load.start()
    late = Shared(at, lanes, 4, None, functools.partial(weight_chunk, w_ref))
    if not big:
        cot_loads = [pltpu.make_async_copy(cot_hbm.at[b], cot_ref.at[b * own_rows:(b + 1) * own_rows, :],
                                           load_sem.at[7 + b]) for b in range(blocks)]
        for load in cot_loads:
            load.start()

    total_experts = experts * blocks
    srows = small_ref.shape[0]
    is_router = lax.broadcasted_iota(jnp.int32, (srows, width), 0) < total_experts
    router_ref[...] = jnp.zeros_like(router_ref)
    router_ref[:srows, :] = jnp.where(is_router, small_ref[...].astype(F32), 0.0).astype(BF16)
    gain_two = small_ref[total_experts + 1:total_experts + 2, :].astype(F32)

    mixes = lanes.slots(4)

    def mix_cols(head):
        return mix_ref.at[:, pl.ds(pl.multiple_of(head * qcols, HEAD), qcols)]

    for head in (at.xn, at.xs, at.sib):
        lanes.put(mixes + at.h, o_ref.at[aligned(head * own_rows, own_rows), :], mix_cols(at.h), head=head)
    mix_ref[:, pl.ds(pl.multiple_of(at.h * qcols, HEAD), qcols)] = o_ref[aligned(at.h * own_rows, own_rows), :]
    for head in (at.sib, at.xn, at.xs):
        lanes.arrived(mixes + head, mix_cols(head), head=head)
    for load in w_loads:
        load.wait()
    for k in (2, 3):
        late.scatter(k)
    for load in wo_load:
        load.wait()
    step = 512
    for i in range(width // step):
        cols = slice(i * step, (i + 1) * step)
        res_out[:, cols] = x_ref[:, cols].astype(F32) + sum(
            mm(mix_ref[:, rows], place[:, cols]) for rows, place in wo_rows)

    def inverse_two():
        res = res_out[...]
        return lax.rsqrt(jnp.mean(res * res, axis=-1, keepdims=True) + NORM_EPSILON)

    n2 = (res_out[...] * inverse_two() * gain_two).astype(BF16)
    chosen = chosen_ref[...] > 0.0
    logits = jnp.where(chosen, mm(n2, router_ref[...], NT), MASKED)
    e_top = jnp.where(chosen, jnp.exp(logits - jnp.max(logits, axis=-1, keepdims=True)), 0.0)
    gates = e_top / jnp.sum(e_top, axis=-1, keepdims=True)
    gates_ref[...] = gates
    own_x = xb_stage if big else xb_ref.at[me]
    own_x[:, :width] = n2
    own_x[:, width:] = split_lanes(gates)

    def move(src, dst):
        copy = pltpu.make_async_copy(src, dst, load_sem.at[3])
        copy.start()
        copy.wait()

    if big:
        move(xb_stage, xb_ref.at[me])
    xs_slot, xs_sent = lanes.slots(blocks), lanes.sends(blocks + 2)

    def xs_copy(b, to, send):
        return remote(xb_ref.at[b], xb_ref.at[b], send_sem.at[xs_sent + send], recv_sem.at[xs_slot + b], blk=to)

    pl.when(me > 0)(lambda: xs_copy(me, me - 1, blocks).start())
    pl.when(me < blocks - 1)(lambda: xs_copy(me, me + 1, blocks + 1).start())

    if big:
        def clear(i, _):
            for e in range(experts):
                for y in range(2):
                    g_ref[e, y, aligned(i * 64, 64), :] = jnp.zeros((64, g_ref.shape[3]), BF16)
            return 0

        lax.fori_loop(0, half // 64, clear, 0)
    else:
        for load in cot_loads:
            load.wait()
    for k in (2, 3):
        late.forward(k)
    for k in (2, 3):
        late.finish(k)
    back = ColumnSum(at, lanes, dx_ref, land_ref)
    lane = lax.broadcasted_iota(jnp.int32, (own_rows, LANES), 1)
    tile = 256

    def y_copy(b):
        return pltpu.make_async_copy(y_ref, y_out.at[b], y_sem)

    def block(b, first):
        if big:
            move(xb_ref.at[b], xb_stage)
            move(cot_hbm.at[b], cot_ref)
        x_in = xb_stage if big else xb_ref.at[b]
        band_all = slice(None) if big else aligned(b * own_rows, own_rows)
        lanes_all = pl.ds(pl.multiple_of(b * own_rows, own_rows), own_rows)
        acc_ref[...] = jnp.zeros_like(acc_ref)
        gg_ref[...] = jnp.zeros_like(gg_ref)

        def hidden(e, _):
            index = me * experts + e
            pack = x_in[:, width:].astype(F32)
            mine = (lane == index) | (lane == index + HALF_LANES)
            gate_ref[...] = jnp.sum(jnp.where(mine, pack, 0.0), axis=1, keepdims=True)

            def inner(t, total):
                low = pl.ds(pl.multiple_of(t * tile, tile), tile)
                high = pl.ds(pl.multiple_of(ffe + t * tile, tile), tile)
                out_cols = slice(width, width + half)
                gate_pre = mm(x_in[:, :half], w_ref[e, 0, :, low]) + mm(x_in[:, half:width], w_ref[e, 1, :, low])
                up = mm(x_in[:, :half], w_ref[e, 0, :, high]) + mm(x_in[:, half:width], w_ref[e, 1, :, high])
                back_h = (mm(cot_ref[band_all, :half], w_ref[e, 0, low, out_cols], NT)
                          + mm(cot_ref[band_all, half:], w_ref[e, 1, low, out_cols], NT))
                value, slope = gelu_parts(gate_pre)
                act = (value * up).astype(BF16).astype(F32)
                gate = gate_ref[...]
                ga_ref[e, :, low] = (gate * act).astype(BF16)
                if not big:
                    gat_ref[e, low, lanes_all] = (gate * act).T.astype(BF16)
                d_act = gate * back_h
                dgu_ref[e, band_all, low] = (d_act * up * slope).astype(BF16)
                dgu_ref[e, band_all, high] = (d_act * value).astype(BF16)
                return total + jnp.sum(act * back_h, axis=1, keepdims=True)

            total = lax.fori_loop(0, ffe // tile, inner, jnp.zeros((own_rows, 1), F32))
            gg_ref[...] += jnp.where(lane == index, total, 0.0)
            for y in range(2):
                acc_ref[:, y * half:(y + 1) * half] += mm(dgu_ref[e, band_all, :], w_ref[e, y, :, :width], NT)
            return 0

        lax.fori_loop(0, experts, hidden, 0)
        part = dx_stage if big else dx_ref.at[b]
        part[:, :width] = acc_ref[...].astype(BF16)
        part[:, width:] = split_lanes(gg_ref[...])
        if big:
            move(dx_stage, dx_ref.at[b])
        back.first_send(b)

        if big:
            xt_ref[...] = x_in[:, :width].astype(F32).T.astype(BF16)

            def weights(e, _):
                gat_ref[0] = ga_ref[e].astype(F32).T.astype(BF16)

                def rows(i, _):
                    band = aligned(i * tile, tile)
                    for y in range(2):
                        x_cols = xt_ref[aligned(y * half + i * tile, tile), :]
                        for n in range(width // step):
                            cols = slice(n * step, (n + 1) * step)
                            total = g_ref[e, y, band, cols].astype(F32) + mm(x_cols, dgu_ref[e, :, cols])
                            g_ref[e, y, band, cols] = total.astype(BF16)
                        out_cols = slice(width, width + half)
                        total = (g_ref[e, y, band, out_cols].astype(F32)
                                 + mm(gat_ref[0, band, :], cot_ref[:, y * half:(y + 1) * half]))
                        g_ref[e, y, band, out_cols] = total.astype(BF16)
                    return 0

                return lax.fori_loop(0, half // tile, rows, 0)

            lax.fori_loop(0, experts, weights, 0)
        else:
            xt_ref[:, lanes_all] = x_in[:, :width].astype(F32).T.astype(BF16)

        pl.when(jnp.logical_not(first))(lambda: y_copy(b).wait())
        for y in range(2):
            total = mm(ga_ref[0], w_ref[0, y, :, width:])
            for e in range(1, experts):
                total = total + mm(ga_ref[e], w_ref[e, y, :, width:])
            y_ref[:, y * half:(y + 1) * half] = total.astype(BF16)
        y_copy(b).start()

    def distance(d, _):
        for b, origin, to in ((me - d, me - 1, me + 1), (me + d, me + 1, me - 1)):
            @pl.when((d > 0) & (b >= 0) & (b < blocks))
            def _(b=b, origin=origin, to=to):
                xs_copy(b, origin, 0).wait_recv()
                pl.when((to >= 0) & (to < blocks))(lambda: xs_copy(b, to, b).start())

        def side(s, _):
            b = jnp.where(s == 0, me - d, me + d)

            @pl.when((b >= 0) & (b < blocks) & ((d > 0) | (s == 0)))
            def _():
                block(jnp.clip(b, 0, blocks - 1), d == 0)

            return 0

        return lax.fori_loop(0, 2, side, 0)

    lax.fori_loop(0, blocks, distance, 0)
    y_copy(me).wait()

    def add(b, rows):
        if big:
            move(dx_ref.at[b, rows, :], dx_stage.at[rows, :])
            move(land_ref.at[b, rows, :], land_stage.at[rows, :])
            dx_stage[rows, :] = (dx_stage[rows, :].astype(F32) + land_stage[rows, :].astype(F32)).astype(BF16)
            move(dx_stage.at[rows, :], dx_ref.at[b, rows, :])
        else:
            dx_ref[b, rows, :] = (dx_ref[b, rows, :].astype(F32) + land_ref[b, rows, :].astype(F32)).astype(BF16)

    late.settle()
    total_ref = g_ref if big else w_ref

    def weights_of(e):
        def rows(i, _):
            cols = pl.ds(pl.multiple_of(i * tile, tile), tile)
            for y in range(2):
                total = mm(xt_ref[y * half:(y + 1) * half, :], dgu_ref[e, :, cols])
                total_ref[e, y, :, cols] = total.astype(BF16)
            return 0

        def outs(i, _):
            for y in range(2):
                cols = pl.ds(pl.multiple_of(y * half + i * tile, tile), tile)
                place = pl.ds(pl.multiple_of(width + i * tile, tile), tile)
                total_ref[e, y, :, place] = mm(gat_ref[e], cot_ref[:, cols]).astype(BF16)
            return 0

        lax.fori_loop(0, 2 * ffe // tile, rows, 0)
        lax.fori_loop(0, half // tile, outs, 0)

    chunks = 4
    piece = half // chunks
    cores = lanes.slots(chunks)
    back.relay(0, 1, add)
    if not big:
        weights_of(1 - at.c)
    for k in range(chunks):
        band = pl.ds(k * piece, piece)
        lanes.put(cores + k, total_ref.at[1 - at.c, :, band, :], core_land.at[:, band, :], head=at.sib)

    def core_sum(k):
        band = pl.ds(k * piece, piece)
        lanes.arrived(cores + k, core_land.at[:, band, :], head=at.sib)
        move(core_land.at[:, band, :], stage_ref)
        for y in range(2):
            total = total_ref[at.c, y, band, :].astype(F32) + stage_ref[y].astype(F32)
            total_ref[at.c, y, band, :] = total.astype(BF16)

    for d in range(2, blocks):
        back.relay(0, d, add)
    if not big:
        weights_of(at.c)
    for d in range(1, blocks):
        back.relay(1, d, add)
    for k in range(chunks):
        core_sum(k)
    keep = pltpu.make_async_copy(total_ref.at[at.c], sums_out, load_sem.at[0])
    keep.start()

    if big:
        move(dx_ref.at[me], dx_stage)
    own_part = dx_stage if big else dx_ref.at[me]
    acc_ref[...] = own_part[:, :width].astype(F32)
    gg_ref[...] = own_part[:, width:].astype(F32)

    def take(slot):
        if big:
            move(land_ref.at[slot], land_stage)
        came = land_stage if big else land_ref.at[slot]
        acc_ref[...] += came[:, :width].astype(F32)
        gg_ref[...] += came[:, width:].astype(F32)

    for side in range(2):
        back.arrive(side, take)
    both = gg_ref[...]
    gate_grads = jnp.where(lane < HALF_LANES, both + pltpu.roll(both, HALF_LANES, 1), 0.0)
    gates = gates_ref[...]
    d_logits = (gates * (gate_grads - jnp.sum(gates * gate_grads, axis=-1, keepdims=True))).astype(BF16)
    inv = inverse_two()
    hat = res_out[...] * inv
    n2 = (hat * gain_two).astype(BF16)
    small_out[...] = mm(d_logits.astype(F32).T.astype(BF16), n2)[:small_out.shape[0], :]
    d_n2 = acc_ref[...] + mm(d_logits, router_ref[...])
    small_out[total_experts + 1:total_experts + 2, :] = jnp.sum(d_n2 * hat, axis=0, keepdims=True)
    pulled = d_n2 * gain_two
    if big:
        move(cot_hbm.at[me], cot_ref)
    own_cot = cot_ref[...] if big else cot_ref[aligned(me * own_rows, own_rows), :]
    grad = own_cot.astype(F32) + inv * (pulled - hat * jnp.mean(pulled * hat, axis=-1, keepdims=True))
    grad_out[...] = grad
    attn_out[...] = grad.astype(BF16)
    keep.wait()
    for b in range(blocks):
        up, down = (b < me) & (me < blocks - 1), (b > me) & (me > 0)
        pl.when(up)(lambda b=b: xs_copy(b, me + 1, b).wait_send())
        pl.when(down)(lambda b=b: xs_copy(b, me - 1, b).wait_send())
    pl.when(me > 0)(lambda: xs_copy(me, me - 1, blocks).wait_send())
    pl.when(me < blocks - 1)(lambda: xs_copy(me, me + 1, blocks + 1).wait_send())
    back.finish()
    lanes.drain()


def expert_layer(o, x, small, chosen, wo, w, cot):
    own_rows, width = x.shape
    blocks = cot.shape[0]
    experts, _, half, wide = w.shape
    ffe = half
    pack = width + LANES
    big = blocks > 4
    kept = own_rows if big else blocks * own_rows
    vm = pl.BlockSpec(memory_space=pltpu.VMEM)
    hbm = pl.BlockSpec(memory_space=pl.ANY)
    sds = jax.ShapeDtypeStruct
    column = [((blocks, own_rows, pack), BF16), ((blocks, own_rows, pack), BF16), ((blocks + 1, own_rows, pack), BF16)]
    if big:
        extra_out, extra_spec = tuple(sds(*c) for c in column), [hbm] * 3
        extra_scratch = [pltpu.VMEM((own_rows, pack), BF16)] * 3 + [pltpu.VMEM(w.shape, BF16)]
    else:
        extra_out, extra_spec = (), []
        extra_scratch = [pltpu.VMEM(*c) for c in column]
    outs = pl.pallas_call(
        expert_kernel,
        out_shape=(
            sds((own_rows, width), F32),
            sds((own_rows, width), F32),
            sds((own_rows, width), BF16),
            sds((-(-(experts * blocks + 2) // 8) * 8, width), F32),
            sds((2, half, wide), BF16),
            sds((blocks, own_rows, width), BF16),
            sds((2, half, wide), BF16),
        ) + extra_out,
        in_specs=[vm] * 4 + [hbm] * 3,
        out_specs=[vm] * 4 + [hbm] * 3 + extra_spec,
        scratch_shapes=extra_scratch + [
            pltpu.VMEM((own_rows, width), BF16),
            pltpu.VMEM(w.shape, BF16),
            pltpu.VMEM((kept, width), BF16),
            pltpu.VMEM((own_rows, width), F32),
            pltpu.VMEM((own_rows, 1), F32),
            pltpu.VMEM((experts, kept, 2 * ffe), BF16),
            pltpu.VMEM((experts, own_rows, ffe), BF16),
            pltpu.VMEM((width, kept), BF16),
            pltpu.VMEM((experts, ffe, kept), BF16),
            pltpu.VMEM((own_rows, LANES), F32),
            pltpu.VMEM((own_rows, width), BF16),
            pltpu.VMEM((2, half // 4, wide), BF16),
            pltpu.VMEM((own_rows, LANES), F32),
            pltpu.VMEM((LANES, width), BF16),
            pltpu.SemaphoreType.DMA((7 + blocks,)),
            pltpu.SemaphoreType.DMA,
        ] + semaphores(blocks),
        compiler_params=pltpu.CompilerParams(
            vmem_limit_bytes=VMEM_BYTES, collective_id=1, has_side_effects=True),
    )(o, x, small, chosen, wo, w, cot)
    return outs[:6]


class ExpertSums:
    CHUNKS = 8

    def __init__(self, at, lanes, grads, own, land_y, land_x, out, load_sem, keep_sem):
        self.at, self.lanes = at, lanes
        self.grads, self.own, self.out = grads, own, out
        self.land_y, self.land_x = land_y, land_x
        self.load_sem, self.keep_sem = load_sem, keep_sem
        self.rows = grads.shape[1] // self.CHUNKS
        n = self.CHUNKS
        self.ys, self.xr, self.cg = [lanes.slots(n) for _ in range(3)]
        self.sent = []
        self.kept = []

    def chunk(self, k):
        return pl.ds(k * self.rows, self.rows)

    def load(self):
        self.loads = [pltpu.make_async_copy(self.grads.at[y], self.own.at[y], self.load_sem.at[i])
                      for i, y in enumerate((self.at.oy, self.at.y))]
        for copy in self.loads:
            copy.start()

    def to_y(self):
        self.loads[0].wait()
        for k in range(self.CHUNKS):
            rows = self.chunk(k)
            self.sent.append(self.lanes.put(
                self.ys + k, self.own.at[self.at.oy, rows, :], self.land_y.at[rows, :], fsdp=self.at.oy))

    def y_sent(self):
        for copy in self.sent:
            self.lanes.settle(copy)

    def to_x(self, k):
        at, rows = self.at, self.chunk(k)
        if k == 0:
            self.loads[1].wait()
        self.lanes.arrived(self.ys + k, self.land_y.at[rows, :], fsdp=at.oy)
        total = self.own[at.y, rows, :].astype(F32) + self.land_y[rows, :].astype(F32)
        self.own[at.y, rows, :] = total.astype(BF16)
        self.lanes.put(self.xr + k, self.own.at[at.y, rows, :], self.land_x.at[rows, :], head=at.xn)

    def share(self, k):
        at, rows = self.at, self.chunk(k)
        self.lanes.arrived(self.xr + k, self.land_x.at[rows, :], head=at.xn)
        total = self.own[at.y, rows, :].astype(F32) + self.land_x[rows, :].astype(F32)
        self.land_x[rows, :] = total.astype(BF16)
        done, place = self.land_x.at[rows, :], self.out.at[at.c, rows, :]
        self.lanes.put(self.cg + k, done, place, head=at.sib)
        keep = pltpu.make_async_copy(done, place, self.keep_sem.at[k])
        keep.start()
        self.kept.append(keep)

    def finish(self):
        at = self.at
        for k in range(self.CHUNKS):
            self.lanes.arrived(self.cg + k, self.out.at[1 - at.c, self.chunk(k), :], head=at.sib)
            self.kept[k].wait()


class OutputSums:
    PARTS = 4

    def __init__(self, at, lanes, grad, land_y, land_z, out):
        self.at, self.lanes, self.grad = at, lanes, grad
        self.land_y, self.land_z, self.out = land_y, land_z, out
        self.rows = grad.shape[0] // self.PARTS
        self.ys = lanes.slots()
        self.zr, self.zg = lanes.slots(at.blocks), lanes.slots(self.PARTS)
        self.xg, self.cg = lanes.slots(), lanes.slots(self.PARTS)
        self.owner, self.giver = at.y == at.x, at.y != at.x
        self.summer = at.z < self.PARTS
        self.part = at.z % self.PARTS
        self.mine = aligned(self.part * self.rows, self.rows)

    def to_z(self):
        at = self.at
        for p in range(self.PARTS):
            self.lanes.put(self.zr + at.z, self.grad.at[pl.ds(p * self.rows, self.rows), :], self.land_z.at[at.z],
                           when=at.z != p, blk=p)

    def to_y(self, fetch):
        at = self.at
        for z in at.others():
            self.lanes.arrived(self.zr + z, self.land_z.at[z], when=self.summer, blk=z)

        @pl.when(self.summer)
        def _():
            total = self.grad[self.mine, :].astype(F32)
            for z in at.others():
                total = total + fetch(self.land_z.at[z])[...].astype(F32)
            self.grad[self.mine, :] = total.astype(BF16)

        self.lanes.put(self.ys, self.grad.at[self.mine, :], self.land_y, when=self.summer & self.giver, fsdp=at.oy)

    def place(self, core, p):
        return self.out.at[aligned(core * self.PARTS * self.rows + p * self.rows, self.rows), :]

    def share(self):
        at, p = self.at, self.part
        ready = self.summer & self.owner
        self.lanes.arrived(self.ys, self.land_y, when=ready, fsdp=at.oy)
        at_rows = aligned(at.c * self.PARTS * self.rows + p * self.rows, self.rows)

        @pl.when(ready)
        def _():
            total = self.grad[self.mine, :].astype(F32) + self.land_y[...].astype(F32)
            self.out[at_rows, :] = total.astype(BF16)

        place = self.place(at.c, p)
        self.lanes.put(self.xg, place, place, when=ready, head=at.xn)
        self.spread(ready)

    def spread(self, ready):
        at, place = self.at, self.place(self.at.c, self.part)
        for z in at.others():
            self.lanes.put(self.zg + self.part, place, place, when=ready, blk=z)
        self.lanes.put(self.cg + self.part, place, place, when=ready, head=at.sib)

    def take_over(self):
        ready = self.summer & self.giver
        self.lanes.arrived(self.xg, self.place(self.at.c, self.part), when=ready, head=self.at.xn)
        self.spread(ready)

    def pass_on(self):
        at = self.at
        for p in range(self.PARTS):
            place, later = self.place(at.c, p), at.z != p
            self.lanes.arrived(self.zg + p, place, when=later, blk=p)
            self.lanes.put(self.cg + p, place, place, when=later, head=at.sib)

    def finish(self):
        at = self.at
        for p in range(self.PARTS):
            self.lanes.arrived(self.cg + p, self.place(1 - at.c, p), head=at.sib)


def back_kernel(attn_ref, q_ref, ot_ref, start_ref, lse_ref, x_ref, cos_ref, sin_ref, gain_ref, small_ref,
                kv_in, wo_hbm, grads_hbm, y_in, res_hbm, res_grad_hbm, n1_hbm, w_hbm,
                block_out, tokens_out, small_out, kv_out, experts_out, output_out, query_out, y_land, *rest):
    blocks = kv_in.shape[0]
    big = blocks > 4
    dkv_stage = dwo_stage = None
    if big:
        yp_ref, dkv_land, dkv_sib, dwo_z, kv_ref, dkv_stage, dwo_stage, y_stage, kv_stage, *rest = rest
    else:
        yp_ref, dkv_land, dkv_sib, dwo_z, kv_ref, *rest = rest
    (dq_ref, dk_ref, dv_ref, kt_ref, delta_ref, do_ref, ag_ref, wo_ref, dwo_ref, dwo_y, dwo_land,
     own_ref, ey_ref, ex_ref, acc_ref, y_other, w_ref, dpre_ref, dn_sib, dn_x, dw_ref, dw_y, dw_z,
     sm_ref, sm_a, sm_b, sm_y, sm_z, land_ref, dkv_ref, n1t_ref, load_sem, keep_sem, send_sem, recv_sem) = rest
    heads, rows, _ = q_ref.shape
    own_rows, width = attn_ref.shape
    half = width // 2
    qcols = heads * HEAD
    gain_row = 2 * blocks
    at = Place(blocks)
    me = at.z
    lanes = Lanes(send_sem, recv_sem)
    at.enter()
    experts = ExpertSums(at, lanes, grads_hbm, own_ref, ey_ref, ex_ref, experts_out, load_sem, keep_sem)
    output = OutputSums(at, lanes, dwo_ref, dwo_y, dwo_z, dwo_land)
    sums = ColumnSum(at, lanes, yp_ref, y_land)
    experts.load()
    forward, near, far, _ = gather_heads(at, lanes, attn_ref, ag_ref)

    def load(src, dst, sem):
        copy = pltpu.make_async_copy(src, dst, load_sem.at[sem])
        copy.start()
        return copy

    def move(src, dst):
        load(src, dst, 5).wait()

    wo_load = load(wo_hbm.at[aligned(at.h * qcols, qcols), :], wo_ref, 2)
    y_load = load(y_in, yp_ref, 3)
    if not big:
        kv_load = load(kv_in, kv_ref, 4)
    experts.to_y()
    y_load.wait()
    for b in range(blocks):
        sums.first_send(b)

    def add(b, band):
        move(y_land.at[b, band, :], y_other.at[band, :])
        if big:
            move(yp_ref.at[b, band, :], y_stage.at[band, :])
            y_stage[band, :] = (y_stage[band, :].astype(F32) + y_other[band, :].astype(F32)).astype(BF16)
            move(y_stage.at[band, :], yp_ref.at[b, band, :])
        else:
            yp_ref[b, band, :] = (yp_ref[b, band, :].astype(F32) + y_other[band, :].astype(F32)).astype(BF16)

    def fetch(stage):
        def get(ref):
            if big:
                move(ref, stage)
                return stage
            return ref
        return get

    wo_load.wait()

    def mix_back(head):
        band = aligned(head * own_rows, own_rows)
        grad = mm(ag_ref[band, :], wo_ref[...], NT).astype(BF16)
        for hh in range(heads):
            do_ref[hh, band, :] = grad[:, hh * HEAD:(hh + 1) * HEAD]

    def turn(i):
        band = slice(i * own_rows, (i + 1) * own_rows)
        move(n1_hbm.at[band, :], y_other)
        n1t_ref[:, band] = y_other[...].astype(F32).T.astype(BF16)

    ag_ref[aligned(at.h * own_rows, own_rows), :] = attn_ref[...]
    mix_back(at.h)
    turn(0)
    near()
    mix_back(at.sib)
    for i in range(1, rows // own_rows):
        turn(i)
    experts.to_x(0)
    forward()
    mix_back(at.xn)
    far()
    mix_back(at.xs)
    step = 512

    def weight_back(i, _):
        cols = pl.ds(pl.multiple_of(i * step, step), step)
        dwo_ref[:, cols] = mm(ot_ref[...], ag_ref[:, cols]).astype(BF16)
        return 0

    lax.fori_loop(0, width // step, weight_back, 0)
    output.to_z()
    kv_from = pl.ds(pl.multiple_of(qcols + at.c * HEAD, HEAD), HEAD)
    w_loads = [load(w_hbm.at[:, :qcols], w_ref.at[:, :qcols], 2), load(w_hbm.at[:, kv_from], w_ref.at[:, qcols:], 3)]
    dq_ref[...] = jnp.zeros_like(dq_ref)
    for hh in range(heads):
        prod = do_ref[hh].astype(F32).T * ot_ref[hh * HEAD:(hh + 1) * HEAD, :].astype(F32)
        delta_ref[hh] = jnp.sum(prod, axis=0, keepdims=True)
    if not big:
        kv_load.wait()

    experts.to_x(1)
    beside = [[(experts.to_x, 2), (experts.share, 0)],
              [(experts.to_x, 3), (experts.share, 1)],
              [(experts.to_x, 4), (experts.share, 2)]]

    def advance():
        for f, k in (beside.pop(0) if beside else ()):
            f(k)

    def opening(b):
        if big:
            move(kv_in.at[b], kv_stage)
        kv = kv_stage if big else kv_ref.at[b]
        kt_ref[...] = kv[0].astype(F32).T.astype(BF16)
        dk_ref[...] = jnp.zeros_like(dk_ref)
        dv_ref[...] = jnp.zeros_like(dv_ref)
        return kv

    def closing(b, kv):
        kv[0] = (dk_ref[...] * LN2).astype(BF16)
        kv[1] = dv_ref[...].astype(BF16)
        if big:
            move(kv_stage, kv_ref.at[b])

    def block(b):
        kv = opening(b)

        def tile(t, _):
            hh, i = t // (rows // TILE), t % (rows // TILE)
            cols = pl.ds(pl.multiple_of(i * TILE, TILE), TILE)
            unattend_tile(hh, cols, kv[0], kv[1], kt_ref[...], q_ref, do_ref,
                          start_ref, lse_ref, delta_ref, dq_ref, dk_ref, dv_ref, b * rows, None)
            return 0

        lax.fori_loop(0, heads * (rows // TILE), tile, 0)
        closing(b, kv)

    pair, column = lanes.slots(blocks), lanes.slots(blocks)

    def to_sibling(b, when):
        lanes.put(pair + b, kv_ref.at[b, 1 - at.c], dkv_sib.at[b], when=when, head=at.sib)

    def to_column(b):
        lanes.arrived(pair + b, dkv_sib.at[b], when=b < me, head=at.sib)

        @pl.when(b < me)
        def _():
            came = fetch(dkv_stage)(dkv_sib.at[b])
            if big:
                move(kv_ref.at[b, at.c], kv_stage.at[at.c])
            kv = kv_stage if big else kv_ref.at[b]
            kv[at.c] = (kv[at.c].astype(F32) + came[...].astype(F32)).astype(BF16)
            if big:
                move(kv_stage.at[at.c], kv_ref.at[b, at.c])

        lanes.put(column + me, kv_ref.at[b, at.c], dkv_land.at[me], when=b < me, blk=b)

    for b in range(blocks - 1):
        pl.when(b < me)(functools.partial(block, b))
        to_sibling(b, b < me)
        sums.relay(0, b + 1, add)
        advance()
        if b > 0:
            to_column(b - 1)
    while beside:
        advance()
    to_column(blocks - 2)

    kv_own = opening(me)
    for i in range(rows // TILE):
        n = (i + 1) * TILE

        def diagonal(hh, _, i=i, n=n):
            unattend_tile(hh, slice(i * TILE, n), kv_own[0, :n, :], kv_own[1, :n, :], kt_ref[:, :n], q_ref, do_ref,
                          start_ref, lse_ref, delta_ref, dq_ref, dk_ref, dv_ref,
                          me * rows, me * rows + i * TILE)
            return 0

        lax.fori_loop(0, heads, diagonal, 0)
    closing(me, kv_own)
    to_sibling(me, None)
    experts.to_x(5)
    for d in range(1, blocks):
        sums.relay(1, d, add)

    def unrotate(u):
        return u * cos_ref[...] - pltpu.roll(u, HEAD // 2, 1) * sin_ref[...]

    for hh in range(heads):
        dpre_ref[:, hh * HEAD:(hh + 1) * HEAD] = unrotate((dq_ref[hh] * SCORE_SCALE).T).astype(BF16)
    for w_load in w_loads:
        w_load.wait()
    parts = 4
    part = half // parts
    band_rows = 256
    query_cols, keyval_cols = slice(0, qcols), slice(qcols, qcols + HEAD)

    def weight_half(y, cols_out):
        def body(i, _):
            band = aligned(y * half + i * band_rows, band_rows)
            dw_ref[band, cols_out] = mm(n1t_ref[band, :], dpre_ref[:, cols_out]).astype(BF16)
            return 0

        lax.fori_loop(0, half // band_rows, body, 0)

    def weight_part(y, p):
        return aligned(y * half + p * part, part)

    ys = (lanes.slots(parts), lanes.slots(parts))

    def weight_to_y(i, cols_out):
        weight_half(at.oy, cols_out)
        for p in range(parts):
            lanes.put(ys[i] + p, dw_ref.at[weight_part(at.oy, p), cols_out],
                      dw_y.at[pl.ds(p * part, part), cols_out], fsdp=at.oy)

    weight_to_y(0, query_cols)
    experts.to_x(6)

    @pl.when(at.c == 0)
    def _():
        dkv_ref[...] = dk_ref[...] * LN2

    @pl.when(at.c == 1)
    def _():
        dkv_ref[...] = dv_ref[...]

    lanes.arrived(pair + me, dkv_sib.at[me], head=at.sib)
    dkv_ref[...] += fetch(dkv_stage)(dkv_sib.at[me])[...].astype(F32)
    for z in range(1, blocks):
        @pl.when(me < z)
        def _(z=z):
            lanes.arrived(column + z, dkv_land.at[z], blk=z)
            dkv_ref[...] += fetch(dkv_stage)(dkv_land.at[z])[...].astype(F32)

    dpre_ref[:, qcols:] = jnp.where(at.c == 0, unrotate(dkv_ref[...]), dkv_ref[...]).astype(BF16)
    weight_to_y(1, keyval_cols)

    def input_part(head):
        return mm(dpre_ref[aligned(head * own_rows, own_rows), :], w_ref[...], NT)

    experts.y_sent()

    def dn_ref(i):
        return own_ref.at[at.oy, i * own_rows:(i + 1) * own_rows, :width]

    relay, direct, across = lanes.slots(), lanes.slots(), lanes.slots()
    dn_ref(0)[...] = input_part(at.xs).astype(BF16)
    lanes.put(relay, dn_ref(0), dn_sib.at[0], head=at.sib)
    dn_ref(2)[...] = input_part(at.sib).astype(BF16)
    lanes.put(direct, dn_ref(2), dn_sib.at[1], head=at.sib)
    lanes.arrived(relay, dn_sib.at[0], head=at.sib)
    dn_ref(1)[...] = (input_part(at.xn) + dn_sib[0].astype(F32)).astype(BF16)
    lanes.put(across, dn_ref(1), dn_x, head=at.xn)
    experts.to_x(7)
    experts.share(3)
    experts.share(4)
    weight_half(at.y, slice(None))
    output.to_y(fetch(dwo_stage))

    zr = lanes.slots(blocks)
    for p in range(parts):
        rows_p = weight_part(at.y, p)
        for i, cols_out in enumerate((query_cols, keyval_cols)):
            lanes.arrived(ys[i] + p, dw_y.at[pl.ds(p * part, part), cols_out], fsdp=at.oy)
        total = dw_ref[rows_p, :].astype(F32) + dw_y[pl.ds(p * part, part), :].astype(F32)
        dw_ref[rows_p, :] = total.astype(BF16)
        lanes.put(zr + at.z, dw_ref.at[rows_p, :], dw_z.at[at.z], when=at.z != p, blk=p)
    experts.share(5)
    output.share()

    move(res_hbm, acc_ref)
    if big:
        move(yp_ref.at[me], y_stage)
    acc_ref[...] += (y_stage if big else yp_ref.at[me])[...].astype(F32)

    def take(slot):
        move(y_land.at[slot], y_other)
        acc_ref[...] += y_other[...].astype(F32)

    for side in range(2):
        sums.arrive(side, take)
    block_out[...] = acc_ref[...].astype(BF16)

    res_load = load(res_grad_hbm, acc_ref, 5)
    own = input_part(at.h)
    lanes.arrived(direct, dn_sib.at[1], head=at.sib)
    own = own + dn_sib[1].astype(F32)
    lanes.arrived(across, dn_x, head=at.xn)
    own = own + dn_x[...].astype(F32)
    x = x_ref[...].astype(F32)
    inv = lax.rsqrt(jnp.mean(x * x, axis=-1, keepdims=True) + NORM_EPSILON)
    hat = x * inv
    pulled = own * gain_ref[gain_row:gain_row + 1, :].astype(F32)
    slope = inv * (pulled - hat * jnp.mean(pulled * hat, axis=-1, keepdims=True))
    res_load.wait()
    tokens_out[...] = (acc_ref[...] + slope).astype(BF16)
    sm_ref[...] = small_ref[...]
    sm_ref[gain_row:gain_row + 1, :] = jnp.sum(own * hat, axis=0, keepdims=True)
    sa, sb, sy, sz = lanes.slots(), lanes.slots(), lanes.slots(), lanes.slots(blocks)
    lanes.put(sa, sm_ref, sm_a, head=at.sib)
    experts.share(6)

    p = at.z % parts
    summer = at.z < parts
    zg, xg, cg, cf = lanes.slots(parts), lanes.slots(parts), lanes.slots(parts), lanes.slots(parts)

    def place(head, q):
        return land_ref.at[head, pl.ds(q * part, part), :]

    for z in at.others():
        lanes.arrived(zr + z, dw_z.at[z], when=summer, blk=z)
    mine_w = weight_part(at.y, p)

    @pl.when(summer)
    def _():
        total = dw_ref[mine_w, :].astype(F32)
        for z in at.others():
            total = total + dw_z[z].astype(F32)
        dw_ref[mine_w, :] = total.astype(BF16)
        land_ref[at.h, aligned(p * part, part), :] = total.astype(BF16)

    for z in at.others():
        lanes.put(zg + p, dw_ref.at[mine_w, :], place(at.h, p), when=summer, blk=z)
    lanes.put(xg + p, dw_ref.at[mine_w, :], place(at.h, p), when=summer, head=at.xn)
    lanes.put(cg + p, dw_ref.at[mine_w, :], place(at.h, p), when=summer, head=at.sib)
    lanes.arrived(sa, sm_a, head=at.sib)
    sm_a[...] = sm_a[...] + sm_ref[...]
    lanes.put(sb, sm_a, sm_b, head=at.xn)
    output.take_over()
    experts.share(7)

    lanes.arrived(sb, sm_b, head=at.xn)
    sm_b[...] = sm_a[...] + sm_b[...]
    mine_cols = pl.ds(pl.multiple_of(at.y * half, half), half)
    other_cols = pl.ds(pl.multiple_of(at.oy * half, half), half)
    lanes.put(sy, sm_b.at[:, other_cols], sm_y, fsdp=at.oy)
    for q in range(parts):
        later = at.z != q
        lanes.arrived(zg + q, place(at.h, q), when=later, blk=q)
        lanes.put(xg + q, place(at.h, q), place(at.h, q), when=later, head=at.xn)
        lanes.put(cg + q, place(at.h, q), place(at.h, q), when=later, head=at.sib)
    lanes.arrived(sy, sm_y, fsdp=at.oy)
    sm_z[at.z] = sm_b[:, mine_cols] + sm_y[...]
    for z in at.others():
        lanes.put(sz + at.z, sm_z.at[at.z], sm_z.at[at.z], blk=z)
    output.pass_on()
    for q in range(parts):
        lanes.arrived(xg + q, place(at.xn, q), head=at.xn)
        lanes.put(cf + q, place(at.xn, q), place(at.xn, q), head=at.sib)
    for z in at.others():
        lanes.arrived(sz + z, sm_z.at[z], blk=z)
    total = sm_z[0]
    for z in range(1, blocks):
        total = total + sm_z[z]
    small_out[...] = total
    output.finish()
    keeps = [load(dwo_land, output_out, 0)]
    for q in range(parts):
        lanes.arrived(cg + q, place(at.sib, q), head=at.sib)
        lanes.arrived(cf + q, place(at.xs, q), head=at.sib)
    for head in range(4):
        keeps.append(load(land_ref.at[head, :, :qcols], query_out.at[:, head * qcols:(head + 1) * qcols], 1 + head))
        column_of = (head % 2 * KEYVALUE_HEADS + head // 2) * HEAD
        keeps.append(load(land_ref.at[head, :, qcols:], kv_out.at[:, column_of:column_of + HEAD], 6 + head))
    experts.finish()
    for keep in keeps:
        keep.wait()
    sums.finish()
    lanes.drain()


def backward(attn_grad, q, ot, start, lse, x, cosine, sine, gain, small, kv, wo, grads, y_parts, res, res_grad, n1, w):
    heads, rows, _ = q.shape
    blocks = kv.shape[0]
    own_rows, width = attn_grad.shape
    qcols = heads * HEAD
    _, half, wide = grads.shape
    cols = qcols + HEAD
    srows = small.shape[0]
    n = ExpertSums.CHUNKS
    vm = pl.BlockSpec(memory_space=pltpu.VMEM)
    hbm = pl.BlockSpec(memory_space=pl.ANY)
    part = qcols // OutputSums.PARTS
    sds = jax.ShapeDtypeStruct
    column = [((blocks, own_rows, width), BF16), ((blocks, rows, HEAD), BF16),
              ((blocks, rows, HEAD), BF16), ((blocks, part, width), BF16), (kv.shape, BF16)]
    if blocks > 4:
        extra_out, extra_spec = tuple(sds(*c) for c in column), [hbm] * 5
        extra_scratch = [pltpu.VMEM((rows, HEAD), BF16), pltpu.VMEM((part, width), BF16),
                         pltpu.VMEM((own_rows, width), BF16), pltpu.VMEM((2, rows, HEAD), BF16)]
    else:
        extra_out, extra_spec = (), []
        extra_scratch = [pltpu.VMEM(*c) for c in column]
    return pl.pallas_call(
        back_kernel,
        out_shape=(
            sds((own_rows, width), BF16),
            sds((own_rows, width), BF16),
            sds((srows, half), F32),
            sds((half, 2 * KEYVALUE_HEADS * HEAD), BF16),
            sds((2, half, wide), BF16),
            sds((2 * qcols, width), BF16),
            sds((half, rows // own_rows * qcols), BF16),
            sds((blocks + 1, own_rows, width), BF16),
        ) + extra_out,
        in_specs=[vm] * 10 + [hbm] * 8,
        out_specs=[vm] * 3 + [hbm] * 5 + extra_spec,
        scratch_shapes=extra_scratch + [
            pltpu.VMEM((heads, HEAD, rows), F32),
            pltpu.VMEM((rows, HEAD), F32),
            pltpu.VMEM((rows, HEAD), F32),
            pltpu.VMEM((HEAD, rows), BF16),
            pltpu.VMEM((heads, 1, rows), F32),
            pltpu.VMEM((heads, rows, HEAD), BF16),
            pltpu.VMEM((rows, width), BF16),
            pltpu.VMEM((qcols, width), BF16),
            pltpu.VMEM((qcols, width), BF16),
            pltpu.VMEM((part, width), BF16),
            pltpu.VMEM((2 * qcols, width), BF16),
            pltpu.VMEM((2, half, wide), BF16),
            pltpu.VMEM((half, wide), BF16),
            pltpu.VMEM((half, wide), BF16),
            pltpu.VMEM((own_rows, width), F32),
            pltpu.VMEM((own_rows, width), BF16),
            pltpu.VMEM((width, cols), BF16),
            pltpu.VMEM((rows, cols), BF16),
            pltpu.VMEM((2, own_rows, width), BF16),
            pltpu.VMEM((own_rows, width), BF16),
            pltpu.VMEM((width, cols), BF16),
            pltpu.VMEM((half, cols), BF16),
            pltpu.VMEM((blocks, half // 4, cols), BF16),
            pltpu.VMEM((srows, width), F32),
            pltpu.VMEM((srows, width), F32),
            pltpu.VMEM((srows, width), F32),
            pltpu.VMEM((srows, half), F32),
            pltpu.VMEM((blocks, srows, half), F32),
            pltpu.VMEM((rows // own_rows, half, cols), BF16),
            pltpu.VMEM((rows, HEAD), F32),
            pltpu.VMEM((width, rows), BF16),
            pltpu.SemaphoreType.DMA((10,)),
            pltpu.SemaphoreType.DMA((n,)),
        ] + semaphores(blocks),
        compiler_params=pltpu.CompilerParams(
            vmem_limit_bytes=VMEM_BYTES, collective_id=2, has_side_effects=True),
    )(attn_grad, q, ot, start, lse, x, cosine, sine, gain, small, kv, wo, grads, y_parts, res, res_grad, n1, w)[:7]


def on_device(tokens, documents, routes, cotangent, first_gain, query_weight, keyvalue_weight, output_weight,
              second_gain, router_weight, expert_in, expert_out):
    z = lax.axis_index("blk")
    blocks = lax.axis_size("blk")
    rows, width = tokens.shape[1:]
    group = lax.axis_size("head") * rows
    experts = router_weight.shape[1]
    half = query_weight.shape[0]

    small_rows = -(-(2 + experts) // 16) * 16
    small = jnp.concatenate([router_weight.T, first_gain[None], second_gain[None],
                             jnp.zeros((small_rows - 2 - experts, half), BF16)], axis=0)
    pos = (z * group + jnp.arange(group, dtype=jnp.int32)).astype(F32)
    inverse = jnp.power(ROPE_BASE, -jnp.arange(HEAD // 2).astype(F32) * 2.0 / HEAD)
    angle = pos[:, None] * inverse[None, :]
    cos, sin = jnp.cos(angle), jnp.sin(angle)
    cosine = jnp.concatenate([cos, cos], axis=-1)
    sine = jnp.concatenate([-sin, sin], axis=-1)
    doc = documents[0]
    doc_q = lax.dynamic_slice_in_dim(doc, z * group, group, 0)
    start = sum(jnp.where(doc_q > d, jnp.sum((doc == d).astype(jnp.int32)), 0) for d in range(DOCUMENTS - 1))[None, :]
    chosen = jnp.any(routes[0][:, :, None] == jnp.arange(LANES, dtype=jnp.int32), axis=1).astype(F32)

    q, mixed, mixed_t, lse, n1, small, wqkv, kv_all, wo, w_experts, cots = front(
        blocks, tokens[0], small, query_weight, keyvalue_weight, output_weight, expert_in, expert_out,
        cotangent[0], cosine, sine, start)
    res1, res_grad, attn_grad, d_small, grads, y_parts = expert_layer(
        mixed, tokens[0], small, chosen, wo, w_experts, cots)
    block_out, tokens_grad, d_small, d_keyval, d_experts, d_wo, d_query = backward(
        attn_grad, q, mixed_t, start, lse, tokens[0], cosine, sine, small, d_small,
        kv_all, wo, grads, y_parts, res1, res_grad, n1, wqkv)
    return (block_out[None], tokens_grad[None], d_small[experts], d_query.astype(F32), d_keyval.astype(F32), d_wo.astype(F32),
            d_small[experts + 1], d_small[:experts].T, d_experts[:, :, :width].astype(F32),
            d_experts[:, :, width:].astype(F32))


def solution(mesh):
    token_spec = P("fsdp", ("blk", "head"), None)
    row_spec = P("fsdp", None)
    in_spec = P("blk", "fsdp", None)
    out_spec = P("blk", None, "fsdp")
    return jax.shard_map(
        on_device,
        mesh=mesh,
        in_specs=(token_spec, row_spec, token_spec, token_spec, P("fsdp"), row_spec, row_spec, row_spec, P("fsdp"),
                  row_spec, in_spec, out_spec),
        out_specs=(token_spec, token_spec, P("fsdp"), row_spec, row_spec, row_spec, P("fsdp"), row_spec, in_spec,
                   out_spec),
        check_vma=False,
    )
```

```python
import functools

import jax
import jax.numpy as jnp
from jax import lax
from jax.experimental import pallas as pl
from jax.experimental.pallas import tpu as pltpu
from jax.sharding import PartitionSpec as P

QUERY_HEADS = 12
KEYVALUE_HEADS = 2
HEAD = 128
NORM_EPSILON = 1e-06
ROPE_BASE = 1000000.0
MASKED = -1e30
DOCUMENTS = 4
LOG2E = 1.4426950408889634
SCORE_LOG2 = HEAD ** (-0.5) * LOG2E
SCORE_SCALE = HEAD ** (-0.5)
LN2 = 1.0 / LOG2E
TILE = 256
BF16 = jnp.bfloat16
F32 = jnp.float32
VMEM_BYTES = 63 * 1024 * 1024

NN = (((1,), (0,)), ((), ()))
NT = (((1,), (1,)), ((), ()))
TN = (((0,), (0,)), ((), ()))


def mm(a, b, dims=NN):
    return lax.dot_general(a, b, dims, preferred_element_type=F32)


def gelu_parts(gate):
    c = 0.7978845608028654
    cube = 0.044715 * gate * gate * gate
    t = jnp.tanh(c * (gate + cube))
    value = 0.5 * gate * (1.0 + t)
    slope = 0.5 * (1.0 + t) + 0.5 * gate * (1.0 - t * t) * c * (1.0 + 3.0 * 0.044715 * gate * gate)
    return value, slope


def score_tile(key_rows, q_tile, start_row, first_key, q_first):
    scores = mm(key_rows, q_tile, NT)
    key_row = lax.broadcasted_iota(jnp.int32, scores.shape, 0)
    allowed = key_row >= start_row - first_key
    if q_first is not None:
        allowed = allowed & (key_row - lax.broadcasted_iota(jnp.int32, scores.shape, 1) <= q_first - first_key)
    return jnp.where(allowed, scores, MASKED)


def attend_tile(hh, cols, key_rows, value_cols, q_ref, start_ref, m_ref, l_ref, acc_ref, first_key, q_first):
    q_tile = q_ref[hh, cols, :]
    scores = score_tile(key_rows, q_tile, start_ref[:, cols], first_key, q_first)
    old = m_ref[hh, :, cols]
    new = jnp.maximum(old, jnp.max(scores, axis=0, keepdims=True))
    factor = jnp.exp2(old - new)
    prob = jnp.exp2(scores - new)
    m_ref[hh, :, cols] = new
    l_ref[hh, :, cols] = l_ref[hh, :, cols] * factor + jnp.sum(prob, axis=0, keepdims=True)
    acc_ref[hh, :, cols] = acc_ref[hh, :, cols] * factor + mm(value_cols, prob.astype(BF16))


def unattend_tile(hh, cols, key_rows, value_rows, key_cols, q_ref, do_ref, start_ref, lse_ref, delta_ref,
                  dq_ref, dk_ref, dv_ref, first_key, q_first):
    n = key_rows.shape[0]
    q_tile = q_ref[hh, cols, :]
    do_tile = do_ref[hh, cols, :]
    scores = score_tile(key_rows, q_tile, start_ref[:, cols], first_key, q_first)
    prob = jnp.exp2(scores - lse_ref[hh, :, cols])
    dv_ref[:n, :] += mm(prob.astype(BF16), do_tile)
    prob_grad = mm(value_rows, do_tile, NT)
    score_grad = (prob * (prob_grad - delta_ref[hh, :, cols])).astype(BF16)
    dk_ref[:n, :] += mm(score_grad, q_tile)
    dq_ref[hh, :, cols] += mm(key_cols, score_grad)


def remote(src, dst, send_sem, recv_sem, **to):
    return pltpu.make_async_remote_copy(
        src_ref=src, dst_ref=dst, send_sem=send_sem, recv_sem=recv_sem, device_id=to,
        device_id_type=pl.DeviceIdType.MESH)


class Lanes:
    def __init__(self, send, recv):
        self.send, self.recv, self.used, self.sent, self.pending = send, recv, 0, 0, []

    def slots(self, count=1):
        first = self.used
        self.used += count
        assert self.used <= self.recv.shape[0]
        return first

    def sends(self, count):
        first = self.sent
        self.sent += count
        assert self.sent <= self.send.shape[0]
        return first

    def put(self, slot, src, dst, when=None, **to):
        assert self.sent < self.send.shape[0]
        copy = remote(src, dst, self.send.at[self.sent], self.recv.at[slot], **to)
        self.sent += 1
        if when is None:
            copy.start()
        else:
            pl.when(when)(copy.start)
        self.pending.append((copy, when))
        return self.pending[-1]

    def settle(self, entry):
        copy, when = entry
        self.pending = [other for other in self.pending if other is not entry]
        if when is None:
            copy.wait_send()
        else:
            pl.when(when)(copy.wait_send)

    def arrived(self, slot, dst, when=None, **origin):
        copy = remote(dst, dst, self.send.at[0], self.recv.at[slot], **origin)
        if when is None:
            copy.wait_recv()
        else:
            pl.when(when)(copy.wait_recv)

    def drain(self):
        for copy, when in self.pending:
            if when is None:
                copy.wait_send()
            else:
                pl.when(when)(copy.wait_send)
        self.pending = []


class Place:
    def __init__(self, blocks):
        self.z, self.h, self.y = lax.axis_index("blk"), lax.axis_index("head"), lax.axis_index("fsdp")
        self.blocks = blocks
        self.x, self.c = self.h // 2, self.h % 2
        self.sib = 2 * self.x + 1 - self.c
        self.xn = 2 * (1 - self.x) + self.c
        self.xs = 2 * (1 - self.x) + 1 - self.c
        self.oy = 1 - self.y

    def others(self):
        return [(self.z + d) % self.blocks for d in range(1, self.blocks)]

    def enter(self):
        barrier = pltpu.get_barrier_semaphore()

        def greet(**to):
            pl.semaphore_signal(barrier, inc=1, device_id=to, device_id_type=pl.DeviceIdType.MESH)

        for head in (self.sib, self.xn, self.xs):
            greet(head=head)
        greet(fsdp=self.oy)
        for z in self.others():
            greet(blk=z)
        pl.semaphore_wait(barrier, 4 + self.blocks - 1)


def gather_heads(at, lanes, own, land):
    s = lanes.slots(3)
    rows = own.shape[0]

    def slot(head):
        return land.at[pl.ds(pl.multiple_of(head * rows, rows), rows), :]

    lanes.put(s, own, slot(at.h), head=at.xn)
    lanes.put(s + 1, own, slot(at.h), head=at.sib)

    passed = []

    def forward():
        lanes.arrived(s, slot(at.xn), head=at.xn)
        passed.append(lanes.put(s + 2, slot(at.xn), slot(at.xn), head=at.sib))

    def near():
        lanes.arrived(s + 1, slot(at.sib), head=at.sib)

    def far():
        lanes.arrived(s + 2, slot(at.xs), head=at.sib)

    return forward, near, far, passed


def aligned(index, size):
    return pl.ds(pl.multiple_of(index, 16), size)


def semaphores(blocks):
    count = 128 + 16 * blocks
    return [pltpu.SemaphoreType.DMA((count,)), pltpu.SemaphoreType.DMA((count,))]


class Shared:
    def __init__(self, at, lanes, chunks, give, hold):
        self.at, self.lanes, self.chunks, self.give, self.hold = at, lanes, chunks, give, hold
        self.pieces = len(give(0)) if give else 0
        self.ys = lanes.slots(chunks * self.pieces)
        self.xn, self.sib, self.far = lanes.slots(chunks), lanes.slots(chunks), lanes.slots(chunks)
        self.sent = []

    def begin(self, k):
        for i, (src, dst) in enumerate(self.give(k)):
            self.lanes.put(self.ys + k * self.pieces + i, src, dst(self.at.y), fsdp=self.at.oy)

    def landed(self, k):
        for i, (src, dst) in enumerate(self.give(k)):
            self.lanes.arrived(self.ys + k * self.pieces + i, dst(self.at.oy), fsdp=self.at.oy)

    def spread(self, k):
        self.landed(k)
        self.scatter(k)

    def scatter(self, k):
        at = self.at
        place = self.hold(k, at.h, at.oy)
        self.sent.append(self.lanes.put(self.xn + k, place, place, head=at.xn))
        self.sent.append(self.lanes.put(self.sib + k, place, place, head=at.sib))

    def forward(self, k):
        at = self.at
        place = self.hold(k, at.xn, at.oy)
        self.lanes.arrived(self.xn + k, place, head=at.xn)
        self.sent.append(self.lanes.put(self.far + k, place, place, head=at.sib))

    def settle(self):
        for entry in self.sent:
            self.lanes.settle(entry)

    def finish(self, k):
        at = self.at
        self.lanes.arrived(self.sib + k, self.hold(k, at.sib, at.oy), head=at.sib)
        self.lanes.arrived(self.far + k, self.hold(k, at.xs, at.oy), head=at.sib)


def weight_chunk(w_ref, k, head, y):
    quarter = w_ref.shape[2] // 4
    piece = quarter // 2
    return w_ref.at[k // 2, y, aligned(head * quarter + k % 2 * piece, piece), :]


class Column:
    def __init__(self, at, lanes, land):
        self.at, self.lanes, self.land = at, lanes, land
        self.slot = lanes.slots(at.blocks)

    def begin(self, own):
        at = self.at
        place = self.land.at[at.z]
        self.lanes.put(self.slot + at.z, own, place, when=at.z < at.blocks - 1, blk=at.z + 1)
        self.lanes.put(self.slot + at.z, own, place, when=at.z > 0, blk=at.z - 1)

    def hand_on(self, d):
        at = self.at
        for b, origin, next_z in ((at.z - d, at.z - 1, at.z + 1), (at.z + d, at.z + 1, at.z - 1)):
            there = (b >= 0) & (b < at.blocks)
            safe = jnp.clip(b, 0, at.blocks - 1)
            self.lanes.arrived(self.slot + safe, self.land.at[safe], when=there, blk=origin)
            self.lanes.put(self.slot + safe, self.land.at[safe], self.land.at[safe],
                           when=there & (next_z >= 0) & (next_z < at.blocks), blk=next_z)


def front_kernel(x_ref, small_ref, wq_hbm, wkv_hbm, wo_hbm, win_hbm, wout_hbm, cot_hbm, cos_ref, sin_ref, start_ref,
                 q_ref, o_ref, ot_ref, lse_ref, n1_ref, small_out, wqkv_out, kv_out, wo_out, w_out, cot_out,
                 xg_ref, small_land, wqkv_ref, kv_ref, m_ref, l_ref, acc_ref, vt_ref, wo_ref, w_ref, cot_ref,
                 load_sem, send_sem, recv_sem):
    heads, rows, _ = q_ref.shape
    own_rows, width = x_ref.shape
    blocks = kv_ref.shape[0]
    half = wq_hbm.shape[0]
    qcols = heads * HEAD
    experts = 2 * blocks
    at = Place(blocks)
    me = at.z
    lanes = Lanes(send_sem, recv_sem)
    at.enter()
    local = []

    def copy_here(src, dst):
        copy = pltpu.make_async_copy(src, dst, load_sem.at[len(local)])
        copy.start()
        local.append(copy)
        return copy

    forward, near, far, _ = gather_heads(at, lanes, x_ref, xg_ref)
    g = at.x
    q_from = pl.ds(pl.multiple_of(at.h * qcols, HEAD), qcols)
    kv_from = pl.ds(pl.multiple_of((at.c * KEYVALUE_HEADS + g) * HEAD, HEAD), HEAD)

    def kv_cols(core):
        return pl.ds(pl.multiple_of(qcols + core * HEAD, HEAD), HEAD)

    columns = ((wq_hbm.at[:, q_from], slice(0, qcols)), (wkv_hbm.at[:, kv_from], kv_cols(at.c)))

    def weight_rows(y, cols):
        return wqkv_ref.at[aligned(y * half, half), cols]

    ws, wc = lanes.slots(2), lanes.slots()
    for i, (src, cols) in reversed(list(enumerate(columns))):
        lanes.put(ws + i, src, weight_rows(at.y, cols), fsdp=at.oy)
    smalls = lanes.slots()
    lanes.put(smalls, small_ref, small_land, fsdp=at.oy)
    kv_other = pl.ds(pl.multiple_of(((1 - at.c) * KEYVALUE_HEADS + g) * HEAD, HEAD), HEAD)
    own_weights = [copy_here(src, weight_rows(at.y, cols))
                   for src, cols in columns + ((wkv_hbm.at[:, kv_other], kv_cols(1 - at.c)),)]
    cots = Column(at, lanes, cot_ref)
    own_half = pl.ds(pl.multiple_of(at.y * half, half), half)
    cot_load = copy_here(cot_hbm, cot_ref.at[me])
    wo_load = copy_here(wo_hbm, wo_ref.at[own_half, :])
    w_loads = [copy_here(win_hbm, w_ref.at[:, at.y, :, :width]), copy_here(wout_hbm, w_ref.at[:, at.y, :, width:])]
    cot_load.wait()
    cots.begin(cot_ref.at[me])

    quarter = half // 4

    def wo_place(k, head, y):
        return wo_ref.at[aligned(y * half + head * quarter, quarter), :]

    shared_wo = Shared(at, lanes, 1,
                       lambda k: [(wo_place(0, at.h, at.y), lambda y: wo_place(0, at.h, y))],
                       wo_place)
    chunks, spread_here = 4, 2

    def w_place(k, head, y):
        return weight_chunk(w_ref, k, head, y)

    def w_give(k):
        return [(w_place(k, at.h, at.y), lambda y: w_place(k, at.h, y))]

    shared_w = Shared(at, lanes, chunks, w_give, w_place)

    small_out[:, :half] = jnp.zeros((small_ref.shape[0], half), BF16)
    lanes.arrived(smalls, small_land, fsdp=at.oy)
    for y in range(2):
        @pl.when(at.y == y)
        def _(y=y):
            small_out[:, y * half:(y + 1) * half] = small_ref[...]
            small_out[:, (1 - y) * half:(2 - y) * half] = small_land[...]

    def norm(head, block):
        x = block.astype(F32)
        inv = lax.rsqrt(jnp.mean(x * x, axis=-1, keepdims=True) + NORM_EPSILON)
        n1_ref[aligned(head * own_rows, own_rows), :] = (x * inv * small_out[experts:experts + 1, :].astype(F32)).astype(BF16)

    def gathered(head):
        return xg_ref[aligned(head * own_rows, own_rows), :]

    norm(at.h, x_ref[...])
    near()
    norm(at.sib, gathered(at.sib))
    forward()
    norm(at.xn, gathered(at.xn))
    far()
    norm(at.xs, gathered(at.xs))
    for copy in own_weights:
        copy.wait()
    for i, (_, cols) in reversed(list(enumerate(columns))):
        lanes.arrived(ws + i, weight_rows(at.oy, cols), fsdp=at.oy)
        if i == 1:
            lanes.put(wc, weight_rows(at.oy, cols), weight_rows(at.oy, cols), head=at.sib)
    lanes.arrived(wc, weight_rows(at.oy, kv_cols(1 - at.c)), head=at.sib)
    wo_load.wait()
    shared_wo.begin(0)
    for load in w_loads:
        load.wait()
    for k in range(chunks):
        shared_w.begin(k)
    cots.hand_on(1)

    def project(i, _):
        band = aligned(i * TILE, TILE)
        pre = mm(n1_ref[band, :], wqkv_ref[...])
        cosine, sine = cos_ref[band, :], sin_ref[band, :]

        def turned(u):
            return (u * cosine + pltpu.roll(u, HEAD // 2, 1) * sine).astype(BF16)

        for hh in range(heads):
            q_ref[hh, band, :] = turned(pre[:, hh * HEAD:(hh + 1) * HEAD] * SCORE_LOG2)
        kv_ref[me, 0, band, :] = turned(pre[:, qcols:qcols + HEAD])
        kv_ref[me, 1, band, :] = pre[:, qcols + HEAD:].astype(BF16)
        return 0

    lax.fori_loop(0, rows // TILE, project, 0)

    kvs, kvc = lanes.slots(blocks), lanes.slots(blocks)

    def kv_half(b, core):
        return kv_ref.at[b, core]

    lanes.put(kvs + me, kv_half(me, at.c), kv_half(me, at.c), when=me < blocks - 1, blk=me + 1)
    late = [copy_here(wqkv_ref, wqkv_out), copy_here(wo_ref.at[own_half, :], wo_out.at[own_half, :]),
            copy_here(w_ref.at[:, at.y], w_out.at[:, at.y])]

    m_ref[...] = jnp.full_like(m_ref, MASKED)
    l_ref[...] = jnp.zeros_like(l_ref)
    acc_ref[...] = jnp.zeros_like(acc_ref)

    def transpose_values(b):
        vt_ref[...] = kv_ref[b, 1].astype(F32).T.astype(BF16)

    transpose_values(me)
    for i in range(rows // TILE):
        n = (i + 1) * TILE

        def diagonal(hh, _, i=i, n=n):
            attend_tile(hh, slice(i * TILE, n), kv_ref[me, 0, :n, :], vt_ref[:, :n], q_ref, start_ref,
                        m_ref, l_ref, acc_ref, me * rows, me * rows + i * TILE)
            return 0

        lax.fori_loop(0, heads, diagonal, 0)

    def block(b):
        transpose_values(b)

        def tile(t, _):
            hh, i = t // (rows // TILE), t % (rows // TILE)
            cols = pl.ds(pl.multiple_of(i * TILE, TILE), TILE)
            attend_tile(hh, cols, kv_ref[b, 0], vt_ref[...], q_ref, start_ref,
                        m_ref, l_ref, acc_ref, b * rows, None)
            return 0

        lax.fori_loop(0, heads * (rows // TILE), tile, 0)

    ticks = [[functools.partial(cots.hand_on, 2), functools.partial(shared_wo.spread, 0),
              functools.partial(shared_w.spread, 0)],
             [functools.partial(shared_w.spread, 1), functools.partial(shared_wo.forward, 0)],
             [functools.partial(shared_w.forward, 0)],
             [functools.partial(shared_w.forward, 1)] + [functools.partial(cots.hand_on, d) for d in range(3, blocks)]]

    def tick():
        if ticks:
            for f in ticks.pop(0):
                f()

    for d in range(1, blocks):
        b = jnp.maximum(me - d, 0)
        there = me >= d
        lanes.arrived(kvs + b, kv_half(b, at.c), when=there, blk=me - 1)
        lanes.put(kvs + b, kv_half(b, at.c), kv_half(b, at.c), when=there & (me < blocks - 1), blk=me + 1)
        lanes.put(kvc + b, kv_half(b, at.c), kv_half(b, at.c), when=there, head=at.sib)
        lanes.arrived(kvc + b, kv_half(b, 1 - at.c), when=there, head=at.sib)
        pl.when(there)(functools.partial(block, b))
        if d < blocks - 1:
            tick()

    for hh in range(heads):
        total = l_ref[hh]
        done = acc_ref[hh] / total
        ot_ref[hh * HEAD:(hh + 1) * HEAD, :] = done.astype(BF16)
        o_ref[:, hh * HEAD:(hh + 1) * HEAD] = done.T.astype(BF16)
        lse_ref[hh] = m_ref[hh] + jnp.log2(total)
    kv_copies = [pltpu.make_async_copy(kv_ref.at[b], kv_out.at[b], load_sem.at[15]) for b in range(blocks)]
    for b, copy in enumerate(kv_copies):
        @pl.when(b <= me)
        def _(copy=copy):
            copy.start()
            copy.wait()
    while ticks:
        tick()
    shared_wo.finish(0)
    other_half = pl.ds(pl.multiple_of(at.oy * half, half), half)
    late.append(copy_here(wo_ref.at[other_half, :], wo_out.at[other_half, :]))
    late.append(copy_here(cot_ref, cot_out))
    for k in range(spread_here):
        shared_w.finish(k)
    for k in range(spread_here, chunks):
        shared_w.landed(k)
    late.append(copy_here(w_ref.at[:, at.oy], w_out.at[:, at.oy]))
    for copy in late:
        copy.wait()
    lanes.drain()


def front(blocks, x, small, wq, wkv, wo, win, wout, cot, cosine, sine, start):
    own_rows, width = x.shape
    rows = cosine.shape[0]
    half = wq.shape[0]
    heads = QUERY_HEADS * own_rows // rows
    qcols = heads * HEAD
    ffe = wout.shape[1]
    vm = pl.BlockSpec(memory_space=pltpu.VMEM)
    hbm = pl.BlockSpec(memory_space=pl.ANY)
    sds = jax.ShapeDtypeStruct
    return pl.pallas_call(
        front_kernel,
        out_shape=(
            sds((heads, rows, HEAD), BF16),
            sds((rows, qcols), BF16),
            sds((qcols, rows), BF16),
            sds((heads, 1, rows), F32),
            sds((rows, width), BF16),
            sds((small.shape[0], width), BF16),
            sds((width, qcols + 2 * HEAD), BF16),
            sds((blocks, 2, rows, HEAD), BF16),
            sds((width, width), BF16),
            sds((2, 2, half, width + half), BF16),
            sds((blocks, own_rows, width), BF16),
        ),
        in_specs=[vm, vm] + [hbm] * 6 + [vm] * 3,
        out_specs=[vm] * 6 + [hbm] * 5,
        scratch_shapes=[
            pltpu.VMEM((rows, width), BF16),
            pltpu.VMEM(small.shape, BF16),
            pltpu.VMEM((width, qcols + 2 * HEAD), BF16),
            pltpu.VMEM((blocks, 2, rows, HEAD), BF16),
            pltpu.VMEM((heads, 1, rows), F32),
            pltpu.VMEM((heads, 1, rows), F32),
            pltpu.VMEM((heads, HEAD, rows), F32),
            pltpu.VMEM((HEAD, rows), BF16),
            pltpu.VMEM((width, width), BF16),
            pltpu.VMEM((2, 2, half, width + half), BF16),
            pltpu.VMEM((blocks, own_rows, width), BF16),
            pltpu.SemaphoreType.DMA((16,)),
        ] + semaphores(blocks),
        compiler_params=pltpu.CompilerParams(
            vmem_limit_bytes=VMEM_BYTES, collective_id=0, has_side_effects=True),
    )(x, small, wq, wkv, wo, win, wout, cot, cosine, sine, start)


class ColumnSum:
    CHUNKS = 4

    def __init__(self, at, lanes, part, land):
        self.at, self.lanes, self.part, self.land = at, lanes, part, land
        self.rows = part.shape[1] // self.CHUNKS
        self.recv = lanes.slots((at.blocks + 1) * self.CHUNKS)
        self.sent = lanes.sends(at.blocks * self.CHUNKS)

    def copy(self, b, ch):
        at = self.at
        travel = jnp.where(b < at.z, -1, 1)
        there = at.z + travel
        slot = jnp.where((there == b) & (b > at.z), at.blocks, b)
        rows = pl.ds(ch * self.rows, self.rows)
        return remote(self.part.at[b, rows, :], self.land.at[slot, rows, :],
                      self.lanes.send.at[self.sent + b * self.CHUNKS + ch],
                      self.lanes.recv.at[self.recv + slot * self.CHUNKS + ch], blk=there)

    def landed(self, slot, ch, origin):
        rows = pl.ds(ch * self.rows, self.rows)
        place = self.land.at[slot, rows, :]
        remote(place, place, self.lanes.send.at[0], self.lanes.recv.at[self.recv + slot * self.CHUNKS + ch],
               blk=origin).wait_recv()

    def first_send(self, b):
        at = self.at

        @pl.when(((b < at.z) & (at.z == at.blocks - 1)) | ((b > at.z) & (at.z == 0)))
        def _():
            for ch in range(self.CHUNKS):
                self.copy(b, ch).start()

    def relay(self, phase, d, add):
        at = self.at
        s = jnp.where(at.z * 2 >= at.blocks, -1, 1) * (1 - 2 * phase)
        b, origin = at.z + s * d, at.z - s
        safe = jnp.clip(b, 0, at.blocks - 1)

        @pl.when((b >= 0) & (b < at.blocks) & (origin >= 0) & (origin < at.blocks))
        def _():
            for ch in range(self.CHUNKS):
                self.landed(safe, ch, origin)
                add(safe, pl.ds(ch * self.rows, self.rows))
                self.copy(safe, ch).start()

    def arrive(self, side, use):
        at = self.at
        slot, origin = (at.z, at.z + 1) if side == 0 else (at.blocks, at.z - 1)

        @pl.when((origin >= 0) & (origin < at.blocks))
        def _():
            for ch in range(self.CHUNKS):
                self.landed(slot, ch, origin)
            use(slot)

    def finish(self):
        at = self.at
        for b in range(at.blocks):
            @pl.when(b != at.z)
            def _(b=b):
                for ch in range(self.CHUNKS):
                    self.copy(b, ch).wait_send()


LANES = 128
HALF_LANES = LANES // 2


def split_lanes(value):
    high = value.astype(BF16).astype(F32)
    return (high + pltpu.roll(value - high, HALF_LANES, 1)).astype(BF16)


def expert_kernel(o_ref, x_ref, small_ref, chosen_ref, wo_hbm, w_hbm, cot_hbm,
                  res_out, grad_out, attn_out, small_out, sums_out, y_out, core_land, *rest):
    big = cot_hbm.shape[0] > 4
    if big:
        xb_ref, dx_ref, land_ref, *rest = rest
        (xb_stage, dx_stage, land_stage, g_ref, *rest) = rest
    else:
        xb_ref, dx_ref, land_ref, *rest = rest
    (mix_ref, w_ref, cot_ref, acc_ref, gate_ref, dgu_ref, ga_ref, xt_ref, gat_ref, gg_ref, y_ref, stage_ref,
     gates_ref, router_ref, load_sem, y_sem, send_sem, recv_sem) = rest
    own_rows, width = x_ref.shape
    blocks = cot_hbm.shape[0]
    qcols = o_ref.shape[1]
    half = width // 2
    experts, _, ffe, _ = w_ref.shape
    at = Place(blocks)
    me = at.z
    lanes = Lanes(send_sem, recv_sem)
    at.enter()
    every = blocks * own_rows
    if big:
        wo_rows = [(slice(y * half, (y + 1) * half), g_ref.at[0, y, :, :width]) for y in range(2)]
    else:
        wo_rows = [(slice(0, every), dgu_ref.at[0]), (slice(every, width), dgu_ref.at[1, :width - every])]
    wo_load = [pltpu.make_async_copy(wo_hbm.at[rows, :], place, load_sem.at[y])
               for y, (rows, place) in enumerate(wo_rows)]
    for load in wo_load:
        load.start()
    quarter = half // 4
    here = aligned(at.h * quarter, quarter)
    w_loads = [pltpu.make_async_copy(w_hbm.at[place], w_ref.at[place], load_sem.at[4 + i])
               for i, place in enumerate(((0,), (1, at.y), (1, at.oy, here)))]
    for load in w_loads:
        load.start()
    late = Shared(at, lanes, 4, None, functools.partial(weight_chunk, w_ref))
    if not big:
        cot_loads = [pltpu.make_async_copy(cot_hbm.at[b], cot_ref.at[b * own_rows:(b + 1) * own_rows, :],
                                           load_sem.at[7 + b]) for b in range(blocks)]
        for load in cot_loads:
            load.start()

    total_experts = experts * blocks
    srows = small_ref.shape[0]
    is_router = lax.broadcasted_iota(jnp.int32, (srows, width), 0) < total_experts
    router_ref[...] = jnp.zeros_like(router_ref)
    router_ref[:srows, :] = jnp.where(is_router, small_ref[...].astype(F32), 0.0).astype(BF16)
    gain_two = small_ref[total_experts + 1:total_experts + 2, :].astype(F32)

    mixes = lanes.slots(4)

    def mix_cols(head):
        return mix_ref.at[:, pl.ds(pl.multiple_of(head * qcols, HEAD), qcols)]

    for head in (at.xn, at.xs, at.sib):
        lanes.put(mixes + at.h, o_ref.at[aligned(head * own_rows, own_rows), :], mix_cols(at.h), head=head)
    mix_ref[:, pl.ds(pl.multiple_of(at.h * qcols, HEAD), qcols)] = o_ref[aligned(at.h * own_rows, own_rows), :]
    for head in (at.sib, at.xn, at.xs):
        lanes.arrived(mixes + head, mix_cols(head), head=head)
    for load in w_loads:
        load.wait()
    for k in (2, 3):
        late.scatter(k)
    for load in wo_load:
        load.wait()
    step = 512
    for i in range(width // step):
        cols = slice(i * step, (i + 1) * step)
        res_out[:, cols] = x_ref[:, cols].astype(F32) + sum(
            mm(mix_ref[:, rows], place[:, cols]) for rows, place in wo_rows)

    def inverse_two():
        res = res_out[...]
        return lax.rsqrt(jnp.mean(res * res, axis=-1, keepdims=True) + NORM_EPSILON)

    n2 = (res_out[...] * inverse_two() * gain_two).astype(BF16)
    chosen = chosen_ref[...] > 0.0
    logits = jnp.where(chosen, mm(n2, router_ref[...], NT), MASKED)
    e_top = jnp.where(chosen, jnp.exp(logits - jnp.max(logits, axis=-1, keepdims=True)), 0.0)
    gates = e_top / jnp.sum(e_top, axis=-1, keepdims=True)
    gates_ref[...] = gates
    own_x = xb_stage if big else xb_ref.at[me]
    own_x[:, :width] = n2
    own_x[:, width:] = split_lanes(gates)

    def move(src, dst):
        copy = pltpu.make_async_copy(src, dst, load_sem.at[3])
        copy.start()
        copy.wait()

    if big:
        move(xb_stage, xb_ref.at[me])
    xs_slot, xs_sent = lanes.slots(blocks), lanes.sends(blocks + 2)

    def xs_copy(b, to, send):
        return remote(xb_ref.at[b], xb_ref.at[b], send_sem.at[xs_sent + send], recv_sem.at[xs_slot + b], blk=to)

    pl.when(me > 0)(lambda: xs_copy(me, me - 1, blocks).start())
    pl.when(me < blocks - 1)(lambda: xs_copy(me, me + 1, blocks + 1).start())

    if big:
        def clear(i, _):
            for e in range(experts):
                for y in range(2):
                    g_ref[e, y, aligned(i * 64, 64), :] = jnp.zeros((64, g_ref.shape[3]), BF16)
            return 0

        lax.fori_loop(0, half // 64, clear, 0)
    else:
        for load in cot_loads:
            load.wait()
    def second_expert():
        for k in (2, 3):
            late.forward(k)
        for k in (2, 3):
            late.finish(k)

    back = ColumnSum(at, lanes, dx_ref, land_ref)
    lane = lax.broadcasted_iota(jnp.int32, (own_rows, LANES), 1)
    tile = 256

    def y_copy(b):
        return pltpu.make_async_copy(y_ref, y_out.at[b], y_sem)

    def block(b, first, between=None):
        if big:
            move(xb_ref.at[b], xb_stage)
            move(cot_hbm.at[b], cot_ref)
        x_in = xb_stage if big else xb_ref.at[b]
        band_all = slice(None) if big else aligned(b * own_rows, own_rows)
        lanes_all = pl.ds(pl.multiple_of(b * own_rows, own_rows), own_rows)
        acc_ref[...] = jnp.zeros_like(acc_ref)
        gg_ref[...] = jnp.zeros_like(gg_ref)

        def hidden(e, _):
            index = me * experts + e
            pack = x_in[:, width:].astype(F32)
            mine = (lane == index) | (lane == index + HALF_LANES)
            gate_ref[...] = jnp.sum(jnp.where(mine, pack, 0.0), axis=1, keepdims=True)

            def inner(t, total):
                low = pl.ds(pl.multiple_of(t * tile, tile), tile)
                high = pl.ds(pl.multiple_of(ffe + t * tile, tile), tile)
                out_cols = slice(width, width + half)
                gate_pre = mm(x_in[:, :half], w_ref[e, 0, :, low]) + mm(x_in[:, half:width], w_ref[e, 1, :, low])
                up = mm(x_in[:, :half], w_ref[e, 0, :, high]) + mm(x_in[:, half:width], w_ref[e, 1, :, high])
                back_h = (mm(cot_ref[band_all, :half], w_ref[e, 0, low, out_cols], NT)
                          + mm(cot_ref[band_all, half:], w_ref[e, 1, low, out_cols], NT))
                value, slope = gelu_parts(gate_pre)
                act = (value * up).astype(BF16).astype(F32)
                gate = gate_ref[...]
                ga_ref[e, :, low] = (gate * act).astype(BF16)
                if not big:
                    gat_ref[e, low, lanes_all] = (gate * act).T.astype(BF16)
                d_act = gate * back_h
                dgu_ref[e, band_all, low] = (d_act * up * slope).astype(BF16)
                dgu_ref[e, band_all, high] = (d_act * value).astype(BF16)
                return total + jnp.sum(act * back_h, axis=1, keepdims=True)

            total = lax.fori_loop(0, ffe // tile, inner, jnp.zeros((own_rows, 1), F32))
            gg_ref[...] += jnp.where(lane == index, total, 0.0)
            for y in range(2):
                acc_ref[:, y * half:(y + 1) * half] += mm(dgu_ref[e, band_all, :], w_ref[e, y, :, :width], NT)
            return 0

        if between is None:
            lax.fori_loop(0, experts, hidden, 0)
        else:
            hidden(0, 0)
            between()
            for e in range(1, experts):
                hidden(e, 0)
        part = dx_stage if big else dx_ref.at[b]
        part[:, :width] = acc_ref[...].astype(BF16)
        part[:, width:] = split_lanes(gg_ref[...])
        if big:
            move(dx_stage, dx_ref.at[b])
        back.first_send(b)

        if big:
            xt_ref[...] = x_in[:, :width].astype(F32).T.astype(BF16)

            def weights(e, _):
                gat_ref[0] = ga_ref[e].astype(F32).T.astype(BF16)

                def rows(i, _):
                    band = aligned(i * tile, tile)
                    for y in range(2):
                        x_cols = xt_ref[aligned(y * half + i * tile, tile), :]
                        for n in range(width // step):
                            cols = slice(n * step, (n + 1) * step)
                            total = g_ref[e, y, band, cols].astype(F32) + mm(x_cols, dgu_ref[e, :, cols])
                            g_ref[e, y, band, cols] = total.astype(BF16)
                        out_cols = slice(width, width + half)
                        total = (g_ref[e, y, band, out_cols].astype(F32)
                                 + mm(gat_ref[0, band, :], cot_ref[:, y * half:(y + 1) * half]))
                        g_ref[e, y, band, out_cols] = total.astype(BF16)
                    return 0

                return lax.fori_loop(0, half // tile, rows, 0)

            lax.fori_loop(0, experts, weights, 0)
        else:
            xt_ref[:, lanes_all] = x_in[:, :width].astype(F32).T.astype(BF16)

        if not first:
            y_copy(b).wait()
        for y in range(2):
            total = mm(ga_ref[0], w_ref[0, y, :, width:])
            for e in range(1, experts):
                total = total + mm(ga_ref[e], w_ref[e, y, :, width:])
            y_ref[:, y * half:(y + 1) * half] = total.astype(BF16)
        y_copy(b).start()

    def distance(d, _):
        for b, origin, to in ((me - d, me - 1, me + 1), (me + d, me + 1, me - 1)):
            @pl.when((b >= 0) & (b < blocks))
            def _(b=b, origin=origin, to=to):
                xs_copy(b, origin, 0).wait_recv()
                pl.when((to >= 0) & (to < blocks))(lambda: xs_copy(b, to, b).start())

        def side(s, _):
            b = jnp.where(s == 0, me - d, me + d)

            @pl.when((b >= 0) & (b < blocks))
            def _():
                block(jnp.clip(b, 0, blocks - 1), False)

            return 0

        return lax.fori_loop(0, 2, side, 0)

    block(me, True, second_expert)
    lax.fori_loop(1, blocks, distance, 0)
    y_copy(me).wait()

    def add(b, rows):
        if big:
            move(dx_ref.at[b, rows, :], dx_stage.at[rows, :])
            move(land_ref.at[b, rows, :], land_stage.at[rows, :])
            dx_stage[rows, :] = (dx_stage[rows, :].astype(F32) + land_stage[rows, :].astype(F32)).astype(BF16)
            move(dx_stage.at[rows, :], dx_ref.at[b, rows, :])
        else:
            dx_ref[b, rows, :] = (dx_ref[b, rows, :].astype(F32) + land_ref[b, rows, :].astype(F32)).astype(BF16)

    late.settle()
    total_ref = g_ref if big else w_ref

    def weights_of(e):
        def rows(i, _):
            cols = pl.ds(pl.multiple_of(i * tile, tile), tile)
            for y in range(2):
                total = mm(xt_ref[y * half:(y + 1) * half, :], dgu_ref[e, :, cols])
                total_ref[e, y, :, cols] = total.astype(BF16)
            return 0

        def outs(i, _):
            for y in range(2):
                cols = pl.ds(pl.multiple_of(y * half + i * tile, tile), tile)
                place = pl.ds(pl.multiple_of(width + i * tile, tile), tile)
                total_ref[e, y, :, place] = mm(gat_ref[e], cot_ref[:, cols]).astype(BF16)
            return 0

        lax.fori_loop(0, 2 * ffe // tile, rows, 0)
        lax.fori_loop(0, half // tile, outs, 0)

    chunks = 4
    piece = half // chunks
    cores = lanes.slots(chunks)
    back.relay(0, 1, add)
    if not big:
        weights_of(1 - at.c)
    for k in range(chunks):
        band = pl.ds(k * piece, piece)
        lanes.put(cores + k, total_ref.at[1 - at.c, :, band, :], core_land.at[:, band, :], head=at.sib)

    def core_sum(k):
        band = pl.ds(k * piece, piece)
        lanes.arrived(cores + k, core_land.at[:, band, :], head=at.sib)
        move(core_land.at[:, band, :], stage_ref)
        for y in range(2):
            total = total_ref[at.c, y, band, :].astype(F32) + stage_ref[y].astype(F32)
            total_ref[at.c, y, band, :] = total.astype(BF16)

    for d in range(2, blocks):
        back.relay(0, d, add)
    if not big:
        weights_of(at.c)
    for d in range(1, blocks):
        back.relay(1, d, add)
    for k in range(chunks):
        core_sum(k)
    keep = pltpu.make_async_copy(total_ref.at[at.c], sums_out, load_sem.at[0])
    keep.start()

    if big:
        move(dx_ref.at[me], dx_stage)
    own_part = dx_stage if big else dx_ref.at[me]
    acc_ref[...] = own_part[:, :width].astype(F32)
    gg_ref[...] = own_part[:, width:].astype(F32)

    def take(slot):
        if big:
            move(land_ref.at[slot], land_stage)
        came = land_stage if big else land_ref.at[slot]
        acc_ref[...] += came[:, :width].astype(F32)
        gg_ref[...] += came[:, width:].astype(F32)

    for side in range(2):
        back.arrive(side, take)
    both = gg_ref[...]
    gate_grads = jnp.where(lane < HALF_LANES, both + pltpu.roll(both, HALF_LANES, 1), 0.0)
    gates = gates_ref[...]
    d_logits = (gates * (gate_grads - jnp.sum(gates * gate_grads, axis=-1, keepdims=True))).astype(BF16)
    inv = inverse_two()
    hat = res_out[...] * inv
    n2 = (hat * gain_two).astype(BF16)
    small_out[...] = mm(d_logits.astype(F32).T.astype(BF16), n2)[:small_out.shape[0], :]
    d_n2 = acc_ref[...] + mm(d_logits, router_ref[...])
    small_out[total_experts + 1:total_experts + 2, :] = jnp.sum(d_n2 * hat, axis=0, keepdims=True)
    pulled = d_n2 * gain_two
    if big:
        move(cot_hbm.at[me], cot_ref)
    own_cot = cot_ref[...] if big else cot_ref[aligned(me * own_rows, own_rows), :]
    grad = own_cot.astype(F32) + inv * (pulled - hat * jnp.mean(pulled * hat, axis=-1, keepdims=True))
    grad_out[...] = grad
    attn_out[...] = grad.astype(BF16)
    keep.wait()
    for b in range(blocks):
        up, down = (b < me) & (me < blocks - 1), (b > me) & (me > 0)
        pl.when(up)(lambda b=b: xs_copy(b, me + 1, b).wait_send())
        pl.when(down)(lambda b=b: xs_copy(b, me - 1, b).wait_send())
    pl.when(me > 0)(lambda: xs_copy(me, me - 1, blocks).wait_send())
    pl.when(me < blocks - 1)(lambda: xs_copy(me, me + 1, blocks + 1).wait_send())
    back.finish()
    lanes.drain()


def expert_layer(o, x, small, chosen, wo, w, cot):
    own_rows, width = x.shape
    blocks = cot.shape[0]
    experts, _, half, wide = w.shape
    ffe = half
    pack = width + LANES
    big = blocks > 4
    kept = own_rows if big else blocks * own_rows
    vm = pl.BlockSpec(memory_space=pltpu.VMEM)
    hbm = pl.BlockSpec(memory_space=pl.ANY)
    sds = jax.ShapeDtypeStruct
    column = [((blocks, own_rows, pack), BF16), ((blocks, own_rows, pack), BF16), ((blocks + 1, own_rows, pack), BF16)]
    if big:
        extra_out, extra_spec = tuple(sds(*c) for c in column), [hbm] * 3
        extra_scratch = [pltpu.VMEM((own_rows, pack), BF16)] * 3 + [pltpu.VMEM(w.shape, BF16)]
    else:
        extra_out, extra_spec = (), []
        extra_scratch = [pltpu.VMEM(*c) for c in column]
    outs = pl.pallas_call(
        expert_kernel,
        out_shape=(
            sds((own_rows, width), F32),
            sds((own_rows, width), F32),
            sds((own_rows, width), BF16),
            sds((-(-(experts * blocks + 2) // 8) * 8, width), F32),
            sds((2, half, wide), BF16),
            sds((blocks, own_rows, width), BF16),
            sds((2, half, wide), BF16),
        ) + extra_out,
        in_specs=[vm] * 4 + [hbm] * 3,
        out_specs=[vm] * 4 + [hbm] * 3 + extra_spec,
        scratch_shapes=extra_scratch + [
            pltpu.VMEM((own_rows, width), BF16),
            pltpu.VMEM(w.shape, BF16),
            pltpu.VMEM((kept, width), BF16),
            pltpu.VMEM((own_rows, width), F32),
            pltpu.VMEM((own_rows, 1), F32),
            pltpu.VMEM((experts, kept, 2 * ffe), BF16),
            pltpu.VMEM((experts, own_rows, ffe), BF16),
            pltpu.VMEM((width, kept), BF16),
            pltpu.VMEM((experts, ffe, kept), BF16),
            pltpu.VMEM((own_rows, LANES), F32),
            pltpu.VMEM((own_rows, width), BF16),
            pltpu.VMEM((2, half // 4, wide), BF16),
            pltpu.VMEM((own_rows, LANES), F32),
            pltpu.VMEM((LANES, width), BF16),
            pltpu.SemaphoreType.DMA((7 + blocks,)),
            pltpu.SemaphoreType.DMA,
        ] + semaphores(blocks),
        compiler_params=pltpu.CompilerParams(
            vmem_limit_bytes=VMEM_BYTES, collective_id=1, has_side_effects=True),
    )(o, x, small, chosen, wo, w, cot)
    return outs[:6]


class ExpertSums:
    CHUNKS = 8

    def __init__(self, at, lanes, grads, own, land_y, land_x, out, load_sem, keep_sem):
        self.at, self.lanes = at, lanes
        self.grads, self.own, self.out = grads, own, out
        self.land_y, self.land_x = land_y, land_x
        self.load_sem, self.keep_sem = load_sem, keep_sem
        self.rows = grads.shape[1] // self.CHUNKS
        n = self.CHUNKS
        self.ys, self.xr, self.cg = [lanes.slots(n) for _ in range(3)]
        self.kept = []

    def chunk(self, k):
        return pl.ds(k * self.rows, self.rows)

    def load(self):
        self.loads = [pltpu.make_async_copy(self.grads.at[y], self.own.at[y], self.load_sem.at[i])
                      for i, y in enumerate((self.at.oy, self.at.y))]
        for copy in self.loads:
            copy.start()

    def to_y(self, first, last):
        if first == 0:
            self.loads[0].wait()
        for k in range(first, last):
            rows = self.chunk(k)
            self.lanes.put(self.ys + k, self.own.at[self.at.oy, rows, :], self.land_y.at[rows, :], fsdp=self.at.oy)

    def to_x(self, k):
        at, rows = self.at, self.chunk(k)
        if k == 0:
            self.loads[1].wait()
        self.lanes.arrived(self.ys + k, self.land_y.at[rows, :], fsdp=at.oy)
        total = self.own[at.y, rows, :].astype(F32) + self.land_y[rows, :].astype(F32)
        self.own[at.y, rows, :] = total.astype(BF16)
        self.lanes.put(self.xr + k, self.own.at[at.y, rows, :], self.land_x.at[rows, :], head=at.xn)

    def share(self, k):
        at, rows = self.at, self.chunk(k)
        self.lanes.arrived(self.xr + k, self.land_x.at[rows, :], head=at.xn)
        total = self.own[at.y, rows, :].astype(F32) + self.land_x[rows, :].astype(F32)
        self.land_x[rows, :] = total.astype(BF16)
        done, place = self.land_x.at[rows, :], self.out.at[at.c, rows, :]
        self.lanes.put(self.cg + k, done, place, head=at.sib)
        keep = pltpu.make_async_copy(done, place, self.keep_sem.at[k])
        keep.start()
        self.kept.append(keep)

    def finish(self):
        at = self.at
        for k in range(self.CHUNKS):
            self.lanes.arrived(self.cg + k, self.out.at[1 - at.c, self.chunk(k), :], head=at.sib)
            self.kept[k].wait()


class OutputSums:
    PARTS = 4

    def __init__(self, at, lanes, grad, land_y, land_z, out):
        self.at, self.lanes, self.grad = at, lanes, grad
        self.land_y, self.land_z, self.out = land_y, land_z, out
        self.rows = grad.shape[0] // self.PARTS
        self.ys = lanes.slots()
        self.zr, self.zg = lanes.slots(at.blocks), lanes.slots(self.PARTS)
        self.xg, self.cg = lanes.slots(), lanes.slots(self.PARTS)
        self.owner, self.giver = at.y == at.x, at.y != at.x
        self.summer = at.z < self.PARTS
        self.part = at.z % self.PARTS
        self.mine = aligned(self.part * self.rows, self.rows)

    def to_z(self):
        at = self.at
        for p in range(self.PARTS):
            self.lanes.put(self.zr + at.z, self.grad.at[pl.ds(p * self.rows, self.rows), :], self.land_z.at[at.z],
                           when=at.z != p, blk=p)

    def to_y(self, fetch):
        at = self.at
        for z in at.others():
            self.lanes.arrived(self.zr + z, self.land_z.at[z], when=self.summer, blk=z)

        @pl.when(self.summer)
        def _():
            total = self.grad[self.mine, :].astype(F32)
            for z in at.others():
                total = total + fetch(self.land_z.at[z])[...].astype(F32)
            self.grad[self.mine, :] = total.astype(BF16)

        self.lanes.put(self.ys, self.grad.at[self.mine, :], self.land_y, when=self.summer & self.giver, fsdp=at.oy)

    def place(self, core, p):
        return self.out.at[aligned(core * self.PARTS * self.rows + p * self.rows, self.rows), :]

    def share(self):
        at, p = self.at, self.part
        ready = self.summer & self.owner
        self.lanes.arrived(self.ys, self.land_y, when=ready, fsdp=at.oy)
        at_rows = aligned(at.c * self.PARTS * self.rows + p * self.rows, self.rows)

        @pl.when(ready)
        def _():
            total = self.grad[self.mine, :].astype(F32) + self.land_y[...].astype(F32)
            self.out[at_rows, :] = total.astype(BF16)

        place = self.place(at.c, p)
        self.lanes.put(self.xg, place, place, when=ready, head=at.xn)
        self.spread(ready)

    def spread(self, ready):
        at, place = self.at, self.place(self.at.c, self.part)
        for z in at.others():
            self.lanes.put(self.zg + self.part, place, place, when=ready, blk=z)
        self.lanes.put(self.cg + self.part, place, place, when=ready, head=at.sib)

    def take_over(self):
        ready = self.summer & self.giver
        self.lanes.arrived(self.xg, self.place(self.at.c, self.part), when=ready, head=self.at.xn)
        self.spread(ready)

    def pass_on(self):
        at = self.at
        for p in range(self.PARTS):
            place, later = self.place(at.c, p), at.z != p
            self.lanes.arrived(self.zg + p, place, when=later, blk=p)
            self.lanes.put(self.cg + p, place, place, when=later, head=at.sib)

    def finish(self):
        at = self.at
        for p in range(self.PARTS):
            self.lanes.arrived(self.cg + p, self.place(1 - at.c, p), head=at.sib)


def back_kernel(attn_ref, q_ref, ot_ref, start_ref, lse_ref, x_ref, cos_ref, sin_ref, gain_ref, small_ref,
                kv_in, wo_hbm, grads_hbm, y_in, res_hbm, res_grad_hbm, n1_hbm, w_hbm,
                block_out, tokens_out, small_out, kv_out, experts_out, output_out, query_out, y_land, *rest):
    blocks = kv_in.shape[0]
    big = blocks > 4
    dkv_stage = dwo_stage = None
    if big:
        yp_ref, dkv_land, dkv_sib, dwo_z, kv_ref, dkv_stage, dwo_stage, y_stage, kv_stage, *rest = rest
    else:
        yp_ref, dkv_land, dkv_sib, dwo_z, kv_ref, *rest = rest
    (dq_ref, dk_ref, dv_ref, kt_ref, delta_ref, do_ref, ag_ref, wo_ref, dwo_ref, dwo_y, dwo_land,
     own_ref, ey_ref, ex_ref, acc_ref, y_other, w_ref, dpre_ref, dn_sib, dn_x, dw_ref, dw_y, dw_z,
     sm_ref, sm_a, sm_b, sm_y, sm_z, land_ref, dkv_ref, n1t_ref, load_sem, keep_sem, send_sem, recv_sem) = rest
    heads, rows, _ = q_ref.shape
    own_rows, width = attn_ref.shape
    half = width // 2
    qcols = heads * HEAD
    gain_row = 2 * blocks
    at = Place(blocks)
    me = at.z
    lanes = Lanes(send_sem, recv_sem)
    at.enter()
    experts = ExpertSums(at, lanes, grads_hbm, own_ref, ey_ref, ex_ref, experts_out, load_sem, keep_sem)
    output = OutputSums(at, lanes, dwo_ref, dwo_y, dwo_z, dwo_land)
    sums = ColumnSum(at, lanes, yp_ref, y_land)
    experts.load()
    forward, near, far, passed = gather_heads(at, lanes, attn_ref, ag_ref)

    def load(src, dst, sem):
        copy = pltpu.make_async_copy(src, dst, load_sem.at[sem])
        copy.start()
        return copy

    def move(src, dst):
        load(src, dst, 5).wait()

    wo_load = load(wo_hbm.at[aligned(at.h * qcols, qcols), :], wo_ref, 2)
    y_load = load(y_in, yp_ref, 3)
    if not big:
        kv_load = load(kv_in, kv_ref, 4)
    experts.to_y(0, 6)
    y_load.wait()
    for b in range(blocks):
        sums.first_send(b)

    def add(b, band):
        move(y_land.at[b, band, :], y_other.at[band, :])
        if big:
            move(yp_ref.at[b, band, :], y_stage.at[band, :])
            y_stage[band, :] = (y_stage[band, :].astype(F32) + y_other[band, :].astype(F32)).astype(BF16)
            move(y_stage.at[band, :], yp_ref.at[b, band, :])
        else:
            yp_ref[b, band, :] = (yp_ref[b, band, :].astype(F32) + y_other[band, :].astype(F32)).astype(BF16)

    def fetch(stage):
        def get(ref):
            if big:
                move(ref, stage)
                return stage
            return ref
        return get

    wo_load.wait()

    def mix_back(head):
        band = aligned(head * own_rows, own_rows)
        grad = mm(ag_ref[band, :], wo_ref[...], NT).astype(BF16)
        for hh in range(heads):
            do_ref[hh, band, :] = grad[:, hh * HEAD:(hh + 1) * HEAD]

    def turn(i):
        band = slice(i * own_rows, (i + 1) * own_rows)
        move(n1_hbm.at[band, :], y_other)
        n1t_ref[:, band] = y_other[...].astype(F32).T.astype(BF16)

    ag_ref[aligned(at.h * own_rows, own_rows), :] = attn_ref[...]
    mix_back(at.h)
    turn(0)
    near()
    mix_back(at.sib)
    for i in range(1, rows // own_rows):
        turn(i)
    experts.to_x(0)
    forward()
    mix_back(at.xn)
    far()
    mix_back(at.xs)
    step = 512

    def weight_back(i, _):
        cols = pl.ds(pl.multiple_of(i * step, step), step)
        dwo_ref[:, cols] = mm(ot_ref[...], ag_ref[:, cols]).astype(BF16)
        return 0

    lax.fori_loop(0, width // step, weight_back, 0)
    output.to_z()
    kv_from = pl.ds(pl.multiple_of(qcols + at.c * HEAD, HEAD), HEAD)
    w_loads = [load(w_hbm.at[:, :qcols], w_ref.at[:, :qcols], 2), load(w_hbm.at[:, kv_from], w_ref.at[:, qcols:], 3)]
    dq_ref[...] = jnp.zeros_like(dq_ref)
    for hh in range(heads):
        prod = do_ref[hh].astype(F32).T * ot_ref[hh * HEAD:(hh + 1) * HEAD, :].astype(F32)
        delta_ref[hh] = jnp.sum(prod, axis=0, keepdims=True)
    if not big:
        kv_load.wait()

    experts.to_x(1)
    beside = [[(experts.to_x, 2), (experts.share, 0)],
              [(experts.to_x, 3), (experts.share, 1)],
              [(experts.to_x, 4), (experts.share, 2)]]

    def advance():
        for f, k in (beside.pop(0) if beside else ()):
            f(k)

    def opening(b):
        if big:
            move(kv_in.at[b], kv_stage)
        kv = kv_stage if big else kv_ref.at[b]
        kt_ref[...] = kv[0].astype(F32).T.astype(BF16)
        dk_ref[...] = jnp.zeros_like(dk_ref)
        dv_ref[...] = jnp.zeros_like(dv_ref)
        return kv

    def closing(b, kv):
        kv[0] = (dk_ref[...] * LN2).astype(BF16)
        kv[1] = dv_ref[...].astype(BF16)
        if big:
            move(kv_stage, kv_ref.at[b])

    def block(b):
        kv = opening(b)

        def tile(t, _):
            hh, i = t // (rows // TILE), t % (rows // TILE)
            cols = pl.ds(pl.multiple_of(i * TILE, TILE), TILE)
            unattend_tile(hh, cols, kv[0], kv[1], kt_ref[...], q_ref, do_ref,
                          start_ref, lse_ref, delta_ref, dq_ref, dk_ref, dv_ref, b * rows, None)
            return 0

        lax.fori_loop(0, heads * (rows // TILE), tile, 0)
        closing(b, kv)

    pair, column = lanes.slots(blocks), lanes.slots(blocks)

    def to_sibling(b, when):
        lanes.put(pair + b, kv_ref.at[b, 1 - at.c], dkv_sib.at[b], when=when, head=at.sib)

    def to_column(b):
        lanes.arrived(pair + b, dkv_sib.at[b], when=b < me, head=at.sib)

        @pl.when(b < me)
        def _():
            came = fetch(dkv_stage)(dkv_sib.at[b])
            if big:
                move(kv_ref.at[b, at.c], kv_stage.at[at.c])
            kv = kv_stage if big else kv_ref.at[b]
            kv[at.c] = (kv[at.c].astype(F32) + came[...].astype(F32)).astype(BF16)
            if big:
                move(kv_stage.at[at.c], kv_ref.at[b, at.c])

        lanes.put(column + me, kv_ref.at[b, at.c], dkv_land.at[me], when=b < me, blk=b)

    for b in range(blocks - 1):
        pl.when(b < me)(functools.partial(block, b))
        to_sibling(b, b < me)
        sums.relay(0, b + 1, add)
        advance()
        if b > 0:
            to_column(b - 1)
    while beside:
        advance()
    to_column(blocks - 2)

    kv_own = opening(me)
    for i in range(rows // TILE):
        n = (i + 1) * TILE

        def diagonal(hh, _, i=i, n=n):
            unattend_tile(hh, slice(i * TILE, n), kv_own[0, :n, :], kv_own[1, :n, :], kt_ref[:, :n], q_ref, do_ref,
                          start_ref, lse_ref, delta_ref, dq_ref, dk_ref, dv_ref,
                          me * rows, me * rows + i * TILE)
            return 0

        lax.fori_loop(0, heads, diagonal, 0)
    closing(me, kv_own)
    to_sibling(me, None)
    experts.to_x(5)
    for d in range(1, blocks):
        sums.relay(1, d, add)

    def unrotate(u):
        return u * cos_ref[...] - pltpu.roll(u, HEAD // 2, 1) * sin_ref[...]

    for hh in range(heads):
        dpre_ref[:, hh * HEAD:(hh + 1) * HEAD] = unrotate((dq_ref[hh] * SCORE_SCALE).T).astype(BF16)
    for w_load in w_loads:
        w_load.wait()
    parts = 4
    part = half // parts
    band_rows = 256
    query_cols, keyval_cols = slice(0, qcols), slice(qcols, qcols + HEAD)

    def weight_half(y, cols_out):
        def body(i, _):
            band = aligned(y * half + i * band_rows, band_rows)
            dw_ref[band, cols_out] = mm(n1t_ref[band, :], dpre_ref[:, cols_out]).astype(BF16)
            return 0

        lax.fori_loop(0, half // band_rows, body, 0)

    def weight_part(y, p):
        return aligned(y * half + p * part, part)

    ys = (lanes.slots(parts), lanes.slots(parts))

    def weight_to_y(i, cols_out):
        weight_half(at.oy, cols_out)
        for p in range(parts):
            lanes.put(ys[i] + p, dw_ref.at[weight_part(at.oy, p), cols_out],
                      dw_y.at[pl.ds(p * part, part), cols_out], fsdp=at.oy)

    weight_to_y(0, query_cols)
    experts.share(3)

    @pl.when(at.c == 0)
    def _():
        dkv_ref[...] = dk_ref[...] * LN2

    @pl.when(at.c == 1)
    def _():
        dkv_ref[...] = dv_ref[...]

    lanes.arrived(pair + me, dkv_sib.at[me], head=at.sib)
    dkv_ref[...] += fetch(dkv_stage)(dkv_sib.at[me])[...].astype(F32)
    for z in range(1, blocks):
        @pl.when(me < z)
        def _(z=z):
            lanes.arrived(column + z, dkv_land.at[z], blk=z)
            dkv_ref[...] += fetch(dkv_stage)(dkv_land.at[z])[...].astype(F32)

    dpre_ref[:, qcols:] = jnp.where(at.c == 0, unrotate(dkv_ref[...]), dkv_ref[...]).astype(BF16)
    weight_to_y(1, keyval_cols)
    experts.to_y(6, 8)

    def input_part(head):
        return mm(dpre_ref[aligned(head * own_rows, own_rows), :], w_ref[...], NT)

    lanes.settle(passed[0])

    def dn_ref(i):
        return ag_ref.at[i * own_rows:(i + 1) * own_rows, :]

    relay, direct, across = lanes.slots(), lanes.slots(), lanes.slots()
    dn_ref(0)[...] = input_part(at.xs).astype(BF16)
    lanes.put(relay, dn_ref(0), dn_sib.at[0], head=at.sib)
    dn_ref(2)[...] = input_part(at.sib).astype(BF16)
    lanes.put(direct, dn_ref(2), dn_sib.at[1], head=at.sib)
    lanes.arrived(relay, dn_sib.at[0], head=at.sib)
    dn_ref(1)[...] = (input_part(at.xn) + dn_sib[0].astype(F32)).astype(BF16)
    lanes.put(across, dn_ref(1), dn_x, head=at.xn)
    experts.share(4)
    weight_half(at.y, slice(None))
    output.to_y(fetch(dwo_stage))

    zr = lanes.slots(blocks)
    for p in range(parts):
        rows_p = weight_part(at.y, p)
        for i, cols_out in enumerate((query_cols, keyval_cols)):
            lanes.arrived(ys[i] + p, dw_y.at[pl.ds(p * part, part), cols_out], fsdp=at.oy)
        total = dw_ref[rows_p, :].astype(F32) + dw_y[pl.ds(p * part, part), :].astype(F32)
        dw_ref[rows_p, :] = total.astype(BF16)
        lanes.put(zr + at.z, dw_ref.at[rows_p, :], dw_z.at[at.z], when=at.z != p, blk=p)
    output.share()
    experts.to_x(6)
    experts.share(5)

    move(res_hbm, acc_ref)
    if big:
        move(yp_ref.at[me], y_stage)
    acc_ref[...] += (y_stage if big else yp_ref.at[me])[...].astype(F32)

    def take(slot):
        move(y_land.at[slot], y_other)
        acc_ref[...] += y_other[...].astype(F32)

    for side in range(2):
        sums.arrive(side, take)
    block_out[...] = acc_ref[...].astype(BF16)

    res_load = load(res_grad_hbm, acc_ref, 5)
    own = input_part(at.h)
    lanes.arrived(direct, dn_sib.at[1], head=at.sib)
    own = own + dn_sib[1].astype(F32)
    lanes.arrived(across, dn_x, head=at.xn)
    own = own + dn_x[...].astype(F32)
    x = x_ref[...].astype(F32)
    inv = lax.rsqrt(jnp.mean(x * x, axis=-1, keepdims=True) + NORM_EPSILON)
    hat = x * inv
    pulled = own * gain_ref[gain_row:gain_row + 1, :].astype(F32)
    slope = inv * (pulled - hat * jnp.mean(pulled * hat, axis=-1, keepdims=True))
    res_load.wait()
    tokens_out[...] = (acc_ref[...] + slope).astype(BF16)
    sm_ref[...] = small_ref[...]
    sm_ref[gain_row:gain_row + 1, :] = jnp.sum(own * hat, axis=0, keepdims=True)
    sa, sb, sy, sz = lanes.slots(), lanes.slots(), lanes.slots(), lanes.slots(blocks)
    lanes.put(sa, sm_ref, sm_a, head=at.sib)
    experts.to_x(7)
    experts.share(6)

    p = at.z % parts
    summer = at.z < parts
    zg, xg, cg, cf = lanes.slots(parts), lanes.slots(parts), lanes.slots(parts), lanes.slots(parts)

    def place(head, q):
        return land_ref.at[head, pl.ds(q * part, part), :]

    for z in at.others():
        lanes.arrived(zr + z, dw_z.at[z], when=summer, blk=z)
    mine_w = weight_part(at.y, p)

    @pl.when(summer)
    def _():
        total = dw_ref[mine_w, :].astype(F32)
        for z in at.others():
            total = total + dw_z[z].astype(F32)
        dw_ref[mine_w, :] = total.astype(BF16)
        land_ref[at.h, aligned(p * part, part), :] = total.astype(BF16)

    for z in at.others():
        lanes.put(zg + p, dw_ref.at[mine_w, :], place(at.h, p), when=summer, blk=z)
    lanes.put(xg + p, dw_ref.at[mine_w, :], place(at.h, p), when=summer, head=at.xn)
    lanes.put(cg + p, dw_ref.at[mine_w, :], place(at.h, p), when=summer, head=at.sib)
    lanes.arrived(sa, sm_a, head=at.sib)
    sm_a[...] = sm_a[...] + sm_ref[...]
    lanes.put(sb, sm_a, sm_b, head=at.xn)
    output.take_over()
    experts.share(7)

    lanes.arrived(sb, sm_b, head=at.xn)
    sm_b[...] = sm_a[...] + sm_b[...]
    mine_cols = pl.ds(pl.multiple_of(at.y * half, half), half)
    other_cols = pl.ds(pl.multiple_of(at.oy * half, half), half)
    lanes.put(sy, sm_b.at[:, other_cols], sm_y, fsdp=at.oy)
    for q in range(parts):
        later = at.z != q
        lanes.arrived(zg + q, place(at.h, q), when=later, blk=q)
        lanes.put(xg + q, place(at.h, q), place(at.h, q), when=later, head=at.xn)
        lanes.put(cg + q, place(at.h, q), place(at.h, q), when=later, head=at.sib)
    lanes.arrived(sy, sm_y, fsdp=at.oy)
    sm_z[at.z] = sm_b[:, mine_cols] + sm_y[...]
    for z in at.others():
        lanes.put(sz + at.z, sm_z.at[at.z], sm_z.at[at.z], blk=z)
    output.pass_on()
    for q in range(parts):
        lanes.arrived(xg + q, place(at.xn, q), head=at.xn)
        lanes.put(cf + q, place(at.xn, q), place(at.xn, q), head=at.sib)
    for z in at.others():
        lanes.arrived(sz + z, sm_z.at[z], blk=z)
    total = sm_z[0]
    for z in range(1, blocks):
        total = total + sm_z[z]
    small_out[...] = total
    output.finish()
    keeps = [load(dwo_land, output_out, 0)]
    for q in range(parts):
        lanes.arrived(cg + q, place(at.sib, q), head=at.sib)
        lanes.arrived(cf + q, place(at.xs, q), head=at.sib)
    for head in range(4):
        keeps.append(load(land_ref.at[head, :, :qcols], query_out.at[:, head * qcols:(head + 1) * qcols], 1 + head))
        column_of = (head % 2 * KEYVALUE_HEADS + head // 2) * HEAD
        keeps.append(load(land_ref.at[head, :, qcols:], kv_out.at[:, column_of:column_of + HEAD], 6 + head))
    experts.finish()
    for keep in keeps:
        keep.wait()
    sums.finish()
    lanes.drain()


def backward(attn_grad, q, ot, start, lse, x, cosine, sine, gain, small, kv, wo, grads, y_parts, res, res_grad, n1, w):
    heads, rows, _ = q.shape
    blocks = kv.shape[0]
    own_rows, width = attn_grad.shape
    qcols = heads * HEAD
    _, half, wide = grads.shape
    cols = qcols + HEAD
    srows = small.shape[0]
    n = ExpertSums.CHUNKS
    vm = pl.BlockSpec(memory_space=pltpu.VMEM)
    hbm = pl.BlockSpec(memory_space=pl.ANY)
    part = qcols // OutputSums.PARTS
    sds = jax.ShapeDtypeStruct
    column = [((blocks, own_rows, width), BF16), ((blocks, rows, HEAD), BF16),
              ((blocks, rows, HEAD), BF16), ((blocks, part, width), BF16), (kv.shape, BF16)]
    if blocks > 4:
        extra_out, extra_spec = tuple(sds(*c) for c in column), [hbm] * 5
        extra_scratch = [pltpu.VMEM((rows, HEAD), BF16), pltpu.VMEM((part, width), BF16),
                         pltpu.VMEM((own_rows, width), BF16), pltpu.VMEM((2, rows, HEAD), BF16)]
    else:
        extra_out, extra_spec = (), []
        extra_scratch = [pltpu.VMEM(*c) for c in column]
    return pl.pallas_call(
        back_kernel,
        out_shape=(
            sds((own_rows, width), BF16),
            sds((own_rows, width), BF16),
            sds((srows, half), F32),
            sds((half, 2 * KEYVALUE_HEADS * HEAD), BF16),
            sds((2, half, wide), BF16),
            sds((2 * qcols, width), BF16),
            sds((half, rows // own_rows * qcols), BF16),
            sds((blocks + 1, own_rows, width), BF16),
        ) + extra_out,
        in_specs=[vm] * 10 + [hbm] * 8,
        out_specs=[vm] * 3 + [hbm] * 5 + extra_spec,
        scratch_shapes=extra_scratch + [
            pltpu.VMEM((heads, HEAD, rows), F32),
            pltpu.VMEM((rows, HEAD), F32),
            pltpu.VMEM((rows, HEAD), F32),
            pltpu.VMEM((HEAD, rows), BF16),
            pltpu.VMEM((heads, 1, rows), F32),
            pltpu.VMEM((heads, rows, HEAD), BF16),
            pltpu.VMEM((rows, width), BF16),
            pltpu.VMEM((qcols, width), BF16),
            pltpu.VMEM((qcols, width), BF16),
            pltpu.VMEM((part, width), BF16),
            pltpu.VMEM((2 * qcols, width), BF16),
            pltpu.VMEM((2, half, wide), BF16),
            pltpu.VMEM((half, wide), BF16),
            pltpu.VMEM((half, wide), BF16),
            pltpu.VMEM((own_rows, width), F32),
            pltpu.VMEM((own_rows, width), BF16),
            pltpu.VMEM((width, cols), BF16),
            pltpu.VMEM((rows, cols), BF16),
            pltpu.VMEM((2, own_rows, width), BF16),
            pltpu.VMEM((own_rows, width), BF16),
            pltpu.VMEM((width, cols), BF16),
            pltpu.VMEM((half, cols), BF16),
            pltpu.VMEM((blocks, half // 4, cols), BF16),
            pltpu.VMEM((srows, width), F32),
            pltpu.VMEM((srows, width), F32),
            pltpu.VMEM((srows, width), F32),
            pltpu.VMEM((srows, half), F32),
            pltpu.VMEM((blocks, srows, half), F32),
            pltpu.VMEM((rows // own_rows, half, cols), BF16),
            pltpu.VMEM((rows, HEAD), F32),
            pltpu.VMEM((width, rows), BF16),
            pltpu.SemaphoreType.DMA((10,)),
            pltpu.SemaphoreType.DMA((n,)),
        ] + semaphores(blocks),
        compiler_params=pltpu.CompilerParams(
            vmem_limit_bytes=VMEM_BYTES, collective_id=2, has_side_effects=True),
    )(attn_grad, q, ot, start, lse, x, cosine, sine, gain, small, kv, wo, grads, y_parts, res, res_grad, n1, w)[:7]


def on_device(tokens, documents, routes, cotangent, first_gain, query_weight, keyvalue_weight, output_weight,
              second_gain, router_weight, expert_in, expert_out):
    z = lax.axis_index("blk")
    blocks = lax.axis_size("blk")
    rows, width = tokens.shape[1:]
    group = lax.axis_size("head") * rows
    experts = router_weight.shape[1]
    half = query_weight.shape[0]

    small_rows = -(-(2 + experts) // 16) * 16
    small = jnp.concatenate([router_weight.T, first_gain[None], second_gain[None],
                             jnp.zeros((small_rows - 2 - experts, half), BF16)], axis=0)
    pos = (z * group + jnp.arange(group, dtype=jnp.int32)).astype(F32)
    inverse = jnp.power(ROPE_BASE, -jnp.arange(HEAD // 2).astype(F32) * 2.0 / HEAD)
    angle = pos[:, None] * inverse[None, :]
    cos, sin = jnp.cos(angle), jnp.sin(angle)
    cosine = jnp.concatenate([cos, cos], axis=-1)
    sine = jnp.concatenate([-sin, sin], axis=-1)
    doc = documents[0]
    doc_q = lax.dynamic_slice_in_dim(doc, z * group, group, 0)
    start = sum(jnp.where(doc_q > d, jnp.sum((doc == d).astype(jnp.int32)), 0) for d in range(DOCUMENTS - 1))[None, :]
    chosen = jnp.any(routes[0][:, :, None] == jnp.arange(LANES, dtype=jnp.int32), axis=1).astype(F32)

    q, mixed, mixed_t, lse, n1, small, wqkv, kv_all, wo, w_experts, cots = front(
        blocks, tokens[0], small, query_weight, keyvalue_weight, output_weight, expert_in, expert_out,
        cotangent[0], cosine, sine, start)
    res1, res_grad, attn_grad, d_small, grads, y_parts = expert_layer(
        mixed, tokens[0], small, chosen, wo, w_experts, cots)
    block_out, tokens_grad, d_small, d_keyval, d_experts, d_wo, d_query = backward(
        attn_grad, q, mixed_t, start, lse, tokens[0], cosine, sine, small, d_small,
        kv_all, wo, grads, y_parts, res1, res_grad, n1, wqkv)
    return (block_out[None], tokens_grad[None], d_small[experts], d_query.astype(F32), d_keyval.astype(F32), d_wo.astype(F32),
            d_small[experts + 1], d_small[:experts].T, d_experts[:, :, :width].astype(F32),
            d_experts[:, :, width:].astype(F32))


def solution(mesh):
    token_spec = P("fsdp", ("blk", "head"), None)
    row_spec = P("fsdp", None)
    in_spec = P("blk", "fsdp", None)
    out_spec = P("blk", None, "fsdp")
    return jax.shard_map(
        on_device,
        mesh=mesh,
        in_specs=(token_spec, row_spec, token_spec, token_spec, P("fsdp"), row_spec, row_spec, row_spec, P("fsdp"),
                  row_spec, in_spec, out_spec),
        out_specs=(token_spec, token_spec, P("fsdp"), row_spec, row_spec, row_spec, P("fsdp"), row_spec, in_spec,
                   out_spec),
        check_vma=False,
    )
```

```python
import functools

import jax
import jax.numpy as jnp
from jax import lax
from jax.experimental import pallas as pl
from jax.experimental.pallas import tpu as pltpu
from jax.sharding import PartitionSpec as P

QUERY_HEADS = 12
KEYVALUE_HEADS = 2
HEAD = 128
NORM_EPSILON = 1e-06
ROPE_BASE = 1000000.0
MASKED = -1e30
DOCUMENTS = 4
LOG2E = 1.4426950408889634
SCORE_LOG2 = HEAD ** (-0.5) * LOG2E
SCORE_SCALE = HEAD ** (-0.5)
LN2 = 1.0 / LOG2E
TILE = 256
BF16 = jnp.bfloat16
F32 = jnp.float32
VMEM_BYTES = 63 * 1024 * 1024

NN = (((1,), (0,)), ((), ()))
NT = (((1,), (1,)), ((), ()))
TN = (((0,), (0,)), ((), ()))


def mm(a, b, dims=NN):
    return lax.dot_general(a, b, dims, preferred_element_type=F32)


def gelu_parts(gate):
    c = 0.7978845608028654
    cube = 0.044715 * gate * gate * gate
    t = jnp.tanh(c * (gate + cube))
    value = 0.5 * gate * (1.0 + t)
    slope = 0.5 * (1.0 + t) + 0.5 * gate * (1.0 - t * t) * c * (1.0 + 3.0 * 0.044715 * gate * gate)
    return value, slope


def score_tile(key_rows, q_tile, start_row, first_key, q_first):
    scores = mm(key_rows, q_tile, NT)
    key_row = lax.broadcasted_iota(jnp.int32, scores.shape, 0)
    allowed = key_row >= start_row - first_key
    if q_first is not None:
        allowed = allowed & (key_row - lax.broadcasted_iota(jnp.int32, scores.shape, 1) <= q_first - first_key)
    return jnp.where(allowed, scores, MASKED)


def attend_tile(hh, cols, key_rows, value_cols, q_ref, start_ref, m_ref, l_ref, acc_ref, first_key, q_first):
    q_tile = q_ref[hh, cols, :]
    scores = score_tile(key_rows, q_tile, start_ref[:, cols], first_key, q_first)
    old = m_ref[hh, :, cols]
    new = jnp.maximum(old, jnp.max(scores, axis=0, keepdims=True))
    factor = jnp.exp2(old - new)
    prob = jnp.exp2(scores - new)
    m_ref[hh, :, cols] = new
    l_ref[hh, :, cols] = l_ref[hh, :, cols] * factor + jnp.sum(prob, axis=0, keepdims=True)
    acc_ref[hh, :, cols] = acc_ref[hh, :, cols] * factor + mm(value_cols, prob.astype(BF16))


def unattend_tile(hh, cols, key_rows, value_rows, key_cols, q_ref, do_ref, start_ref, lse_ref, delta_ref,
                  dq_ref, dk_ref, dv_ref, first_key, q_first):
    n = key_rows.shape[0]
    q_tile = q_ref[hh, cols, :]
    do_tile = do_ref[hh, cols, :]
    scores = score_tile(key_rows, q_tile, start_ref[:, cols], first_key, q_first)
    prob = jnp.exp2(scores - lse_ref[hh, :, cols])
    dv_ref[:n, :] += mm(prob.astype(BF16), do_tile)
    prob_grad = mm(value_rows, do_tile, NT)
    score_grad = (prob * (prob_grad - delta_ref[hh, :, cols])).astype(BF16)
    dk_ref[:n, :] += mm(score_grad, q_tile)
    dq_ref[hh, :, cols] += mm(key_cols, score_grad)


def remote(src, dst, send_sem, recv_sem, **to):
    return pltpu.make_async_remote_copy(
        src_ref=src, dst_ref=dst, send_sem=send_sem, recv_sem=recv_sem, device_id=to,
        device_id_type=pl.DeviceIdType.MESH)


class Lanes:
    def __init__(self, send, recv):
        self.send, self.recv, self.used, self.sent, self.pending = send, recv, 0, 0, []

    def slots(self, count=1):
        first = self.used
        self.used += count
        assert self.used <= self.recv.shape[0]
        return first

    def sends(self, count):
        first = self.sent
        self.sent += count
        assert self.sent <= self.send.shape[0]
        return first

    def put(self, slot, src, dst, when=None, **to):
        assert self.sent < self.send.shape[0]
        copy = remote(src, dst, self.send.at[self.sent], self.recv.at[slot], **to)
        self.sent += 1
        if when is None:
            copy.start()
        else:
            pl.when(when)(copy.start)
        self.pending.append((copy, when))
        return self.pending[-1]

    def settle(self, entry):
        copy, when = entry
        self.pending = [other for other in self.pending if other is not entry]
        if when is None:
            copy.wait_send()
        else:
            pl.when(when)(copy.wait_send)

    def arrived(self, slot, dst, when=None, **origin):
        copy = remote(dst, dst, self.send.at[0], self.recv.at[slot], **origin)
        if when is None:
            copy.wait_recv()
        else:
            pl.when(when)(copy.wait_recv)

    def drain(self):
        for copy, when in self.pending:
            if when is None:
                copy.wait_send()
            else:
                pl.when(when)(copy.wait_send)
        self.pending = []


class Place:
    def __init__(self, blocks):
        self.z, self.h, self.y = lax.axis_index("blk"), lax.axis_index("head"), lax.axis_index("fsdp")
        self.blocks = blocks
        self.x, self.c = self.h // 2, self.h % 2
        self.sib = 2 * self.x + 1 - self.c
        self.xn = 2 * (1 - self.x) + self.c
        self.xs = 2 * (1 - self.x) + 1 - self.c
        self.oy = 1 - self.y

    def others(self):
        return [(self.z + d) % self.blocks for d in range(1, self.blocks)]

    def enter(self):
        barrier = pltpu.get_barrier_semaphore()

        def greet(**to):
            pl.semaphore_signal(barrier, inc=1, device_id=to, device_id_type=pl.DeviceIdType.MESH)

        for head in (self.sib, self.xn, self.xs):
            greet(head=head)
        greet(fsdp=self.oy)
        for z in self.others():
            greet(blk=z)
        pl.semaphore_wait(barrier, 4 + self.blocks - 1)


def gather_heads(at, lanes, own, land):
    s = lanes.slots(3)
    rows = own.shape[0]

    def slot(head):
        return land.at[pl.ds(pl.multiple_of(head * rows, rows), rows), :]

    lanes.put(s, own, slot(at.h), head=at.xn)
    lanes.put(s + 1, own, slot(at.h), head=at.sib)

    passed = []

    def forward():
        lanes.arrived(s, slot(at.xn), head=at.xn)
        passed.append(lanes.put(s + 2, slot(at.xn), slot(at.xn), head=at.sib))

    def near():
        lanes.arrived(s + 1, slot(at.sib), head=at.sib)

    def far():
        lanes.arrived(s + 2, slot(at.xs), head=at.sib)

    return forward, near, far, passed


def aligned(index, size):
    return pl.ds(pl.multiple_of(index, 16), size)


def semaphores(blocks):
    count = 128 + 16 * blocks
    return [pltpu.SemaphoreType.DMA((count,)), pltpu.SemaphoreType.DMA((count,))]


class Shared:
    def __init__(self, at, lanes, chunks, give, hold):
        self.at, self.lanes, self.chunks, self.give, self.hold = at, lanes, chunks, give, hold
        self.pieces = len(give(0)) if give else 0
        self.ys = lanes.slots(chunks * self.pieces)
        self.xn, self.sib, self.far = lanes.slots(chunks), lanes.slots(chunks), lanes.slots(chunks)
        self.sent = []

    def begin(self, k):
        for i, (src, dst) in enumerate(self.give(k)):
            self.lanes.put(self.ys + k * self.pieces + i, src, dst(self.at.y), fsdp=self.at.oy)

    def landed(self, k):
        for i, (src, dst) in enumerate(self.give(k)):
            self.lanes.arrived(self.ys + k * self.pieces + i, dst(self.at.oy), fsdp=self.at.oy)

    def spread(self, k):
        self.landed(k)
        self.scatter(k)

    def scatter(self, k):
        at = self.at
        place = self.hold(k, at.h, at.oy)
        self.sent.append(self.lanes.put(self.xn + k, place, place, head=at.xn))
        self.sent.append(self.lanes.put(self.sib + k, place, place, head=at.sib))

    def forward(self, k):
        at = self.at
        place = self.hold(k, at.xn, at.oy)
        self.lanes.arrived(self.xn + k, place, head=at.xn)
        self.sent.append(self.lanes.put(self.far + k, place, place, head=at.sib))

    def settle(self):
        for entry in self.sent:
            self.lanes.settle(entry)

    def finish(self, k):
        at = self.at
        self.lanes.arrived(self.sib + k, self.hold(k, at.sib, at.oy), head=at.sib)
        self.lanes.arrived(self.far + k, self.hold(k, at.xs, at.oy), head=at.sib)


def weight_chunk(w_ref, k, head, y):
    quarter = w_ref.shape[2] // 4
    piece = quarter // 2
    return w_ref.at[k // 2, y, aligned(head * quarter + k % 2 * piece, piece), :]


class Column:
    def __init__(self, at, lanes, land):
        self.at, self.lanes, self.land = at, lanes, land
        self.slot = lanes.slots(at.blocks)

    def begin(self, own):
        at = self.at
        place = self.land.at[at.z]
        self.lanes.put(self.slot + at.z, own, place, when=at.z < at.blocks - 1, blk=at.z + 1)
        self.lanes.put(self.slot + at.z, own, place, when=at.z > 0, blk=at.z - 1)

    def hand_on(self, d):
        at = self.at
        for b, origin, next_z in ((at.z - d, at.z - 1, at.z + 1), (at.z + d, at.z + 1, at.z - 1)):
            there = (b >= 0) & (b < at.blocks)
            safe = jnp.clip(b, 0, at.blocks - 1)
            self.lanes.arrived(self.slot + safe, self.land.at[safe], when=there, blk=origin)
            self.lanes.put(self.slot + safe, self.land.at[safe], self.land.at[safe],
                           when=there & (next_z >= 0) & (next_z < at.blocks), blk=next_z)


def front_kernel(x_ref, small_ref, wq_hbm, wkv_hbm, wo_hbm, win_hbm, wout_hbm, cot_hbm, cos_ref, sin_ref, start_ref,
                 o_ref, ot_ref, lse_ref, small_out, q_out, n1_out, wqkv_out, kv_out, wo_out, w_out, cot_out,
                 q_ref, n1_ref,
                 xg_ref, small_land, wqkv_ref, kv_ref, m_ref, l_ref, acc_ref, vt_ref, wo_ref, w_ref, cot_ref,
                 load_sem, send_sem, recv_sem):
    heads, rows, _ = q_ref.shape
    own_rows, width = x_ref.shape
    blocks = kv_ref.shape[0]
    half = wq_hbm.shape[0]
    qcols = heads * HEAD
    experts = 2 * blocks
    at = Place(blocks)
    me = at.z
    lanes = Lanes(send_sem, recv_sem)
    at.enter()
    local = []

    def copy_here(src, dst):
        copy = pltpu.make_async_copy(src, dst, load_sem.at[len(local)])
        copy.start()
        local.append(copy)
        return copy

    forward, near, far, _ = gather_heads(at, lanes, x_ref, xg_ref)
    g = at.x
    q_from = pl.ds(pl.multiple_of(at.h * qcols, HEAD), qcols)
    kv_from = pl.ds(pl.multiple_of((at.c * KEYVALUE_HEADS + g) * HEAD, HEAD), HEAD)

    def kv_cols(core):
        return pl.ds(pl.multiple_of(qcols + core * HEAD, HEAD), HEAD)

    columns = ((wq_hbm.at[:, q_from], slice(0, qcols)), (wkv_hbm.at[:, kv_from], kv_cols(at.c)))

    def weight_rows(y, cols):
        return wqkv_ref.at[aligned(y * half, half), cols]

    ws, wc = lanes.slots(2), lanes.slots()
    for i, (src, cols) in reversed(list(enumerate(columns))):
        lanes.put(ws + i, src, weight_rows(at.y, cols), fsdp=at.oy)
    smalls = lanes.slots()
    lanes.put(smalls, small_ref, small_land, fsdp=at.oy)
    kv_other = pl.ds(pl.multiple_of(((1 - at.c) * KEYVALUE_HEADS + g) * HEAD, HEAD), HEAD)
    own_weights = [copy_here(src, weight_rows(at.y, cols))
                   for src, cols in columns + ((wkv_hbm.at[:, kv_other], kv_cols(1 - at.c)),)]
    cots = Column(at, lanes, cot_ref)
    own_half = pl.ds(pl.multiple_of(at.y * half, half), half)
    cot_load = copy_here(cot_hbm, cot_ref.at[me])
    wo_load = copy_here(wo_hbm, wo_ref.at[own_half, :])
    w_loads = [copy_here(win_hbm, w_ref.at[:, at.y, :, :width]), copy_here(wout_hbm, w_ref.at[:, at.y, :, width:])]
    cot_load.wait()
    cots.begin(cot_ref.at[me])

    quarter = half // 4

    def wo_place(k, head, y):
        return wo_ref.at[aligned(y * half + head * quarter, quarter), :]

    shared_wo = Shared(at, lanes, 1,
                       lambda k: [(wo_place(0, at.h, at.y), lambda y: wo_place(0, at.h, y))],
                       wo_place)
    chunks, spread_here = 4, 2

    def w_place(k, head, y):
        return weight_chunk(w_ref, k, head, y)

    def w_give(k):
        return [(w_place(k, at.h, at.y), lambda y: w_place(k, at.h, y))]

    shared_w = Shared(at, lanes, chunks, w_give, w_place)

    small_out[:, :half] = jnp.zeros((small_ref.shape[0], half), BF16)
    lanes.arrived(smalls, small_land, fsdp=at.oy)
    for y in range(2):
        @pl.when(at.y == y)
        def _(y=y):
            small_out[:, y * half:(y + 1) * half] = small_ref[...]
            small_out[:, (1 - y) * half:(2 - y) * half] = small_land[...]

    def norm(head, block):
        x = block.astype(F32)
        inv = lax.rsqrt(jnp.mean(x * x, axis=-1, keepdims=True) + NORM_EPSILON)
        n1_ref[aligned(head * own_rows, own_rows), :] = (x * inv * small_out[experts:experts + 1, :].astype(F32)).astype(BF16)

    def gathered(head):
        return xg_ref[aligned(head * own_rows, own_rows), :]

    norm(at.h, x_ref[...])
    near()
    norm(at.sib, gathered(at.sib))
    forward()
    norm(at.xn, gathered(at.xn))
    far()
    norm(at.xs, gathered(at.xs))
    for copy in own_weights:
        copy.wait()
    for i, (_, cols) in reversed(list(enumerate(columns))):
        lanes.arrived(ws + i, weight_rows(at.oy, cols), fsdp=at.oy)
        if i == 1:
            lanes.put(wc, weight_rows(at.oy, cols), weight_rows(at.oy, cols), head=at.sib)
    lanes.arrived(wc, weight_rows(at.oy, kv_cols(1 - at.c)), head=at.sib)
    wo_load.wait()
    shared_wo.begin(0)
    for load in w_loads:
        load.wait()
    for k in range(chunks):
        shared_w.begin(k)
    cots.hand_on(1)

    def project(i, _):
        band = aligned(i * TILE, TILE)
        pre = mm(n1_ref[band, :], wqkv_ref[...])
        cosine, sine = cos_ref[band, :], sin_ref[band, :]

        def turned(u):
            return (u * cosine + pltpu.roll(u, HEAD // 2, 1) * sine).astype(BF16)

        for hh in range(heads):
            q_ref[hh, band, :] = turned(pre[:, hh * HEAD:(hh + 1) * HEAD] * SCORE_LOG2)
        kv_ref[me, 0, band, :] = turned(pre[:, qcols:qcols + HEAD])
        kv_ref[me, 1, band, :] = pre[:, qcols + HEAD:].astype(BF16)
        return 0

    lax.fori_loop(0, rows // TILE, project, 0)

    kvs, kvc = lanes.slots(blocks), lanes.slots(blocks)

    def kv_half(b, core):
        return kv_ref.at[b, core]

    lanes.put(kvs + me, kv_half(me, at.c), kv_half(me, at.c), when=me < blocks - 1, blk=me + 1)
    late = [copy_here(q_ref, q_out), copy_here(n1_ref, n1_out), copy_here(wqkv_ref, wqkv_out), copy_here(wo_ref.at[own_half, :], wo_out.at[own_half, :]),
            copy_here(w_ref.at[:, at.y], w_out.at[:, at.y])]

    m_ref[...] = jnp.full_like(m_ref, MASKED)
    l_ref[...] = jnp.zeros_like(l_ref)
    acc_ref[...] = jnp.zeros_like(acc_ref)

    def transpose_values(b):
        vt_ref[...] = kv_ref[b, 1].astype(F32).T.astype(BF16)

    transpose_values(me)
    for i in range(rows // TILE):
        n = (i + 1) * TILE

        def diagonal(hh, _, i=i, n=n):
            attend_tile(hh, slice(i * TILE, n), kv_ref[me, 0, :n, :], vt_ref[:, :n], q_ref, start_ref,
                        m_ref, l_ref, acc_ref, me * rows, me * rows + i * TILE)
            return 0

        lax.fori_loop(0, heads, diagonal, 0)

    def block(b):
        transpose_values(b)

        def tile(t, _):
            hh, i = t // (rows // TILE), t % (rows // TILE)
            cols = pl.ds(pl.multiple_of(i * TILE, TILE), TILE)
            attend_tile(hh, cols, kv_ref[b, 0], vt_ref[...], q_ref, start_ref,
                        m_ref, l_ref, acc_ref, b * rows, None)
            return 0

        lax.fori_loop(0, heads * (rows // TILE), tile, 0)

    ticks = [[functools.partial(cots.hand_on, 2), functools.partial(shared_wo.spread, 0),
              functools.partial(shared_w.spread, 0)],
             [functools.partial(shared_w.spread, 1), functools.partial(shared_wo.forward, 0)],
             [functools.partial(shared_w.forward, 0)],
             [functools.partial(shared_w.forward, 1)] + [functools.partial(cots.hand_on, d) for d in range(3, blocks)]]

    def tick():
        if ticks:
            for f in ticks.pop(0):
                f()

    for d in range(1, blocks):
        b = jnp.maximum(me - d, 0)
        there = me >= d
        lanes.arrived(kvs + b, kv_half(b, at.c), when=there, blk=me - 1)
        lanes.put(kvs + b, kv_half(b, at.c), kv_half(b, at.c), when=there & (me < blocks - 1), blk=me + 1)
        lanes.put(kvc + b, kv_half(b, at.c), kv_half(b, at.c), when=there, head=at.sib)
        lanes.arrived(kvc + b, kv_half(b, 1 - at.c), when=there, head=at.sib)
        pl.when(there)(functools.partial(block, b))
        if d < blocks - 1:
            tick()

    for hh in range(heads):
        total = l_ref[hh]
        done = acc_ref[hh] / total
        ot_ref[hh * HEAD:(hh + 1) * HEAD, :] = done.astype(BF16)
        o_ref[:, hh * HEAD:(hh + 1) * HEAD] = done.T.astype(BF16)
        lse_ref[hh] = m_ref[hh] + jnp.log2(total)
    kv_copies = [pltpu.make_async_copy(kv_ref.at[b], kv_out.at[b], load_sem.at[16 + b]) for b in range(blocks)]
    for b, copy in enumerate(kv_copies):
        pl.when(b <= me)(copy.start)
    while ticks:
        tick()
    shared_wo.finish(0)
    other_half = pl.ds(pl.multiple_of(at.oy * half, half), half)
    late.append(copy_here(wo_ref.at[other_half, :], wo_out.at[other_half, :]))
    late.append(copy_here(cot_ref, cot_out))
    for k in range(spread_here):
        shared_w.finish(k)
    for k in range(spread_here, chunks):
        shared_w.landed(k)
    late.append(copy_here(w_ref.at[:, at.oy], w_out.at[:, at.oy]))
    for copy in late:
        copy.wait()
    for b, copy in enumerate(kv_copies):
        pl.when(b <= me)(copy.wait)
    lanes.drain()


def front(blocks, x, small, wq, wkv, wo, win, wout, cot, cosine, sine, start):
    own_rows, width = x.shape
    rows = cosine.shape[0]
    half = wq.shape[0]
    heads = QUERY_HEADS * own_rows // rows
    qcols = heads * HEAD
    ffe = wout.shape[1]
    vm = pl.BlockSpec(memory_space=pltpu.VMEM)
    hbm = pl.BlockSpec(memory_space=pl.ANY)
    sds = jax.ShapeDtypeStruct
    return pl.pallas_call(
        front_kernel,
        out_shape=(
            sds((rows, qcols), BF16),
            sds((qcols, rows), BF16),
            sds((heads, 1, rows), F32),
            sds((small.shape[0], width), BF16),
            sds((heads, rows, HEAD), BF16),
            sds((rows, width), BF16),
            sds((width, qcols + 2 * HEAD), BF16),
            sds((blocks, 2, rows, HEAD), BF16),
            sds((width, width), BF16),
            sds((2, 2, half, width + half), BF16),
            sds((blocks, own_rows, width), BF16),
        ),
        in_specs=[vm, vm] + [hbm] * 6 + [vm] * 3,
        out_specs=[vm] * 4 + [hbm] * 7,
        scratch_shapes=[
            pltpu.VMEM((heads, rows, HEAD), BF16),
            pltpu.VMEM((rows, width), BF16),
            pltpu.VMEM((rows, width), BF16),
            pltpu.VMEM(small.shape, BF16),
            pltpu.VMEM((width, qcols + 2 * HEAD), BF16),
            pltpu.VMEM((blocks, 2, rows, HEAD), BF16),
            pltpu.VMEM((heads, 1, rows), F32),
            pltpu.VMEM((heads, 1, rows), F32),
            pltpu.VMEM((heads, HEAD, rows), F32),
            pltpu.VMEM((HEAD, rows), BF16),
            pltpu.VMEM((width, width), BF16),
            pltpu.VMEM((2, 2, half, width + half), BF16),
            pltpu.VMEM((blocks, own_rows, width), BF16),
            pltpu.SemaphoreType.DMA((16 + blocks,)),
        ] + semaphores(blocks),
        compiler_params=pltpu.CompilerParams(
            vmem_limit_bytes=VMEM_BYTES, collective_id=0, has_side_effects=True),
    )(x, small, wq, wkv, wo, win, wout, cot, cosine, sine, start)


class ColumnSum:
    CHUNKS = 4

    def __init__(self, at, lanes, part, land):
        self.at, self.lanes, self.part, self.land = at, lanes, part, land
        self.rows = part.shape[1] // self.CHUNKS
        self.recv = lanes.slots((at.blocks + 1) * self.CHUNKS)
        self.sent = lanes.sends(at.blocks * self.CHUNKS)

    def copy(self, b, ch):
        at = self.at
        travel = jnp.where(b < at.z, -1, 1)
        there = at.z + travel
        slot = jnp.where((there == b) & (b > at.z), at.blocks, b)
        rows = pl.ds(ch * self.rows, self.rows)
        return remote(self.part.at[b, rows, :], self.land.at[slot, rows, :],
                      self.lanes.send.at[self.sent + b * self.CHUNKS + ch],
                      self.lanes.recv.at[self.recv + slot * self.CHUNKS + ch], blk=there)

    def landed(self, slot, ch, origin):
        rows = pl.ds(ch * self.rows, self.rows)
        place = self.land.at[slot, rows, :]
        remote(place, place, self.lanes.send.at[0], self.lanes.recv.at[self.recv + slot * self.CHUNKS + ch],
               blk=origin).wait_recv()

    def first_send(self, b):
        at = self.at

        @pl.when(((b < at.z) & (at.z == at.blocks - 1)) | ((b > at.z) & (at.z == 0)))
        def _():
            for ch in range(self.CHUNKS):
                self.copy(b, ch).start()

    def relay(self, phase, d, add):
        at = self.at
        s = jnp.where(at.z * 2 >= at.blocks, -1, 1) * (1 - 2 * phase)
        b, origin = at.z + s * d, at.z - s
        safe = jnp.clip(b, 0, at.blocks - 1)

        @pl.when((b >= 0) & (b < at.blocks) & (origin >= 0) & (origin < at.blocks))
        def _():
            for ch in range(self.CHUNKS):
                self.landed(safe, ch, origin)
                add(safe, pl.ds(ch * self.rows, self.rows))
                self.copy(safe, ch).start()

    def arrive(self, side, use):
        at = self.at
        slot, origin = (at.z, at.z + 1) if side == 0 else (at.blocks, at.z - 1)

        @pl.when((origin >= 0) & (origin < at.blocks))
        def _():
            for ch in range(self.CHUNKS):
                self.landed(slot, ch, origin)
            use(slot)

    def finish(self):
        at = self.at
        for b in range(at.blocks):
            @pl.when(b != at.z)
            def _(b=b):
                for ch in range(self.CHUNKS):
                    self.copy(b, ch).wait_send()


LANES = 128
HALF_LANES = LANES // 2


def split_lanes(value):
    high = value.astype(BF16).astype(F32)
    return (high + pltpu.roll(value - high, HALF_LANES, 1)).astype(BF16)


def expert_kernel(o_ref, x_ref, small_ref, chosen_ref, wo_hbm, w_hbm, cot_hbm,
                  res_out, grad_out, attn_out, small_out, sums_out, y_out, core_land, *rest):
    big = cot_hbm.shape[0] > 4
    if big:
        xb_ref, dx_ref, land_ref, *rest = rest
        (xb_stage, dx_stage, land_stage, g_ref, *rest) = rest
    else:
        xb_ref, dx_ref, land_ref, *rest = rest
    (mix_ref, w_ref, cot_ref, acc_ref, gate_ref, dgu_ref, ga_ref, xt_ref, gat_ref, gg_ref, y_ref, stage_ref,
     gates_ref, router_ref, load_sem, y_sem, send_sem, recv_sem) = rest
    own_rows, width = x_ref.shape
    blocks = cot_hbm.shape[0]
    qcols = o_ref.shape[1]
    half = width // 2
    experts, _, ffe, _ = w_ref.shape
    at = Place(blocks)
    me = at.z
    lanes = Lanes(send_sem, recv_sem)
    at.enter()
    every = blocks * own_rows
    if big:
        wo_rows = [(slice(y * half, (y + 1) * half), g_ref.at[0, y, :, :width]) for y in range(2)]
    else:
        wo_rows = [(slice(0, every), dgu_ref.at[0]), (slice(every, width), dgu_ref.at[1, :width - every])]
    wo_load = [pltpu.make_async_copy(wo_hbm.at[rows, :], place, load_sem.at[y])
               for y, (rows, place) in enumerate(wo_rows)]
    for load in wo_load:
        load.start()
    quarter = half // 4
    here = aligned(at.h * quarter, quarter)
    w_loads = [pltpu.make_async_copy(w_hbm.at[place], w_ref.at[place], load_sem.at[4 + i])
               for i, place in enumerate(((0,), (1, at.y), (1, at.oy, here)))]
    for load in w_loads:
        load.start()
    late = Shared(at, lanes, 4, None, functools.partial(weight_chunk, w_ref))
    if not big:
        cot_loads = [pltpu.make_async_copy(cot_hbm.at[b], cot_ref.at[b * own_rows:(b + 1) * own_rows, :],
                                           load_sem.at[7 + b]) for b in range(blocks)]
        for load in cot_loads:
            load.start()

    total_experts = experts * blocks
    srows = small_ref.shape[0]
    is_router = lax.broadcasted_iota(jnp.int32, (srows, width), 0) < total_experts
    router_ref[...] = jnp.zeros_like(router_ref)
    router_ref[:srows, :] = jnp.where(is_router, small_ref[...].astype(F32), 0.0).astype(BF16)
    gain_two = small_ref[total_experts + 1:total_experts + 2, :].astype(F32)

    mixes = lanes.slots(4)

    def mix_cols(head):
        return mix_ref.at[:, pl.ds(pl.multiple_of(head * qcols, HEAD), qcols)]

    for head in (at.xn, at.xs, at.sib):
        lanes.put(mixes + at.h, o_ref.at[aligned(head * own_rows, own_rows), :], mix_cols(at.h), head=head)
    mix_ref[:, pl.ds(pl.multiple_of(at.h * qcols, HEAD), qcols)] = o_ref[aligned(at.h * own_rows, own_rows), :]
    for head in (at.sib, at.xn, at.xs):
        lanes.arrived(mixes + head, mix_cols(head), head=head)
    for load in w_loads:
        load.wait()
    for k in (2, 3):
        late.scatter(k)
    for load in wo_load:
        load.wait()
    step = 512
    for i in range(width // step):
        cols = slice(i * step, (i + 1) * step)
        res_out[:, cols] = x_ref[:, cols].astype(F32) + sum(
            mm(mix_ref[:, rows], place[:, cols]) for rows, place in wo_rows)

    def inverse_two():
        res = res_out[...]
        return lax.rsqrt(jnp.mean(res * res, axis=-1, keepdims=True) + NORM_EPSILON)

    n2 = (res_out[...] * inverse_two() * gain_two).astype(BF16)
    chosen = chosen_ref[...] > 0.0
    logits = jnp.where(chosen, mm(n2, router_ref[...], NT), MASKED)
    e_top = jnp.where(chosen, jnp.exp(logits - jnp.max(logits, axis=-1, keepdims=True)), 0.0)
    gates = e_top / jnp.sum(e_top, axis=-1, keepdims=True)
    gates_ref[...] = gates
    own_x = xb_stage if big else xb_ref.at[me]
    own_x[:, :width] = n2
    own_x[:, width:] = split_lanes(gates)

    def move(src, dst):
        copy = pltpu.make_async_copy(src, dst, load_sem.at[3])
        copy.start()
        copy.wait()

    if big:
        move(xb_stage, xb_ref.at[me])
    xs_slot, xs_sent = lanes.slots(blocks), lanes.sends(blocks + 2)

    def xs_copy(b, to, send):
        return remote(xb_ref.at[b], xb_ref.at[b], send_sem.at[xs_sent + send], recv_sem.at[xs_slot + b], blk=to)

    pl.when(me > 0)(lambda: xs_copy(me, me - 1, blocks).start())
    pl.when(me < blocks - 1)(lambda: xs_copy(me, me + 1, blocks + 1).start())

    if big:
        def clear(i, _):
            for e in range(experts):
                for y in range(2):
                    g_ref[e, y, aligned(i * 64, 64), :] = jnp.zeros((64, g_ref.shape[3]), BF16)
            return 0

        lax.fori_loop(0, half // 64, clear, 0)
    else:
        for load in cot_loads:
            load.wait()
    def second_expert():
        for k in (2, 3):
            late.forward(k)
        for k in (2, 3):
            late.finish(k)

    back = ColumnSum(at, lanes, dx_ref, land_ref)
    lane = lax.broadcasted_iota(jnp.int32, (own_rows, LANES), 1)
    tile = 256

    def y_copy(b):
        return pltpu.make_async_copy(y_ref, y_out.at[b], y_sem)

    def block(b, first, between=None):
        if big:
            move(xb_ref.at[b], xb_stage)
            move(cot_hbm.at[b], cot_ref)
        x_in = xb_stage if big else xb_ref.at[b]
        band_all = slice(None) if big else aligned(b * own_rows, own_rows)
        lanes_all = pl.ds(pl.multiple_of(b * own_rows, own_rows), own_rows)
        acc_ref[...] = jnp.zeros_like(acc_ref)
        gg_ref[...] = jnp.zeros_like(gg_ref)

        def hidden(e, _):
            index = me * experts + e
            pack = x_in[:, width:].astype(F32)
            mine = (lane == index) | (lane == index + HALF_LANES)
            gate_ref[...] = jnp.sum(jnp.where(mine, pack, 0.0), axis=1, keepdims=True)

            def inner(t, total):
                low = pl.ds(pl.multiple_of(t * tile, tile), tile)
                high = pl.ds(pl.multiple_of(ffe + t * tile, tile), tile)
                out_cols = slice(width, width + half)
                gate_pre = mm(x_in[:, :half], w_ref[e, 0, :, low]) + mm(x_in[:, half:width], w_ref[e, 1, :, low])
                up = mm(x_in[:, :half], w_ref[e, 0, :, high]) + mm(x_in[:, half:width], w_ref[e, 1, :, high])
                back_h = (mm(cot_ref[band_all, :half], w_ref[e, 0, low, out_cols], NT)
                          + mm(cot_ref[band_all, half:], w_ref[e, 1, low, out_cols], NT))
                value, slope = gelu_parts(gate_pre)
                act = (value * up).astype(BF16).astype(F32)
                gate = gate_ref[...]
                ga_ref[e, :, low] = (gate * act).astype(BF16)
                if not big:
                    gat_ref[e, low, lanes_all] = (gate * act).T.astype(BF16)
                d_act = gate * back_h
                dgu_ref[e, band_all, low] = (d_act * up * slope).astype(BF16)
                dgu_ref[e, band_all, high] = (d_act * value).astype(BF16)
                return total + jnp.sum(act * back_h, axis=1, keepdims=True)

            total = lax.fori_loop(0, ffe // tile, inner, jnp.zeros((own_rows, 1), F32))
            gg_ref[...] += jnp.where(lane == index, total, 0.0)
            for y in range(2):
                acc_ref[:, y * half:(y + 1) * half] += mm(dgu_ref[e, band_all, :], w_ref[e, y, :, :width], NT)
            return 0

        if between is None:
            lax.fori_loop(0, experts, hidden, 0)
        else:
            hidden(0, 0)
            between()
            for e in range(1, experts):
                hidden(e, 0)
        part = dx_stage if big else dx_ref.at[b]
        part[:, :width] = acc_ref[...].astype(BF16)
        part[:, width:] = split_lanes(gg_ref[...])
        if big:
            move(dx_stage, dx_ref.at[b])
        back.first_send(b)

        if big:
            xt_ref[...] = x_in[:, :width].astype(F32).T.astype(BF16)

            def weights(e, _):
                gat_ref[0] = ga_ref[e].astype(F32).T.astype(BF16)

                def rows(i, _):
                    band = aligned(i * tile, tile)
                    for y in range(2):
                        x_cols = xt_ref[aligned(y * half + i * tile, tile), :]
                        for n in range(width // step):
                            cols = slice(n * step, (n + 1) * step)
                            total = g_ref[e, y, band, cols].astype(F32) + mm(x_cols, dgu_ref[e, :, cols])
                            g_ref[e, y, band, cols] = total.astype(BF16)
                        out_cols = slice(width, width + half)
                        total = (g_ref[e, y, band, out_cols].astype(F32)
                                 + mm(gat_ref[0, band, :], cot_ref[:, y * half:(y + 1) * half]))
                        g_ref[e, y, band, out_cols] = total.astype(BF16)
                    return 0

                return lax.fori_loop(0, half // tile, rows, 0)

            lax.fori_loop(0, experts, weights, 0)
        else:
            xt_ref[:, lanes_all] = x_in[:, :width].astype(F32).T.astype(BF16)

        if not first:
            y_copy(b).wait()
        for y in range(2):
            total = mm(ga_ref[0], w_ref[0, y, :, width:])
            for e in range(1, experts):
                total = total + mm(ga_ref[e], w_ref[e, y, :, width:])
            y_ref[:, y * half:(y + 1) * half] = total.astype(BF16)
        y_copy(b).start()

    def distance(d, _):
        for b, origin, to in ((me - d, me - 1, me + 1), (me + d, me + 1, me - 1)):
            @pl.when((b >= 0) & (b < blocks))
            def _(b=b, origin=origin, to=to):
                xs_copy(b, origin, 0).wait_recv()
                pl.when((to >= 0) & (to < blocks))(lambda: xs_copy(b, to, b).start())

        def side(s, _):
            b = jnp.where(s == 0, me - d, me + d)

            @pl.when((b >= 0) & (b < blocks))
            def _():
                block(jnp.clip(b, 0, blocks - 1), False)

            return 0

        return lax.fori_loop(0, 2, side, 0)

    block(me, True, second_expert)
    lax.fori_loop(1, blocks, distance, 0)
    y_copy(me).wait()

    def add(b, rows):
        if big:
            move(dx_ref.at[b, rows, :], dx_stage.at[rows, :])
            move(land_ref.at[b, rows, :], land_stage.at[rows, :])
            dx_stage[rows, :] = (dx_stage[rows, :].astype(F32) + land_stage[rows, :].astype(F32)).astype(BF16)
            move(dx_stage.at[rows, :], dx_ref.at[b, rows, :])
        else:
            dx_ref[b, rows, :] = (dx_ref[b, rows, :].astype(F32) + land_ref[b, rows, :].astype(F32)).astype(BF16)

    late.settle()
    total_ref = g_ref if big else w_ref

    def weights_of(e):
        def rows(i, _):
            cols = pl.ds(pl.multiple_of(i * tile, tile), tile)
            for y in range(2):
                total = mm(xt_ref[y * half:(y + 1) * half, :], dgu_ref[e, :, cols])
                total_ref[e, y, :, cols] = total.astype(BF16)
            return 0

        def outs(i, _):
            for y in range(2):
                cols = pl.ds(pl.multiple_of(y * half + i * tile, tile), tile)
                place = pl.ds(pl.multiple_of(width + i * tile, tile), tile)
                total_ref[e, y, :, place] = mm(gat_ref[e], cot_ref[:, cols]).astype(BF16)
            return 0

        lax.fori_loop(0, 2 * ffe // tile, rows, 0)
        lax.fori_loop(0, half // tile, outs, 0)

    chunks = 4
    piece = half // chunks
    cores = lanes.slots(chunks)
    back.relay(0, 1, add)
    if not big:
        weights_of(1 - at.c)
    for k in range(chunks):
        band = pl.ds(k * piece, piece)
        lanes.put(cores + k, total_ref.at[1 - at.c, :, band, :], core_land.at[:, band, :], head=at.sib)

    def core_sum(k):
        band = pl.ds(k * piece, piece)
        lanes.arrived(cores + k, core_land.at[:, band, :], head=at.sib)
        move(core_land.at[:, band, :], stage_ref)
        for y in range(2):
            total = total_ref[at.c, y, band, :].astype(F32) + stage_ref[y].astype(F32)
            total_ref[at.c, y, band, :] = total.astype(BF16)

    for d in range(2, blocks):
        back.relay(0, d, add)
    if not big:
        weights_of(at.c)
    for d in range(1, blocks):
        back.relay(1, d, add)
    for k in range(chunks):
        core_sum(k)
    keep = pltpu.make_async_copy(total_ref.at[at.c], sums_out, load_sem.at[0])
    keep.start()

    if big:
        move(dx_ref.at[me], dx_stage)
    own_part = dx_stage if big else dx_ref.at[me]
    acc_ref[...] = own_part[:, :width].astype(F32)
    gg_ref[...] = own_part[:, width:].astype(F32)

    def take(slot):
        if big:
            move(land_ref.at[slot], land_stage)
        came = land_stage if big else land_ref.at[slot]
        acc_ref[...] += came[:, :width].astype(F32)
        gg_ref[...] += came[:, width:].astype(F32)

    for side in range(2):
        back.arrive(side, take)
    both = gg_ref[...]
    gate_grads = jnp.where(lane < HALF_LANES, both + pltpu.roll(both, HALF_LANES, 1), 0.0)
    gates = gates_ref[...]
    d_logits = (gates * (gate_grads - jnp.sum(gates * gate_grads, axis=-1, keepdims=True))).astype(BF16)
    inv = inverse_two()
    hat = res_out[...] * inv
    n2 = (hat * gain_two).astype(BF16)
    small_out[...] = mm(d_logits.astype(F32).T.astype(BF16), n2)[:small_out.shape[0], :]
    d_n2 = acc_ref[...] + mm(d_logits, router_ref[...])
    small_out[total_experts + 1:total_experts + 2, :] = jnp.sum(d_n2 * hat, axis=0, keepdims=True)
    pulled = d_n2 * gain_two
    if big:
        move(cot_hbm.at[me], cot_ref)
    own_cot = cot_ref[...] if big else cot_ref[aligned(me * own_rows, own_rows), :]
    grad = own_cot.astype(F32) + inv * (pulled - hat * jnp.mean(pulled * hat, axis=-1, keepdims=True))
    grad_out[...] = grad
    attn_out[...] = grad.astype(BF16)
    keep.wait()
    for b in range(blocks):
        up, down = (b < me) & (me < blocks - 1), (b > me) & (me > 0)
        pl.when(up)(lambda b=b: xs_copy(b, me + 1, b).wait_send())
        pl.when(down)(lambda b=b: xs_copy(b, me - 1, b).wait_send())
    pl.when(me > 0)(lambda: xs_copy(me, me - 1, blocks).wait_send())
    pl.when(me < blocks - 1)(lambda: xs_copy(me, me + 1, blocks + 1).wait_send())
    back.finish()
    lanes.drain()


def expert_layer(o, x, small, chosen, wo, w, cot):
    own_rows, width = x.shape
    blocks = cot.shape[0]
    experts, _, half, wide = w.shape
    ffe = half
    pack = width + LANES
    big = blocks > 4
    kept = own_rows if big else blocks * own_rows
    vm = pl.BlockSpec(memory_space=pltpu.VMEM)
    hbm = pl.BlockSpec(memory_space=pl.ANY)
    sds = jax.ShapeDtypeStruct
    column = [((blocks, own_rows, pack), BF16), ((blocks, own_rows, pack), BF16), ((blocks + 1, own_rows, pack), BF16)]
    if big:
        extra_out, extra_spec = tuple(sds(*c) for c in column), [hbm] * 3
        extra_scratch = [pltpu.VMEM((own_rows, pack), BF16)] * 3 + [pltpu.VMEM(w.shape, BF16)]
    else:
        extra_out, extra_spec = (), []
        extra_scratch = [pltpu.VMEM(*c) for c in column]
    outs = pl.pallas_call(
        expert_kernel,
        out_shape=(
            sds((own_rows, width), F32),
            sds((own_rows, width), F32),
            sds((own_rows, width), BF16),
            sds((-(-(experts * blocks + 2) // 8) * 8, width), F32),
            sds((2, half, wide), BF16),
            sds((blocks, own_rows, width), BF16),
            sds((2, half, wide), BF16),
        ) + extra_out,
        in_specs=[vm] * 4 + [hbm] * 3,
        out_specs=[vm] * 4 + [hbm] * 3 + extra_spec,
        scratch_shapes=extra_scratch + [
            pltpu.VMEM((own_rows, width), BF16),
            pltpu.VMEM(w.shape, BF16),
            pltpu.VMEM((kept, width), BF16),
            pltpu.VMEM((own_rows, width), F32),
            pltpu.VMEM((own_rows, 1), F32),
            pltpu.VMEM((experts, kept, 2 * ffe), BF16),
            pltpu.VMEM((experts, own_rows, ffe), BF16),
            pltpu.VMEM((width, kept), BF16),
            pltpu.VMEM((experts, ffe, kept), BF16),
            pltpu.VMEM((own_rows, LANES), F32),
            pltpu.VMEM((own_rows, width), BF16),
            pltpu.VMEM((2, half // 4, wide), BF16),
            pltpu.VMEM((own_rows, LANES), F32),
            pltpu.VMEM((LANES, width), BF16),
            pltpu.SemaphoreType.DMA((7 + blocks,)),
            pltpu.SemaphoreType.DMA,
        ] + semaphores(blocks),
        compiler_params=pltpu.CompilerParams(
            vmem_limit_bytes=VMEM_BYTES, collective_id=1, has_side_effects=True),
    )(o, x, small, chosen, wo, w, cot)
    return outs[:6]


class ExpertSums:
    CHUNKS = 8

    def __init__(self, at, lanes, grads, own, land_y, land_x, out, load_sem, keep_sem):
        self.at, self.lanes = at, lanes
        self.grads, self.own, self.out = grads, own, out
        self.land_y, self.land_x = land_y, land_x
        self.load_sem, self.keep_sem = load_sem, keep_sem
        self.rows = grads.shape[1] // self.CHUNKS
        n = self.CHUNKS
        self.ys, self.xr, self.cg = [lanes.slots(n) for _ in range(3)]
        self.kept = []

    def chunk(self, k):
        return pl.ds(k * self.rows, self.rows)

    def load(self):
        self.loads = [pltpu.make_async_copy(self.grads.at[y], self.own.at[y], self.load_sem.at[i])
                      for i, y in enumerate((self.at.oy, self.at.y))]
        for copy in self.loads:
            copy.start()

    def to_y(self, first, last):
        if first == 0:
            self.loads[0].wait()
        for k in range(first, last):
            rows = self.chunk(k)
            self.lanes.put(self.ys + k, self.own.at[self.at.oy, rows, :], self.land_y.at[rows, :], fsdp=self.at.oy)

    def to_x(self, k):
        at, rows = self.at, self.chunk(k)
        if k == 0:
            self.loads[1].wait()
        self.lanes.arrived(self.ys + k, self.land_y.at[rows, :], fsdp=at.oy)
        total = self.own[at.y, rows, :].astype(F32) + self.land_y[rows, :].astype(F32)
        self.own[at.y, rows, :] = total.astype(BF16)
        self.lanes.put(self.xr + k, self.own.at[at.y, rows, :], self.land_x.at[rows, :], head=at.xn)

    def share(self, k):
        at, rows = self.at, self.chunk(k)
        self.lanes.arrived(self.xr + k, self.land_x.at[rows, :], head=at.xn)
        total = self.own[at.y, rows, :].astype(F32) + self.land_x[rows, :].astype(F32)
        self.land_x[rows, :] = total.astype(BF16)
        done, place = self.land_x.at[rows, :], self.out.at[at.c, rows, :]
        self.lanes.put(self.cg + k, done, place, head=at.sib)
        keep = pltpu.make_async_copy(done, place, self.keep_sem.at[k])
        keep.start()
        self.kept.append(keep)

    def finish(self):
        at = self.at
        for k in range(self.CHUNKS):
            self.lanes.arrived(self.cg + k, self.out.at[1 - at.c, self.chunk(k), :], head=at.sib)
            self.kept[k].wait()


class OutputSums:
    PARTS = 4

    def __init__(self, at, lanes, grad, land_y, land_z, out):
        self.at, self.lanes, self.grad = at, lanes, grad
        self.land_y, self.land_z, self.out = land_y, land_z, out
        self.rows = grad.shape[0] // self.PARTS
        self.ys = lanes.slots()
        self.zr, self.zg = lanes.slots(at.blocks), lanes.slots(self.PARTS)
        self.xg, self.cg = lanes.slots(), lanes.slots(self.PARTS)
        self.owner, self.giver = at.y == at.x, at.y != at.x
        self.summer = at.z < self.PARTS
        self.part = at.z % self.PARTS
        self.mine = aligned(self.part * self.rows, self.rows)

    def to_z(self):
        at = self.at
        for p in range(self.PARTS):
            self.lanes.put(self.zr + at.z, self.grad.at[pl.ds(p * self.rows, self.rows), :], self.land_z.at[at.z],
                           when=at.z != p, blk=p)

    def to_y(self, fetch):
        at = self.at
        for z in at.others():
            self.lanes.arrived(self.zr + z, self.land_z.at[z], when=self.summer, blk=z)

        @pl.when(self.summer)
        def _():
            total = self.grad[self.mine, :].astype(F32)
            for z in at.others():
                total = total + fetch(self.land_z.at[z])[...].astype(F32)
            self.grad[self.mine, :] = total.astype(BF16)

        self.lanes.put(self.ys, self.grad.at[self.mine, :], self.land_y, when=self.summer & self.giver, fsdp=at.oy)

    def place(self, core, p):
        return self.out.at[aligned(core * self.PARTS * self.rows + p * self.rows, self.rows), :]

    def share(self):
        at, p = self.at, self.part
        ready = self.summer & self.owner
        self.lanes.arrived(self.ys, self.land_y, when=ready, fsdp=at.oy)
        at_rows = aligned(at.c * self.PARTS * self.rows + p * self.rows, self.rows)

        @pl.when(ready)
        def _():
            total = self.grad[self.mine, :].astype(F32) + self.land_y[...].astype(F32)
            self.out[at_rows, :] = total.astype(BF16)

        place = self.place(at.c, p)
        self.lanes.put(self.xg, place, place, when=ready, head=at.xn)
        self.spread(ready)

    def spread(self, ready):
        at, place = self.at, self.place(self.at.c, self.part)
        for z in at.others():
            self.lanes.put(self.zg + self.part, place, place, when=ready, blk=z)
        self.lanes.put(self.cg + self.part, place, place, when=ready, head=at.sib)

    def take_over(self):
        ready = self.summer & self.giver
        self.lanes.arrived(self.xg, self.place(self.at.c, self.part), when=ready, head=self.at.xn)
        self.spread(ready)

    def pass_on(self):
        at = self.at
        for p in range(self.PARTS):
            place, later = self.place(at.c, p), at.z != p
            self.lanes.arrived(self.zg + p, place, when=later, blk=p)
            self.lanes.put(self.cg + p, place, place, when=later, head=at.sib)

    def finish(self):
        at = self.at
        for p in range(self.PARTS):
            self.lanes.arrived(self.cg + p, self.place(1 - at.c, p), head=at.sib)


def back_kernel(attn_ref, q_ref, ot_ref, start_ref, lse_ref, x_ref, cos_ref, sin_ref, gain_ref, small_ref,
                kv_in, wo_hbm, grads_hbm, y_in, res_hbm, res_grad_hbm, n1_hbm, w_hbm,
                block_out, tokens_out, small_out, kv_out, experts_out, output_out, query_out, y_land, *rest):
    blocks = kv_in.shape[0]
    big = blocks > 4
    dkv_stage = dwo_stage = None
    if big:
        yp_ref, dkv_land, dkv_sib, dwo_z, kv_ref, dkv_stage, dwo_stage, y_stage, kv_stage, *rest = rest
    else:
        yp_ref, dkv_land, dkv_sib, dwo_z, kv_ref, *rest = rest
    (dq_ref, dk_ref, dv_ref, kt_ref, delta_ref, do_ref, ag_ref, wo_ref, dwo_ref, dwo_y, dwo_land,
     own_ref, ey_ref, ex_ref, acc_ref, y_other, w_ref, dpre_ref, dn_sib, dn_x, dw_ref, dw_y, dw_z,
     sm_ref, sm_a, sm_b, sm_y, sm_z, land_ref, dkv_ref, n1t_ref, load_sem, keep_sem, send_sem, recv_sem) = rest
    heads, rows, _ = q_ref.shape
    own_rows, width = attn_ref.shape
    half = width // 2
    qcols = heads * HEAD
    gain_row = 2 * blocks
    at = Place(blocks)
    me = at.z
    lanes = Lanes(send_sem, recv_sem)
    at.enter()
    experts = ExpertSums(at, lanes, grads_hbm, own_ref, ey_ref, ex_ref, experts_out, load_sem, keep_sem)
    output = OutputSums(at, lanes, dwo_ref, dwo_y, dwo_z, dwo_land)
    sums = ColumnSum(at, lanes, yp_ref, y_land)
    experts.load()
    forward, near, far, passed = gather_heads(at, lanes, attn_ref, ag_ref)

    def load(src, dst, sem):
        copy = pltpu.make_async_copy(src, dst, load_sem.at[sem])
        copy.start()
        return copy

    def move(src, dst):
        load(src, dst, 5).wait()

    wo_load = load(wo_hbm.at[aligned(at.h * qcols, qcols), :], wo_ref, 2)
    y_load = load(y_in, yp_ref, 3)
    if not big:
        kv_load = load(kv_in, kv_ref, 4)
    experts.to_y(0, 6)
    y_load.wait()
    for b in range(blocks):
        sums.first_send(b)

    def add(b, band):
        move(y_land.at[b, band, :], y_other.at[band, :])
        if big:
            move(yp_ref.at[b, band, :], y_stage.at[band, :])
            y_stage[band, :] = (y_stage[band, :].astype(F32) + y_other[band, :].astype(F32)).astype(BF16)
            move(y_stage.at[band, :], yp_ref.at[b, band, :])
        else:
            yp_ref[b, band, :] = (yp_ref[b, band, :].astype(F32) + y_other[band, :].astype(F32)).astype(BF16)

    def fetch(stage):
        def get(ref):
            if big:
                move(ref, stage)
                return stage
            return ref
        return get

    wo_load.wait()

    def mix_back(head):
        band = aligned(head * own_rows, own_rows)
        grad = mm(ag_ref[band, :], wo_ref[...], NT).astype(BF16)
        for hh in range(heads):
            do_ref[hh, band, :] = grad[:, hh * HEAD:(hh + 1) * HEAD]

    def turn(i):
        band = slice(i * own_rows, (i + 1) * own_rows)
        move(n1_hbm.at[band, :], y_other)
        n1t_ref[:, band] = y_other[...].astype(F32).T.astype(BF16)

    ag_ref[aligned(at.h * own_rows, own_rows), :] = attn_ref[...]
    mix_back(at.h)
    turn(0)
    near()
    mix_back(at.sib)
    for i in range(1, rows // own_rows):
        turn(i)
    experts.to_x(0)
    forward()
    mix_back(at.xn)
    far()
    mix_back(at.xs)
    step = 512

    def weight_back(i, _):
        cols = pl.ds(pl.multiple_of(i * step, step), step)
        dwo_ref[:, cols] = mm(ot_ref[...], ag_ref[:, cols]).astype(BF16)
        return 0

    lax.fori_loop(0, width // step, weight_back, 0)
    output.to_z()
    kv_from = pl.ds(pl.multiple_of(qcols + at.c * HEAD, HEAD), HEAD)
    w_loads = [load(w_hbm.at[:, :qcols], w_ref.at[:, :qcols], 2), load(w_hbm.at[:, kv_from], w_ref.at[:, qcols:], 3)]
    dq_ref[...] = jnp.zeros_like(dq_ref)
    for hh in range(heads):
        prod = do_ref[hh].astype(F32).T * ot_ref[hh * HEAD:(hh + 1) * HEAD, :].astype(F32)
        delta_ref[hh] = jnp.sum(prod, axis=0, keepdims=True)
    if not big:
        kv_load.wait()

    experts.to_x(1)
    beside = [[(experts.to_x, 2), (experts.share, 0)],
              [(experts.to_x, 3), (experts.share, 1)],
              [(experts.to_x, 4), (experts.share, 2)]]

    def advance():
        for f, k in (beside.pop(0) if beside else ()):
            f(k)

    def opening(b):
        if big:
            move(kv_in.at[b], kv_stage)
        kv = kv_stage if big else kv_ref.at[b]
        kt_ref[...] = kv[0].astype(F32).T.astype(BF16)
        dk_ref[...] = jnp.zeros_like(dk_ref)
        dv_ref[...] = jnp.zeros_like(dv_ref)
        return kv

    def closing(b, kv):
        kv[0] = (dk_ref[...] * LN2).astype(BF16)
        kv[1] = dv_ref[...].astype(BF16)
        if big:
            move(kv_stage, kv_ref.at[b])

    def block(b):
        kv = opening(b)

        def tile(t, _):
            hh, i = t // (rows // TILE), t % (rows // TILE)
            cols = pl.ds(pl.multiple_of(i * TILE, TILE), TILE)
            unattend_tile(hh, cols, kv[0], kv[1], kt_ref[...], q_ref, do_ref,
                          start_ref, lse_ref, delta_ref, dq_ref, dk_ref, dv_ref, b * rows, None)
            return 0

        lax.fori_loop(0, heads * (rows // TILE), tile, 0)
        closing(b, kv)

    pair, column = lanes.slots(blocks), lanes.slots(blocks)

    def to_sibling(b, when):
        lanes.put(pair + b, kv_ref.at[b, 1 - at.c], dkv_sib.at[b], when=when, head=at.sib)

    def to_column(b):
        lanes.arrived(pair + b, dkv_sib.at[b], when=b < me, head=at.sib)

        @pl.when(b < me)
        def _():
            came = fetch(dkv_stage)(dkv_sib.at[b])
            if big:
                move(kv_ref.at[b, at.c], kv_stage.at[at.c])
            kv = kv_stage if big else kv_ref.at[b]
            kv[at.c] = (kv[at.c].astype(F32) + came[...].astype(F32)).astype(BF16)
            if big:
                move(kv_stage.at[at.c], kv_ref.at[b, at.c])

        lanes.put(column + me, kv_ref.at[b, at.c], dkv_land.at[me], when=b < me, blk=b)

    for b in range(blocks - 1):
        pl.when(b < me)(functools.partial(block, b))
        to_sibling(b, b < me)
        sums.relay(0, b + 1, add)
        advance()
        if b > 0:
            to_column(b - 1)
    while beside:
        advance()
    to_column(blocks - 2)

    kv_own = opening(me)
    for i in range(rows // TILE):
        n = (i + 1) * TILE

        def diagonal(hh, _, i=i, n=n):
            unattend_tile(hh, slice(i * TILE, n), kv_own[0, :n, :], kv_own[1, :n, :], kt_ref[:, :n], q_ref, do_ref,
                          start_ref, lse_ref, delta_ref, dq_ref, dk_ref, dv_ref,
                          me * rows, me * rows + i * TILE)
            return 0

        lax.fori_loop(0, heads, diagonal, 0)
    closing(me, kv_own)
    to_sibling(me, None)
    experts.to_x(5)
    output.to_y(fetch(dwo_stage))
    for d in range(1, blocks):
        sums.relay(1, d, add)

    def unrotate(u):
        return u * cos_ref[...] - pltpu.roll(u, HEAD // 2, 1) * sin_ref[...]

    for hh in range(heads):
        dpre_ref[:, hh * HEAD:(hh + 1) * HEAD] = unrotate((dq_ref[hh] * SCORE_SCALE).T).astype(BF16)
    for w_load in w_loads:
        w_load.wait()
    parts = 4
    part = half // parts
    band_rows = 256
    query_cols, keyval_cols = slice(0, qcols), slice(qcols, qcols + HEAD)

    def weight_half(y, cols_out):
        def body(i, _):
            band = aligned(y * half + i * band_rows, band_rows)
            dw_ref[band, cols_out] = mm(n1t_ref[band, :], dpre_ref[:, cols_out]).astype(BF16)
            return 0

        lax.fori_loop(0, half // band_rows, body, 0)

    def weight_part(y, p):
        return aligned(y * half + p * part, part)

    ys = (lanes.slots(parts), lanes.slots(parts))

    def weight_to_y(i, cols_out):
        weight_half(at.oy, cols_out)
        for p in range(parts):
            lanes.put(ys[i] + p, dw_ref.at[weight_part(at.oy, p), cols_out],
                      dw_y.at[pl.ds(p * part, part), cols_out], fsdp=at.oy)

    weight_to_y(0, query_cols)
    experts.share(3)

    @pl.when(at.c == 0)
    def _():
        dkv_ref[...] = dk_ref[...] * LN2

    @pl.when(at.c == 1)
    def _():
        dkv_ref[...] = dv_ref[...]

    lanes.arrived(pair + me, dkv_sib.at[me], head=at.sib)
    dkv_ref[...] += fetch(dkv_stage)(dkv_sib.at[me])[...].astype(F32)
    for z in range(1, blocks):
        @pl.when(me < z)
        def _(z=z):
            lanes.arrived(column + z, dkv_land.at[z], blk=z)
            dkv_ref[...] += fetch(dkv_stage)(dkv_land.at[z])[...].astype(F32)

    dpre_ref[:, qcols:] = jnp.where(at.c == 0, unrotate(dkv_ref[...]), dkv_ref[...]).astype(BF16)
    weight_to_y(1, keyval_cols)
    experts.to_y(6, 8)
    output.share()

    def input_part(head):
        return mm(dpre_ref[aligned(head * own_rows, own_rows), :], w_ref[...], NT)

    lanes.settle(passed[0])

    def dn_ref(i):
        return ag_ref.at[i * own_rows:(i + 1) * own_rows, :]

    relay, direct, across = lanes.slots(), lanes.slots(), lanes.slots()
    dn_ref(0)[...] = input_part(at.xs).astype(BF16)
    lanes.put(relay, dn_ref(0), dn_sib.at[0], head=at.sib)
    dn_ref(2)[...] = input_part(at.sib).astype(BF16)
    lanes.put(direct, dn_ref(2), dn_sib.at[1], head=at.sib)
    lanes.arrived(relay, dn_sib.at[0], head=at.sib)
    dn_ref(1)[...] = (input_part(at.xn) + dn_sib[0].astype(F32)).astype(BF16)
    lanes.put(across, dn_ref(1), dn_x, head=at.xn)
    experts.share(4)
    weight_half(at.y, slice(None))
    output.take_over()

    zr = lanes.slots(blocks)
    for p in range(parts):
        rows_p = weight_part(at.y, p)
        for i, cols_out in enumerate((query_cols, keyval_cols)):
            lanes.arrived(ys[i] + p, dw_y.at[pl.ds(p * part, part), cols_out], fsdp=at.oy)
        total = dw_ref[rows_p, :].astype(F32) + dw_y[pl.ds(p * part, part), :].astype(F32)
        dw_ref[rows_p, :] = total.astype(BF16)
        lanes.put(zr + at.z, dw_ref.at[rows_p, :], dw_z.at[at.z], when=at.z != p, blk=p)
    experts.to_x(6)
    experts.share(5)

    move(res_hbm, acc_ref)
    if big:
        move(yp_ref.at[me], y_stage)
    acc_ref[...] += (y_stage if big else yp_ref.at[me])[...].astype(F32)

    def take(slot):
        move(y_land.at[slot], y_other)
        acc_ref[...] += y_other[...].astype(F32)

    for side in range(2):
        sums.arrive(side, take)
    block_out[...] = acc_ref[...].astype(BF16)

    res_load = load(res_grad_hbm, acc_ref, 5)
    own = input_part(at.h)
    lanes.arrived(direct, dn_sib.at[1], head=at.sib)
    own = own + dn_sib[1].astype(F32)
    lanes.arrived(across, dn_x, head=at.xn)
    own = own + dn_x[...].astype(F32)
    x = x_ref[...].astype(F32)
    inv = lax.rsqrt(jnp.mean(x * x, axis=-1, keepdims=True) + NORM_EPSILON)
    hat = x * inv
    pulled = own * gain_ref[gain_row:gain_row + 1, :].astype(F32)
    slope = inv * (pulled - hat * jnp.mean(pulled * hat, axis=-1, keepdims=True))
    res_load.wait()
    tokens_out[...] = (acc_ref[...] + slope).astype(BF16)
    sm_ref[...] = small_ref[...]
    sm_ref[gain_row:gain_row + 1, :] = jnp.sum(own * hat, axis=0, keepdims=True)
    sa, sb, sy, sz = lanes.slots(), lanes.slots(), lanes.slots(), lanes.slots(blocks)
    lanes.put(sa, sm_ref, sm_a, head=at.sib)
    experts.to_x(7)
    experts.share(6)

    p = at.z % parts
    summer = at.z < parts
    zg, xg, cg, cf = lanes.slots(parts), lanes.slots(parts), lanes.slots(parts), lanes.slots(parts)

    def place(head, q):
        return land_ref.at[head, pl.ds(q * part, part), :]

    for z in at.others():
        lanes.arrived(zr + z, dw_z.at[z], when=summer, blk=z)
    mine_w = weight_part(at.y, p)

    @pl.when(summer)
    def _():
        total = dw_ref[mine_w, :].astype(F32)
        for z in at.others():
            total = total + dw_z[z].astype(F32)
        dw_ref[mine_w, :] = total.astype(BF16)
        land_ref[at.h, aligned(p * part, part), :] = total.astype(BF16)

    for z in at.others():
        lanes.put(zg + p, dw_ref.at[mine_w, :], place(at.h, p), when=summer, blk=z)
    lanes.put(xg + p, dw_ref.at[mine_w, :], place(at.h, p), when=summer, head=at.xn)
    lanes.put(cg + p, dw_ref.at[mine_w, :], place(at.h, p), when=summer, head=at.sib)
    lanes.arrived(sa, sm_a, head=at.sib)
    sm_a[...] = sm_a[...] + sm_ref[...]
    lanes.put(sb, sm_a, sm_b, head=at.xn)
    experts.share(7)

    lanes.arrived(sb, sm_b, head=at.xn)
    sm_b[...] = sm_a[...] + sm_b[...]
    mine_cols = pl.ds(pl.multiple_of(at.y * half, half), half)
    other_cols = pl.ds(pl.multiple_of(at.oy * half, half), half)
    lanes.put(sy, sm_b.at[:, other_cols], sm_y, fsdp=at.oy)
    for q in range(parts):
        later = at.z != q
        lanes.arrived(zg + q, place(at.h, q), when=later, blk=q)
        lanes.put(xg + q, place(at.h, q), place(at.h, q), when=later, head=at.xn)
        lanes.put(cg + q, place(at.h, q), place(at.h, q), when=later, head=at.sib)
    lanes.arrived(sy, sm_y, fsdp=at.oy)
    sm_z[at.z] = sm_b[:, mine_cols] + sm_y[...]
    for z in at.others():
        lanes.put(sz + at.z, sm_z.at[at.z], sm_z.at[at.z], blk=z)
    output.pass_on()
    for q in range(parts):
        lanes.arrived(xg + q, place(at.xn, q), head=at.xn)
        lanes.put(cf + q, place(at.xn, q), place(at.xn, q), head=at.sib)
    for z in at.others():
        lanes.arrived(sz + z, sm_z.at[z], blk=z)
    total = sm_z[0]
    for z in range(1, blocks):
        total = total + sm_z[z]
    small_out[...] = total
    output.finish()
    keeps = [load(dwo_land, output_out, 0)]
    for q in range(parts):
        lanes.arrived(cg + q, place(at.sib, q), head=at.sib)
        lanes.arrived(cf + q, place(at.xs, q), head=at.sib)
    for head in range(4):
        keeps.append(load(land_ref.at[head, :, :qcols], query_out.at[:, head * qcols:(head + 1) * qcols], 1 + head))
        column_of = (head % 2 * KEYVALUE_HEADS + head // 2) * HEAD
        keeps.append(load(land_ref.at[head, :, qcols:], kv_out.at[:, column_of:column_of + HEAD], 6 + head))
    experts.finish()
    for keep in keeps:
        keep.wait()
    sums.finish()
    lanes.drain()


def backward(attn_grad, q, ot, start, lse, x, cosine, sine, gain, small, kv, wo, grads, y_parts, res, res_grad, n1, w):
    heads, rows, _ = q.shape
    blocks = kv.shape[0]
    own_rows, width = attn_grad.shape
    qcols = heads * HEAD
    _, half, wide = grads.shape
    cols = qcols + HEAD
    srows = small.shape[0]
    n = ExpertSums.CHUNKS
    vm = pl.BlockSpec(memory_space=pltpu.VMEM)
    hbm = pl.BlockSpec(memory_space=pl.ANY)
    part = qcols // OutputSums.PARTS
    sds = jax.ShapeDtypeStruct
    column = [((blocks, own_rows, width), BF16), ((blocks, rows, HEAD), BF16),
              ((blocks, rows, HEAD), BF16), ((blocks, part, width), BF16), (kv.shape, BF16)]
    if blocks > 4:
        extra_out, extra_spec = tuple(sds(*c) for c in column), [hbm] * 5
        extra_scratch = [pltpu.VMEM((rows, HEAD), BF16), pltpu.VMEM((part, width), BF16),
                         pltpu.VMEM((own_rows, width), BF16), pltpu.VMEM((2, rows, HEAD), BF16)]
    else:
        extra_out, extra_spec = (), []
        extra_scratch = [pltpu.VMEM(*c) for c in column]
    return pl.pallas_call(
        back_kernel,
        out_shape=(
            sds((own_rows, width), BF16),
            sds((own_rows, width), BF16),
            sds((srows, half), F32),
            sds((half, 2 * KEYVALUE_HEADS * HEAD), BF16),
            sds((2, half, wide), BF16),
            sds((2 * qcols, width), BF16),
            sds((half, rows // own_rows * qcols), BF16),
            sds((blocks + 1, own_rows, width), BF16),
        ) + extra_out,
        in_specs=[vm] * 10 + [hbm] * 8,
        out_specs=[vm] * 3 + [hbm] * 5 + extra_spec,
        scratch_shapes=extra_scratch + [
            pltpu.VMEM((heads, HEAD, rows), F32),
            pltpu.VMEM((rows, HEAD), F32),
            pltpu.VMEM((rows, HEAD), F32),
            pltpu.VMEM((HEAD, rows), BF16),
            pltpu.VMEM((heads, 1, rows), F32),
            pltpu.VMEM((heads, rows, HEAD), BF16),
            pltpu.VMEM((rows, width), BF16),
            pltpu.VMEM((qcols, width), BF16),
            pltpu.VMEM((qcols, width), BF16),
            pltpu.VMEM((part, width), BF16),
            pltpu.VMEM((2 * qcols, width), BF16),
            pltpu.VMEM((2, half, wide), BF16),
            pltpu.VMEM((half, wide), BF16),
            pltpu.VMEM((half, wide), BF16),
            pltpu.VMEM((own_rows, width), F32),
            pltpu.VMEM((own_rows, width), BF16),
            pltpu.VMEM((width, cols), BF16),
            pltpu.VMEM((rows, cols), BF16),
            pltpu.VMEM((2, own_rows, width), BF16),
            pltpu.VMEM((own_rows, width), BF16),
            pltpu.VMEM((width, cols), BF16),
            pltpu.VMEM((half, cols), BF16),
            pltpu.VMEM((blocks, half // 4, cols), BF16),
            pltpu.VMEM((srows, width), F32),
            pltpu.VMEM((srows, width), F32),
            pltpu.VMEM((srows, width), F32),
            pltpu.VMEM((srows, half), F32),
            pltpu.VMEM((blocks, srows, half), F32),
            pltpu.VMEM((rows // own_rows, half, cols), BF16),
            pltpu.VMEM((rows, HEAD), F32),
            pltpu.VMEM((width, rows), BF16),
            pltpu.SemaphoreType.DMA((10,)),
            pltpu.SemaphoreType.DMA((n,)),
        ] + semaphores(blocks),
        compiler_params=pltpu.CompilerParams(
            vmem_limit_bytes=VMEM_BYTES, collective_id=2, has_side_effects=True),
    )(attn_grad, q, ot, start, lse, x, cosine, sine, gain, small, kv, wo, grads, y_parts, res, res_grad, n1, w)[:7]


def on_device(tokens, documents, routes, cotangent, first_gain, query_weight, keyvalue_weight, output_weight,
              second_gain, router_weight, expert_in, expert_out):
    z = lax.axis_index("blk")
    blocks = lax.axis_size("blk")
    rows, width = tokens.shape[1:]
    group = lax.axis_size("head") * rows
    experts = router_weight.shape[1]
    half = query_weight.shape[0]

    small_rows = -(-(2 + experts) // 16) * 16
    small = jnp.concatenate([router_weight.T, first_gain[None], second_gain[None],
                             jnp.zeros((small_rows - 2 - experts, half), BF16)], axis=0)
    pos = (z * group + jnp.arange(group, dtype=jnp.int32)).astype(F32)
    inverse = jnp.power(ROPE_BASE, -jnp.arange(HEAD // 2).astype(F32) * 2.0 / HEAD)
    angle = pos[:, None] * inverse[None, :]
    cos, sin = jnp.cos(angle), jnp.sin(angle)
    cosine = jnp.concatenate([cos, cos], axis=-1)
    sine = jnp.concatenate([-sin, sin], axis=-1)
    doc = documents[0]
    doc_q = lax.dynamic_slice_in_dim(doc, z * group, group, 0)
    start = sum(jnp.where(doc_q > d, jnp.sum((doc == d).astype(jnp.int32)), 0) for d in range(DOCUMENTS - 1))[None, :]
    chosen = jnp.any(routes[0][:, :, None] == jnp.arange(LANES, dtype=jnp.int32), axis=1).astype(F32)

    mixed, mixed_t, lse, small, q, n1, wqkv, kv_all, wo, w_experts, cots = front(
        blocks, tokens[0], small, query_weight, keyvalue_weight, output_weight, expert_in, expert_out,
        cotangent[0], cosine, sine, start)
    res1, res_grad, attn_grad, d_small, grads, y_parts = expert_layer(
        mixed, tokens[0], small, chosen, wo, w_experts, cots)
    block_out, tokens_grad, d_small, d_keyval, d_experts, d_wo, d_query = backward(
        attn_grad, q, mixed_t, start, lse, tokens[0], cosine, sine, small, d_small,
        kv_all, wo, grads, y_parts, res1, res_grad, n1, wqkv)
    return (block_out[None], tokens_grad[None], d_small[experts], d_query.astype(F32), d_keyval.astype(F32), d_wo.astype(F32),
            d_small[experts + 1], d_small[:experts].T, d_experts[:, :, :width].astype(F32),
            d_experts[:, :, width:].astype(F32))


def solution(mesh):
    token_spec = P("fsdp", ("blk", "head"), None)
    row_spec = P("fsdp", None)
    in_spec = P("blk", "fsdp", None)
    out_spec = P("blk", None, "fsdp")
    return jax.shard_map(
        on_device,
        mesh=mesh,
        in_specs=(token_spec, row_spec, token_spec, token_spec, P("fsdp"), row_spec, row_spec, row_spec, P("fsdp"),
                  row_spec, in_spec, out_spec),
        out_specs=(token_spec, token_spec, P("fsdp"), row_spec, row_spec, row_spec, P("fsdp"), row_spec, in_spec,
                   out_spec),
        check_vma=False,
    )
```

```python
import functools

import jax
import jax.numpy as jnp
from jax import lax
from jax.experimental import pallas as pl
from jax.experimental.pallas import tpu as pltpu
from jax.sharding import PartitionSpec as P

QUERY_HEADS = 12
KEYVALUE_HEADS = 2
HEAD = 128
NORM_EPSILON = 1e-06
ROPE_BASE = 1000000.0
MASKED = -1e30
DOCUMENTS = 4
LOG2E = 1.4426950408889634
SCORE_LOG2 = HEAD ** (-0.5) * LOG2E
SCORE_SCALE = HEAD ** (-0.5)
LN2 = 1.0 / LOG2E
TILE = 256
BF16 = jnp.bfloat16
F32 = jnp.float32
VMEM_BYTES = 63 * 1024 * 1024

NN = (((1,), (0,)), ((), ()))
NT = (((1,), (1,)), ((), ()))
TN = (((0,), (0,)), ((), ()))


def mm(a, b, dims=NN):
    return lax.dot_general(a, b, dims, preferred_element_type=F32)


def gelu_parts(gate):
    c = 0.7978845608028654
    cube = 0.044715 * gate * gate * gate
    t = jnp.tanh(c * (gate + cube))
    value = 0.5 * gate * (1.0 + t)
    slope = 0.5 * (1.0 + t) + 0.5 * gate * (1.0 - t * t) * c * (1.0 + 3.0 * 0.044715 * gate * gate)
    return value, slope


def score_tile(key_rows, q_tile, start_row, first_key, q_first):
    scores = mm(key_rows, q_tile, NT)
    key_row = lax.broadcasted_iota(jnp.int32, scores.shape, 0)
    allowed = key_row >= start_row - first_key
    if q_first is not None:
        allowed = allowed & (key_row - lax.broadcasted_iota(jnp.int32, scores.shape, 1) <= q_first - first_key)
    return jnp.where(allowed, scores, MASKED)


def attend_tile(hh, cols, key_rows, value_cols, q_ref, start_ref, m_ref, l_ref, acc_ref, first_key, q_first):
    q_tile = q_ref[hh, cols, :]
    scores = score_tile(key_rows, q_tile, start_ref[:, cols], first_key, q_first)
    old = m_ref[hh, :, cols]
    new = jnp.maximum(old, jnp.max(scores, axis=0, keepdims=True))
    factor = jnp.exp2(old - new)
    prob = jnp.exp2(scores - new)
    m_ref[hh, :, cols] = new
    l_ref[hh, :, cols] = l_ref[hh, :, cols] * factor + jnp.sum(prob, axis=0, keepdims=True)
    acc_ref[hh, :, cols] = acc_ref[hh, :, cols] * factor + mm(value_cols, prob.astype(BF16))


def unattend_tile(hh, cols, key_rows, value_rows, key_cols, q_ref, do_ref, start_ref, lse_ref, delta_ref,
                  dq_ref, dk_ref, dv_ref, first_key, q_first):
    n = key_rows.shape[0]
    q_tile = q_ref[hh, cols, :]
    do_tile = do_ref[hh, cols, :]
    scores = score_tile(key_rows, q_tile, start_ref[:, cols], first_key, q_first)
    prob = jnp.exp2(scores - lse_ref[hh, :, cols])
    dv_ref[:n, :] += mm(prob.astype(BF16), do_tile)
    prob_grad = mm(value_rows, do_tile, NT)
    score_grad = (prob * (prob_grad - delta_ref[hh, :, cols])).astype(BF16)
    dk_ref[:n, :] += mm(score_grad, q_tile)
    dq_ref[hh, :, cols] += mm(key_cols, score_grad)


def remote(src, dst, send_sem, recv_sem, **to):
    return pltpu.make_async_remote_copy(
        src_ref=src, dst_ref=dst, send_sem=send_sem, recv_sem=recv_sem, device_id=to,
        device_id_type=pl.DeviceIdType.MESH)


class Lanes:
    def __init__(self, send, recv):
        self.send, self.recv, self.used, self.sent, self.pending = send, recv, 0, 0, []

    def slots(self, count=1):
        first = self.used
        self.used += count
        assert self.used <= self.recv.shape[0]
        return first

    def sends(self, count):
        first = self.sent
        self.sent += count
        assert self.sent <= self.send.shape[0]
        return first

    def put(self, slot, src, dst, when=None, **to):
        assert self.sent < self.send.shape[0]
        copy = remote(src, dst, self.send.at[self.sent], self.recv.at[slot], **to)
        self.sent += 1
        if when is None:
            copy.start()
        else:
            pl.when(when)(copy.start)
        self.pending.append((copy, when))
        return self.pending[-1]

    def settle(self, entry):
        copy, when = entry
        self.pending = [other for other in self.pending if other is not entry]
        if when is None:
            copy.wait_send()
        else:
            pl.when(when)(copy.wait_send)

    def arrived(self, slot, dst, when=None, **origin):
        copy = remote(dst, dst, self.send.at[0], self.recv.at[slot], **origin)
        if when is None:
            copy.wait_recv()
        else:
            pl.when(when)(copy.wait_recv)

    def drain(self):
        for copy, when in self.pending:
            if when is None:
                copy.wait_send()
            else:
                pl.when(when)(copy.wait_send)
        self.pending = []


class Place:
    def __init__(self, blocks):
        self.z, self.h, self.y = lax.axis_index("blk"), lax.axis_index("head"), lax.axis_index("fsdp")
        self.blocks = blocks
        self.x, self.c = self.h // 2, self.h % 2
        self.sib = 2 * self.x + 1 - self.c
        self.xn = 2 * (1 - self.x) + self.c
        self.xs = 2 * (1 - self.x) + 1 - self.c
        self.oy = 1 - self.y

    def others(self):
        return [(self.z + d) % self.blocks for d in range(1, self.blocks)]

    def enter(self):
        barrier = pltpu.get_barrier_semaphore()

        def greet(**to):
            pl.semaphore_signal(barrier, inc=1, device_id=to, device_id_type=pl.DeviceIdType.MESH)

        for head in (self.sib, self.xn, self.xs):
            greet(head=head)
        greet(fsdp=self.oy)
        for z in self.others():
            greet(blk=z)
        pl.semaphore_wait(barrier, 4 + self.blocks - 1)


def gather_heads(at, lanes, own, land):
    s = lanes.slots(3)
    rows = own.shape[0]

    def slot(head):
        return land.at[pl.ds(pl.multiple_of(head * rows, rows), rows), :]

    lanes.put(s, own, slot(at.h), head=at.xn)
    lanes.put(s + 1, own, slot(at.h), head=at.sib)

    passed = []

    def forward():
        lanes.arrived(s, slot(at.xn), head=at.xn)
        passed.append(lanes.put(s + 2, slot(at.xn), slot(at.xn), head=at.sib))

    def near():
        lanes.arrived(s + 1, slot(at.sib), head=at.sib)

    def far():
        lanes.arrived(s + 2, slot(at.xs), head=at.sib)

    return forward, near, far, passed


def aligned(index, size):
    return pl.ds(pl.multiple_of(index, 16), size)


def semaphores(blocks):
    count = 128 + 16 * blocks
    return [pltpu.SemaphoreType.DMA((count,)), pltpu.SemaphoreType.DMA((count,))]


class Shared:
    def __init__(self, at, lanes, chunks, give, hold):
        self.at, self.lanes, self.chunks, self.give, self.hold = at, lanes, chunks, give, hold
        self.pieces = len(give(0)) if give else 0
        self.ys = lanes.slots(chunks * self.pieces)
        self.xn, self.sib, self.far = lanes.slots(chunks), lanes.slots(chunks), lanes.slots(chunks)
        self.sent = []

    def begin(self, k):
        for i, (src, dst) in enumerate(self.give(k)):
            self.lanes.put(self.ys + k * self.pieces + i, src, dst(self.at.y), fsdp=self.at.oy)

    def landed(self, k):
        for i, (src, dst) in enumerate(self.give(k)):
            self.lanes.arrived(self.ys + k * self.pieces + i, dst(self.at.oy), fsdp=self.at.oy)

    def spread(self, k):
        self.landed(k)
        self.scatter(k)

    def scatter(self, k):
        at = self.at
        place = self.hold(k, at.h, at.oy)
        self.sent.append(self.lanes.put(self.xn + k, place, place, head=at.xn))
        self.sent.append(self.lanes.put(self.sib + k, place, place, head=at.sib))

    def forward(self, k):
        at = self.at
        place = self.hold(k, at.xn, at.oy)
        self.lanes.arrived(self.xn + k, place, head=at.xn)
        self.sent.append(self.lanes.put(self.far + k, place, place, head=at.sib))

    def settle(self):
        for entry in self.sent:
            self.lanes.settle(entry)

    def finish(self, k):
        at = self.at
        self.lanes.arrived(self.sib + k, self.hold(k, at.sib, at.oy), head=at.sib)
        self.lanes.arrived(self.far + k, self.hold(k, at.xs, at.oy), head=at.sib)


def weight_chunk(w_ref, k, head, y):
    quarter = w_ref.shape[2] // 4
    piece = quarter // 2
    return w_ref.at[k // 2, y, aligned(head * quarter + k % 2 * piece, piece), :]


class Column:
    def __init__(self, at, lanes, land):
        self.at, self.lanes, self.land = at, lanes, land
        self.slot = lanes.slots(at.blocks)

    def begin(self, own):
        at = self.at
        place = self.land.at[at.z]
        self.lanes.put(self.slot + at.z, own, place, when=at.z < at.blocks - 1, blk=at.z + 1)
        self.lanes.put(self.slot + at.z, own, place, when=at.z > 0, blk=at.z - 1)

    def hand_on(self, d):
        at = self.at
        for b, origin, next_z in ((at.z - d, at.z - 1, at.z + 1), (at.z + d, at.z + 1, at.z - 1)):
            there = (b >= 0) & (b < at.blocks)
            safe = jnp.clip(b, 0, at.blocks - 1)
            self.lanes.arrived(self.slot + safe, self.land.at[safe], when=there, blk=origin)
            self.lanes.put(self.slot + safe, self.land.at[safe], self.land.at[safe],
                           when=there & (next_z >= 0) & (next_z < at.blocks), blk=next_z)


def front_kernel(x_ref, small_ref, wq_hbm, wkv_hbm, wo_hbm, win_hbm, wout_hbm, cot_hbm, cos_ref, sin_ref, start_ref,
                 o_ref, ot_ref, lse_ref, small_out, q_out, n1_out, wqkv_out, kv_out, wo_out, w_out, cot_out,
                 q_ref, n1_ref,
                 xg_ref, small_land, wqkv_ref, kv_ref, m_ref, l_ref, acc_ref, vt_ref, wo_ref, w_ref, cot_ref,
                 load_sem, send_sem, recv_sem):
    heads, rows, _ = q_ref.shape
    own_rows, width = x_ref.shape
    blocks = kv_ref.shape[0]
    half = wq_hbm.shape[0]
    qcols = heads * HEAD
    experts = 2 * blocks
    at = Place(blocks)
    me = at.z
    lanes = Lanes(send_sem, recv_sem)
    at.enter()
    local = []

    def copy_here(src, dst):
        copy = pltpu.make_async_copy(src, dst, load_sem.at[len(local)])
        copy.start()
        local.append(copy)
        return copy

    forward, near, far, _ = gather_heads(at, lanes, x_ref, xg_ref)
    g = at.x
    q_from = pl.ds(pl.multiple_of(at.h * qcols, HEAD), qcols)
    kv_from = pl.ds(pl.multiple_of((at.c * KEYVALUE_HEADS + g) * HEAD, HEAD), HEAD)

    def kv_cols(core):
        return pl.ds(pl.multiple_of(qcols + core * HEAD, HEAD), HEAD)

    columns = ((wq_hbm.at[:, q_from], slice(0, qcols)), (wkv_hbm.at[:, kv_from], kv_cols(at.c)))

    def weight_rows(y, cols):
        return wqkv_ref.at[aligned(y * half, half), cols]

    ws, wc = lanes.slots(2), lanes.slots()
    for i, (src, cols) in reversed(list(enumerate(columns))):
        lanes.put(ws + i, src, weight_rows(at.y, cols), fsdp=at.oy)
    smalls = lanes.slots()
    lanes.put(smalls, small_ref, small_land, fsdp=at.oy)
    kv_other = pl.ds(pl.multiple_of(((1 - at.c) * KEYVALUE_HEADS + g) * HEAD, HEAD), HEAD)
    own_weights = [copy_here(src, weight_rows(at.y, cols))
                   for src, cols in columns + ((wkv_hbm.at[:, kv_other], kv_cols(1 - at.c)),)]
    cots = Column(at, lanes, cot_ref)
    own_half = pl.ds(pl.multiple_of(at.y * half, half), half)
    cot_load = copy_here(cot_hbm, cot_ref.at[me])
    wo_load = copy_here(wo_hbm, wo_ref.at[own_half, :])
    w_loads = [copy_here(win_hbm, w_ref.at[:, at.y, :, :width]), copy_here(wout_hbm, w_ref.at[:, at.y, :, width:])]
    cot_load.wait()
    cots.begin(cot_ref.at[me])

    quarter = half // 4

    def wo_place(k, head, y):
        return wo_ref.at[aligned(y * half + head * quarter, quarter), :]

    shared_wo = Shared(at, lanes, 1,
                       lambda k: [(wo_place(0, at.h, at.y), lambda y: wo_place(0, at.h, y))],
                       wo_place)
    chunks, spread_here = 4, 2

    def w_place(k, head, y):
        return weight_chunk(w_ref, k, head, y)

    def w_give(k):
        return [(w_place(k, at.h, at.y), lambda y: w_place(k, at.h, y))]

    shared_w = Shared(at, lanes, chunks, w_give, w_place)

    small_out[:, :half] = jnp.zeros((small_ref.shape[0], half), BF16)
    lanes.arrived(smalls, small_land, fsdp=at.oy)
    for y in range(2):
        @pl.when(at.y == y)
        def _(y=y):
            small_out[:, y * half:(y + 1) * half] = small_ref[...]
            small_out[:, (1 - y) * half:(2 - y) * half] = small_land[...]

    def norm(head, block):
        x = block.astype(F32)
        inv = lax.rsqrt(jnp.mean(x * x, axis=-1, keepdims=True) + NORM_EPSILON)
        n1_ref[aligned(head * own_rows, own_rows), :] = (x * inv * small_out[experts:experts + 1, :].astype(F32)).astype(BF16)

    def gathered(head):
        return xg_ref[aligned(head * own_rows, own_rows), :]

    norm(at.h, x_ref[...])
    near()
    norm(at.sib, gathered(at.sib))
    forward()
    norm(at.xn, gathered(at.xn))
    far()
    norm(at.xs, gathered(at.xs))
    for copy in own_weights:
        copy.wait()
    for i, (_, cols) in reversed(list(enumerate(columns))):
        lanes.arrived(ws + i, weight_rows(at.oy, cols), fsdp=at.oy)
        if i == 1:
            lanes.put(wc, weight_rows(at.oy, cols), weight_rows(at.oy, cols), head=at.sib)
    lanes.arrived(wc, weight_rows(at.oy, kv_cols(1 - at.c)), head=at.sib)
    wo_load.wait()
    shared_wo.begin(0)
    for load in w_loads:
        load.wait()
    for k in range(chunks):
        shared_w.begin(k)
    cots.hand_on(1)

    def project(i, _):
        band = aligned(i * TILE, TILE)
        pre = mm(n1_ref[band, :], wqkv_ref[...])
        cosine, sine = cos_ref[band, :], sin_ref[band, :]

        def turned(u):
            return (u * cosine + pltpu.roll(u, HEAD // 2, 1) * sine).astype(BF16)

        for hh in range(heads):
            q_ref[hh, band, :] = turned(pre[:, hh * HEAD:(hh + 1) * HEAD] * SCORE_LOG2)
        kv_ref[me, 0, band, :] = turned(pre[:, qcols:qcols + HEAD])
        kv_ref[me, 1, band, :] = pre[:, qcols + HEAD:].astype(BF16)
        return 0

    lax.fori_loop(0, rows // TILE, project, 0)

    kvs, kvc = lanes.slots(blocks), lanes.slots(blocks)

    def kv_half(b, core):
        return kv_ref.at[b, core]

    lanes.put(kvs + me, kv_half(me, at.c), kv_half(me, at.c), when=me < blocks - 1, blk=me + 1)
    late = [copy_here(q_ref, q_out), copy_here(n1_ref, n1_out), copy_here(wqkv_ref, wqkv_out), copy_here(wo_ref.at[own_half, :], wo_out.at[own_half, :]),
            copy_here(w_ref.at[:, at.y], w_out.at[:, at.y])]

    m_ref[...] = jnp.full_like(m_ref, MASKED)
    l_ref[...] = jnp.zeros_like(l_ref)
    acc_ref[...] = jnp.zeros_like(acc_ref)

    def transpose_values(b):
        vt_ref[...] = kv_ref[b, 1].astype(F32).T.astype(BF16)

    transpose_values(me)
    for i in range(rows // TILE):
        n = (i + 1) * TILE

        def diagonal(hh, _, i=i, n=n):
            attend_tile(hh, slice(i * TILE, n), kv_ref[me, 0, :n, :], vt_ref[:, :n], q_ref, start_ref,
                        m_ref, l_ref, acc_ref, me * rows, me * rows + i * TILE)
            return 0

        lax.fori_loop(0, heads, diagonal, 0)

    def block(b):
        transpose_values(b)

        def tile(t, _):
            hh, i = t // (rows // TILE), t % (rows // TILE)
            cols = pl.ds(pl.multiple_of(i * TILE, TILE), TILE)
            attend_tile(hh, cols, kv_ref[b, 0], vt_ref[...], q_ref, start_ref,
                        m_ref, l_ref, acc_ref, b * rows, None)
            return 0

        lax.fori_loop(0, heads * (rows // TILE), tile, 0)

    ticks = [[functools.partial(cots.hand_on, 2), functools.partial(shared_wo.spread, 0),
              functools.partial(shared_w.spread, 0)],
             [functools.partial(shared_w.spread, 1), functools.partial(shared_wo.forward, 0)],
             [functools.partial(shared_w.forward, 0)],
             [functools.partial(shared_w.forward, 1)] + [functools.partial(cots.hand_on, d) for d in range(3, blocks)]]

    def tick():
        if ticks:
            for f in ticks.pop(0):
                f()

    for d in range(1, blocks):
        b = jnp.maximum(me - d, 0)
        there = me >= d
        lanes.arrived(kvs + b, kv_half(b, at.c), when=there, blk=me - 1)
        lanes.put(kvs + b, kv_half(b, at.c), kv_half(b, at.c), when=there & (me < blocks - 1), blk=me + 1)
        lanes.put(kvc + b, kv_half(b, at.c), kv_half(b, at.c), when=there, head=at.sib)
        lanes.arrived(kvc + b, kv_half(b, 1 - at.c), when=there, head=at.sib)
        pl.when(there)(functools.partial(block, b))
        if d < blocks - 1:
            tick()

    for hh in range(heads):
        total = l_ref[hh]
        done = acc_ref[hh] / total
        ot_ref[hh * HEAD:(hh + 1) * HEAD, :] = done.astype(BF16)
        o_ref[:, hh * HEAD:(hh + 1) * HEAD] = done.T.astype(BF16)
        lse_ref[hh] = m_ref[hh] + jnp.log2(total)
    kv_copies = [pltpu.make_async_copy(kv_ref.at[b], kv_out.at[b], load_sem.at[16 + b]) for b in range(blocks)]
    for b, copy in enumerate(kv_copies):
        pl.when(b <= me)(copy.start)
    while ticks:
        tick()
    shared_wo.finish(0)
    other_half = pl.ds(pl.multiple_of(at.oy * half, half), half)
    late.append(copy_here(wo_ref.at[other_half, :], wo_out.at[other_half, :]))
    late.append(copy_here(cot_ref, cot_out))
    for k in range(spread_here):
        shared_w.finish(k)
    for k in range(spread_here, chunks):
        shared_w.landed(k)
    late.append(copy_here(w_ref.at[:, at.oy], w_out.at[:, at.oy]))
    for copy in late:
        copy.wait()
    for b, copy in enumerate(kv_copies):
        pl.when(b <= me)(copy.wait)
    lanes.drain()


def front(blocks, x, small, wq, wkv, wo, win, wout, cot, cosine, sine, start):
    own_rows, width = x.shape
    rows = cosine.shape[0]
    half = wq.shape[0]
    heads = QUERY_HEADS * own_rows // rows
    qcols = heads * HEAD
    ffe = wout.shape[1]
    vm = pl.BlockSpec(memory_space=pltpu.VMEM)
    hbm = pl.BlockSpec(memory_space=pl.ANY)
    sds = jax.ShapeDtypeStruct
    return pl.pallas_call(
        front_kernel,
        out_shape=(
            sds((rows, qcols), BF16),
            sds((qcols, rows), BF16),
            sds((heads, 1, rows), F32),
            sds((small.shape[0], width), BF16),
            sds((heads, rows, HEAD), BF16),
            sds((rows, width), BF16),
            sds((width, qcols + 2 * HEAD), BF16),
            sds((blocks, 2, rows, HEAD), BF16),
            sds((width, width), BF16),
            sds((2, 2, half, width + half), BF16),
            sds((blocks, own_rows, width), BF16),
        ),
        in_specs=[vm, vm] + [hbm] * 6 + [vm] * 3,
        out_specs=[vm] * 4 + [hbm] * 7,
        scratch_shapes=[
            pltpu.VMEM((heads, rows, HEAD), BF16),
            pltpu.VMEM((rows, width), BF16),
            pltpu.VMEM((rows, width), BF16),
            pltpu.VMEM(small.shape, BF16),
            pltpu.VMEM((width, qcols + 2 * HEAD), BF16),
            pltpu.VMEM((blocks, 2, rows, HEAD), BF16),
            pltpu.VMEM((heads, 1, rows), F32),
            pltpu.VMEM((heads, 1, rows), F32),
            pltpu.VMEM((heads, HEAD, rows), F32),
            pltpu.VMEM((HEAD, rows), BF16),
            pltpu.VMEM((width, width), BF16),
            pltpu.VMEM((2, 2, half, width + half), BF16),
            pltpu.VMEM((blocks, own_rows, width), BF16),
            pltpu.SemaphoreType.DMA((16 + blocks,)),
        ] + semaphores(blocks),
        compiler_params=pltpu.CompilerParams(
            vmem_limit_bytes=VMEM_BYTES, collective_id=0, has_side_effects=True),
    )(x, small, wq, wkv, wo, win, wout, cot, cosine, sine, start)


class ColumnSum:
    CHUNKS = 4

    def __init__(self, at, lanes, part, land):
        self.at, self.lanes, self.part, self.land = at, lanes, part, land
        self.rows = part.shape[1] // self.CHUNKS
        self.recv = lanes.slots((at.blocks + 1) * self.CHUNKS)
        self.sent = lanes.sends(at.blocks * self.CHUNKS)

    def copy(self, b, ch):
        at = self.at
        travel = jnp.where(b < at.z, -1, 1)
        there = at.z + travel
        slot = jnp.where((there == b) & (b > at.z), at.blocks, b)
        rows = pl.ds(ch * self.rows, self.rows)
        return remote(self.part.at[b, rows, :], self.land.at[slot, rows, :],
                      self.lanes.send.at[self.sent + b * self.CHUNKS + ch],
                      self.lanes.recv.at[self.recv + slot * self.CHUNKS + ch], blk=there)

    def landed(self, slot, ch, origin):
        rows = pl.ds(ch * self.rows, self.rows)
        place = self.land.at[slot, rows, :]
        remote(place, place, self.lanes.send.at[0], self.lanes.recv.at[self.recv + slot * self.CHUNKS + ch],
               blk=origin).wait_recv()

    def first_send(self, b):
        at = self.at

        @pl.when(((b < at.z) & (at.z == at.blocks - 1)) | ((b > at.z) & (at.z == 0)))
        def _():
            for ch in range(self.CHUNKS):
                self.copy(b, ch).start()

    def relay(self, phase, d, add):
        at = self.at
        s = jnp.where(at.z * 2 >= at.blocks, -1, 1) * (1 - 2 * phase)
        b, origin = at.z + s * d, at.z - s
        safe = jnp.clip(b, 0, at.blocks - 1)

        @pl.when((b >= 0) & (b < at.blocks) & (origin >= 0) & (origin < at.blocks))
        def _():
            for ch in range(self.CHUNKS):
                self.landed(safe, ch, origin)
                add(safe, pl.ds(ch * self.rows, self.rows))
                self.copy(safe, ch).start()

    def arrive(self, side, use):
        at = self.at
        slot, origin = (at.z, at.z + 1) if side == 0 else (at.blocks, at.z - 1)

        @pl.when((origin >= 0) & (origin < at.blocks))
        def _():
            for ch in range(self.CHUNKS):
                self.landed(slot, ch, origin)
            use(slot)

    def finish(self):
        at = self.at
        for b in range(at.blocks):
            @pl.when(b != at.z)
            def _(b=b):
                for ch in range(self.CHUNKS):
                    self.copy(b, ch).wait_send()


LANES = 128
HALF_LANES = LANES // 2


def split_lanes(value):
    high = value.astype(BF16).astype(F32)
    return (high + pltpu.roll(value - high, HALF_LANES, 1)).astype(BF16)


def expert_kernel(o_ref, x_ref, small_ref, chosen_ref, wo_hbm, w_hbm, cot_hbm,
                  res_out, grad_out, attn_out, small_out, sums_out, y_out, core_land, *rest):
    big = cot_hbm.shape[0] > 4
    if big:
        xb_ref, dx_ref, land_ref, *rest = rest
        (xb_stage, dx_stage, land_stage, g_ref, *rest) = rest
    else:
        xb_ref, dx_ref, land_ref, *rest = rest
    (mix_ref, w_ref, cot_ref, acc_ref, gate_ref, dgu_ref, ga_ref, xt_ref, gat_ref, gg_ref, y_ref, stage_ref,
     gates_ref, router_ref, load_sem, y_sem, send_sem, recv_sem) = rest
    own_rows, width = x_ref.shape
    blocks = cot_hbm.shape[0]
    qcols = o_ref.shape[1]
    half = width // 2
    experts, _, ffe, _ = w_ref.shape
    at = Place(blocks)
    me = at.z
    lanes = Lanes(send_sem, recv_sem)
    at.enter()
    every = blocks * own_rows
    if big:
        wo_rows = [(slice(y * half, (y + 1) * half), g_ref.at[0, y, :, :width]) for y in range(2)]
    else:
        wo_rows = [(slice(0, every), dgu_ref.at[0]), (slice(every, width), dgu_ref.at[1, :width - every])]
    wo_load = [pltpu.make_async_copy(wo_hbm.at[rows, :], place, load_sem.at[y])
               for y, (rows, place) in enumerate(wo_rows)]
    for load in wo_load:
        load.start()
    quarter = half // 4
    here = aligned(at.h * quarter, quarter)
    w_loads = [pltpu.make_async_copy(w_hbm.at[place], w_ref.at[place], load_sem.at[4 + i])
               for i, place in enumerate(((0,), (1, at.y), (1, at.oy, here)))]
    for load in w_loads:
        load.start()
    late = Shared(at, lanes, 4, None, functools.partial(weight_chunk, w_ref))
    if not big:
        cot_loads = [pltpu.make_async_copy(cot_hbm.at[b], cot_ref.at[b * own_rows:(b + 1) * own_rows, :],
                                           load_sem.at[7 + b]) for b in range(blocks)]
        for load in cot_loads:
            load.start()

    total_experts = experts * blocks
    srows = small_ref.shape[0]
    is_router = lax.broadcasted_iota(jnp.int32, (srows, width), 0) < total_experts
    router_ref[...] = jnp.zeros_like(router_ref)
    router_ref[:srows, :] = jnp.where(is_router, small_ref[...].astype(F32), 0.0).astype(BF16)
    gain_two = small_ref[total_experts + 1:total_experts + 2, :].astype(F32)

    mixes = lanes.slots(4)

    def mix_cols(head):
        return mix_ref.at[:, pl.ds(pl.multiple_of(head * qcols, HEAD), qcols)]

    for head in (at.xn, at.xs, at.sib):
        lanes.put(mixes + at.h, o_ref.at[aligned(head * own_rows, own_rows), :], mix_cols(at.h), head=head)
    mix_ref[:, pl.ds(pl.multiple_of(at.h * qcols, HEAD), qcols)] = o_ref[aligned(at.h * own_rows, own_rows), :]
    for head in (at.sib, at.xn, at.xs):
        lanes.arrived(mixes + head, mix_cols(head), head=head)
    for load in w_loads:
        load.wait()
    for k in (2, 3):
        late.scatter(k)
    for load in wo_load:
        load.wait()
    step = 512
    for i in range(width // step):
        cols = slice(i * step, (i + 1) * step)
        res_out[:, cols] = x_ref[:, cols].astype(F32) + sum(
            mm(mix_ref[:, rows], place[:, cols]) for rows, place in wo_rows)

    def inverse_two():
        res = res_out[...]
        return lax.rsqrt(jnp.mean(res * res, axis=-1, keepdims=True) + NORM_EPSILON)

    n2 = (res_out[...] * inverse_two() * gain_two).astype(BF16)
    chosen = chosen_ref[...] > 0.0
    logits = jnp.where(chosen, mm(n2, router_ref[...], NT), MASKED)
    e_top = jnp.where(chosen, jnp.exp(logits - jnp.max(logits, axis=-1, keepdims=True)), 0.0)
    gates = e_top / jnp.sum(e_top, axis=-1, keepdims=True)
    gates_ref[...] = gates
    own_x = xb_stage if big else xb_ref.at[me]
    own_x[:, :width] = n2
    own_x[:, width:] = split_lanes(gates)

    def move(src, dst):
        copy = pltpu.make_async_copy(src, dst, load_sem.at[3])
        copy.start()
        copy.wait()

    if big:
        move(xb_stage, xb_ref.at[me])
    xs_slot, xs_sent = lanes.slots(blocks), lanes.sends(blocks + 2)

    def xs_copy(b, to, send):
        return remote(xb_ref.at[b], xb_ref.at[b], send_sem.at[xs_sent + send], recv_sem.at[xs_slot + b], blk=to)

    pl.when(me > 0)(lambda: xs_copy(me, me - 1, blocks).start())
    pl.when(me < blocks - 1)(lambda: xs_copy(me, me + 1, blocks + 1).start())

    if big:
        def clear(i, _):
            for e in range(experts):
                for y in range(2):
                    g_ref[e, y, aligned(i * 64, 64), :] = jnp.zeros((64, g_ref.shape[3]), BF16)
            return 0

        lax.fori_loop(0, half // 64, clear, 0)
    else:
        for load in cot_loads:
            load.wait()
    def second_expert():
        for k in (2, 3):
            late.forward(k)
        for k in (2, 3):
            late.finish(k)

    back = ColumnSum(at, lanes, dx_ref, land_ref)
    lane = lax.broadcasted_iota(jnp.int32, (own_rows, LANES), 1)
    tile = 256

    def y_copy(b):
        return pltpu.make_async_copy(y_ref, y_out.at[b], y_sem)

    def block(b, first, between=None):
        if big:
            move(xb_ref.at[b], xb_stage)
            move(cot_hbm.at[b], cot_ref)
        x_in = xb_stage if big else xb_ref.at[b]
        band_all = slice(None) if big else aligned(b * own_rows, own_rows)
        lanes_all = pl.ds(pl.multiple_of(b * own_rows, own_rows), own_rows)
        acc_ref[...] = jnp.zeros_like(acc_ref)
        gg_ref[...] = jnp.zeros_like(gg_ref)

        def hidden(e, _):
            index = me * experts + e
            pack = x_in[:, width:].astype(F32)
            mine = (lane == index) | (lane == index + HALF_LANES)
            gate_ref[...] = jnp.sum(jnp.where(mine, pack, 0.0), axis=1, keepdims=True)

            def inner(t, total):
                low = pl.ds(pl.multiple_of(t * tile, tile), tile)
                high = pl.ds(pl.multiple_of(ffe + t * tile, tile), tile)
                out_cols = slice(width, width + half)
                gate_pre = mm(x_in[:, :half], w_ref[e, 0, :, low]) + mm(x_in[:, half:width], w_ref[e, 1, :, low])
                up = mm(x_in[:, :half], w_ref[e, 0, :, high]) + mm(x_in[:, half:width], w_ref[e, 1, :, high])
                back_h = (mm(cot_ref[band_all, :half], w_ref[e, 0, low, out_cols], NT)
                          + mm(cot_ref[band_all, half:], w_ref[e, 1, low, out_cols], NT))
                value, slope = gelu_parts(gate_pre)
                act = (value * up).astype(BF16).astype(F32)
                gate = gate_ref[...]
                ga_ref[e, :, low] = (gate * act).astype(BF16)
                if not big:
                    gat_ref[e, low, lanes_all] = (gate * act).T.astype(BF16)
                d_act = gate * back_h
                dgu_ref[e, band_all, low] = (d_act * up * slope).astype(BF16)
                dgu_ref[e, band_all, high] = (d_act * value).astype(BF16)
                return total + jnp.sum(act * back_h, axis=1, keepdims=True)

            total = lax.fori_loop(0, ffe // tile, inner, jnp.zeros((own_rows, 1), F32))
            gg_ref[...] += jnp.where(lane == index, total, 0.0)
            for y in range(2):
                acc_ref[:, y * half:(y + 1) * half] += mm(dgu_ref[e, band_all, :], w_ref[e, y, :, :width], NT)
            return 0

        if between is None:
            lax.fori_loop(0, experts, hidden, 0)
        else:
            hidden(0, 0)
            between()
            for e in range(1, experts):
                hidden(e, 0)
        part = dx_stage if big else dx_ref.at[b]
        part[:, :width] = acc_ref[...].astype(BF16)
        part[:, width:] = split_lanes(gg_ref[...])
        if big:
            move(dx_stage, dx_ref.at[b])
        back.first_send(b)

        if big:
            xt_ref[...] = x_in[:, :width].astype(F32).T.astype(BF16)

            def weights(e, _):
                gat_ref[0] = ga_ref[e].astype(F32).T.astype(BF16)

                def rows(i, _):
                    band = aligned(i * tile, tile)
                    for y in range(2):
                        x_cols = xt_ref[aligned(y * half + i * tile, tile), :]
                        for n in range(width // step):
                            cols = slice(n * step, (n + 1) * step)
                            total = g_ref[e, y, band, cols].astype(F32) + mm(x_cols, dgu_ref[e, :, cols])
                            g_ref[e, y, band, cols] = total.astype(BF16)
                        out_cols = slice(width, width + half)
                        total = (g_ref[e, y, band, out_cols].astype(F32)
                                 + mm(gat_ref[0, band, :], cot_ref[:, y * half:(y + 1) * half]))
                        g_ref[e, y, band, out_cols] = total.astype(BF16)
                    return 0

                return lax.fori_loop(0, half // tile, rows, 0)

            lax.fori_loop(0, experts, weights, 0)
        else:
            xt_ref[:, lanes_all] = x_in[:, :width].astype(F32).T.astype(BF16)

        if not first:
            y_copy(b).wait()
        for y in range(2):
            total = mm(ga_ref[0], w_ref[0, y, :, width:])
            for e in range(1, experts):
                total = total + mm(ga_ref[e], w_ref[e, y, :, width:])
            y_ref[:, y * half:(y + 1) * half] = total.astype(BF16)
        y_copy(b).start()

    def distance(d, _):
        for b, origin, to in ((me - d, me - 1, me + 1), (me + d, me + 1, me - 1)):
            @pl.when((b >= 0) & (b < blocks))
            def _(b=b, origin=origin, to=to):
                xs_copy(b, origin, 0).wait_recv()
                pl.when((to >= 0) & (to < blocks))(lambda: xs_copy(b, to, b).start())

        def side(s, _):
            b = jnp.where(s == 0, me - d, me + d)

            @pl.when((b >= 0) & (b < blocks))
            def _():
                block(jnp.clip(b, 0, blocks - 1), False)

            return 0

        return lax.fori_loop(0, 2, side, 0)

    block(me, True, second_expert)
    lax.fori_loop(1, blocks, distance, 0)
    y_copy(me).wait()

    def add(b, rows):
        if big:
            move(dx_ref.at[b, rows, :], dx_stage.at[rows, :])
            move(land_ref.at[b, rows, :], land_stage.at[rows, :])
            dx_stage[rows, :] = (dx_stage[rows, :].astype(F32) + land_stage[rows, :].astype(F32)).astype(BF16)
            move(dx_stage.at[rows, :], dx_ref.at[b, rows, :])
        else:
            dx_ref[b, rows, :] = (dx_ref[b, rows, :].astype(F32) + land_ref[b, rows, :].astype(F32)).astype(BF16)

    late.settle()
    total_ref = g_ref if big else w_ref

    def weights_of(e):
        def rows(i, _):
            cols = pl.ds(pl.multiple_of(i * tile, tile), tile)
            for y in range(2):
                total = mm(xt_ref[y * half:(y + 1) * half, :], dgu_ref[e, :, cols])
                total_ref[e, y, :, cols] = total.astype(BF16)
            return 0

        def outs(i, _):
            for y in range(2):
                cols = pl.ds(pl.multiple_of(y * half + i * tile, tile), tile)
                place = pl.ds(pl.multiple_of(width + i * tile, tile), tile)
                total_ref[e, y, :, place] = mm(gat_ref[e], cot_ref[:, cols]).astype(BF16)
            return 0

        lax.fori_loop(0, 2 * ffe // tile, rows, 0)
        lax.fori_loop(0, half // tile, outs, 0)

    chunks = 4
    piece = half // chunks
    cores = lanes.slots(chunks)
    back.relay(0, 1, add)
    if not big:
        weights_of(1 - at.c)
    for k in range(chunks):
        band = pl.ds(k * piece, piece)
        lanes.put(cores + k, total_ref.at[1 - at.c, :, band, :], core_land.at[:, band, :], head=at.sib)

    def core_sum(k):
        band = pl.ds(k * piece, piece)
        lanes.arrived(cores + k, core_land.at[:, band, :], head=at.sib)
        move(core_land.at[:, band, :], stage_ref)
        for y in range(2):
            total = total_ref[at.c, y, band, :].astype(F32) + stage_ref[y].astype(F32)
            total_ref[at.c, y, band, :] = total.astype(BF16)

    for d in range(2, blocks):
        back.relay(0, d, add)
    if not big:
        weights_of(at.c)
    for d in range(1, blocks):
        back.relay(1, d, add)
    for k in range(chunks):
        core_sum(k)
    keep = pltpu.make_async_copy(total_ref.at[at.c], sums_out, load_sem.at[0])
    keep.start()

    if big:
        move(dx_ref.at[me], dx_stage)
    own_part = dx_stage if big else dx_ref.at[me]
    acc_ref[...] = own_part[:, :width].astype(F32)
    gg_ref[...] = own_part[:, width:].astype(F32)

    def take(slot):
        if big:
            move(land_ref.at[slot], land_stage)
        came = land_stage if big else land_ref.at[slot]
        acc_ref[...] += came[:, :width].astype(F32)
        gg_ref[...] += came[:, width:].astype(F32)

    for side in range(2):
        back.arrive(side, take)
    both = gg_ref[...]
    gate_grads = jnp.where(lane < HALF_LANES, both + pltpu.roll(both, HALF_LANES, 1), 0.0)
    gates = gates_ref[...]
    d_logits = (gates * (gate_grads - jnp.sum(gates * gate_grads, axis=-1, keepdims=True))).astype(BF16)
    inv = inverse_two()
    hat = res_out[...] * inv
    n2 = (hat * gain_two).astype(BF16)
    small_out[...] = mm(d_logits.astype(F32).T.astype(BF16), n2)[:small_out.shape[0], :]
    d_n2 = acc_ref[...] + mm(d_logits, router_ref[...])
    small_out[total_experts + 1:total_experts + 2, :] = jnp.sum(d_n2 * hat, axis=0, keepdims=True)
    pulled = d_n2 * gain_two
    if big:
        move(cot_hbm.at[me], cot_ref)
    own_cot = cot_ref[...] if big else cot_ref[aligned(me * own_rows, own_rows), :]
    grad = own_cot.astype(F32) + inv * (pulled - hat * jnp.mean(pulled * hat, axis=-1, keepdims=True))
    grad_out[...] = grad
    attn_out[...] = grad.astype(BF16)
    keep.wait()
    for b in range(blocks):
        up, down = (b < me) & (me < blocks - 1), (b > me) & (me > 0)
        pl.when(up)(lambda b=b: xs_copy(b, me + 1, b).wait_send())
        pl.when(down)(lambda b=b: xs_copy(b, me - 1, b).wait_send())
    pl.when(me > 0)(lambda: xs_copy(me, me - 1, blocks).wait_send())
    pl.when(me < blocks - 1)(lambda: xs_copy(me, me + 1, blocks + 1).wait_send())
    back.finish()
    lanes.drain()


def expert_layer(o, x, small, chosen, wo, w, cot):
    own_rows, width = x.shape
    blocks = cot.shape[0]
    experts, _, half, wide = w.shape
    ffe = half
    pack = width + LANES
    big = blocks > 4
    kept = own_rows if big else blocks * own_rows
    vm = pl.BlockSpec(memory_space=pltpu.VMEM)
    hbm = pl.BlockSpec(memory_space=pl.ANY)
    sds = jax.ShapeDtypeStruct
    column = [((blocks, own_rows, pack), BF16), ((blocks, own_rows, pack), BF16), ((blocks + 1, own_rows, pack), BF16)]
    if big:
        extra_out, extra_spec = tuple(sds(*c) for c in column), [hbm] * 3
        extra_scratch = [pltpu.VMEM((own_rows, pack), BF16)] * 3 + [pltpu.VMEM(w.shape, BF16)]
    else:
        extra_out, extra_spec = (), []
        extra_scratch = [pltpu.VMEM(*c) for c in column]
    outs = pl.pallas_call(
        expert_kernel,
        out_shape=(
            sds((own_rows, width), F32),
            sds((own_rows, width), F32),
            sds((own_rows, width), BF16),
            sds((-(-(experts * blocks + 2) // 8) * 8, width), F32),
            sds((2, half, wide), BF16),
            sds((blocks, own_rows, width), BF16),
            sds((2, half, wide), BF16),
        ) + extra_out,
        in_specs=[vm] * 4 + [hbm] * 3,
        out_specs=[vm] * 4 + [hbm] * 3 + extra_spec,
        scratch_shapes=extra_scratch + [
            pltpu.VMEM((own_rows, width), BF16),
            pltpu.VMEM(w.shape, BF16),
            pltpu.VMEM((kept, width), BF16),
            pltpu.VMEM((own_rows, width), F32),
            pltpu.VMEM((own_rows, 1), F32),
            pltpu.VMEM((experts, kept, 2 * ffe), BF16),
            pltpu.VMEM((experts, own_rows, ffe), BF16),
            pltpu.VMEM((width, kept), BF16),
            pltpu.VMEM((experts, ffe, kept), BF16),
            pltpu.VMEM((own_rows, LANES), F32),
            pltpu.VMEM((own_rows, width), BF16),
            pltpu.VMEM((2, half // 4, wide), BF16),
            pltpu.VMEM((own_rows, LANES), F32),
            pltpu.VMEM((LANES, width), BF16),
            pltpu.SemaphoreType.DMA((7 + blocks,)),
            pltpu.SemaphoreType.DMA,
        ] + semaphores(blocks),
        compiler_params=pltpu.CompilerParams(
            vmem_limit_bytes=VMEM_BYTES, collective_id=1, has_side_effects=True),
    )(o, x, small, chosen, wo, w, cot)
    return outs[:6]


class ExpertSums:
    CHUNKS = 8

    def __init__(self, at, lanes, grads, own, land_y, land_x, out, load_sem, keep_sem):
        self.at, self.lanes = at, lanes
        self.grads, self.own, self.out = grads, own, out
        self.land_y, self.land_x = land_y, land_x
        self.load_sem, self.keep_sem = load_sem, keep_sem
        self.rows = grads.shape[1] // self.CHUNKS
        n = self.CHUNKS
        self.ys, self.xr, self.cg = [lanes.slots(n) for _ in range(3)]
        self.kept = []

    def chunk(self, k):
        return pl.ds(k * self.rows, self.rows)

    def load(self):
        self.loads = [pltpu.make_async_copy(self.grads.at[y], self.own.at[y], self.load_sem.at[i])
                      for i, y in enumerate((self.at.oy, self.at.y))]
        for copy in self.loads:
            copy.start()

    def to_y(self, first, last):
        if first == 0:
            self.loads[0].wait()
        for k in range(first, last):
            rows = self.chunk(k)
            self.lanes.put(self.ys + k, self.own.at[self.at.oy, rows, :], self.land_y.at[rows, :], fsdp=self.at.oy)

    def to_x(self, k):
        at, rows = self.at, self.chunk(k)
        if k == 0:
            self.loads[1].wait()
        self.lanes.arrived(self.ys + k, self.land_y.at[rows, :], fsdp=at.oy)
        total = self.own[at.y, rows, :].astype(F32) + self.land_y[rows, :].astype(F32)
        self.own[at.y, rows, :] = total.astype(BF16)
        self.lanes.put(self.xr + k, self.own.at[at.y, rows, :], self.land_x.at[rows, :], head=at.xn)

    def share(self, k):
        at, rows = self.at, self.chunk(k)
        self.lanes.arrived(self.xr + k, self.land_x.at[rows, :], head=at.xn)
        total = self.own[at.y, rows, :].astype(F32) + self.land_x[rows, :].astype(F32)
        self.land_x[rows, :] = total.astype(BF16)
        done, place = self.land_x.at[rows, :], self.out.at[at.c, rows, :]
        self.lanes.put(self.cg + k, done, place, head=at.sib)
        keep = pltpu.make_async_copy(done, place, self.keep_sem.at[k])
        keep.start()
        self.kept.append(keep)

    def finish(self):
        at = self.at
        for k in range(self.CHUNKS):
            self.lanes.arrived(self.cg + k, self.out.at[1 - at.c, self.chunk(k), :], head=at.sib)
            self.kept[k].wait()


class OutputSums:
    PARTS = 4

    def __init__(self, at, lanes, grad, land_y, land_z, out):
        self.at, self.lanes, self.grad = at, lanes, grad
        self.land_y, self.land_z, self.out = land_y, land_z, out
        self.rows = grad.shape[0] // self.PARTS
        self.ys = lanes.slots()
        self.zr, self.zg = lanes.slots(at.blocks), lanes.slots(self.PARTS)
        self.xg, self.cg = lanes.slots(), lanes.slots(self.PARTS)
        self.owner, self.giver = at.y == at.x, at.y != at.x
        self.summer = at.z < self.PARTS
        self.part = at.z % self.PARTS
        self.mine = aligned(self.part * self.rows, self.rows)

    def to_z(self):
        at = self.at
        for p in range(self.PARTS):
            self.lanes.put(self.zr + at.z, self.grad.at[pl.ds(p * self.rows, self.rows), :], self.land_z.at[at.z],
                           when=at.z != p, blk=p)

    def to_y(self, fetch):
        at = self.at
        for z in at.others():
            self.lanes.arrived(self.zr + z, self.land_z.at[z], when=self.summer, blk=z)

        @pl.when(self.summer)
        def _():
            total = self.grad[self.mine, :].astype(F32)
            for z in at.others():
                total = total + fetch(self.land_z.at[z])[...].astype(F32)
            self.grad[self.mine, :] = total.astype(BF16)

        self.lanes.put(self.ys, self.grad.at[self.mine, :], self.land_y, when=self.summer & self.giver, fsdp=at.oy)

    def place(self, core, p):
        return self.out.at[aligned(core * self.PARTS * self.rows + p * self.rows, self.rows), :]

    def share(self):
        at, p = self.at, self.part
        ready = self.summer & self.owner
        self.lanes.arrived(self.ys, self.land_y, when=ready, fsdp=at.oy)
        at_rows = aligned(at.c * self.PARTS * self.rows + p * self.rows, self.rows)

        @pl.when(ready)
        def _():
            total = self.grad[self.mine, :].astype(F32) + self.land_y[...].astype(F32)
            self.out[at_rows, :] = total.astype(BF16)

        place = self.place(at.c, p)
        self.lanes.put(self.xg, place, place, when=ready, head=at.xn)
        self.spread(ready)

    def spread(self, ready):
        at, place = self.at, self.place(self.at.c, self.part)
        for z in at.others():
            self.lanes.put(self.zg + self.part, place, place, when=ready, blk=z)
        self.lanes.put(self.cg + self.part, place, place, when=ready, head=at.sib)

    def take_over(self):
        ready = self.summer & self.giver
        self.lanes.arrived(self.xg, self.place(self.at.c, self.part), when=ready, head=self.at.xn)
        self.spread(ready)

    def pass_on(self):
        at = self.at
        for p in range(self.PARTS):
            place, later = self.place(at.c, p), at.z != p
            self.lanes.arrived(self.zg + p, place, when=later, blk=p)
            self.lanes.put(self.cg + p, place, place, when=later, head=at.sib)

    def finish(self):
        at = self.at
        for p in range(self.PARTS):
            self.lanes.arrived(self.cg + p, self.place(1 - at.c, p), head=at.sib)


def back_kernel(attn_ref, q_ref, ot_ref, start_ref, lse_ref, x_ref, cos_ref, sin_ref, gain_ref, small_ref,
                kv_in, wo_hbm, grads_hbm, y_in, res_hbm, res_grad_hbm, n1_hbm, w_hbm,
                block_out, tokens_out, small_out, kv_out, experts_out, output_out, query_out, y_land, *rest):
    blocks = kv_in.shape[0]
    big = blocks > 4
    dkv_stage = dwo_stage = None
    if big:
        yp_ref, dkv_land, dkv_sib, dwo_z, kv_ref, dkv_stage, dwo_stage, y_stage, kv_stage, *rest = rest
    else:
        yp_ref, dkv_land, dkv_sib, dwo_z, kv_ref, *rest = rest
    (dq_ref, dk_ref, dv_ref, kt_ref, delta_ref, do_ref, ag_ref, wo_ref, dwo_ref, dwo_y, dwo_land,
     own_ref, ey_ref, ex_ref, acc_ref, y_other, w_ref, dpre_ref, dn_sib, dn_x, dw_ref, dw_y, dw_z,
     sm_ref, sm_a, sm_b, sm_y, sm_z, land_ref, dkv_ref, n1t_ref, load_sem, keep_sem, send_sem, recv_sem) = rest
    heads, rows, _ = q_ref.shape
    own_rows, width = attn_ref.shape
    half = width // 2
    qcols = heads * HEAD
    gain_row = 2 * blocks
    at = Place(blocks)
    me = at.z
    lanes = Lanes(send_sem, recv_sem)
    at.enter()
    experts = ExpertSums(at, lanes, grads_hbm, own_ref, ey_ref, ex_ref, experts_out, load_sem, keep_sem)
    output = OutputSums(at, lanes, dwo_ref, dwo_y, dwo_z, dwo_land)
    sums = ColumnSum(at, lanes, yp_ref, y_land)
    experts.load()
    forward, near, far, passed = gather_heads(at, lanes, attn_ref, ag_ref)

    def load(src, dst, sem):
        copy = pltpu.make_async_copy(src, dst, load_sem.at[sem])
        copy.start()
        return copy

    def move(src, dst):
        load(src, dst, 5).wait()

    wo_load = load(wo_hbm.at[aligned(at.h * qcols, qcols), :], wo_ref, 2)
    y_load = load(y_in, yp_ref, 3)
    if not big:
        kv_load = load(kv_in, kv_ref, 4)
    experts.to_y(0, 6)
    y_load.wait()
    for b in range(blocks):
        sums.first_send(b)

    def add(b, band):
        move(y_land.at[b, band, :], y_other.at[band, :])
        if big:
            move(yp_ref.at[b, band, :], y_stage.at[band, :])
            y_stage[band, :] = (y_stage[band, :].astype(F32) + y_other[band, :].astype(F32)).astype(BF16)
            move(y_stage.at[band, :], yp_ref.at[b, band, :])
        else:
            yp_ref[b, band, :] = (yp_ref[b, band, :].astype(F32) + y_other[band, :].astype(F32)).astype(BF16)

    def fetch(stage):
        def get(ref):
            if big:
                move(ref, stage)
                return stage
            return ref
        return get

    wo_load.wait()

    def mix_back(head):
        band = aligned(head * own_rows, own_rows)
        grad = mm(ag_ref[band, :], wo_ref[...], NT).astype(BF16)
        for hh in range(heads):
            do_ref[hh, band, :] = grad[:, hh * HEAD:(hh + 1) * HEAD]

    def turn(i):
        band = slice(i * own_rows, (i + 1) * own_rows)
        move(n1_hbm.at[band, :], y_other)
        n1t_ref[:, band] = y_other[...].astype(F32).T.astype(BF16)

    ag_ref[aligned(at.h * own_rows, own_rows), :] = attn_ref[...]
    mix_back(at.h)
    turn(0)
    near()
    mix_back(at.sib)
    for i in range(1, rows // own_rows):
        turn(i)
    experts.to_x(0)
    forward()
    mix_back(at.xn)
    far()
    mix_back(at.xs)
    step = 512

    def weight_back(i, _):
        cols = pl.ds(pl.multiple_of(i * step, step), step)
        dwo_ref[:, cols] = mm(ot_ref[...], ag_ref[:, cols]).astype(BF16)
        return 0

    lax.fori_loop(0, width // step, weight_back, 0)
    output.to_z()
    kv_from = pl.ds(pl.multiple_of(qcols + at.c * HEAD, HEAD), HEAD)
    w_loads = [load(w_hbm.at[:, :qcols], w_ref.at[:, :qcols], 2), load(w_hbm.at[:, kv_from], w_ref.at[:, qcols:], 3)]
    dq_ref[...] = jnp.zeros_like(dq_ref)
    for hh in range(heads):
        prod = do_ref[hh].astype(F32).T * ot_ref[hh * HEAD:(hh + 1) * HEAD, :].astype(F32)
        delta_ref[hh] = jnp.sum(prod, axis=0, keepdims=True)
    if not big:
        kv_load.wait()

    experts.to_x(1)
    beside = [[(experts.to_x, 2), (experts.share, 0)],
              [(experts.to_x, 3), (experts.share, 1)],
              [(experts.to_x, 4), (experts.share, 2)]]

    def advance():
        for f, k in (beside.pop(0) if beside else ()):
            f(k)

    def opening(b):
        if big:
            move(kv_in.at[b], kv_stage)
        kv = kv_stage if big else kv_ref.at[b]
        kt_ref[...] = kv[0].astype(F32).T.astype(BF16)
        dk_ref[...] = jnp.zeros_like(dk_ref)
        dv_ref[...] = jnp.zeros_like(dv_ref)
        return kv

    def closing(b, kv):
        kv[0] = (dk_ref[...] * LN2).astype(BF16)
        kv[1] = dv_ref[...].astype(BF16)
        if big:
            move(kv_stage, kv_ref.at[b])

    def block(b):
        kv = opening(b)

        def tile(t, _):
            hh, i = t // (rows // TILE), t % (rows // TILE)
            cols = pl.ds(pl.multiple_of(i * TILE, TILE), TILE)
            unattend_tile(hh, cols, kv[0], kv[1], kt_ref[...], q_ref, do_ref,
                          start_ref, lse_ref, delta_ref, dq_ref, dk_ref, dv_ref, b * rows, None)
            return 0

        lax.fori_loop(0, heads * (rows // TILE), tile, 0)
        closing(b, kv)

    pair, column = lanes.slots(blocks), lanes.slots(blocks)

    def to_sibling(b, when):
        lanes.put(pair + b, kv_ref.at[b, 1 - at.c], dkv_sib.at[b], when=when, head=at.sib)

    def to_column(b):
        lanes.arrived(pair + b, dkv_sib.at[b], when=b < me, head=at.sib)

        @pl.when(b < me)
        def _():
            came = fetch(dkv_stage)(dkv_sib.at[b])
            if big:
                move(kv_ref.at[b, at.c], kv_stage.at[at.c])
            kv = kv_stage if big else kv_ref.at[b]
            kv[at.c] = (kv[at.c].astype(F32) + came[...].astype(F32)).astype(BF16)
            if big:
                move(kv_stage.at[at.c], kv_ref.at[b, at.c])

        lanes.put(column + me, kv_ref.at[b, at.c], dkv_land.at[me], when=b < me, blk=b)

    for b in range(blocks - 1):
        pl.when(b < me)(functools.partial(block, b))
        to_sibling(b, b < me)
        sums.relay(0, b + 1, add)
        advance()
        if b > 0:
            to_column(b - 1)
    while beside:
        advance()
    to_column(blocks - 2)

    kv_own = opening(me)
    for i in range(rows // TILE):
        n = (i + 1) * TILE

        def diagonal(hh, _, i=i, n=n):
            unattend_tile(hh, slice(i * TILE, n), kv_own[0, :n, :], kv_own[1, :n, :], kt_ref[:, :n], q_ref, do_ref,
                          start_ref, lse_ref, delta_ref, dq_ref, dk_ref, dv_ref,
                          me * rows, me * rows + i * TILE)
            return 0

        lax.fori_loop(0, heads, diagonal, 0)
    closing(me, kv_own)
    to_sibling(me, None)
    experts.to_x(5)
    for d in range(1, blocks):
        sums.relay(1, d, add)

    def unrotate(u):
        return u * cos_ref[...] - pltpu.roll(u, HEAD // 2, 1) * sin_ref[...]

    for hh in range(heads):
        dpre_ref[:, hh * HEAD:(hh + 1) * HEAD] = unrotate((dq_ref[hh] * SCORE_SCALE).T).astype(BF16)
    for w_load in w_loads:
        w_load.wait()
    parts = 4
    part = half // parts
    band_rows = 256
    query_cols, keyval_cols = slice(0, qcols), slice(qcols, qcols + HEAD)

    def weight_half(y, cols_out):
        def body(i, _):
            band = aligned(y * half + i * band_rows, band_rows)
            dw_ref[band, cols_out] = mm(n1t_ref[band, :], dpre_ref[:, cols_out]).astype(BF16)
            return 0

        lax.fori_loop(0, half // band_rows, body, 0)

    def weight_part(y, p):
        return aligned(y * half + p * part, part)

    ys = (lanes.slots(parts), lanes.slots(parts))

    def weight_to_y(i, cols_out):
        weight_half(at.oy, cols_out)
        for p in range(parts):
            lanes.put(ys[i] + p, dw_ref.at[weight_part(at.oy, p), cols_out],
                      dw_y.at[pl.ds(p * part, part), cols_out], fsdp=at.oy)

    weight_to_y(0, query_cols)
    experts.share(3)

    @pl.when(at.c == 0)
    def _():
        dkv_ref[...] = dk_ref[...] * LN2

    @pl.when(at.c == 1)
    def _():
        dkv_ref[...] = dv_ref[...]

    lanes.arrived(pair + me, dkv_sib.at[me], head=at.sib)
    dkv_ref[...] += fetch(dkv_stage)(dkv_sib.at[me])[...].astype(F32)
    for z in range(1, blocks):
        @pl.when(me < z)
        def _(z=z):
            lanes.arrived(column + z, dkv_land.at[z], blk=z)
            dkv_ref[...] += fetch(dkv_stage)(dkv_land.at[z])[...].astype(F32)

    dpre_ref[:, qcols:] = jnp.where(at.c == 0, unrotate(dkv_ref[...]), dkv_ref[...]).astype(BF16)
    weight_to_y(1, keyval_cols)
    experts.to_y(6, 8)

    def input_part(head):
        return mm(dpre_ref[aligned(head * own_rows, own_rows), :], w_ref[...], NT)

    lanes.settle(passed[0])

    def dn_ref(i):
        return ag_ref.at[i * own_rows:(i + 1) * own_rows, :]

    relay, direct, across = lanes.slots(), lanes.slots(), lanes.slots()
    dn_ref(0)[...] = input_part(at.xs).astype(BF16)
    lanes.put(relay, dn_ref(0), dn_sib.at[0], head=at.sib)
    dn_ref(2)[...] = input_part(at.sib).astype(BF16)
    lanes.put(direct, dn_ref(2), dn_sib.at[1], head=at.sib)
    lanes.arrived(relay, dn_sib.at[0], head=at.sib)
    dn_ref(1)[...] = (input_part(at.xn) + dn_sib[0].astype(F32)).astype(BF16)
    lanes.put(across, dn_ref(1), dn_x, head=at.xn)
    experts.share(4)
    weight_half(at.y, slice(None))
    output.to_y(fetch(dwo_stage))

    zr = lanes.slots(blocks)
    for p in range(parts):
        rows_p = weight_part(at.y, p)
        for i, cols_out in enumerate((query_cols, keyval_cols)):
            lanes.arrived(ys[i] + p, dw_y.at[pl.ds(p * part, part), cols_out], fsdp=at.oy)
        total = dw_ref[rows_p, :].astype(F32) + dw_y[pl.ds(p * part, part), :].astype(F32)
        dw_ref[rows_p, :] = total.astype(BF16)
        lanes.put(zr + at.z, dw_ref.at[rows_p, :], dw_z.at[at.z], when=at.z != p, blk=p)
    output.share()
    experts.to_x(6)
    experts.share(5)

    move(res_hbm, acc_ref)
    if big:
        move(yp_ref.at[me], y_stage)
    acc_ref[...] += (y_stage if big else yp_ref.at[me])[...].astype(F32)

    def take(slot):
        move(y_land.at[slot], y_other)
        acc_ref[...] += y_other[...].astype(F32)

    for side in range(2):
        sums.arrive(side, take)
    block_out[...] = acc_ref[...].astype(BF16)

    res_load = load(res_grad_hbm, acc_ref, 5)
    own = input_part(at.h)
    lanes.arrived(direct, dn_sib.at[1], head=at.sib)
    own = own + dn_sib[1].astype(F32)
    lanes.arrived(across, dn_x, head=at.xn)
    own = own + dn_x[...].astype(F32)
    x = x_ref[...].astype(F32)
    inv = lax.rsqrt(jnp.mean(x * x, axis=-1, keepdims=True) + NORM_EPSILON)
    hat = x * inv
    pulled = own * gain_ref[gain_row:gain_row + 1, :].astype(F32)
    slope = inv * (pulled - hat * jnp.mean(pulled * hat, axis=-1, keepdims=True))
    res_load.wait()
    tokens_out[...] = (acc_ref[...] + slope).astype(BF16)
    sm_ref[...] = small_ref[...]
    sm_ref[gain_row:gain_row + 1, :] = jnp.sum(own * hat, axis=0, keepdims=True)
    sa, sb, sy, sz = lanes.slots(), lanes.slots(), lanes.slots(), lanes.slots(blocks)
    lanes.put(sa, sm_ref, sm_a, head=at.sib)
    experts.to_x(7)
    experts.share(6)

    p = at.z % parts
    summer = at.z < parts
    zg, xg, cg, cf = lanes.slots(parts), lanes.slots(parts), lanes.slots(parts), lanes.slots(parts)

    def place(head, q):
        return land_ref.at[head, pl.ds(q * part, part), :]

    for z in at.others():
        lanes.arrived(zr + z, dw_z.at[z], when=summer, blk=z)
    mine_w = weight_part(at.y, p)

    @pl.when(summer)
    def _():
        total = dw_ref[mine_w, :].astype(F32)
        for z in at.others():
            total = total + dw_z[z].astype(F32)
        dw_ref[mine_w, :] = total.astype(BF16)
        land_ref[at.h, aligned(p * part, part), :] = total.astype(BF16)

    for z in at.others():
        lanes.put(zg + p, dw_ref.at[mine_w, :], place(at.h, p), when=summer, blk=z)
    lanes.put(xg + p, dw_ref.at[mine_w, :], place(at.h, p), when=summer, head=at.xn)
    lanes.put(cg + p, dw_ref.at[mine_w, :], place(at.h, p), when=summer, head=at.sib)
    lanes.arrived(sa, sm_a, head=at.sib)
    sm_a[...] = sm_a[...] + sm_ref[...]
    lanes.put(sb, sm_a, sm_b, head=at.xn)
    output.take_over()
    experts.share(7)

    lanes.arrived(sb, sm_b, head=at.xn)
    sm_b[...] = sm_a[...] + sm_b[...]
    mine_cols = pl.ds(pl.multiple_of(at.y * half, half), half)
    other_cols = pl.ds(pl.multiple_of(at.oy * half, half), half)
    lanes.put(sy, sm_b.at[:, other_cols], sm_y, fsdp=at.oy)
    for q in range(parts):
        later = at.z != q
        lanes.arrived(zg + q, place(at.h, q), when=later, blk=q)
        lanes.put(xg + q, place(at.h, q), place(at.h, q), when=later, head=at.xn)
        lanes.put(cg + q, place(at.h, q), place(at.h, q), when=later, head=at.sib)
    lanes.arrived(sy, sm_y, fsdp=at.oy)
    sm_z[at.z] = sm_b[:, mine_cols] + sm_y[...]
    for z in at.others():
        lanes.put(sz + at.z, sm_z.at[at.z], sm_z.at[at.z], blk=z)
    output.pass_on()
    for q in range(parts):
        lanes.arrived(xg + q, place(at.xn, q), head=at.xn)
        lanes.put(cf + q, place(at.xn, q), place(at.xn, q), head=at.sib)
    for z in at.others():
        lanes.arrived(sz + z, sm_z.at[z], blk=z)
    total = sm_z[0]
    for z in range(1, blocks):
        total = total + sm_z[z]
    small_out[...] = total
    output.finish()
    keeps = [load(dwo_land, output_out, 0)]
    for q in range(parts):
        lanes.arrived(cg + q, place(at.sib, q), head=at.sib)
        lanes.arrived(cf + q, place(at.xs, q), head=at.sib)
    for head in range(4):
        keeps.append(load(land_ref.at[head, :, :qcols], query_out.at[:, head * qcols:(head + 1) * qcols], 1 + head))
        column_of = (head % 2 * KEYVALUE_HEADS + head // 2) * HEAD
        keeps.append(load(land_ref.at[head, :, qcols:], kv_out.at[:, column_of:column_of + HEAD], 6 + head))
    experts.finish()
    for keep in keeps:
        keep.wait()
    sums.finish()
    lanes.drain()


def backward(attn_grad, q, ot, start, lse, x, cosine, sine, gain, small, kv, wo, grads, y_parts, res, res_grad, n1, w):
    heads, rows, _ = q.shape
    blocks = kv.shape[0]
    own_rows, width = attn_grad.shape
    qcols = heads * HEAD
    _, half, wide = grads.shape
    cols = qcols + HEAD
    srows = small.shape[0]
    n = ExpertSums.CHUNKS
    vm = pl.BlockSpec(memory_space=pltpu.VMEM)
    hbm = pl.BlockSpec(memory_space=pl.ANY)
    part = qcols // OutputSums.PARTS
    sds = jax.ShapeDtypeStruct
    column = [((blocks, own_rows, width), BF16), ((blocks, rows, HEAD), BF16),
              ((blocks, rows, HEAD), BF16), ((blocks, part, width), BF16), (kv.shape, BF16)]
    if blocks > 4:
        extra_out, extra_spec = tuple(sds(*c) for c in column), [hbm] * 5
        extra_scratch = [pltpu.VMEM((rows, HEAD), BF16), pltpu.VMEM((part, width), BF16),
                         pltpu.VMEM((own_rows, width), BF16), pltpu.VMEM((2, rows, HEAD), BF16)]
    else:
        extra_out, extra_spec = (), []
        extra_scratch = [pltpu.VMEM(*c) for c in column]
    return pl.pallas_call(
        back_kernel,
        out_shape=(
            sds((own_rows, width), BF16),
            sds((own_rows, width), BF16),
            sds((srows, half), F32),
            sds((half, 2 * KEYVALUE_HEADS * HEAD), BF16),
            sds((2, half, wide), BF16),
            sds((2 * qcols, width), BF16),
            sds((half, rows // own_rows * qcols), BF16),
            sds((blocks + 1, own_rows, width), BF16),
        ) + extra_out,
        in_specs=[vm] * 10 + [hbm] * 8,
        out_specs=[vm] * 3 + [hbm] * 5 + extra_spec,
        scratch_shapes=extra_scratch + [
            pltpu.VMEM((heads, HEAD, rows), F32),
            pltpu.VMEM((rows, HEAD), F32),
            pltpu.VMEM((rows, HEAD), F32),
            pltpu.VMEM((HEAD, rows), BF16),
            pltpu.VMEM((heads, 1, rows), F32),
            pltpu.VMEM((heads, rows, HEAD), BF16),
            pltpu.VMEM((rows, width), BF16),
            pltpu.VMEM((qcols, width), BF16),
            pltpu.VMEM((qcols, width), BF16),
            pltpu.VMEM((part, width), BF16),
            pltpu.VMEM((2 * qcols, width), BF16),
            pltpu.VMEM((2, half, wide), BF16),
            pltpu.VMEM((half, wide), BF16),
            pltpu.VMEM((half, wide), BF16),
            pltpu.VMEM((own_rows, width), F32),
            pltpu.VMEM((own_rows, width), BF16),
            pltpu.VMEM((width, cols), BF16),
            pltpu.VMEM((rows, cols), BF16),
            pltpu.VMEM((2, own_rows, width), BF16),
            pltpu.VMEM((own_rows, width), BF16),
            pltpu.VMEM((width, cols), BF16),
            pltpu.VMEM((half, cols), BF16),
            pltpu.VMEM((blocks, half // 4, cols), BF16),
            pltpu.VMEM((srows, width), F32),
            pltpu.VMEM((srows, width), F32),
            pltpu.VMEM((srows, width), F32),
            pltpu.VMEM((srows, half), F32),
            pltpu.VMEM((blocks, srows, half), F32),
            pltpu.VMEM((rows // own_rows, half, cols), BF16),
            pltpu.VMEM((rows, HEAD), F32),
            pltpu.VMEM((width, rows), BF16),
            pltpu.SemaphoreType.DMA((10,)),
            pltpu.SemaphoreType.DMA((n,)),
        ] + semaphores(blocks),
        compiler_params=pltpu.CompilerParams(
            vmem_limit_bytes=VMEM_BYTES, collective_id=2, has_side_effects=True),
    )(attn_grad, q, ot, start, lse, x, cosine, sine, gain, small, kv, wo, grads, y_parts, res, res_grad, n1, w)[:7]


def on_device(tokens, documents, routes, cotangent, first_gain, query_weight, keyvalue_weight, output_weight,
              second_gain, router_weight, expert_in, expert_out):
    z = lax.axis_index("blk")
    blocks = lax.axis_size("blk")
    rows, width = tokens.shape[1:]
    group = lax.axis_size("head") * rows
    experts = router_weight.shape[1]
    half = query_weight.shape[0]

    small_rows = -(-(2 + experts) // 16) * 16
    small = jnp.concatenate([router_weight.T, first_gain[None], second_gain[None],
                             jnp.zeros((small_rows - 2 - experts, half), BF16)], axis=0)
    pos = (z * group + jnp.arange(group, dtype=jnp.int32)).astype(F32)
    inverse = jnp.power(ROPE_BASE, -jnp.arange(HEAD // 2).astype(F32) * 2.0 / HEAD)
    angle = pos[:, None] * inverse[None, :]
    cos, sin = jnp.cos(angle), jnp.sin(angle)
    cosine = jnp.concatenate([cos, cos], axis=-1)
    sine = jnp.concatenate([-sin, sin], axis=-1)
    doc = documents[0]
    doc_q = lax.dynamic_slice_in_dim(doc, z * group, group, 0)
    start = sum(jnp.where(doc_q > d, jnp.sum((doc == d).astype(jnp.int32)), 0) for d in range(DOCUMENTS - 1))[None, :]
    chosen = jnp.any(routes[0][:, :, None] == jnp.arange(LANES, dtype=jnp.int32), axis=1).astype(F32)

    mixed, mixed_t, lse, small, q, n1, wqkv, kv_all, wo, w_experts, cots = front(
        blocks, tokens[0], small, query_weight, keyvalue_weight, output_weight, expert_in, expert_out,
        cotangent[0], cosine, sine, start)
    res1, res_grad, attn_grad, d_small, grads, y_parts = expert_layer(
        mixed, tokens[0], small, chosen, wo, w_experts, cots)
    block_out, tokens_grad, d_small, d_keyval, d_experts, d_wo, d_query = backward(
        attn_grad, q, mixed_t, start, lse, tokens[0], cosine, sine, small, d_small,
        kv_all, wo, grads, y_parts, res1, res_grad, n1, wqkv)
    return (block_out[None], tokens_grad[None], d_small[experts], d_query.astype(F32), d_keyval.astype(F32), d_wo.astype(F32),
            d_small[experts + 1], d_small[:experts].T, d_experts[:, :, :width].astype(F32),
            d_experts[:, :, width:].astype(F32))


def solution(mesh):
    token_spec = P("fsdp", ("blk", "head"), None)
    row_spec = P("fsdp", None)
    in_spec = P("blk", "fsdp", None)
    out_spec = P("blk", None, "fsdp")
    return jax.shard_map(
        on_device,
        mesh=mesh,
        in_specs=(token_spec, row_spec, token_spec, token_spec, P("fsdp"), row_spec, row_spec, row_spec, P("fsdp"),
                  row_spec, in_spec, out_spec),
        out_specs=(token_spec, token_spec, P("fsdp"), row_spec, row_spec, row_spec, P("fsdp"), row_spec, in_spec,
                   out_spec),
        check_vma=False,
    )
```
